32 devices in a mesh: section: 8 (over y, x, core), dp: 4 (over z).
Axes of the slice: x: 2, y: 2, z: 4, core: 2. Of those that a mesh axis runs over, the one named last changes fastest.
Arguments:
- inputs: bfloat16 [512, 4096], P(None, 'dp'), may hold values from -6 to 6
- targets: int32 [4096], P('dp'), may hold values from 0 to 255
- mel: bfloat16 [80, 16], P(None, 'dp'), may hold values from -6 to 6
- speakers: int32 [16, 2], P('dp'), may hold values from 0 to 108
- speaker_sample_counts: int32 [109], replicated, may hold values from 16 to 4111
- segment_offsets: int32 [16, 2], P('dp'), may hold values from 64 to 256, as said below
- dilations: int32 [8], P('section'), may hold values from 1 to 32, as said below
- dilated_kernel: bfloat16 [8, 1024, 1024], P('section'), may hold values from -0.1875 to 0.1875
- conditioning_projection: bfloat16 [8, 1024, 80], P('section'), may hold values from -0.5 to 0.5
- dilated_gate_bias: bfloat16 [8, 1024], P('section'), may hold values from -3 to 3
- residual_projection: bfloat16 [8, 512, 512], P('section'), may hold values from -0.75 to 0.75
- skip_projection: bfloat16 [8, 512, 512], P('section'), may hold values from -0.75 to 0.75
- upsample_weight: bfloat16 [256, 80, 80], replicated, may hold values from -0.625 to 0.625
- speaker_table: bfloat16 [80, 109], replicated, may hold values from -5 to 5
- first_output_projection: bfloat16 [512, 512], replicated, may hold values from -0.5 to 0.5
- class_projection: bfloat16 [256, 512], replicated, may hold values from -0.75 to 0.75
Outputs:
- loss: float32 [], replicated
- grad_inputs: bfloat16 [512, 4096], P('section', 'dp')
- grad_w_dil: float32 [8, 1024, 1024], P('section')
- grad_w_cond: float32 [8, 1024, 80], P('section')
- grad_b_gate: float32 [8, 1024], P('section')
- grad_w_res: float32 [8, 512, 512], P('section')
- grad_w_skip: float32 [8, 512, 512], P('section')
- grad_w_up: float32 [256, 80, 80], replicated
- grad_spk_table: float32 [80, 109], replicated
- grad_w_post: float32 [512, 512], replicated
- grad_w_out: float32 [256, 512], replicated
The draws below stay inside these ranges and needn't reach their ends.
Inputs may be any that keep to these rules, and one draw needn't show every extreme that they name: `segment_offsets`: per micro-batch: the second segment begins after 256 // 4 to 128 samples and has 64 to 128 samples; the second column is where it ends. `dilations`: each a power of two.
All inputs are finite; a program needn't handle non-finite values.
Results may differ from the reference program's by a relative error of at most 0.03.
Values may be sent and summed in bfloat16 or wider, within the bound.
A program may use at most 128 MiB of HBM per device.

```python
import math
import jax
import jax.numpy as jnp
import numpy as np
from jax import lax

RESIDUAL_WIDTH = 512
GATE_CHANNELS = 1024
SKIP = 512
MEL = 80
CLS = 256
NSPK = 109
HOP = 256
MBLEN = 256
LAYER_COUNT = 8
MB = 4
BATCHES = 16
TOKENS = 4096
FRAMES = 16
N_DP = 4


def draw_segment_offsets(key, part):
    key = jax.random.fold_in(key, 11)
    key_lead, key_trail, key_rank = jax.random.split(key, 3)
    shortest = MBLEN // 4
    longest = MBLEN // 2
    leading = jax.random.randint(key_lead, (BATCHES,), shortest, longest + 1)
    trailing = jax.random.randint(key_trail, (BATCHES,), shortest, longest + 1)
    ranking = jax.random.permutation(key_rank, BATCHES)
    row_index = jnp.arange(BATCHES)
    full_row = row_index == ranking[0]
    short_row = row_index == ranking[1]
    leading = jnp.where(full_row, longest, jnp.where(short_row, shortest, leading))
    trailing = jnp.where(full_row, longest, trailing)
    return jnp.stack([leading, leading + trailing], axis=1).astype(jnp.int32)


def draw_dilations(key, part):
    key = jax.random.fold_in(key, 23)
    key_level, key_rank = jax.random.split(key)
    top_level = (MBLEN // 8).bit_length() - 1
    levels = jax.random.randint(key_level, (LAYER_COUNT,), 0, top_level + 1)
    ranking = jax.random.permutation(key_rank, LAYER_COUNT)
    layer_index = jnp.arange(LAYER_COUNT)
    levels = jnp.where(layer_index == ranking[0], top_level, levels)
    levels = jnp.where(layer_index == ranking[1], 0, levels)
    return jnp.left_shift(jnp.ones((LAYER_COUNT,), jnp.int32), levels.astype(jnp.int32)).astype(jnp.int32)


def draw_speaker_sample_counts(key, part):
    key = jax.random.fold_in(key, 37)
    key_level, key_extra, key_rank = jax.random.split(key, 3)
    levels = jax.random.randint(key_level, (NSPK,), 4, 13)
    extra = jax.random.randint(key_extra, (NSPK,), 0, 16)
    counts = jnp.left_shift(jnp.ones((NSPK,), jnp.int32), levels.astype(jnp.int32)) + extra
    ranking = jax.random.permutation(key_rank, NSPK)
    speaker_index = jnp.arange(NSPK)
    counts = jnp.where(speaker_index == ranking[0], 4111, counts)
    counts = jnp.where(speaker_index == ranking[1], 16, counts)
    return counts.astype(jnp.int32)


def place_ends(entries, key, smallest, top_value):
    place = [jax.random.randint(jax.random.fold_in(key, axis), (), 0, length) for axis, length in enumerate(entries.shape)]
    widest = entries.shape.index(max(entries.shape))
    next_to = place[:widest] + [(place[widest] + 1) % entries.shape[widest]] + place[widest + 1:]
    return entries.at[tuple(place)].set(smallest).at[tuple(next_to)].set(top_value)


def shard_levels(stream_key, dims, cuts, least, top_value):
    def one(position, blocks):
        draws = jax.random.uniform(jax.random.fold_in(jax.random.fold_in(stream_key, 6), position), (blocks,), jnp.float32, least / len(cuts), top_value / len(cuts))
        return jnp.repeat(jnp.exp(draws), dims[position] // blocks).reshape((-1,) + (1,) * (len(dims) - position - 1))

    factor_of = one(*cuts[0])
    for cut in cuts[1:]:
        factor_of = factor_of * one(*cut)
    return factor_of


def cumulative_ranks(amount, lean):
    portions = [(1 << 20) // math.isqrt(rank ** lean) + 1 for rank in range(1, amount + 1)]
    deviation = 1 + sum(portions) // (1 << 30)
    return np.cumsum(np.array([max(1, weight // deviation) for weight in portions]))


def ranked_ids(stream_key, dims, number_of, skew):
    listing = cumulative_ranks(number_of, skew)
    pick = jax.random.randint(jax.random.fold_in(stream_key, 1), dims, 0, int(listing[number_of - 1]))
    rank = jnp.searchsorted(jnp.asarray(listing, jnp.int32), pick, side="right")
    return jax.random.permutation(jax.random.fold_in(stream_key, 2), number_of)[rank].astype(jnp.int32)


def noise(own_key, dims, deviation, most, cuts=(), kind=jnp.bfloat16):
    array = deviation * jax.random.normal(own_key, dims, jnp.float32)
    if cuts:
        array = array * shard_levels(own_key, dims, cuts, -0.22, 0.18)
    return jnp.clip(array, -most, most).astype(kind)


def setup_inputs(seed: int = 0) -> dict:
    keys = jax.random.split(jax.random.key(seed), 17)
    return {
        "inputs": noise(keys[0], (RESIDUAL_WIDTH, TOKENS), 1.0, 6.0, ((1, 4),)),
        "targets": place_ends(jax.random.randint(keys[1], (TOKENS,), 0, CLS), jax.random.fold_in(keys[1], 1), 0, CLS - 1).astype(jnp.int32),
        "mel": noise(keys[2], (MEL, FRAMES), 1.0, 6.0, ((1, 4),)),
        "speakers": place_ends(ranked_ids(keys[3], (BATCHES, 2), NSPK, 2), jax.random.fold_in(keys[3], 3), 0, NSPK - 1).astype(jnp.int32),
        "speaker_sample_counts": draw_speaker_sample_counts(jax.random.fold_in(keys[16], 71), 0),
        "segment_offsets": draw_segment_offsets(jax.random.fold_in(keys[16], 71), 0),
        "dilations": draw_dilations(jax.random.fold_in(keys[16], 71), 0),
        "dilated_kernel": noise(keys[7], (LAYER_COUNT, GATE_CHANNELS, 2 * RESIDUAL_WIDTH), (2 * RESIDUAL_WIDTH) ** -0.5, 0.1875, ((0, 8),)),
        "conditioning_projection": noise(keys[8], (LAYER_COUNT, GATE_CHANNELS, MEL), (2 * MEL) ** -0.5, 0.5, ((0, 8),)),
        "dilated_gate_bias": noise(keys[9], (LAYER_COUNT, GATE_CHANNELS), 0.5, 3.0, ((0, 8),)),
        "residual_projection": noise(keys[10], (LAYER_COUNT, RESIDUAL_WIDTH, GATE_CHANNELS // 2), 64 ** -0.5, 0.75, ((0, 8),)),
        "skip_projection": noise(keys[11], (LAYER_COUNT, SKIP, GATE_CHANNELS // 2), 64 ** -0.5, 0.75, ((0, 8),)),
        "upsample_weight": noise(keys[12], (HOP, MEL, MEL), MEL ** -0.5, 0.625),
        "speaker_table": noise(keys[13], (MEL, NSPK), 1.0, 5.0),
        "first_output_projection": noise(keys[14], (SKIP, SKIP), (SKIP // 4) ** -0.5, 0.5),
        "class_projection": noise(keys[15], (CLS, SKIP), 64 ** -0.5, 0.75),
    }


@jax.custom_vjp
def low(v):
    return lax.optimization_barrier(v.astype(jnp.bfloat16)).astype(jnp.float32)

@jax.custom_vjp
def low_back(v):
    return v

def low_keep(v):
    return (low(v), None)

def low_pass(kept, grad):
    return (grad,)

def back_keep(v):
    return (v, None)

def back_low(kept, grad):
    return (low(grad),)
low.defvjp(low_keep, low_pass)
low_back.defvjp(back_keep, back_low)
HALF_ROOT = 0.7071067811865476
WEIGHT_SCALE = 64.0
HIGHEST_LEVEL = lax.Precision.HIGHEST

def causal_shift(values, dilation_factor):
    length = values.shape[-1]
    padded = jnp.concatenate([jnp.zeros_like(values), values], axis=-1)
    return lax.dynamic_slice_in_dim(padded, length - dilation_factor, length, axis=values.ndim - 1)

def group_loss(parameters, field_in, mel_group, offsets, speaker_ids, target_ids, speaker_sample_counts, dilations):
    dilated_kernel, conditioning_projection, dilated_gate_bias, residual_projection, skip_projection, upsample_weight, speaker_table, first_output_projection, class_projection = parameters
    micro_count, res_ch, length = field_in.shape
    half_gate = residual_projection.shape[2]
    time_index = jnp.arange(length, dtype=jnp.int32)
    up_sampled = jnp.einsum('kca,baf->bcfk', upsample_weight, mel_group, precision=HIGHEST_LEVEL).reshape(micro_count, -1, length)
    later_mask = time_index[None, :] >= offsets[:, 0:1]
    sample_spk = jnp.where(later_mask, speaker_ids[:, 1:2], speaker_ids[:, 0:1])
    spk_onehot = (sample_spk[:, None, :] == jnp.arange(speaker_table.shape[1], dtype=jnp.int32)[None, :, None]).astype(jnp.float32)
    spk_vectors = jnp.einsum('cn,bnt->bct', speaker_table, spk_onehot, precision=HIGHEST_LEVEL)
    cond_all = low(up_sampled + spk_vectors)
    seg_start = jnp.where(later_mask, offsets[:, 0:1], 0)
    live_mask = (time_index[None, :] < offsets[:, 1:2]).astype(jnp.float32)
    sample_weight = live_mask * WEIGHT_SCALE * lax.rsqrt(speaker_sample_counts[sample_spk].astype(jnp.float32))

    def single_layer_step(state_carry, packed_parameters):
        stream_x, skip_sum = state_carry
        dilated_weight, conditioning_weight, bias_of_gate, residual_weight, skip_matrix, dilation_factor = packed_parameters
        keep_mask = (time_index[None, :] - dilation_factor >= seg_start).astype(jnp.float32)[:, None, :]
        shifted = causal_shift(stream_x, dilation_factor) * keep_mask
        stacked_layers = jnp.concatenate([shifted, stream_x], axis=1)
        gate_preactivation = jnp.einsum('ym,hmq->hyq', dilated_weight, stacked_layers, precision=HIGHEST_LEVEL)
        gate_preactivation = gate_preactivation + jnp.einsum('gc,bct->bgt', conditioning_weight, cond_all, precision=HIGHEST_LEVEL) + bias_of_gate[None, :, None]
        gate_preactivation = low_back(gate_preactivation)
        hidden = low(jnp.tanh(gate_preactivation[:, :half_gate]) * jax.nn.sigmoid(gate_preactivation[:, half_gate:]))
        residual = jnp.einsum('rh,bht->brt', residual_weight, hidden, precision=HIGHEST_LEVEL)
        skipped = jnp.einsum('sh,bht->bst', skip_matrix, hidden, precision=HIGHEST_LEVEL)
        stream_x = low_back(low((stream_x + residual) * HALF_ROOT))
        skip_sum = skip_sum + skipped
        return ((stream_x, skip_sum), None)
    initial_residual = low_back(field_in)
    initial_skip = jnp.zeros((micro_count, skip_projection.shape[1], length), jnp.float32)
    (final_residual, skip_running_sum), unused_value = lax.scan(single_layer_step, (initial_residual, initial_skip), (dilated_kernel, conditioning_projection, dilated_gate_bias, residual_projection, skip_projection, dilations))
    total_skip = low_back(low(skip_running_sum))
    head_scale = 1.0 / math.sqrt(LAYER_COUNT)
    first_act = low(jax.nn.silu(total_skip * head_scale))
    post_pre = low_back(jnp.einsum('pq,bqt->bpt', first_output_projection, first_act, precision=HIGHEST_LEVEL))
    second_act = low(jax.nn.silu(post_pre))
    logits = low_back(jnp.einsum('kq,bqt->bkt', class_projection, second_act, precision=HIGHEST_LEVEL))
    log_norm = jax.nn.logsumexp(logits, axis=1)
    classes = jnp.arange(class_projection.shape[0], dtype=jnp.int32)
    picked = lax.optimization_barrier(jnp.sum(jnp.where(target_ids[:, None, :] == classes[None, :, None], logits, 0.0), axis=1))
    return jnp.sum(sample_weight * (log_norm - picked))

def reference(inputs, targets, mel, speakers, speaker_sample_counts, segment_offsets, dilations, dilated_kernel, conditioning_projection, dilated_gate_bias, residual_projection, skip_projection, upsample_weight, speaker_table, first_output_projection, class_projection):
    parameters = tuple((value_result.astype(jnp.float32) for value_result in (dilated_kernel, conditioning_projection, dilated_gate_bias, residual_projection, skip_projection, upsample_weight, speaker_table, first_output_projection, class_projection)))
    per_frame = MBLEN // HOP
    field_all = inputs.astype(jnp.float32).reshape(RESIDUAL_WIDTH, N_DP, MB, MBLEN).transpose(1, 2, 0, 3)
    mel_all = mel.astype(jnp.float32).reshape(MEL, N_DP, MB, per_frame).transpose(1, 2, 0, 3)
    target_all = targets.reshape(N_DP, MB, MBLEN)
    offset_all = segment_offsets.reshape(N_DP, MB, 2)
    speaker_all = speakers.reshape(N_DP, MB, 2)

    def group_step(state_carry, item):
        grad_sums, loss_sum = state_carry
        field_in, mel_group, offsets, speaker_ids, target_ids = item

        def loss_of(parameters, field_in):
            return group_loss(parameters, field_in, mel_group, offsets, speaker_ids, target_ids, speaker_sample_counts, dilations)
        loss_value, pullback = jax.vjp(loss_of, parameters, field_in)
        grad_params, grad_field = pullback(jnp.ones_like(loss_value))
        grad_sums = tuple((left + right for left, right in zip(grad_sums, grad_params)))
        return ((grad_sums, loss_sum + loss_value), grad_field)
    init_state = (tuple((jnp.zeros_like(value_result) for value_result in parameters)), jnp.zeros((), jnp.float32))
    (grad_sums, loss_total), grad_fields = lax.scan(group_step, init_state, (field_all, mel_all, offset_all, speaker_all, target_all))
    grad_inputs = grad_fields.transpose(2, 0, 1, 3).reshape(RESIDUAL_WIDTH, TOKENS).astype(jnp.bfloat16)
    return (loss_total, grad_inputs, grad_sums[0], grad_sums[1], grad_sums[2], grad_sums[3], grad_sums[4], grad_sums[5], grad_sums[6], grad_sums[7], grad_sums[8])
```

```python
import functools
import math

import jax
import jax.numpy as jnp
from jax import lax
from jax.experimental import pallas as pl
from jax.experimental.pallas import tpu as pltpu
from jax.sharding import PartitionSpec as P

HALF_ROOT = 0.7071067811865476
WEIGHT_SCALE = 64.0
MESH = pl.DeviceIdType.MESH
BF16 = jnp.bfloat16
F32 = jnp.float32

PIECE = 128
EXT = 96
WIDE = 1024
BLOCK = 48
LAG = 3
HEAD_AT = 8


def dot(left, right):
    return jnp.dot(left, right, preferred_element_type=F32)


def dot_nt(left, right):
    return lax.dot_general(left, right, (((1,), (1,)), ((), ())), preferred_element_type=F32)


def sigmoid(values):
    return 0.5 * jnp.tanh(0.5 * values) + 0.5


def step_kernel(
    dims,
    dil_ref,
    offs_ref,
    spk_ref,
    cnt_ref,
    inp_ref,
    tgt_ref,
    cond_ref,
    extra_ref,
    wd_ref,
    wc_ref,
    wr_ref,
    ws_ref,
    wp_ref,
    wk_ref,
    o_acc,
    o_g,
    o_gin,
    x_buf,
    sg_buf,
    gx_buf,
    gc_buf,
    hid_buf,
    d1_buf,
    d2_buf,
    x_out,
    k_out,
    gx_out,
    gc_out,
    gate_buf,
    gh_buf,
    gg_buf,
    shift_buf,
    wc_n,
    wd_t,
    wr_t,
    ws_t,
    wp_t,
    wk_t,
    gl_buf,
    a2_buf,
    gp_buf,
    a1_buf,
    acc,
    part_out,
    part_in,
    gin_buf,
    inp_sem,
    loc_sem,
    x_ss,
    x_rs,
    k_ss,
    k_rs,
    gs_ss,
    gs_rs,
    gx_ss,
    gx_rs,
    gc_ss,
    gc_rs,
    zi_ss,
    zo_ss,
    zp_rs,
    zt_rs,
    hd_ss,
    hd_rs,
    g_rs,
    gown_ss,
    gpeer_ss,
    gup_ss,
    gdn_ss,
    gin_ss,
    gin_rs,
):
    sections, groups, micro, res, half, classes, slots, mel_rows = dims
    pieces = 2 * micro
    s = lax.axis_index("section")
    z = lax.axis_index("dp")
    is_first = s == 0
    is_last = s == sections - 1
    head_scale = 1.0 / math.sqrt(sections)
    main_rows = 2 * half + EXT + half
    head_rows = half // 2 + classes // 2
    main_blocks = main_rows // BLOCK
    head_blocks = head_rows // BLOCK
    share = res // sections

    barrier = pltpu.get_barrier_semaphore()

    def greet(cond, dev_s, dev_z):
        @pl.when(cond)
        def _():
            pl.semaphore_signal(barrier, 1, device_id=(dev_s, dev_z), device_id_type=MESH)

    greet(s > 0, s - 1, z)
    greet(s < sections - 1, s + 1, z)
    greet(z > 0, s, z - 1)
    greet(z < groups - 1, s, z + 1)
    greet(s >= 2, 0, z)

    @pl.when(is_first)
    def _():
        @pl.loop(2, sections)
        def _(other):
            pl.semaphore_signal(barrier, 1, device_id=(other, z), device_id_type=MESH)

    @pl.when(s == 2)
    def _():
        for other in range(groups):
            greet((other > z + 1) | (other < z - 1), s, other)

    def flag(cond):
        return jnp.where(cond, 1, 0)

    z_near = flag(z > 0) + flag(z < groups - 1)
    expected = (
        flag(s > 0)
        + flag(s < sections - 1)
        + z_near
        + jnp.where(is_first, sections - 2, flag(s >= 2))
        + jnp.where(s == 2, groups - 1 - z_near, 0)
    )

    def input_copy(c):
        return pltpu.make_async_copy(
            inp_ref.at[:, pl.ds(pl.multiple_of(c * PIECE, PIECE), PIECE)],
            x_buf.at[c],
            inp_sem.at[c],
        )

    @pl.when(is_first)
    def _():
        @pl.loop(0, pieces)
        def _(c):
            input_copy(c).start()

    wc_n[...] = jnp.transpose(wc_ref[...])

    def prepare():
        wd_t[...] = jnp.transpose(wd_ref[...])
        wr_t[...] = jnp.transpose(wr_ref[...])
        ws_t[...] = jnp.transpose(ws_ref[...])
        acc[...] = jnp.zeros_like(acc)

    pl.semaphore_wait(barrier, expected)

    @pl.when(s > 0)
    def _():
        prepare()

    @pl.when(is_last)
    def _():
        wp_t[...] = jnp.transpose(wp_ref[...])
        wk_t[...] = jnp.transpose(wk_ref[...])
        gx_buf[...] = jnp.zeros_like(gx_buf)

    def remote(src, dst, send_sem, recv_sem, dev_s, dev_z):
        return pltpu.make_async_remote_copy(
            src_ref=src,
            dst_ref=dst,
            send_sem=send_sem,
            recv_sem=recv_sem,
            device_id=(dev_s, dev_z),
            device_id_type=MESH,
        )

    def x_copy(c):
        slot = lax.rem(c, slots)
        return remote(x_out.at[slot], x_buf.at[c], x_ss.at[slot], x_rs.at[c], s + 1, z)

    def k_copy(c):
        slot = lax.rem(c, slots)
        return remote(k_out.at[slot], sg_buf.at[c], k_ss.at[slot], k_rs.at[c], s + 1, z)

    def gs_copy(c):
        return remote(sg_buf.at[c], sg_buf.at[c], gs_ss.at[c], gs_rs.at[c], s - 1, z)

    def gx_copy(c):
        slot = lax.rem(c, slots)
        return remote(gx_out.at[slot], gx_buf.at[c], gx_ss.at[slot], gx_rs.at[c], s - 1, z)

    def gc_copy(c):
        slot = lax.rem(c, slots)
        return remote(gc_out.at[slot], gc_buf.at[c], gc_ss.at[slot], gc_rs.at[c], s - 1, z)

    def reuse(copy, c):
        if pieces > slots:

            @pl.when(c >= slots)
            def _():
                copy(c).wait_send()

    def build_shift(m):
        dilation = dil_ref[0]
        middle = offs_ref[m, 0]
        source = lax.broadcasted_iota(jnp.int32, (2 * PIECE, 2 * PIECE), 0)
        target = lax.broadcasted_iota(jnp.int32, (2 * PIECE, 2 * PIECE), 1)
        start = jnp.where(target >= middle, middle, 0)
        hit = (source == target - dilation) & (source >= start)
        shift_buf[...] = jnp.where(hit, 1.0, 0.0).astype(BF16)

    def head(m, h, total):
        c = 2 * m + h
        total = total.astype(BF16).astype(F32) * head_scale
        sig_1 = sigmoid(total)
        act_1 = (total * sig_1).astype(BF16)
        slope_1 = sig_1 * (1.0 + total * (1.0 - sig_1))
        post = dot(wp_ref[...], act_1)
        sig_2 = sigmoid(post)
        act_2 = (post * sig_2).astype(BF16)
        slope_2 = sig_2 * (1.0 + post * (1.0 - sig_2))
        logits = dot(wk_ref[...], act_2)
        top = jnp.max(logits, axis=0, keepdims=True)
        expo = jnp.exp(logits - top)
        denominator = jnp.sum(expo, axis=0, keepdims=True)
        hit = tgt_ref[c] == lax.broadcasted_iota(jnp.int32, (classes, PIECE), 0)
        picked = jnp.sum(jnp.where(hit, logits, 0.0), axis=0, keepdims=True)
        time = lax.broadcasted_iota(jnp.int32, (1, PIECE), 1) + h * PIECE

        def speaker_weight(which):
            count = cnt_ref[spk_ref[m, which]].astype(F32)
            return WEIGHT_SCALE * lax.rsqrt(jnp.full((1, PIECE), count, F32))

        weight = jnp.where(time >= offs_ref[m, 0], speaker_weight(1), speaker_weight(0))
        weight = jnp.where(time < offs_ref[m, 1], weight, 0.0)
        loss_row = weight * (top + jnp.log(denominator) - picked)
        grad_logits = (weight * (expo / denominator - jnp.where(hit, 1.0, 0.0))).astype(BF16)
        grad_post = (dot(wk_t[...], grad_logits) * slope_2).astype(BF16)
        grad_total = dot(wp_t[...], grad_post) * slope_1 * head_scale
        sg_buf[c] = grad_total.astype(BF16)
        gs_copy(c).start()
        gl_buf[h] = grad_logits
        a2_buf[h] = act_2
        gp_buf[h] = grad_post
        a1_buf[h] = act_1
        high = loss_row.astype(BF16)
        rest = loss_row - high.astype(F32)
        middle = rest.astype(BF16)
        low = (rest - middle.astype(F32)).astype(BF16)
        row = lax.broadcasted_iota(jnp.int32, (EXT, PIECE), 0)
        message = jnp.where(row == mel_rows + 2, high.astype(F32), 0.0)
        message = jnp.where(row == mel_rows + 3, middle.astype(F32), message)
        message = jnp.where(row == mel_rows + 4, low.astype(F32), message)
        gc_buf[c] = message.astype(BF16)

    def forward(m, h):
        c = 2 * m + h

        @pl.when(is_first)
        def _():
            input_copy(c).wait()

        @pl.when(s > 0)
        def _():
            x_copy(c).wait_recv()

        x = x_buf[c]
        if h == 0:
            prev = dot(x, shift_buf[0:PIECE, 0:PIECE])
        else:
            both = jnp.concatenate([x_buf[2 * m], x], axis=1)
            prev = dot(both, shift_buf[:, PIECE : 2 * PIECE])
        stack = jnp.concatenate([prev.astype(BF16), x], axis=0)
        gate_buf[...] = dot(wd_ref[...], stack) + dot(wc_n[...], cond_ref[c])
        th = jnp.tanh(gate_buf[0:half])
        sg = sigmoid(gate_buf[half : 2 * half])
        hidden = (th * sg).astype(BF16)
        hid_buf[c] = hidden

        @pl.when(s < sections - 1)
        def _():
            reuse(x_copy, c)
            out = (x_buf[c].astype(F32) + dot(wr_ref[...], hid_buf[c])) * HALF_ROOT
            x_out[lax.rem(c, slots)] = out.astype(BF16)
            x_copy(c).start()

        gh_buf[...] = dot(ws_ref[...], hid_buf[c])
        th = jnp.tanh(gate_buf[0:half])
        sg = sigmoid(gate_buf[half : 2 * half])
        d1_buf[c] = (sg * (1.0 - th * th)).astype(BF16)
        d2_buf[c] = (th * sg * (1.0 - sg)).astype(BF16)

        @pl.when(s > 0)
        def _():
            k_copy(c).wait_recv()
            gh_buf[...] += sg_buf[c].astype(F32)

        @pl.when(s < sections - 1)
        def _():
            reuse(k_copy, c)
            k_out[lax.rem(c, slots)] = gh_buf[...].astype(BF16)
            k_copy(c).start()

        @pl.when(is_last)
        def _():
            head(m, h, gh_buf[...])

    def backward(m, h):
        c = 2 * m + h

        @pl.when(s < sections - 1)
        def _():
            gs_copy(c).wait_recv()

            @pl.when(s > 0)
            def _():
                gs_copy(c).start()

        gh_buf[...] = dot(ws_t[...], sg_buf[c])

        @pl.when(s < sections - 1)
        def _():
            gx_copy(c).wait_recv()
            gh_buf[...] += HALF_ROOT * dot(wr_t[...], gx_buf[c])

        grad_hidden = gh_buf[...]
        grad_gate = jnp.concatenate(
            [grad_hidden * d1_buf[c].astype(F32), grad_hidden * d2_buf[c].astype(F32)], axis=0
        ).astype(BF16)
        gg_buf[h] = grad_gate
        if h == 1:
            back = dot_nt(grad_gate, shift_buf[PIECE:, PIECE:])
        else:
            both = jnp.concatenate([grad_gate, gg_buf[1]], axis=1)
            back = dot_nt(both, shift_buf[0:PIECE, :])
        grad_x = (
            HALF_ROOT * gx_buf[c].astype(F32)
            + dot(wd_t[res : 2 * res], grad_gate)
            + dot(wd_t[0:res], back.astype(BF16))
        ).astype(BF16)

        @pl.when(s > 0)
        def _():
            reuse(gx_copy, c)
            gx_out[lax.rem(c, slots)] = grad_x
            gx_copy(c).start()

        row = lax.broadcasted_iota(jnp.int32, (EXT, PIECE), 0)
        message = jnp.where(row < mel_rows, dot(wc_ref[...], gg_buf[h]), 0.0)

        @pl.when(s < sections - 1)
        def _():
            gc_copy(c).wait_recv()

        message = message + gc_buf[c].astype(F32)

        @pl.when(s > 0)
        def _():
            reuse(gc_copy, c)
            gc_out[lax.rem(c, slots)] = message.astype(BF16)
            gc_copy(c).start()

        @pl.when(is_first)
        def _():
            d1_buf[c] = grad_x
            gc_buf[c] = message.astype(BF16)
            if h == 0:
                gc_buf[c, mel_rows:EXT, :] = (message[mel_rows:EXT] + extra_ref[m].astype(F32)).astype(BF16)

    def add_halves(first_row, value):
        rows = value.shape[0] // 2
        acc[first_row : first_row + rows, 0:half] += value[0:rows]
        acc[first_row : first_row + rows, half : 2 * half] += value[rows : 2 * rows]

    def weight_gradients(m):
        def pair(ref, first):
            return jnp.concatenate([ref[first], ref[first + 1]], axis=1)

        grad_gate = pair(gg_buf, 0)
        x = pair(x_buf, 2 * m)
        prev = dot(x, shift_buf[...]).astype(BF16)
        acc[0 : 2 * half, 0:res] += dot_nt(grad_gate, prev)
        acc[0 : 2 * half, res : 2 * res] += dot_nt(grad_gate, x)
        acc[2 * half : 2 * half + EXT, :] += dot_nt(pair(cond_ref, 2 * m), grad_gate)
        hidden = pair(hid_buf, 2 * m)
        row = 2 * half + EXT

        @pl.when(s < sections - 1)
        def _():
            add_halves(row, HALF_ROOT * dot_nt(pair(gx_buf, 2 * m), hidden))

        add_halves(row + half // 2, dot_nt(pair(sg_buf, 2 * m), hidden))

        @pl.when(is_last)
        def _():
            add_halves(main_rows, dot_nt(pair(gp_buf, 0), pair(a1_buf, 0)))
            add_halves(main_rows + half // 2, dot_nt(pair(gl_buf, 0), pair(a2_buf, 0)))

    @pl.loop(0, 2 * micro)
    def _(step):
        m = jnp.where(is_last, step // 2, lax.rem(step, micro))
        is_forward = jnp.where(is_last, lax.rem(step, 2) == 0, step < micro)
        build_shift(m)

        @pl.when(is_forward)
        def _():
            forward(m, 0)
            forward(m, 1)

        @pl.when(is_first & (step == micro))
        def _():
            prepare()

        @pl.when(jnp.logical_not(is_forward))
        def _():
            backward(m, 1)
            backward(m, 0)
            weight_gradients(m)

    def gin_copy(other):
        return remote(
            d1_buf.at[:, pl.ds(pl.multiple_of(other * share, share), share), :],
            gin_buf,
            gin_ss.at[other],
            gin_rs.at[0],
            other,
            z,
        )

    def own_local():
        return pltpu.make_async_copy(gc_buf, o_g.at[z], loc_sem.at[0])

    def own_first():
        return remote(gc_buf, o_g.at[z], gown_ss.at[0], g_rs.at[z], s + 1, z)

    def part_up(j):
        return remote(o_g.at[j], o_g.at[j], gup_ss.at[j], g_rs.at[j], s + 1, z)

    def part_down(j):
        return remote(o_g.at[j], o_g.at[j], gdn_ss.at[j], g_rs.at[j], s - 1, z)

    def own_peer(other):
        return remote(o_g.at[z], o_g.at[z], gpeer_ss.at[other], g_rs.at[z], s, other)

    @pl.when(is_first)
    def _():
        own_local().start()
        own_first().start()

        @pl.loop(1, sections)
        def _(other):
            gin_copy(other).start()

        gin_buf[...] = d1_buf[:, 0:share, :]

    left = z < groups // 2
    inward = jnp.where(left, z + 1, z - 1)
    outward = jnp.where(left, z - 1, z + 1)
    is_edge = (z == 0) | (z == groups - 1)
    is_mid = (z == groups // 2 - 1) | (z == groups // 2)
    count = jnp.where(is_last, main_blocks + head_blocks, main_blocks)

    def block_of(i):
        return jnp.where(is_last, jnp.where(i < head_blocks, i + main_blocks, i - head_blocks), i)

    def rows_of(b):
        return pl.ds(pl.multiple_of(b * BLOCK, BLOCK), BLOCK)

    def swap_copy(b):
        return remote(part_out.at[rows_of(b)], o_acc.at[rows_of(b)], zi_ss.at[b], zt_rs.at[b], s, inward)

    def part_copy(b):
        return remote(part_out.at[rows_of(b)], part_in.at[rows_of(b)], zi_ss.at[b], zp_rs.at[b], s, inward)

    def total_copy(b):
        return remote(o_acc.at[rows_of(b)], o_acc.at[rows_of(b)], zo_ss.at[b], zt_rs.at[b], s, outward)

    def head_copy(j):
        rows = rows_of(main_blocks + j)
        return remote(o_acc.at[rows], o_acc.at[rows], hd_ss.at[j], hd_rs.at[j], s - 1, z)

    def send_part(b):
        rows = rows_of(b)

        @pl.when(is_edge)
        def _():
            part_out[rows, :] = acc[rows, :].astype(BF16)

        @pl.when(jnp.logical_not(is_edge))
        def _():
            part_copy(b).wait_recv()
            part_out[rows, :] = (acc[rows, :] + part_in[rows, :].astype(F32)).astype(BF16)

        @pl.when(is_mid)
        def _():
            swap_copy(b).start()

        @pl.when(jnp.logical_not(is_mid))
        def _():
            part_copy(b).start()

    def finish_part(b):
        rows = rows_of(b)
        swap_copy(b).wait_recv()

        @pl.when(is_mid)
        def _():
            o_acc[rows, :] = (part_out[rows, :].astype(F32) + o_acc[rows, :].astype(F32)).astype(BF16)

        @pl.when(jnp.logical_not(is_edge))
        def _():
            total_copy(b).start()

    last_step = main_blocks + LAG - 1
    own_at = jnp.minimum(2 + 4 * s, last_step)
    rest_at = jnp.where(s >= 3, 16 + 3 * (s - 2), jnp.where(s == 2, 16, jnp.where(s == 1, 14, last_step)))
    rest_at = jnp.minimum(rest_at, last_step)

    @pl.loop(0, main_blocks + head_blocks + LAG)
    def _(i):
        @pl.when(i < count)
        def _():
            send_part(block_of(i))

        @pl.when((i >= LAG) & (i < count + LAG))
        def _():
            b = block_of(i - LAG)
            finish_part(b)

            @pl.when(b >= main_blocks)
            def _():
                head_copy(b - main_blocks).start()

        @pl.when(jnp.logical_not(is_last) & (i >= HEAD_AT) & (i < HEAD_AT + head_blocks))
        def _():
            j = i - HEAD_AT
            head_copy(j).wait_recv()

            @pl.when(s > 0)
            def _():
                head_copy(j).start()

        @pl.when((s > 0) & (i == own_at))
        def _():
            part_up(z).wait_recv()

            @pl.when(s < sections - 1)
            def _():
                part_up(z).start()

            @pl.when(s == 2)
            def _():
                for other in range(groups):

                    @pl.when(z != other)
                    def _():
                        own_peer(other).start()

        @pl.when(i == rest_at)
        def _():
            for j in range(groups):

                @pl.when(z != j)
                def _():
                    part_up(j).wait_recv()

                    @pl.when((s >= 2) & (s < sections - 1))
                    def _():
                        part_up(j).start()

                    @pl.when((s == 1) | (s == 2))
                    def _():
                        part_down(j).start()

    @pl.when(s > 0)
    def _():
        gin_copy(0).wait_recv()

    for c in range(pieces):
        o_gin[:, c * PIECE : (c + 1) * PIECE] = gin_buf[c]

    @pl.when(is_first)
    def _():
        own_local().wait()
        own_first().wait_send()

        @pl.loop(1, sections)
        def _(other):
            gin_copy(other).wait_send()

    @pl.when((s > 0) & (s < sections - 1))
    def _():
        part_up(z).wait_send()

    @pl.when(s == 2)
    def _():
        for other in range(groups):

            @pl.when(z != other)
            def _():
                own_peer(other).wait_send()

    for j in range(groups):

        @pl.when((z != j) & (s >= 2) & (s < sections - 1))
        def _():
            part_up(j).wait_send()

        @pl.when((z != j) & ((s == 1) | (s == 2)))
        def _():
            part_down(j).wait_send()

    @pl.when(s > 0)
    def _():
        @pl.loop(0, head_blocks)
        def _(j):
            head_copy(j).wait_send()

    @pl.loop(0, count)
    def _(b):
        part_copy(b).wait_send()

        @pl.when(jnp.logical_not(is_edge))
        def _():
            total_copy(b).wait_send()

    @pl.loop(0, slots)
    def _(c):
        @pl.when(s < sections - 1)
        def _():
            x_copy(c).wait_send()
            k_copy(c).wait_send()

        @pl.when(s > 0)
        def _():
            gx_copy(c).wait_send()
            gc_copy(c).wait_send()

    @pl.when(s > 0)
    def _():
        @pl.loop(0, pieces)
        def _(c):
            gs_copy(c).wait_send()


def run_step(dims, dilations, offsets, speakers, counts, inputs, targets, cond, extra, weights):
    sections, groups, micro, res, half, classes, slots, mel_rows = dims
    pieces = 2 * micro
    rows = 2 * half + EXT + half + half // 2 + classes // 2
    blocks = rows // BLOCK
    head_blocks = (half // 2 + classes // 2) // BLOCK
    share = res // sections
    smem = pl.BlockSpec(memory_space=pltpu.SMEM)
    vmem = pl.BlockSpec(memory_space=pltpu.VMEM)
    anywhere = pl.BlockSpec(memory_space=pl.ANY)
    dma = pltpu.SemaphoreType.DMA

    def tile(*shape, dtype=BF16):
        return pltpu.VMEM(shape, dtype)

    scratch = [
        tile(pieces, res, PIECE),
        tile(pieces, half, PIECE),
        tile(pieces, res, PIECE),
        tile(pieces, EXT, PIECE),
        tile(pieces, half, PIECE),
        tile(pieces, half, PIECE),
        tile(pieces, half, PIECE),
        tile(slots, res, PIECE),
        tile(slots, half, PIECE),
        tile(slots, res, PIECE),
        tile(slots, EXT, PIECE),
        tile(2 * half, PIECE, dtype=F32),
        tile(half, PIECE, dtype=F32),
        tile(2, 2 * half, PIECE),
        tile(2 * PIECE, 2 * PIECE),
        tile(2 * half, EXT),
        tile(2 * res, 2 * half),
        tile(half, res),
        tile(half, half),
        tile(half, half),
        tile(half, classes),
        tile(2, classes, PIECE),
        tile(2, half, PIECE),
        tile(2, half, PIECE),
        tile(2, half, PIECE),
        tile(rows, WIDE, dtype=F32),
        tile(rows, WIDE),
        tile(rows, WIDE),
        tile(pieces, share, PIECE),
        dma((pieces,)),
        dma((1,)),
        dma((slots,)),
        dma((pieces,)),
        dma((slots,)),
        dma((pieces,)),
        dma((pieces,)),
        dma((pieces,)),
        dma((slots,)),
        dma((pieces,)),
        dma((slots,)),
        dma((pieces,)),
        dma((blocks,)),
        dma((blocks,)),
        dma((blocks,)),
        dma((blocks,)),
        dma((head_blocks,)),
        dma((head_blocks,)),
        dma((groups,)),
        dma((1,)),
        dma((groups,)),
        dma((groups,)),
        dma((groups,)),
        dma((sections,)),
        dma((1,)),
    ]
    return pl.pallas_call(
        functools.partial(step_kernel, dims),
        out_shape=(
            jax.ShapeDtypeStruct((rows, WIDE), BF16),
            jax.ShapeDtypeStruct((groups, pieces, EXT, PIECE), BF16),
            jax.ShapeDtypeStruct((share, pieces * PIECE), BF16),
        ),
        in_specs=[smem] * 4 + [anywhere] + [vmem] * 9,
        out_specs=(vmem, anywhere, vmem),
        scratch_shapes=scratch,
        compiler_params=pltpu.CompilerParams(
            collective_id=0, has_side_effects=True, vmem_limit_bytes=63 * 2**20
        ),
        cost_estimate=pl.CostEstimate(flops=10**10, bytes_accessed=3 * 10**7, transcendentals=10**6),
        name="train_step",
    )(dilations, offsets, speakers, counts, inputs, targets, cond, extra, *weights)


def local(
    inputs,
    targets,
    mel,
    speakers,
    speaker_sample_counts,
    segment_offsets,
    dilations,
    dilated_kernel,
    conditioning_projection,
    dilated_gate_bias,
    residual_projection,
    skip_projection,
    upsample_weight,
    speaker_table,
    first_output_projection,
    class_projection,
):
    sections = lax.axis_size("section")
    groups = lax.axis_size("dp")
    micro = segment_offsets.shape[0]
    res, tokens = inputs.shape
    length = tokens // micro
    mel_rows = mel.shape[0]
    hop = upsample_weight.shape[0]
    half = residual_projection.shape[2]
    classes = class_projection.shape[0]
    pieces = 2 * micro
    assert length == 2 * PIECE and hop == length and mel_rows + 16 == EXT and 2 * half == WIDE

    speaker_index = jnp.arange(speaker_table.shape[1], dtype=jnp.int32)
    onehot = (speakers[:, :, None] == speaker_index).astype(BF16)
    table_columns = jnp.einsum("cn,mjn->mjc", speaker_table, onehot, preferred_element_type=F32)
    time = jnp.arange(length, dtype=jnp.int32)
    later = time[None, :] >= segment_offsets[:, 0:1]
    spk_part = jnp.where(
        later[:, None, :], table_columns[:, 1, :, None], table_columns[:, 0, :, None]
    )
    upsampled = jnp.einsum("kca,af->fck", upsample_weight, mel, preferred_element_type=F32)
    cond = (upsampled + spk_part).astype(BF16)
    cond = jnp.concatenate(
        [cond, jnp.ones((micro, 1, length), BF16), jnp.zeros((micro, EXT - mel_rows - 1, length), BF16)],
        axis=1,
    )
    cond = cond.reshape(micro, EXT, 2, PIECE).transpose(0, 2, 1, 3).reshape(pieces, EXT, PIECE)
    weight_cond = jnp.concatenate(
        [
            conditioning_projection[0].T,
            dilated_gate_bias,
            jnp.zeros((EXT - mel_rows - 1, 2 * half), BF16),
        ],
        axis=0,
    )
    ids = jnp.concatenate([speakers, segment_offsets], axis=1).astype(BF16)
    extra = jnp.stack(
        [
            jnp.pad(mel.T, ((0, 0), (0, PIECE - mel_rows))),
            jnp.pad(ids, ((0, 0), (0, PIECE - 4))),
        ],
        axis=1,
    )
    extra = jnp.pad(extra, ((0, 0), (0, 14), (0, 0)))

    slots = pieces if pieces <= 8 else 4
    dims = (sections, groups, micro, res, half, classes, slots, mel_rows)
    sums, shared, grad_inputs = run_step(
        dims,
        dilations,
        segment_offsets,
        speakers,
        speaker_sample_counts,
        inputs,
        targets.reshape(pieces, 1, PIECE),
        cond,
        extra,
        (
            dilated_kernel[0],
            weight_cond,
            residual_projection[0],
            skip_projection[0],
            first_output_projection,
            class_projection,
        ),
    )

    def halves(first, rows):
        block = sums[first : first + rows].astype(F32)
        return jnp.concatenate([block[:, :half], block[:, half:]], axis=0)

    row = 2 * half
    grad_dil = sums[:row].astype(F32)
    cond_block = sums[row : row + EXT].astype(F32)
    grad_cond = cond_block[:mel_rows].T
    grad_bias = cond_block[mel_rows]
    row += EXT
    grad_res = halves(row, half // 2)
    grad_skip = halves(row + half // 2, half // 2)
    grad_post = halves(row + half, half // 2)
    grad_out = halves(row + half + half // 2, classes // 2)

    frames = groups * micro
    shared = shared.reshape(frames, 2, EXT, PIECE)
    field = shared[:, :, :mel_rows]
    mel_all = shared[:, 0, mel_rows, :mel_rows]
    ids_all = shared[:, 0, mel_rows + 1, :4].astype(jnp.int32)
    loss = jnp.sum(shared[:, :, mel_rows + 2 : mel_rows + 5].astype(F32))
    field_3 = field.transpose(2, 0, 1, 3).reshape(mel_rows, frames, length)
    grad_up = jnp.einsum("cfk,fa->cak", field_3, mel_all, preferred_element_type=F32)
    grad_up = grad_up.transpose(2, 0, 1)
    later_all = time[None, :] >= ids_all[:, 2:3]
    seg_mask = jnp.stack([jnp.logical_not(later_all), later_all], axis=1).astype(BF16)
    seg_sums = jnp.einsum("cfk,fjk->cfj", field_3, seg_mask, preferred_element_type=F32)
    seg_hot = (ids_all[:, :2, None] == speaker_index).astype(F32)
    grad_table = jnp.einsum("cfj,fjn->cn", seg_sums, seg_hot, precision=lax.Precision.HIGHEST)
    return (
        loss,
        grad_inputs,
        grad_dil[None],
        grad_cond[None],
        grad_bias[None],
        grad_res[None],
        grad_skip[None],
        grad_up,
        grad_table,
        grad_post,
        grad_out,
    )


def solution(mesh):
    return jax.shard_map(
        local,
        mesh=mesh,
        in_specs=(
            P(None, "dp"),
            P("dp"),
            P(None, "dp"),
            P("dp", None),
            P(),
            P("dp", None),
            P("section"),
            P("section", None, None),
            P("section", None, None),
            P("section", None),
            P("section", None, None),
            P("section", None, None),
            P(),
            P(),
            P(),
            P(),
        ),
        out_specs=(
            P(),
            P("section", "dp"),
            P("section", None, None),
            P("section", None, None),
            P("section", None),
            P("section", None, None),
            P("section", None, None),
            P(),
            P(),
            P(),
            P(),
        ),
        check_vma=False,
    )
```

```python
import functools
import math

import jax
import jax.numpy as jnp
from jax import lax
from jax.experimental import pallas as pl
from jax.experimental.pallas import tpu as pltpu
from jax.sharding import PartitionSpec as P

HALF_ROOT = 0.7071067811865476
WEIGHT_SCALE = 64.0
MESH = pl.DeviceIdType.MESH
BF16 = jnp.bfloat16
F32 = jnp.float32

PIECE = 128
EXT = 96
WIDE = 1024
BLOCK = 48
HUB = 2
LAG = 4


def dot(left, right):
    return jnp.dot(left, right, preferred_element_type=F32)


def dot_nt(left, right):
    return lax.dot_general(left, right, (((1,), (1,)), ((), ())), preferred_element_type=F32)


def sigmoid(values):
    return 0.5 * jnp.tanh(0.5 * values) + 0.5


def step_kernel(
    dims,
    dil_ref,
    offs_ref,
    spk_ref,
    cnt_ref,
    tgt_ref,
    mel_ref,
    tab_ref,
    wc_in,
    bias_in,
    inp_hbm,
    up_hbm,
    wd_hbm,
    wr_hbm,
    ws_hbm,
    wp_hbm,
    wk_hbm,
    o_acc,
    o_g,
    o_gin,
    x_buf,
    sg_buf,
    gx_buf,
    gc_buf,
    hid_buf,
    d1_buf,
    d2_buf,
    x_out,
    k_out,
    gx_out,
    gc_out,
    gate_buf,
    gh_buf,
    gg_buf,
    shift_buf,
    cond_ref,
    wc_ref,
    wd_ref,
    wr_ref,
    ws_ref,
    wp_ref,
    wk_ref,
    wc_n,
    wd_t,
    wr_t,
    ws_t,
    wp_t,
    wk_t,
    gl_buf,
    a2_buf,
    gp_buf,
    a1_buf,
    acc,
    part_out,
    part_in,
    gin_buf,
    up_buf,
    extra_buf,
    inp_sem,
    load_sem,
    loc_sem,
    x_ss,
    x_rs,
    k_ss,
    k_rs,
    gs_ss,
    gs_rs,
    gx_ss,
    gx_rs,
    gc_ss,
    gc_rs,
    zi_ss,
    zo_ss,
    zp_rs,
    zt_rs,
    hd_ss,
    hd_rs,
    g_rs,
    gown_ss,
    gpeer_ss,
    ghub_ss,
    gnext_ss,
    gin_ss,
    gin_rs,
):
    sections, groups, micro, res, half, classes, slots, keep, mel_rows = dims
    pieces = 2 * micro
    s = lax.axis_index("section")
    z = lax.axis_index("dp")
    is_first = s == 0
    is_last = s == sections - 1
    is_hub = s == HUB
    head_scale = 1.0 / math.sqrt(sections)
    main_rows = 2 * half + EXT + half
    head_rows = half // 2 + classes // 2
    main_blocks = main_rows // BLOCK
    head_blocks = head_rows // BLOCK
    share = res // sections

    barrier = pltpu.get_barrier_semaphore()

    def greet(cond, dev_s, dev_z):
        @pl.when(cond)
        def _():
            pl.semaphore_signal(barrier, 1, device_id=(dev_s, dev_z), device_id_type=MESH)

    greet(s > 0, s - 1, z)
    greet(s < sections - 1, s + 1, z)
    greet(z > 0, s, z - 1)
    greet(z < groups - 1, s, z + 1)
    greet(s >= 2, 0, z)
    greet((s > HUB + 1) & (lax.rem(s, 2) == 0), HUB, z)

    @pl.when(is_first)
    def _():
        @pl.loop(2, sections)
        def _(other):
            pl.semaphore_signal(barrier, 1, device_id=(other, z), device_id_type=MESH)

    @pl.when(is_hub)
    def _():
        @pl.loop(HUB // 2 + 1, sections // 2)
        def _(chip):
            pl.semaphore_signal(barrier, 1, device_id=(2 * chip, z), device_id_type=MESH)

        for other in range(groups):
            greet((other > z + 1) | (other < z - 1), s, other)

    def flag(cond):
        return jnp.where(cond, 1, 0)

    z_near = flag(z > 0) + flag(z < groups - 1)
    expected = (
        flag(s > 0)
        + flag(s < sections - 1)
        + z_near
        + jnp.where(is_first, sections - 2, flag(s >= 2))
        + flag((s > HUB + 1) & (lax.rem(s, 2) == 0))
        + jnp.where(is_hub, groups - 1 - z_near + sections // 2 - HUB // 2 - 1, 0)
    )

    def input_copy(c):
        return pltpu.make_async_copy(
            inp_hbm.at[:, pl.ds(pl.multiple_of(c * PIECE, PIECE), PIECE)],
            x_buf.at[c],
            inp_sem.at[c],
        )

    quarter = mel_rows // 4
    loads = [
        pltpu.make_async_copy(
            up_hbm.at[pl.ds(q * quarter * mel_rows, quarter * mel_rows), :],
            part_out.at[pl.ds(0, quarter * mel_rows), pl.ds(q * 2 * PIECE, 2 * PIECE)],
            load_sem.at[q],
        )
        for q in range(4)
    ]
    weight_refs = ((wd_hbm, wd_ref), (wr_hbm, wr_ref), (ws_hbm, ws_ref), (wp_hbm, wp_ref), (wk_hbm, wk_ref))
    for position, (source, target) in enumerate(weight_refs):
        loads.append(pltpu.make_async_copy(source, target, load_sem.at[4 + position]))
    for load in loads[:5]:
        load.start()

    @pl.when(is_first)
    def _():
        @pl.loop(0, pieces)
        def _(c):
            input_copy(c).start()

    for load in loads[5:]:
        load.start()
    wc_ref[0:mel_rows] = wc_in[...]
    spare = lax.broadcasted_iota(jnp.int32, (EXT - mel_rows, 2 * half), 0)
    bias = jnp.broadcast_to(bias_in[...].astype(F32), (EXT - mel_rows, 2 * half))
    wc_ref[mel_rows:EXT] = jnp.where(spare == 0, bias, 0.0).astype(BF16)
    wc_n[...] = jnp.transpose(wc_ref[...])

    for load in loads[:4]:
        load.wait()

    @pl.loop(0, quarter)
    def _(row):
        for q in range(4):
            matrix = part_out[pl.ds(pl.multiple_of(row * mel_rows, 16), mel_rows), q * 2 * PIECE : (q + 1) * 2 * PIECE]
            frames = dot(mel_ref[...], matrix)
            for h in range(2):
                up_buf[h, pl.ds(q * quarter + row, micro, stride=mel_rows), :] = frames[:, h * PIECE : (h + 1) * PIECE]

    speaker_lane = lax.broadcasted_iota(jnp.int32, tab_ref.shape, 1)
    spare = lax.broadcasted_iota(jnp.int32, (EXT - mel_rows, PIECE), 0)
    table = tab_ref[...].astype(F32)

    @pl.loop(0, micro)
    def _(m):
        def column(which):
            return jnp.sum(jnp.where(speaker_lane == spk_ref[which, m], table, 0.0), axis=1, keepdims=True)

        first, second = column(0), column(1)
        for h in range(2):
            time = lax.broadcasted_iota(jnp.int32, (mel_rows, PIECE), 1) + h * PIECE
            speaker = jnp.where(time >= offs_ref[0, m], second, first)
            rows = pl.ds(pl.multiple_of(m * mel_rows, 16), mel_rows)
            cond_ref[2 * m + h, 0:mel_rows, :] = (up_buf[h, rows, :] + speaker).astype(BF16)
            cond_ref[2 * m + h, mel_rows:EXT, :] = jnp.where(spare == 0, 1.0, 0.0).astype(BF16)

    def prepare():
        wd_t[...] = jnp.transpose(wd_ref[...])
        wr_t[...] = jnp.transpose(wr_ref[...])
        ws_t[...] = jnp.transpose(ws_ref[...])
        acc[...] = jnp.zeros_like(acc)

    for load in loads[4:]:
        load.wait()

    pl.semaphore_wait(barrier, expected)

    @pl.when(s > 0)
    def _():
        prepare()

    @pl.when(is_last)
    def _():
        wp_t[...] = jnp.transpose(wp_ref[...])
        wk_t[...] = jnp.transpose(wk_ref[...])
        gx_buf[...] = jnp.zeros_like(gx_buf)

    def remote(src, dst, send_sem, recv_sem, dev_s, dev_z):
        return pltpu.make_async_remote_copy(
            src_ref=src,
            dst_ref=dst,
            send_sem=send_sem,
            recv_sem=recv_sem,
            device_id=(dev_s, dev_z),
            device_id_type=MESH,
        )

    def x_copy(c):
        slot = lax.rem(c, slots)
        return remote(x_out.at[slot], x_buf.at[c], x_ss.at[slot], x_rs.at[c], s + 1, z)

    def k_copy(c):
        slot = lax.rem(c, slots)
        return remote(k_out.at[slot], sg_buf.at[c], k_ss.at[slot], k_rs.at[c], s + 1, z)

    def gs_copy(c):
        return remote(sg_buf.at[c], sg_buf.at[c], gs_ss.at[c], gs_rs.at[c], s - 1, z)

    def gx_copy(c):
        slot = lax.rem(c, slots)
        return remote(gx_out.at[slot], gx_buf.at[c], gx_ss.at[slot], gx_rs.at[c], s - 1, z)

    def gc_copy(c):
        slot = lax.rem(c, slots)
        return remote(gc_out.at[slot], gc_buf.at[c], gc_ss.at[slot], gc_rs.at[c], s - 1, z)

    def reuse(copy, c):
        if pieces > slots:

            @pl.when(c >= slots)
            def _():
                copy(c).wait_send()

    def build_shift(m):
        dilation = dil_ref[0]
        middle = offs_ref[0, m]
        source = lax.broadcasted_iota(jnp.int32, (2 * PIECE, 2 * PIECE), 0)
        target = lax.broadcasted_iota(jnp.int32, (2 * PIECE, 2 * PIECE), 1)
        start = jnp.where(target >= middle, middle, 0)
        hit = (source == target - dilation) & (source >= start)
        shift_buf[...] = jnp.where(hit, 1.0, 0.0).astype(BF16)

    def columns(ref, first, parts):
        return jnp.concatenate([ref[first + h] for h in parts], axis=1)

    def put(ref, first, parts, value):
        for position, h in enumerate(parts):
            ref[first + h] = value[:, position * PIECE : (position + 1) * PIECE]

    def head(m, total):
        parts = (0, 1)
        width = 2 * PIECE
        total = total.astype(BF16).astype(F32) * head_scale
        sig_1 = sigmoid(total)
        act_1 = (total * sig_1).astype(BF16)
        slope_1 = sig_1 * (1.0 + total * (1.0 - sig_1)) * head_scale
        post = dot(wp_ref[...], act_1)
        sig_2 = sigmoid(post)
        act_2 = (post * sig_2).astype(BF16)
        slope_2 = sig_2 * (1.0 + post * (1.0 - sig_2))
        logits = dot(wk_ref[...], act_2)
        top = jnp.max(logits, axis=0, keepdims=True)
        expo = jnp.exp(logits - top)
        denominator = jnp.sum(expo, axis=0, keepdims=True)
        hit = tgt_ref[m] == lax.broadcasted_iota(jnp.int32, (classes, width), 0)
        picked = jnp.sum(jnp.where(hit, logits, 0.0), axis=0, keepdims=True)
        time = lax.broadcasted_iota(jnp.int32, (1, width), 1)

        def speaker_weight(which):
            count = cnt_ref[spk_ref[which, m]].astype(F32)
            return WEIGHT_SCALE * lax.rsqrt(jnp.full((1, width), count, F32))

        weight = jnp.where(time >= offs_ref[0, m], speaker_weight(1), speaker_weight(0))
        weight = jnp.where(time < offs_ref[1, m], weight, 0.0)
        grad_logits = (weight * (expo / denominator - jnp.where(hit, 1.0, 0.0))).astype(BF16)
        grad_post = (dot(wk_t[...], grad_logits) * slope_2).astype(BF16)
        grad_total = (dot(wp_t[...], grad_post) * slope_1).astype(BF16)
        put(sg_buf, 2 * m, parts, grad_total)
        for h in (1, 0):
            gs_copy(2 * m + h).start()
        kept = 2 * lax.rem(m, keep)
        put(gl_buf, kept, parts, grad_logits)
        put(a2_buf, kept, parts, act_2)
        put(gp_buf, kept, parts, grad_post)
        put(a1_buf, kept, parts, act_1)
        loss_row = weight * (top + jnp.log(denominator) - picked)
        high = loss_row.astype(BF16)
        rest = loss_row - high.astype(F32)
        middle = rest.astype(BF16)
        low = (rest - middle.astype(F32)).astype(BF16)
        row = lax.broadcasted_iota(jnp.int32, (EXT, width), 0)
        message = jnp.where(row == mel_rows + 2, high.astype(F32), 0.0)
        message = jnp.where(row == mel_rows + 3, middle.astype(F32), message)
        message = jnp.where(row == mel_rows + 4, low.astype(F32), message)
        put(gc_buf, 2 * m, parts, message.astype(BF16))

    def forward(m, parts):
        wide = pl.ds(0, len(parts) * PIECE)
        for h in parts:
            c = 2 * m + h

            @pl.when(is_first)
            def _():
                input_copy(c).wait()

            @pl.when(s > 0)
            def _():
                x_copy(c).wait_recv()

        x = columns(x_buf, 2 * m, parts)
        if parts == (0,):
            prev = dot(x, shift_buf[0:PIECE, 0:PIECE])
        elif parts == (1,):
            prev = dot(columns(x_buf, 2 * m, (0, 1)), shift_buf[:, PIECE : 2 * PIECE])
        else:
            prev = dot(x, shift_buf[...])
        stack = jnp.concatenate([prev.astype(BF16), x], axis=0)
        gate = dot(wd_ref[...], stack) + dot(wc_n[...], columns(cond_ref, 2 * m, parts))
        th = jnp.tanh(gate[0:half])
        sg = sigmoid(gate[half : 2 * half])
        gate_buf[0:half, wide] = th
        gate_buf[half : 2 * half, wide] = sg
        put(hid_buf, 2 * m, parts, (th * sg).astype(BF16))

    def forward_rest(m, parts):
        wide = pl.ds(0, len(parts) * PIECE)
        th = gate_buf[0:half, wide]
        sg = gate_buf[half : 2 * half, wide]
        put(d1_buf, 2 * m, parts, (sg * (1.0 - th * th)).astype(BF16))
        put(d2_buf, 2 * m, parts, (th * sg * (1.0 - sg)).astype(BF16))

    def forward_piece(m, h):
        c = 2 * m + h
        forward(m, (h,))
        reuse(x_copy, c)
        out = (x_buf[c].astype(F32) + dot(wr_ref[...], hid_buf[c])) * HALF_ROOT
        x_out[lax.rem(c, slots)] = out.astype(BF16)
        x_copy(c).start()
        gh_buf[:, 0:PIECE] = dot(ws_ref[...], hid_buf[c])
        forward_rest(m, (h,))

        @pl.when(s > 0)
        def _():
            k_copy(c).wait_recv()
            gh_buf[:, 0:PIECE] += sg_buf[c].astype(F32)

        reuse(k_copy, c)
        k_out[lax.rem(c, slots)] = gh_buf[:, 0:PIECE].astype(BF16)
        k_copy(c).start()

    def forward_head(m):
        forward(m, (0, 1))
        total = dot(ws_ref[...], columns(hid_buf, 2 * m, (0, 1)))
        for h in (0, 1):
            k_copy(2 * m + h).wait_recv()
        head(m, total + columns(sg_buf, 2 * m, (0, 1)).astype(F32))
        forward_rest(m, (0, 1))

    def grad_field(m, parts, grad_hidden):
        kept = 2 * lax.rem(m, keep)
        grad_gate = jnp.concatenate(
            [
                grad_hidden * columns(d1_buf, 2 * m, parts).astype(F32),
                grad_hidden * columns(d2_buf, 2 * m, parts).astype(F32),
            ],
            axis=0,
        ).astype(BF16)
        put(gg_buf, kept, parts, grad_gate)
        if parts == (1,):
            back = dot_nt(grad_gate, shift_buf[PIECE:, PIECE:])
        elif parts == (0,):
            both = jnp.concatenate([grad_gate, gg_buf[kept + 1]], axis=1)
            back = dot_nt(both, shift_buf[0:PIECE, :])
        else:
            back = dot_nt(grad_gate, shift_buf[...])
        return dot(wd_t[res : 2 * res], grad_gate) + dot(wd_t[0:res], back.astype(BF16))

    def cond_message(m, parts):
        kept = 2 * lax.rem(m, keep)
        row = lax.broadcasted_iota(jnp.int32, (EXT, len(parts) * PIECE), 0)
        own = jnp.where(row < mel_rows, dot(wc_ref[...], columns(gg_buf, kept, parts)), 0.0)
        return own + columns(gc_buf, 2 * m, parts).astype(F32)

    def backward_piece(m, h):
        c = 2 * m + h
        gs_copy(c).wait_recv()

        @pl.when(s > 0)
        def _():
            gs_copy(c).start()

        gh_buf[:, 0:PIECE] = dot(ws_t[...], sg_buf[c])
        gx_copy(c).wait_recv()
        grad_hidden = gh_buf[:, 0:PIECE] + HALF_ROOT * dot(wr_t[...], gx_buf[c])
        grad_x = (HALF_ROOT * gx_buf[c].astype(F32) + grad_field(m, (h,), grad_hidden)).astype(BF16)

        @pl.when(s > 0)
        def _():
            reuse(gx_copy, c)
            gx_out[lax.rem(c, slots)] = grad_x
            gx_copy(c).start()

        gc_copy(c).wait_recv()
        message = cond_message(m, (h,))

        @pl.when(s > 0)
        def _():
            reuse(gc_copy, c)
            gc_out[lax.rem(c, slots)] = message.astype(BF16)
            gc_copy(c).start()

        @pl.when(is_first)
        def _():
            d1_buf[c] = grad_x
            gc_buf[c, 0:mel_rows, :] = message[0:mel_rows].astype(BF16)
            tail = message[mel_rows:EXT]
            if h == 0:
                frame = lax.broadcasted_iota(jnp.int32, mel_ref.shape, 0) == m
                extra_buf[0:1, 0:mel_rows] = jnp.sum(
                    jnp.where(frame, mel_ref[...].astype(F32), 0.0), axis=0, keepdims=True
                )
                lane = lax.broadcasted_iota(jnp.int32, (1, PIECE), 1)
                ids = jnp.where(lane == 0, spk_ref[0, m], 0)
                ids = jnp.where(lane == 1, spk_ref[1, m], ids)
                ids = jnp.where(lane == 2, offs_ref[0, m], ids)
                extra_buf[1:2, :] = ids.astype(F32)
                tail = tail + extra_buf[...]
            gc_buf[c, mel_rows:EXT, :] = tail.astype(BF16)

    def backward_pair(m):
        parts = (0, 1)
        grad_hidden = dot(ws_t[...], columns(sg_buf, 2 * m, parts))
        grad_x = grad_field(m, parts, grad_hidden).astype(BF16)
        for h in (1, 0):
            c = 2 * m + h
            reuse(gx_copy, c)
            gx_out[lax.rem(c, slots)] = grad_x[:, h * PIECE : (h + 1) * PIECE]
            gx_copy(c).start()
        message = cond_message(m, parts).astype(BF16)
        for h in (1, 0):
            c = 2 * m + h
            reuse(gc_copy, c)
            gc_out[lax.rem(c, slots)] = message[:, h * PIECE : (h + 1) * PIECE]
            gc_copy(c).start()

    def add_halves(first_row, value):
        rows = value.shape[0] // 2
        acc[first_row : first_row + rows, 0:half] += value[0:rows]
        acc[first_row : first_row + rows, half : 2 * half] += value[rows : 2 * rows]

    def weight_gradients(m):
        parts = (0, 1)
        kept = 2 * lax.rem(m, keep)
        grad_gate = columns(gg_buf, kept, parts)
        x = columns(x_buf, 2 * m, parts)
        prev = dot(x, shift_buf[...]).astype(BF16)
        acc[0 : 2 * half, 0:res] += dot_nt(grad_gate, prev)
        acc[0 : 2 * half, res : 2 * res] += dot_nt(grad_gate, x)
        acc[2 * half : 2 * half + EXT, :] += dot_nt(columns(cond_ref, 2 * m, parts), grad_gate)
        hidden = columns(hid_buf, 2 * m, parts)
        row = 2 * half + EXT

        @pl.when(s < sections - 1)
        def _():
            add_halves(row, HALF_ROOT * dot_nt(columns(gx_buf, 2 * m, parts), hidden))

        add_halves(row + half // 2, dot_nt(columns(sg_buf, 2 * m, parts), hidden))

        @pl.when(is_last)
        def _():
            add_halves(main_rows, dot_nt(columns(gp_buf, kept, parts), columns(a1_buf, kept, parts)))
            add_halves(main_rows + half // 2, dot_nt(columns(gl_buf, kept, parts), columns(a2_buf, kept, parts)))

    late = keep == micro

    @pl.when(is_last)
    def _():
        @pl.loop(0, micro)
        def _(m):
            build_shift(m)
            forward_head(m)
            backward_pair(m)
            if not late:
                weight_gradients(m)

    @pl.when(jnp.logical_not(is_last))
    def _():
        @pl.loop(0, micro)
        def _(m):
            build_shift(m)
            forward_piece(m, 0)
            forward_piece(m, 1)

        @pl.when(is_first)
        def _():
            prepare()
            extra_buf[...] = jnp.zeros_like(extra_buf)

    @pl.loop(0, micro)
    def _(m):
        build_shift(m)

        @pl.when(jnp.logical_not(is_last))
        def _():
            backward_piece(m, 1)
            backward_piece(m, 0)

        if late:
            weight_gradients(m)
        else:

            @pl.when(jnp.logical_not(is_last))
            def _():
                weight_gradients(m)

    def gin_copy(other):
        return remote(
            d1_buf.at[:, pl.ds(pl.multiple_of(other * share, share), share), :],
            gin_buf,
            gin_ss.at[other],
            gin_rs.at[0],
            other,
            z,
        )

    def own_local():
        return pltpu.make_async_copy(gc_buf, o_g.at[z], loc_sem.at[0])

    def own_hub():
        return remote(gc_buf, o_g.at[z], gown_ss.at[0], g_rs.at[z], HUB, z)

    def own_peer(other):
        return remote(o_g.at[z], o_g.at[z], gpeer_ss.at[other], g_rs.at[z], HUB, other)

    def part_chip(j, chip):
        return remote(o_g.at[j], o_g.at[j], ghub_ss.at[j, chip], g_rs.at[j], 2 * chip, z)

    def part_next(j):
        return remote(o_g.at[j], o_g.at[j], gnext_ss.at[j], g_rs.at[j], s + 1, z)

    def spread(j):
        part_next(j).start()

        @pl.loop(0, sections // 2)
        def _(chip):
            @pl.when((chip != HUB // 2) & ((chip > 0) | (z != j)))
            def _():
                part_chip(j, chip).start()

    @pl.when(is_first)
    def _():
        own_local().start()
        own_hub().start()
        own_local().wait()

        @pl.loop(1, sections)
        def _(other):
            gin_copy(other).start()

        gin_buf[...] = d1_buf[:, 0:share, :]

    left = z < groups // 2
    inward = jnp.where(left, z + 1, z - 1)
    outward = jnp.where(left, z - 1, z + 1)
    is_edge = (z == 0) | (z == groups - 1)
    is_mid = (z == groups // 2 - 1) | (z == groups // 2)
    distance = jnp.where(left, groups // 2 - 1 - z, z - groups // 2)
    lag = LAG * (2 * distance + 1)
    count = jnp.where(is_last, main_blocks + head_blocks, main_blocks)

    def block_of(i):
        return jnp.where(is_last, jnp.where(i < head_blocks, i + main_blocks, i - head_blocks), i)

    def rows_of(b):
        return pl.ds(pl.multiple_of(b * BLOCK, BLOCK), BLOCK)

    def swap_copy(b):
        return remote(part_out.at[rows_of(b)], o_acc.at[rows_of(b)], zi_ss.at[b], zt_rs.at[b], s, inward)

    def part_copy(b):
        return remote(part_out.at[rows_of(b)], part_in.at[rows_of(b)], zi_ss.at[b], zp_rs.at[b], s, inward)

    def total_copy(b):
        return remote(o_acc.at[rows_of(b)], o_acc.at[rows_of(b)], zo_ss.at[b], zt_rs.at[b], s, outward)

    def head_copy(j):
        rows = rows_of(main_blocks + j)
        return remote(o_acc.at[rows], o_acc.at[rows], hd_ss.at[j], hd_rs.at[j], s - 1, z)

    def send_part(b):
        rows = rows_of(b)

        @pl.when(is_edge)
        def _():
            part_out[rows, :] = acc[rows, :].astype(BF16)

        @pl.when(jnp.logical_not(is_edge))
        def _():
            part_copy(b).wait_recv()
            part_out[rows, :] = (acc[rows, :] + part_in[rows, :].astype(F32)).astype(BF16)

        @pl.when(is_mid)
        def _():
            swap_copy(b).start()

        @pl.when(jnp.logical_not(is_mid))
        def _():
            part_copy(b).start()

    def finish_part(b):
        rows = rows_of(b)
        swap_copy(b).wait_recv()

        @pl.when(is_mid)
        def _():
            o_acc[rows, :] = (part_out[rows, :].astype(F32) + o_acc[rows, :].astype(F32)).astype(BF16)

        @pl.when(jnp.logical_not(is_edge))
        def _():
            total_copy(b).start()

    last_step = main_blocks + lag - 1
    head_at = lag + 2
    own_at = jnp.minimum(9 + 6 * distance, last_step)
    rest_at = jnp.where(is_first, 20, jnp.where(is_hub, 17, jnp.where(s < sections // 2 + 2, 28, 31)))
    rest_at = jnp.minimum(rest_at + 6 * distance, last_step)

    @pl.loop(0, count + lag)
    def _(i):
        @pl.when(i < count)
        def _():
            send_part(block_of(i))

        @pl.when(i >= lag)
        def _():
            b = block_of(i - lag)
            finish_part(b)

            @pl.when(b >= main_blocks)
            def _():
                head_copy(b - main_blocks).start()

        @pl.when(jnp.logical_not(is_last) & (i >= head_at) & (i < head_at + head_blocks))
        def _():
            j = i - head_at
            head_copy(j).wait_recv()

            @pl.when(s > 0)
            def _():
                head_copy(j).start()

        @pl.when(is_hub & (i == own_at))
        def _():
            own_hub().wait_recv()
            for other in range(groups):

                @pl.when(z != other)
                def _():
                    own_peer(other).start()

            spread(z)

        @pl.when((lax.rem(s, 2) == 0) & (i == rest_at))
        def _():
            for j in range(groups):

                @pl.when((z != j) | (s > HUB))
                def _():
                    part_next(j).wait_recv()

                @pl.when(is_hub & (z != j))
                def _():
                    spread(j)

                @pl.when(jnp.logical_not(is_hub))
                def _():
                    part_next(j).start()

    @pl.when(s > 0)
    def _():
        gin_copy(0).wait_recv()

    for c in range(pieces):
        o_gin[:, c * PIECE : (c + 1) * PIECE] = gin_buf[c]

    @pl.when(is_first)
    def _():
        own_hub().wait_send()

        @pl.loop(1, sections)
        def _(other):
            gin_copy(other).wait_send()

    @pl.when(is_hub)
    def _():
        for j in range(groups):

            @pl.when(z != j)
            def _():
                own_peer(j).wait_send()

            @pl.loop(0, sections // 2)
            def _(chip):
                @pl.when((chip != HUB // 2) & ((chip > 0) | (z != j)))
                def _():
                    part_chip(j, chip).wait_send()

    for j in range(groups):

        @pl.when(lax.rem(s, 2) == 0)
        def _():
            part_next(j).wait_send()

        @pl.when(lax.rem(s, 2) == 1)
        def _():
            part_next(j).wait_recv()

    @pl.when(s > 0)
    def _():
        @pl.loop(0, head_blocks)
        def _(j):
            head_copy(j).wait_send()

    @pl.loop(0, count)
    def _(b):
        part_copy(b).wait_send()

        @pl.when(jnp.logical_not(is_edge))
        def _():
            total_copy(b).wait_send()

    @pl.loop(0, slots)
    def _(c):
        @pl.when(s < sections - 1)
        def _():
            x_copy(c).wait_send()
            k_copy(c).wait_send()

        @pl.when(s > 0)
        def _():
            gx_copy(c).wait_send()
            gc_copy(c).wait_send()

    @pl.when(s > 0)
    def _():
        @pl.loop(0, pieces)
        def _(c):
            gs_copy(c).wait_send()


def run_step(dims, tables, arrays, weights):
    sections, groups, micro, res, half, classes, slots, keep, mel_rows = dims
    pieces = 2 * micro
    rows = 2 * half + EXT + half + half // 2 + classes // 2
    blocks = rows // BLOCK
    head_blocks = (half // 2 + classes // 2) // BLOCK
    share = res // sections
    smem = pl.BlockSpec(memory_space=pltpu.SMEM)
    vmem = pl.BlockSpec(memory_space=pltpu.VMEM)
    anywhere = pl.BlockSpec(memory_space=pl.ANY)
    dma = pltpu.SemaphoreType.DMA

    def tile(*shape, dtype=BF16):
        return pltpu.VMEM(shape, dtype)

    scratch = [
        tile(pieces, res, PIECE),
        tile(pieces, half, PIECE),
        tile(pieces, res, PIECE),
        tile(pieces, EXT, PIECE),
        tile(pieces, half, PIECE),
        tile(pieces, half, PIECE),
        tile(pieces, half, PIECE),
        tile(slots, res, PIECE),
        tile(slots, half, PIECE),
        tile(slots, res, PIECE),
        tile(slots, EXT, PIECE),
        tile(2 * half, 2 * PIECE, dtype=F32),
        tile(half, PIECE, dtype=F32),
        tile(2 * keep, 2 * half, PIECE),
        tile(2 * PIECE, 2 * PIECE),
        tile(pieces, EXT, PIECE),
        tile(EXT, 2 * half),
        tile(2 * half, 2 * res),
        tile(res, half),
        tile(half, half),
        tile(half, half),
        tile(classes, half),
        tile(2 * half, EXT),
        tile(2 * res, 2 * half),
        tile(half, res),
        tile(half, half),
        tile(half, half),
        tile(half, classes),
        tile(2 * keep, classes, PIECE),
        tile(2 * keep, half, PIECE),
        tile(2 * keep, half, PIECE),
        tile(2 * keep, half, PIECE),
        tile(rows, WIDE, dtype=F32),
        tile(rows, WIDE),
        tile(rows, WIDE),
        tile(pieces, share, PIECE),
        tile(2, micro * mel_rows, PIECE, dtype=F32),
        tile(EXT - mel_rows, PIECE, dtype=F32),
        dma((pieces,)),
        dma((9,)),
        dma((1,)),
        dma((slots,)),
        dma((pieces,)),
        dma((slots,)),
        dma((pieces,)),
        dma((pieces,)),
        dma((pieces,)),
        dma((slots,)),
        dma((pieces,)),
        dma((slots,)),
        dma((pieces,)),
        dma((blocks,)),
        dma((blocks,)),
        dma((blocks,)),
        dma((blocks,)),
        dma((head_blocks,)),
        dma((head_blocks,)),
        dma((groups,)),
        dma((1,)),
        dma((groups,)),
        dma((groups, sections // 2)),
        dma((groups,)),
        dma((sections,)),
        dma((1,)),
    ]
    return pl.pallas_call(
        functools.partial(step_kernel, dims),
        out_shape=(
            jax.ShapeDtypeStruct((rows, WIDE), BF16),
            jax.ShapeDtypeStruct((groups, pieces, EXT, PIECE), BF16),
            jax.ShapeDtypeStruct((share, pieces * PIECE), BF16),
        ),
        in_specs=[smem] * 4 + [vmem] * 5 + [anywhere] * 7,
        out_specs=(vmem, anywhere, vmem),
        scratch_shapes=scratch,
        compiler_params=pltpu.CompilerParams(
            collective_id=0, has_side_effects=True, vmem_limit_bytes=63 * 2**20
        ),
        cost_estimate=pl.CostEstimate(flops=10**10, bytes_accessed=3 * 10**7, transcendentals=10**6),
        name="train_step",
    )(*tables, *arrays, *weights)


def finish_kernel(
    dims, steps, dil, cond, res, skip, post, out, shared, o_dil, o_cond, o_bias, o_res, o_skip, o_post, o_out,
    o_up, o_table, o_loss, field, mel_rows_buf, mel_columns, table,
):
    mel_rows, half = dims
    i = pl.program_id(0)
    frames = shared.shape[0]

    @pl.when(i == 0)
    def _():
        table[...] = jnp.zeros_like(table)
        lane = lax.broadcasted_iota(jnp.int32, (mel_rows, PIECE), 1)
        number = lane.astype(F32)

        def one(f, loss):
            extra = shared[f, 0, mel_rows:EXT, :].astype(F32)
            loss = loss + extra + shared[f, 1, mel_rows:EXT, :].astype(F32)
            mel_rows_buf[pl.ds(f, 1), :] = extra[0:1]
            ids = extra[1:2]
            first = jnp.zeros((mel_rows, 1), F32)
            second = jnp.zeros((mel_rows, 1), F32)
            for h in range(2):
                part = shared[f, h, 0:mel_rows, :].astype(F32)
                field[h, pl.ds(pl.multiple_of(f * mel_rows, 16), mel_rows), :] = part
                later = number + float(h * PIECE) >= ids[:, 2:3]
                first = first + jnp.sum(jnp.where(later, 0.0, part), axis=1, keepdims=True)
                second = second + jnp.sum(jnp.where(later, part, 0.0), axis=1, keepdims=True)
            table[...] += jnp.where(number == ids[:, 0:1], first, 0.0)
            table[...] += jnp.where(number == ids[:, 1:2], second, 0.0)
            return loss

        loss = lax.fori_loop(0, frames, one, jnp.zeros((EXT - mel_rows, PIECE), F32))
        row = lax.broadcasted_iota(jnp.int32, loss.shape, 0)
        loss = jnp.where((row >= 2) & (row < 5), loss, 0.0)
        o_loss[...] = jnp.sum(jnp.sum(loss, axis=1, keepdims=True), axis=0, keepdims=True)
        o_table[...] = table[:, 0 : o_table.shape[1]]
        mel_columns[...] = jnp.transpose(mel_rows_buf[...])[0:mel_rows].astype(BF16)

    o_dil[0] = dil[...].astype(F32)
    for source, target in ((res, o_res), (skip, o_skip), (post, o_post), (out, o_out)):
        target[0] = source[:, 0:half].astype(F32)
        target[1] = source[:, half : 2 * half].astype(F32)

    @pl.when(i < mel_rows // 16)
    def _():
        o_cond[...] = cond[...].astype(F32)

    @pl.when(i == mel_rows // 16)
    def _():
        o_bias[...] = cond[...].astype(F32)[0:1]

    channels = mel_rows // steps
    for j in range(channels):
        rows = pl.ds(i * channels + j, frames, stride=mel_rows)
        matrix = jnp.concatenate([field[0, rows, :], field[1, rows, :]], axis=1)
        o_up[j] = dot(mel_columns[...], matrix.astype(BF16))


def finish(sums, shared, half, classes, mel_rows, speakers):
    steps = 8
    frames = shared.shape[0]
    first = 2 * half
    small = half // 2 // steps
    last = classes // 2 // steps
    res_at = (first + EXT) // small
    per = half // 2 // small
    rows = mel_rows // 16

    def strip(height, index):
        return pl.BlockSpec((height, WIDE), index)

    def two(height):
        return pl.BlockSpec((2, height, half), lambda i: (0, i, 0))

    def fixed(*shape):
        return pl.BlockSpec(shape, lambda i: (0,) * len(shape))

    def f32(*shape):
        return jax.ShapeDtypeStruct(shape, F32)

    return pl.pallas_call(
        functools.partial(finish_kernel, (mel_rows, half), steps),
        grid=(steps,),
        out_shape=(
            f32(1, first, WIDE),
            f32(mel_rows, WIDE),
            f32(1, WIDE),
            f32(2, half // 2, half),
            f32(2, half // 2, half),
            f32(2, half // 2, half),
            f32(2, classes // 2, half),
            f32(mel_rows, mel_rows, 2 * PIECE),
            f32(mel_rows, speakers),
            f32(1, 1),
        ),
        in_specs=[
            strip(first // steps, lambda i: (i, 0)),
            strip(16, lambda i: (first // 16 + jnp.minimum(i, rows), 0)),
            strip(small, lambda i: (res_at + i, 0)),
            strip(small, lambda i: (res_at + per + i, 0)),
            strip(small, lambda i: (res_at + 2 * per + i, 0)),
            strip(last, lambda i: ((first + EXT + half + half // 2) // last + i, 0)),
            pl.BlockSpec(memory_space=pltpu.VMEM),
        ],
        out_specs=(
            pl.BlockSpec((1, first // steps, WIDE), lambda i: (0, i, 0)),
            strip(16, lambda i: (jnp.minimum(i, rows - 1), 0)),
            fixed(1, WIDE),
            two(small),
            two(small),
            two(small),
            two(last),
            pl.BlockSpec((mel_rows // steps, mel_rows, 2 * PIECE), lambda i: (i, 0, 0)),
            fixed(mel_rows, speakers),
            fixed(1, 1),
        ),
        scratch_shapes=[
            pltpu.VMEM((2, frames * mel_rows, PIECE), F32),
            pltpu.VMEM((frames, PIECE), F32),
            pltpu.VMEM((mel_rows, frames), BF16),
            pltpu.VMEM((mel_rows, PIECE), F32),
        ],
        compiler_params=pltpu.CompilerParams(
            vmem_limit_bytes=48 * 2**20, dimension_semantics=("arbitrary",)
        ),
        name="finish",
    )(sums, sums, sums, sums, sums, sums, shared)


def local(
    inputs,
    targets,
    mel,
    speakers,
    speaker_sample_counts,
    segment_offsets,
    dilations,
    dilated_kernel,
    conditioning_projection,
    dilated_gate_bias,
    residual_projection,
    skip_projection,
    upsample_weight,
    speaker_table,
    first_output_projection,
    class_projection,
):
    sections = lax.axis_size("section")
    groups = lax.axis_size("dp")
    micro = segment_offsets.shape[0]
    res, tokens = inputs.shape
    length = tokens // micro
    mel_rows = mel.shape[0]
    hop = upsample_weight.shape[0]
    half = residual_projection.shape[2]
    classes = class_projection.shape[0]
    pieces = 2 * micro
    assert length == 2 * PIECE and hop == length and mel_rows + 16 == EXT and 2 * half == WIDE

    slots, keep = (pieces, micro) if pieces <= 8 else (2, 1)
    dims = (sections, groups, micro, res, half, classes, slots, keep, mel_rows)
    sums, shared, grad_inputs = run_step(
        dims,
        (dilations, segment_offsets.T, speakers.T, speaker_sample_counts),
        (
            targets.reshape(micro, 1, length),
            mel.T,
            speaker_table,
            conditioning_projection[0].T,
            dilated_gate_bias,
        ),
        (
            inputs,
            upsample_weight.transpose(1, 2, 0).reshape(mel_rows * mel_rows, hop),
            dilated_kernel[0],
            residual_projection[0],
            skip_projection[0],
            first_output_projection,
            class_projection,
        ),
    )
    shared = shared.reshape(groups * micro, 2, EXT, PIECE)
    dil, cond, bias, grad_res, grad_skip, post, out, up, table, loss = finish(
        sums, shared, half, classes, mel_rows, speaker_table.shape[1]
    )
    return (
        loss.reshape(()),
        grad_inputs,
        dil,
        cond.T[None],
        bias,
        grad_res.reshape(1, half, half),
        grad_skip.reshape(1, half, half),
        up.transpose(2, 0, 1),
        table,
        post.reshape(half, half),
        out.reshape(classes, half),
    )


def solution(mesh):
    return jax.shard_map(
        local,
        mesh=mesh,
        in_specs=(
            P(None, "dp"),
            P("dp"),
            P(None, "dp"),
            P("dp", None),
            P(),
            P("dp", None),
            P("section"),
            P("section", None, None),
            P("section", None, None),
            P("section", None),
            P("section", None, None),
            P("section", None, None),
            P(),
            P(),
            P(),
            P(),
        ),
        out_specs=(
            P(),
            P("section", "dp"),
            P("section", None, None),
            P("section", None, None),
            P("section", None),
            P("section", None, None),
            P("section", None, None),
            P(),
            P(),
            P(),
            P(),
        ),
        check_vma=False,
    )
```

```python
import functools
import math

import jax
import jax.numpy as jnp
from jax import lax
from jax.experimental import pallas as pl
from jax.experimental.pallas import tpu as pltpu
from jax.sharding import PartitionSpec as P

HALF_ROOT = 0.7071067811865476
WEIGHT_SCALE = 64.0
MESH = pl.DeviceIdType.MESH
BF16 = jnp.bfloat16
F32 = jnp.float32

PIECE = 128
EXT = 96
WIDE = 1024
BLOCK = 32
HUB = 2
LAG = 3


def dot(left, right):
    return jnp.dot(left, right, preferred_element_type=F32)


def dot_nt(left, right):
    return lax.dot_general(left, right, (((1,), (1,)), ((), ())), preferred_element_type=F32)


def dot_tn(left, right):
    return lax.dot_general(left, right, (((0,), (0,)), ((), ())), preferred_element_type=F32)


def sigmoid(values):
    return 0.5 * jnp.tanh(0.5 * values) + 0.5


def step_kernel(
    dims,
    dil_ref,
    offs_ref,
    spk_ref,
    cnt_ref,
    tgt_ref,
    mel_ref,
    tab_ref,
    bias_in,
    inp_hbm,
    up_hbm,
    wc_hbm,
    wd_hbm,
    wr_hbm,
    ws_hbm,
    wp_hbm,
    wk_hbm,
    o_acc,
    o_g,
    o_gin,
    x_buf,
    sg_buf,
    gx_buf,
    gc_buf,
    hid_buf,
    d1_buf,
    d2_buf,
    x_out,
    k_out,
    gx_out,
    gc_out,
    gate_buf,
    gh_buf,
    gg_buf,
    inp_buf,
    shift_buf,
    shift_back,
    cond_ref,
    cond_t,
    wc_ref,
    wd_ref,
    wr_ref,
    ws_ref,
    wp_ref,
    wk_ref,
    wd_t,
    wr_t,
    ws_t,
    wp_t,
    wk_t,
    gl_buf,
    a2_buf,
    gp_buf,
    a1_buf,
    acc,
    part_out,
    part_in,
    gin_buf,
    up_buf,
    extra_buf,
    inp_sem,
    load_sem,
    loc_sem,
    x_ss,
    x_rs,
    k_ss,
    k_rs,
    gs_ss,
    gs_rs,
    gx_ss,
    gx_rs,
    gc_ss,
    gc_rs,
    zi_ss,
    zo_ss,
    zp_rs,
    zt_rs,
    hd_ss,
    hd_rs,
    g_rs,
    gown_ss,
    gpeer_ss,
    ghub_ss,
    gnext_ss,
    gin_ss,
    gin_rs,
):
    sections, groups, micro, res, half, classes, slots, keep, mel_rows = dims
    pieces = 2 * micro
    s = lax.axis_index("section")
    z = lax.axis_index("dp")
    is_first = s == 0
    is_last = s == sections - 1
    is_hub = s == HUB
    head_scale = 1.0 / math.sqrt(sections)
    main_rows = 2 * half + EXT + half
    head_rows = half // 2 + classes // 2
    main_blocks = main_rows // BLOCK
    head_blocks = head_rows // BLOCK
    share = res // sections
    feeder = sections - 3 if sections > 4 else sections - 1

    barrier = pltpu.get_barrier_semaphore()

    def greet(cond, dev_s, dev_z):
        @pl.when(cond)
        def _():
            pl.semaphore_signal(barrier, 1, device_id=(dev_s, dev_z), device_id_type=MESH)

    greet(s > 0, s - 1, z)
    greet(s < sections - 1, s + 1, z)
    greet(z > 0, s, z - 1)
    greet(z < groups - 1, s, z + 1)
    greet(s >= 2, 0, z)
    greet((s > HUB + 1) & (lax.rem(s, 2) == 0), HUB, z)

    @pl.when(is_first)
    def _():
        @pl.loop(2, sections)
        def _(other):
            pl.semaphore_signal(barrier, 1, device_id=(other, z), device_id_type=MESH)

    @pl.when(is_hub)
    def _():
        @pl.loop(HUB // 2 + 1, sections // 2)
        def _(chip):
            pl.semaphore_signal(barrier, 1, device_id=(2 * chip, z), device_id_type=MESH)

        for other in range(groups):
            greet((other > z + 1) | (other < z - 1), s, other)

    far = (lax.rem(s, 2) == 1) & (s > 1) & (s < sections - 1)
    greet(far, sections - 1, z)

    @pl.when(is_last)
    def _():
        @pl.loop(1, sections // 2 - 1)
        def _(chip):
            pl.semaphore_signal(barrier, 1, device_id=(2 * chip + 1, z), device_id_type=MESH)

    greet(s == 1, feeder, z)
    greet(s == feeder, 1, z)

    def flag(cond):
        return jnp.where(cond, 1, 0)

    z_near = flag(z > 0) + flag(z < groups - 1)
    expected = (
        flag(s > 0)
        + flag(s < sections - 1)
        + z_near
        + jnp.where(is_first, sections - 2, flag(s >= 2))
        + flag((s > HUB + 1) & (lax.rem(s, 2) == 0))
        + flag(far)
        + flag(s == 1)
        + flag(s == feeder)
        + jnp.where(is_last, sections // 2 - 2, 0)
        + jnp.where(is_hub, groups - 1 - z_near + sections // 2 - HUB // 2 - 1, 0)
    )

    def input_copy(c):
        slot = lax.rem(c, slots)
        return pltpu.make_async_copy(
            inp_hbm.at[:, pl.ds(pl.multiple_of(c * PIECE, PIECE), PIECE)],
            inp_buf.at[slot],
            inp_sem.at[slot],
        )

    quarter = mel_rows // 4
    weight_refs = (
        (wd_hbm, wd_ref),
        (wr_hbm, wr_ref),
        (ws_hbm, ws_ref),
        (wc_hbm, wc_ref.at[0:mel_rows]),
        (wp_hbm, wp_ref),
        (wk_hbm, wk_ref),
    )
    loads = [
        pltpu.make_async_copy(source, target, load_sem.at[4 + position])
        for position, (source, target) in enumerate(weight_refs)
    ]
    frame_loads = [
        pltpu.make_async_copy(
            up_hbm.at[pl.ds(q * quarter * mel_rows, quarter * mel_rows), :],
            part_out.at[pl.ds(0, quarter * mel_rows), pl.ds(q * 2 * PIECE, 2 * PIECE)],
            load_sem.at[q],
        )
        for q in range(4)
    ]
    for load in loads[:4] + frame_loads:
        load.start()

    @pl.when(is_first)
    def _():
        @pl.loop(0, slots)
        def _(c):
            input_copy(c).start()

    for load in loads[4:]:
        load.start()
    spare = lax.broadcasted_iota(jnp.int32, (EXT - mel_rows, 2 * half), 0)
    bias = jnp.broadcast_to(bias_in[...].astype(F32), (EXT - mel_rows, 2 * half))
    wc_ref[mel_rows:EXT] = jnp.where(spare == 0, bias, 0.0).astype(BF16)
    loads[0].wait()
    wd_t[...] = jnp.transpose(wd_ref[...])
    for load in loads[1:]:
        load.wait()
    wr_t[...] = jnp.transpose(wr_ref[...])
    ws_t[...] = jnp.transpose(ws_ref[...])

    for load in frame_loads:
        load.wait()

    @pl.loop(0, quarter // 4)
    def _(group):
        for q in range(4):
            for part in range(4):
                row = group * 4 + part
                lanes = slice(q * 2 * PIECE, (q + 1) * 2 * PIECE)
                matrix = part_out[pl.ds(pl.multiple_of(row * mel_rows, 16), mel_rows), lanes]
                frames = dot(mel_ref[...], matrix)
                rows = pl.ds(q * quarter + row, micro, stride=mel_rows)
                for h in range(2):
                    up_buf[h, rows, :] = frames[:, h * PIECE : (h + 1) * PIECE]

    speaker_lane = lax.broadcasted_iota(jnp.int32, tab_ref.shape, 1)
    spare = lax.broadcasted_iota(jnp.int32, (EXT - mel_rows, PIECE), 0)
    table = tab_ref[...].astype(F32)

    @pl.loop(0, micro)
    def _(m):
        def column(which):
            return jnp.sum(jnp.where(speaker_lane == spk_ref[which, m], table, 0.0), axis=1, keepdims=True)

        first, second = column(0), column(1)
        for h in range(2):
            time = lax.broadcasted_iota(jnp.int32, (mel_rows, PIECE), 1) + h * PIECE
            speaker = jnp.where(time >= offs_ref[0, m], second, first)
            rows = pl.ds(pl.multiple_of(m * mel_rows, 16), mel_rows)
            cond_ref[2 * m + h, 0:mel_rows, :] = (up_buf[h, rows, :] + speaker).astype(BF16)
            cond_ref[2 * m + h, mel_rows:EXT, :] = jnp.where(spare == 0, 1.0, 0.0).astype(BF16)
            cond_t[2 * m + h] = jnp.transpose(cond_ref[2 * m + h])

    @pl.when(s > 0)
    def _():
        acc[...] = jnp.zeros_like(acc)

    @pl.when(is_last)
    def _():
        wp_t[...] = jnp.transpose(wp_ref[...])
        wk_t[...] = jnp.transpose(wk_ref[...])
        gx_buf[...] = jnp.zeros_like(gx_buf)

    pl.semaphore_wait(barrier, expected)

    def remote(src, dst, send_sem, recv_sem, dev_s, dev_z):
        return pltpu.make_async_remote_copy(
            src_ref=src,
            dst_ref=dst,
            send_sem=send_sem,
            recv_sem=recv_sem,
            device_id=(dev_s, dev_z),
            device_id_type=MESH,
        )

    ring = pieces > slots

    def send_of(semaphores, slot):
        return semaphores.at[slot if ring else 0]

    def x_copy(c):
        slot = lax.rem(c, slots)
        return remote(x_out.at[slot], x_buf.at[c], send_of(x_ss, slot), x_rs.at[c], s + 1, z)

    def k_copy(c):
        slot = lax.rem(c, slots)
        return remote(k_out.at[slot], sg_buf.at[c], send_of(k_ss, slot), k_rs.at[c], s + 1, z)

    def gx_copy(c):
        slot = lax.rem(c, slots)
        return remote(gx_out.at[slot], gx_buf.at[c], send_of(gx_ss, slot), gx_rs.at[c], s - 1, z)

    def gc_copy(c):
        slot = lax.rem(c, slots)
        return remote(gc_out.at[slot], gc_buf.at[c], send_of(gc_ss, slot), gc_rs.at[c], s - 1, z)

    def reuse(copy, c):
        if ring:

            @pl.when(c >= slots)
            def _():
                copy(c).wait_send()

    def drain(copy, whole):
        if ring:

            @pl.loop(0, slots)
            def _(c):
                copy(c).wait_send()

        else:
            whole().wait_send()

    chips = sections // 2
    far_chips = range(chips - 2, 0, -1)

    def gs_copy(c):
        return remote(sg_buf.at[c], sg_buf.at[c], gs_ss.at[0], gs_rs.at[c], s - 1, z)

    def gs_first(c):
        return remote(sg_buf.at[c], sg_buf.at[c], gs_ss.at[1], gs_rs.at[c], 1, z)

    def gs_chip(c, chip):
        return remote(sg_buf.at[c], sg_buf.at[c], gs_ss.at[1 + chip], gs_rs.at[c], 2 * chip + 1, z)

    def gs_whole(position):
        return remote(sg_buf, sg_buf, gs_ss.at[position], gs_rs.at[0], s - 1, z)

    def build_shift(m):
        dilation = dil_ref[0]
        middle = offs_ref[0, m]
        shape = (2 * PIECE, 2 * PIECE)

        def matrix(source, target):
            start = jnp.where(target >= middle, middle, 0)
            hit = (source == target - dilation) & (source >= start)
            return jnp.where(hit, 1.0, 0.0).astype(BF16)

        rows = lax.broadcasted_iota(jnp.int32, shape, 0)
        lanes = lax.broadcasted_iota(jnp.int32, shape, 1)
        shift_buf[...] = matrix(lanes, rows)
        shift_back[...] = matrix(rows, lanes)

    def pair(ref, first):
        return jnp.concatenate([ref[first], ref[first + 1]], axis=1)

    def put_pair(ref, first, value):
        for h in range(2):
            ref[first + h] = value[:, h * PIECE : (h + 1) * PIECE]

    def both(ref, first, parts):
        return jnp.concatenate([ref[first + h] for h in parts], axis=0)

    def put(ref, first, parts, value):
        for position, h in enumerate(parts):
            ref[first + h] = value[position * PIECE : (position + 1) * PIECE]

    def head(m, total):
        width = 2 * PIECE
        total = jnp.transpose(total.astype(BF16)).astype(F32) * head_scale
        sig_1 = sigmoid(total)
        act_1 = (total * sig_1).astype(BF16)
        slope_1 = sig_1 * (1.0 + total * (1.0 - sig_1)) * head_scale
        post = dot(wp_ref[...], act_1)
        sig_2 = sigmoid(post)
        act_2 = (post * sig_2).astype(BF16)
        slope_2 = sig_2 * (1.0 + post * (1.0 - sig_2))
        logits = dot(wk_ref[...], act_2)
        top = jnp.max(logits, axis=0, keepdims=True)
        expo = jnp.exp(logits - top)
        denominator = jnp.sum(expo, axis=0, keepdims=True)
        hit = tgt_ref[m] == lax.broadcasted_iota(jnp.int32, (classes, width), 0)
        picked = jnp.sum(jnp.where(hit, logits, 0.0), axis=0, keepdims=True)
        time = lax.broadcasted_iota(jnp.int32, (1, width), 1)

        def speaker_weight(which):
            count = cnt_ref[spk_ref[which, m]].astype(F32)
            return WEIGHT_SCALE * lax.rsqrt(jnp.full((1, width), count, F32))

        weight = jnp.where(time >= offs_ref[0, m], speaker_weight(1), speaker_weight(0))
        weight = jnp.where(time < offs_ref[1, m], weight, 0.0)
        grad_logits = (weight * (expo / denominator - jnp.where(hit, 1.0, 0.0))).astype(BF16)
        grad_post = (dot(wk_t[...], grad_logits) * slope_2).astype(BF16)
        grad_total = (dot(wp_t[...], grad_post) * slope_1).astype(BF16)
        put(sg_buf, 2 * m, (0, 1), jnp.transpose(grad_total))
        for h in (1, 0):
            c = 2 * m + h
            for chip in far_chips:
                gs_chip(c, chip).start()
            gs_copy(c).start()
            if feeder == sections - 1:
                gs_first(c).start()
        kept = 2 * lax.rem(m, keep)
        put_pair(gl_buf, kept, grad_logits)
        put_pair(a2_buf, kept, act_2)
        put_pair(gp_buf, kept, grad_post)
        put_pair(a1_buf, kept, act_1)
        loss_row = weight * (top + jnp.log(denominator) - picked)
        high = loss_row.astype(BF16)
        rest = loss_row - high.astype(F32)
        middle = rest.astype(BF16)
        low = (rest - middle.astype(F32)).astype(BF16)
        row = lax.broadcasted_iota(jnp.int32, (EXT, width), 0)
        message = jnp.where(row == mel_rows + 2, high.astype(F32), 0.0)
        message = jnp.where(row == mel_rows + 3, middle.astype(F32), message)
        message = jnp.where(row == mel_rows + 4, low.astype(F32), message)
        put_pair(gc_buf, 2 * m, message.astype(BF16))

    def forward(m, parts):
        high = len(parts) * PIECE
        for h in parts:
            c = 2 * m + h

            @pl.when(is_first)
            def _():
                input_copy(c).wait()
                x_buf[c] = jnp.transpose(inp_buf[lax.rem(c, slots)])
                if ring:

                    @pl.when(c + slots < pieces)
                    def _():
                        input_copy(c + slots).start()

            @pl.when(s > 0)
            def _():
                x_copy(c).wait_recv()

        x = both(x_buf, 2 * m, parts)
        if parts == (0,):
            prev = dot(shift_buf[0:PIECE, 0:PIECE], x)
        elif parts == (1,):
            prev = dot(shift_buf[PIECE : 2 * PIECE, :], both(x_buf, 2 * m, (0, 1)))
        else:
            prev = dot(shift_buf[...], x)
        gate = (
            dot(x, wd_t[res : 2 * res])
            + dot(both(cond_t, 2 * m, parts), wc_ref[...])
            + dot(prev.astype(BF16), wd_t[0:res])
        )
        th = jnp.tanh(gate[:, 0:half])
        sg = sigmoid(gate[:, half : 2 * half])
        gate_buf[0:high, 0:half] = th
        gate_buf[0:high, half : 2 * half] = sg
        put(hid_buf, 2 * m, parts, (th * sg).astype(BF16))

    def forward_rest(m, parts):
        high = len(parts) * PIECE
        th = gate_buf[0:high, 0:half]
        sg = gate_buf[0:high, half : 2 * half]
        put(d1_buf, 2 * m, parts, (sg * (1.0 - th * th)).astype(BF16))
        put(d2_buf, 2 * m, parts, (th * sg * (1.0 - sg)).astype(BF16))

    def forward_piece(m, h):
        c = 2 * m + h
        forward(m, (h,))
        reuse(x_copy, c)
        out = (x_buf[c].astype(F32) + dot(hid_buf[c], wr_t[...])) * HALF_ROOT
        x_out[lax.rem(c, slots)] = out.astype(BF16)
        x_copy(c).start()
        gh_buf[...] = dot(hid_buf[c], ws_t[...])
        forward_rest(m, (h,))

        @pl.when(s > 0)
        def _():
            k_copy(c).wait_recv()
            gh_buf[...] += sg_buf[c].astype(F32)

        reuse(k_copy, c)
        k_out[lax.rem(c, slots)] = gh_buf[...].astype(BF16)
        k_copy(c).start()

    def forward_head(m):
        forward(m, (0, 1))
        total = dot(both(hid_buf, 2 * m, (0, 1)), ws_t[...])
        for h in (0, 1):
            k_copy(2 * m + h).wait_recv()
        head(m, total + both(sg_buf, 2 * m, (0, 1)).astype(F32))
        forward_rest(m, (0, 1))

    def grad_field(m, parts, grad_hidden):
        kept = 2 * lax.rem(m, keep)
        grad_gate = jnp.concatenate(
            [
                grad_hidden * both(d1_buf, 2 * m, parts).astype(F32),
                grad_hidden * both(d2_buf, 2 * m, parts).astype(F32),
            ],
            axis=1,
        ).astype(BF16)
        put(gg_buf, kept, parts, grad_gate)
        if parts == (1,):
            back = dot(shift_back[PIECE:, PIECE:], grad_gate)
        elif parts == (0,):
            back = dot(shift_back[0:PIECE, :], jnp.concatenate([grad_gate, gg_buf[kept + 1]], axis=0))
        else:
            back = dot(shift_back[...], grad_gate)
        return dot(grad_gate, wd_ref[:, res : 2 * res]) + dot(back.astype(BF16), wd_ref[:, 0:res])

    def cond_message(m, h):
        kept = 2 * lax.rem(m, keep)
        row = lax.broadcasted_iota(jnp.int32, (EXT, PIECE), 0)
        own = jnp.where(row < mel_rows, dot_nt(wc_ref[...], gg_buf[kept + h]), 0.0)
        return own + gc_buf[2 * m + h].astype(F32)

    def backward_piece(m, h):
        c = 2 * m + h
        gs_copy(c).wait_recv()

        @pl.when(lax.rem(s, 2) == 1)
        def _():
            gs_copy(c).start()

        if feeder < sections - 1:

            @pl.when(s == feeder)
            def _():
                gs_first(c).start()

        gh_buf[...] = dot(sg_buf[c], ws_ref[...])
        gx_copy(c).wait_recv()
        grad_hidden = gh_buf[...] + HALF_ROOT * dot(gx_buf[c], wr_ref[...])
        grad_x = (HALF_ROOT * gx_buf[c].astype(F32) + grad_field(m, (h,), grad_hidden)).astype(BF16)

        @pl.when(s > 0)
        def _():
            reuse(gx_copy, c)
            gx_out[lax.rem(c, slots)] = grad_x
            gx_copy(c).start()

        @pl.when(is_first)
        def _():
            inp_buf[lax.rem(c, slots)] = jnp.transpose(grad_x)

        gc_copy(c).wait_recv()
        message = cond_message(m, h)

        @pl.when(s > 0)
        def _():
            reuse(gc_copy, c)
            gc_out[lax.rem(c, slots)] = message.astype(BF16)
            gc_copy(c).start()

        @pl.when(is_first)
        def _():
            gc_buf[c, 0:mel_rows, :] = message[0:mel_rows].astype(BF16)
            tail = message[mel_rows:EXT]
            if h == 0:
                frame = lax.broadcasted_iota(jnp.int32, mel_ref.shape, 0) == m
                extra_buf[0:1, 0:mel_rows] = jnp.sum(
                    jnp.where(frame, mel_ref[...].astype(F32), 0.0), axis=0, keepdims=True
                )
                lane = lax.broadcasted_iota(jnp.int32, (1, PIECE), 1)
                ids = jnp.where(lane == 0, spk_ref[0, m], 0)
                ids = jnp.where(lane == 1, spk_ref[1, m], ids)
                ids = jnp.where(lane == 2, offs_ref[0, m], ids)
                extra_buf[1:2, :] = ids.astype(F32)
                tail = tail + extra_buf[...]
            gc_buf[c, mel_rows:EXT, :] = tail.astype(BF16)

    def backward_pair(m):
        grad_hidden = dot(both(sg_buf, 2 * m, (0, 1)), ws_ref[...])
        grad_x = grad_field(m, (0, 1), grad_hidden).astype(BF16)
        for h in (1, 0):
            c = 2 * m + h
            reuse(gx_copy, c)
            gx_out[lax.rem(c, slots)] = grad_x[h * PIECE : (h + 1) * PIECE]
            gx_copy(c).start()
        for h in (1, 0):
            c = 2 * m + h
            reuse(gc_copy, c)
            gc_out[lax.rem(c, slots)] = cond_message(m, h).astype(BF16)
            gc_copy(c).start()

    def add_halves(first_row, value):
        rows = value.shape[0] // 2
        acc[first_row : first_row + rows, 0:half] += value[0:rows]
        acc[first_row : first_row + rows, half : 2 * half] += value[rows : 2 * rows]

    def weight_gradients(m):
        parts = (0, 1)
        kept = 2 * lax.rem(m, keep)
        grad_gate = both(gg_buf, kept, parts)
        x = both(x_buf, 2 * m, parts)
        prev = dot(shift_buf[...], x).astype(BF16)
        acc[0 : 2 * half, :] += dot_tn(grad_gate, jnp.concatenate([prev, x], axis=1))
        acc[2 * half : 2 * half + EXT, :] += dot(pair(cond_ref, 2 * m), grad_gate)
        hidden = both(hid_buf, 2 * m, parts)
        row = 2 * half + EXT

        @pl.when(s < sections - 1)
        def _():
            add_halves(row, HALF_ROOT * dot_tn(both(gx_buf, 2 * m, parts), hidden))

        add_halves(row + half // 2, dot_tn(both(sg_buf, 2 * m, parts), hidden))

        @pl.when(is_last)
        def _():
            add_halves(main_rows, dot_nt(pair(gp_buf, kept), pair(a1_buf, kept)))
            add_halves(main_rows + half // 2, dot_nt(pair(gl_buf, kept), pair(a2_buf, kept)))

    def gin_rows(other, group):
        return remote(
            inp_buf.at[:, pl.ds(pl.multiple_of(other * share, share), share), :],
            gin_buf.at[pl.ds(pl.multiple_of(group * slots, slots), slots)],
            gin_ss.at[0],
            gin_rs.at[0],
            other,
            z,
        )

    def gin_sent():
        return remote(
            inp_buf.at[:, share:res, :], inp_buf.at[:, share:res, :], gin_ss.at[0], gin_rs.at[0], 1, z
        )

    def gin_arrived():
        return remote(gin_buf, gin_buf, gin_ss.at[0], gin_rs.at[0], 1, z)

    def hand_out(group):
        @pl.loop(1, sections)
        def _(other):
            gin_rows(other, group).start()

        gin_buf[pl.ds(pl.multiple_of(group * slots, slots), slots)] = inp_buf[:, 0:share, :]

    @pl.when(is_last)
    def _():
        @pl.loop(0, micro)
        def _(m):
            build_shift(m)
            forward_head(m)
            backward_pair(m)
            if keep < micro:
                weight_gradients(m)

    @pl.when(jnp.logical_not(is_last))
    def _():
        @pl.loop(0, micro)
        def _(m):
            build_shift(m)
            forward_piece(m, 0)
            forward_piece(m, 1)

        @pl.when(is_first)
        def _():
            acc[...] = jnp.zeros_like(acc)
            extra_buf[...] = jnp.zeros_like(extra_buf)

    late = (s >= sections // 2) if keep == micro else is_last

    @pl.loop(0, 2 * micro)
    def _(step):
        m = jnp.where(late, lax.rem(step, micro), step // 2)
        is_back = jnp.where(late, step < micro, lax.rem(step, 2) == 0)
        build_shift(m)

        @pl.when(is_back & jnp.logical_not(is_last))
        def _():
            if ring:

                @pl.when(is_first & (m > 0))
                def _():
                    gin_sent().wait_send()

            backward_piece(m, 1)
            backward_piece(m, 0)

            @pl.when(is_first & (lax.rem(2 * m + 2, slots) == 0))
            def _():
                hand_out((2 * m + 2) // slots - 1)

        @pl.when(jnp.logical_not(is_back) & ((keep == micro) | jnp.logical_not(is_last)))
        def _():
            weight_gradients(m)

    def own_local():
        return pltpu.make_async_copy(gc_buf, o_g.at[z], loc_sem.at[0])

    def own_hub():
        return remote(gc_buf, o_g.at[z], gown_ss.at[0], g_rs.at[z], HUB, z)

    def own_peer(other):
        return remote(o_g.at[z], o_g.at[z], gpeer_ss.at[other], g_rs.at[z], HUB, other)

    def part_chip(j, chip):
        return remote(o_g.at[j], o_g.at[j], ghub_ss.at[j, chip], g_rs.at[j], 2 * chip, z)

    def part_next(j):
        return remote(o_g.at[j], o_g.at[j], gnext_ss.at[j], g_rs.at[j], s + 1, z)

    def spread(j):
        part_next(j).start()

        @pl.loop(0, sections // 2)
        def _(chip):
            @pl.when((chip != HUB // 2) & ((chip > 0) | (z != j)))
            def _():
                part_chip(j, chip).start()

    @pl.when(is_first)
    def _():
        own_local().start()
        own_hub().start()
        own_local().wait()

    left = z < groups // 2
    inward = jnp.where(left, z + 1, z - 1)
    outward = jnp.where(left, z - 1, z + 1)
    is_edge = (z == 0) | (z == groups - 1)
    is_mid = (z == groups // 2 - 1) | (z == groups // 2)
    distance = jnp.where(left, groups // 2 - 1 - z, z - groups // 2)
    lag = LAG * (2 * distance + 1) + 4 * distance
    count = jnp.where(is_last, main_blocks + head_blocks, main_blocks)

    def block_of(i):
        return jnp.where(is_last, jnp.where(i < head_blocks, i + main_blocks, i - head_blocks), i)

    def rows_of(b):
        return pl.ds(pl.multiple_of(b * BLOCK, BLOCK), BLOCK)

    cycle = zp_rs.shape[0]

    def swap_copy(i):
        rows = rows_of(block_of(i))
        return remote(part_out.at[rows], o_acc.at[rows], zi_ss.at[0], zt_rs.at[lax.rem(i, cycle)], s, inward)

    def part_copy(i):
        rows = rows_of(block_of(i))
        return remote(part_out.at[rows], part_in.at[rows], zi_ss.at[0], zp_rs.at[lax.rem(i, cycle)], s, inward)

    def total_copy(i):
        rows = rows_of(block_of(i))
        return remote(o_acc.at[rows], o_acc.at[rows], zo_ss.at[0], zt_rs.at[lax.rem(i, cycle)], s, outward)

    def head_copy(j):
        rows = rows_of(main_blocks + j)
        return remote(o_acc.at[rows], o_acc.at[rows], hd_ss.at[0], hd_rs.at[j], s - 1, z)

    def send_part(i):
        rows = rows_of(block_of(i))

        @pl.when(is_edge)
        def _():
            part_out[rows, :] = acc[rows, :].astype(BF16)

        @pl.when(jnp.logical_not(is_edge))
        def _():
            part_copy(i).wait_recv()
            part_out[rows, :] = (acc[rows, :] + part_in[rows, :].astype(F32)).astype(BF16)

        @pl.when(is_mid)
        def _():
            swap_copy(i).start()

        @pl.when(jnp.logical_not(is_mid))
        def _():
            part_copy(i).start()

    def finish_part(i):
        rows = rows_of(block_of(i))
        swap_copy(i).wait_recv()

        @pl.when(is_mid)
        def _():
            o_acc[rows, :] = (part_out[rows, :].astype(F32) + o_acc[rows, :].astype(F32)).astype(BF16)

        @pl.when(jnp.logical_not(is_edge))
        def _():
            total_copy(i).start()

    last_step = main_blocks + lag - 1
    head_at = lag + 2
    own_at = jnp.minimum(12 + 9 * distance, last_step)
    rest_at = jnp.where(is_first, 32, jnp.where(is_hub, 27, jnp.where(s < sections // 2 + 2, 46, 51)))
    rest_at = jnp.minimum(rest_at + 9 * distance, last_step)

    @pl.loop(0, count + lag)
    def _(i):
        @pl.when(i < count)
        def _():
            send_part(i)

        @pl.when(i >= lag)
        def _():
            finish_part(i - lag)
            b = block_of(i - lag)

            @pl.when(b >= main_blocks)
            def _():
                head_copy(b - main_blocks).start()

        @pl.when(jnp.logical_not(is_last) & (i >= head_at) & (i < head_at + head_blocks))
        def _():
            j = i - head_at
            head_copy(j).wait_recv()

            @pl.when(s > 0)
            def _():
                head_copy(j).start()

        @pl.when(is_hub & (i == own_at))
        def _():
            own_hub().wait_recv()
            for other in range(groups):

                @pl.when(z != other)
                def _():
                    own_peer(other).start()

            spread(z)

        @pl.when((lax.rem(s, 2) == 0) & (i == rest_at))
        def _():
            for j in range(groups):

                @pl.when((z != j) | (s > HUB))
                def _():
                    part_next(j).wait_recv()

                @pl.when(is_hub & (z != j))
                def _():
                    spread(j)

                @pl.when(jnp.logical_not(is_hub))
                def _():
                    part_next(j).start()

    @pl.when(s > 0)
    def _():
        gin_arrived().wait_recv()

    for c in range(pieces):
        o_gin[:, c * PIECE : (c + 1) * PIECE] = gin_buf[c]

    @pl.when(is_first)
    def _():
        own_hub().wait_send()
        gin_sent().wait_send()

    @pl.when(is_hub)
    def _():
        for j in range(groups):

            @pl.when(z != j)
            def _():
                own_peer(j).wait_send()

            @pl.loop(0, sections // 2)
            def _(chip):
                @pl.when((chip != HUB // 2) & ((chip > 0) | (z != j)))
                def _():
                    part_chip(j, chip).wait_send()

    for j in range(groups):

        @pl.when(lax.rem(s, 2) == 0)
        def _():
            part_next(j).wait_send()

        @pl.when(lax.rem(s, 2) == 1)
        def _():
            part_next(j).wait_recv()

    def sum_sent(rows):
        remote(part_out.at[rows], part_out.at[rows], zi_ss.at[0], zp_rs.at[0], s, inward).wait_send()

        @pl.when(jnp.logical_not(is_edge))
        def _():
            remote(o_acc.at[rows], o_acc.at[rows], zo_ss.at[0], zt_rs.at[0], s, outward).wait_send()

    @pl.when(is_last)
    def _():
        sum_sent(pl.ds(0, main_rows + head_rows))

    @pl.when(jnp.logical_not(is_last))
    def _():
        sum_sent(pl.ds(0, main_rows))
        drain(x_copy, lambda: remote(x_out, x_out, x_ss.at[0], x_rs.at[0], s + 1, z))
        drain(k_copy, lambda: remote(k_out, k_out, k_ss.at[0], k_rs.at[0], s + 1, z))

    @pl.when(s > 0)
    def _():
        rows = pl.ds(main_rows, head_rows)
        remote(o_acc.at[rows], o_acc.at[rows], hd_ss.at[0], hd_rs.at[0], s - 1, z).wait_send()
        drain(gx_copy, lambda: remote(gx_out, gx_out, gx_ss.at[0], gx_rs.at[0], s - 1, z))
        drain(gc_copy, lambda: remote(gc_out, gc_out, gc_ss.at[0], gc_rs.at[0], s - 1, z))

    @pl.when(lax.rem(s, 2) == 1)
    def _():
        gs_whole(0).wait_send()

    @pl.when(is_last)
    def _():
        for chip in far_chips:
            gs_whole(1 + chip).wait_send()

    @pl.when(s == feeder)
    def _():
        gs_whole(1).wait_send()


def run_step(dims, tables, arrays, weights):
    sections, groups, micro, res, half, classes, slots, keep, mel_rows = dims
    pieces = 2 * micro
    rows = 2 * half + EXT + half + half // 2 + classes // 2
    head_blocks = (half // 2 + classes // 2) // BLOCK
    share = res // sections
    smem = pl.BlockSpec(memory_space=pltpu.SMEM)
    vmem = pl.BlockSpec(memory_space=pltpu.VMEM)
    anywhere = pl.BlockSpec(memory_space=pl.ANY)
    dma = pltpu.SemaphoreType.DMA

    def tile(*shape, dtype=BF16):
        return pltpu.VMEM(shape, dtype)

    distance = groups // 2 - 1
    cycle = max(LAG * (2 * distance + 1) + 4 * distance + 4, 2 * LAG + 4)
    sends = slots if pieces > slots else 1

    scratch = [
        tile(pieces, PIECE, res),
        tile(pieces, PIECE, half),
        tile(pieces, PIECE, res),
        tile(pieces, EXT, PIECE),
        tile(pieces, PIECE, half),
        tile(pieces, PIECE, half),
        tile(pieces, PIECE, half),
        tile(slots, PIECE, res),
        tile(slots, PIECE, half),
        tile(slots, PIECE, res),
        tile(slots, EXT, PIECE),
        tile(2 * PIECE, 2 * half, dtype=F32),
        tile(PIECE, half, dtype=F32),
        tile(2 * keep, PIECE, 2 * half),
        tile(slots, res, PIECE),
        tile(2 * PIECE, 2 * PIECE),
        tile(2 * PIECE, 2 * PIECE),
        tile(pieces, EXT, PIECE),
        tile(pieces, PIECE, EXT),
        tile(EXT, 2 * half),
        tile(2 * half, 2 * res),
        tile(res, half),
        tile(half, half),
        tile(half, half),
        tile(classes, half),
        tile(2 * res, 2 * half),
        tile(half, res),
        tile(half, half),
        tile(half, half),
        tile(half, classes),
        tile(2 * keep, classes, PIECE),
        tile(2 * keep, half, PIECE),
        tile(2 * keep, half, PIECE),
        tile(2 * keep, half, PIECE),
        tile(rows, WIDE, dtype=F32),
        tile(rows, WIDE),
        tile(rows, WIDE),
        tile(pieces, share, PIECE),
        tile(2, micro * mel_rows, PIECE, dtype=F32),
        tile(EXT - mel_rows, PIECE, dtype=F32),
        dma((slots,)),
        dma((10,)),
        dma((1,)),
        dma((sends,)),
        dma((pieces,)),
        dma((sends,)),
        dma((pieces,)),
        dma((max(2, sections // 2),)),
        dma((pieces,)),
        dma((sends,)),
        dma((pieces,)),
        dma((sends,)),
        dma((pieces,)),
        dma((1,)),
        dma((1,)),
        dma((cycle,)),
        dma((cycle,)),
        dma((1,)),
        dma((head_blocks,)),
        dma((groups,)),
        dma((1,)),
        dma((groups,)),
        dma((groups, sections // 2)),
        dma((groups,)),
        dma((1,)),
        dma((1,)),
    ]
    return pl.pallas_call(
        functools.partial(step_kernel, dims),
        out_shape=(
            jax.ShapeDtypeStruct((rows, WIDE), BF16),
            jax.ShapeDtypeStruct((groups, pieces, EXT, PIECE), BF16),
            jax.ShapeDtypeStruct((share, pieces * PIECE), BF16),
        ),
        in_specs=[smem] * 4 + [vmem] * 4 + [anywhere] * 8,
        out_specs=(vmem, anywhere, vmem),
        scratch_shapes=scratch,
        compiler_params=pltpu.CompilerParams(
            collective_id=0, has_side_effects=True, vmem_limit_bytes=63 * 2**20
        ),
        cost_estimate=pl.CostEstimate(flops=10**10, bytes_accessed=3 * 10**7, transcendentals=10**6),
        name="train_step",
    )(*tables, *arrays, *weights)


def finish_kernel(
    dims, steps, dil, cond, res, skip, post, out, gin, shared, o_gin, o_dil, o_cond, o_bias, o_res, o_skip, o_post, o_out,
    o_up, o_table, o_loss, field, mel_rows_buf, mel_columns, table,
):
    mel_rows, half = dims
    i = pl.program_id(0)
    frames = shared.shape[0]

    @pl.when(i == 0)
    def _():
        table[...] = jnp.zeros_like(table)
        lane = lax.broadcasted_iota(jnp.int32, (mel_rows, PIECE), 1)
        number = lane.astype(F32)

        def one(f, loss):
            extra = shared[f, 0, mel_rows:EXT, :].astype(F32)
            loss = loss + extra + shared[f, 1, mel_rows:EXT, :].astype(F32)
            mel_rows_buf[pl.ds(f, 1), :] = extra[0:1]
            ids = extra[1:2]
            first = jnp.zeros((mel_rows, 1), F32)
            second = jnp.zeros((mel_rows, 1), F32)
            for h in range(2):
                part = shared[f, h, 0:mel_rows, :].astype(F32)
                field[h, pl.ds(pl.multiple_of(f * mel_rows, 16), mel_rows), :] = part
                later = number + float(h * PIECE) >= ids[:, 2:3]
                first = first + jnp.sum(jnp.where(later, 0.0, part), axis=1, keepdims=True)
                second = second + jnp.sum(jnp.where(later, part, 0.0), axis=1, keepdims=True)
            table[...] += jnp.where(number == ids[:, 0:1], first, 0.0)
            table[...] += jnp.where(number == ids[:, 1:2], second, 0.0)
            return loss

        loss = lax.fori_loop(0, frames, one, jnp.zeros((EXT - mel_rows, PIECE), F32))
        row = lax.broadcasted_iota(jnp.int32, loss.shape, 0)
        loss = jnp.where((row >= 2) & (row < 5), loss, 0.0)
        o_loss[...] = jnp.sum(jnp.sum(loss, axis=1, keepdims=True), axis=0, keepdims=True)
        o_table[...] = table[:, 0 : o_table.shape[1]]
        mel_columns[...] = jnp.transpose(mel_rows_buf[...])[0:mel_rows].astype(BF16)

    o_gin[...] = gin[...]
    o_dil[0] = dil[...].astype(F32)
    for source, target in ((res, o_res), (skip, o_skip), (post, o_post), (out, o_out)):
        target[0] = source[:, 0:half].astype(F32)
        target[1] = source[:, half : 2 * half].astype(F32)

    @pl.when(i < mel_rows // 16)
    def _():
        o_cond[...] = cond[...].astype(F32)

    @pl.when(i == mel_rows // 16)
    def _():
        o_bias[...] = cond[...].astype(F32)[0:1]

    channels = mel_rows // steps
    for j in range(channels):
        rows = pl.ds(i * channels + j, frames, stride=mel_rows)
        matrix = jnp.concatenate([field[0, rows, :], field[1, rows, :]], axis=1)
        o_up[j] = dot(mel_columns[...], matrix.astype(BF16))


def finish(sums, shared, grad_inputs, half, classes, mel_rows, speakers):
    steps = 8
    frames = shared.shape[0]
    first = 2 * half
    small = half // 2 // steps
    last = classes // 2 // steps
    res_at = (first + EXT) // small
    per = half // 2 // small
    rows = mel_rows // 16

    def strip(height, index):
        return pl.BlockSpec((height, WIDE), index)

    def two(height):
        return pl.BlockSpec((2, height, half), lambda i: (0, i, 0))

    def fixed(*shape):
        return pl.BlockSpec(shape, lambda i: (0,) * len(shape))

    def f32(*shape):
        return jax.ShapeDtypeStruct(shape, F32)

    return pl.pallas_call(
        functools.partial(finish_kernel, (mel_rows, half), steps),
        grid=(steps,),
        out_shape=(
            jax.ShapeDtypeStruct(grad_inputs.shape, grad_inputs.dtype),
            f32(1, first, WIDE),
            f32(mel_rows, WIDE),
            f32(1, WIDE),
            f32(2, half // 2, half),
            f32(2, half // 2, half),
            f32(2, half // 2, half),
            f32(2, classes // 2, half),
            f32(mel_rows, mel_rows, 2 * PIECE),
            f32(mel_rows, speakers),
            f32(1, 1),
        ),
        in_specs=[
            strip(first // steps, lambda i: (i, 0)),
            strip(16, lambda i: (first // 16 + jnp.minimum(i, rows), 0)),
            strip(small, lambda i: (res_at + i, 0)),
            strip(small, lambda i: (res_at + per + i, 0)),
            strip(small, lambda i: (res_at + 2 * per + i, 0)),
            strip(last, lambda i: ((first + EXT + half + half // 2) // last + i, 0)),
            pl.BlockSpec((grad_inputs.shape[0], grad_inputs.shape[1] // steps), lambda i: (0, i)),
            pl.BlockSpec(memory_space=pltpu.VMEM),
        ],
        out_specs=(
            pl.BlockSpec((grad_inputs.shape[0], grad_inputs.shape[1] // steps), lambda i: (0, i)),
            pl.BlockSpec((1, first // steps, WIDE), lambda i: (0, i, 0)),
            strip(16, lambda i: (jnp.minimum(i, rows - 1), 0)),
            fixed(1, WIDE),
            two(small),
            two(small),
            two(small),
            two(last),
            pl.BlockSpec((mel_rows // steps, mel_rows, 2 * PIECE), lambda i: (i, 0, 0)),
            fixed(mel_rows, speakers),
            fixed(1, 1),
        ),
        scratch_shapes=[
            pltpu.VMEM((2, frames * mel_rows, PIECE), F32),
            pltpu.VMEM((frames, PIECE), F32),
            pltpu.VMEM((mel_rows, frames), BF16),
            pltpu.VMEM((mel_rows, PIECE), F32),
        ],
        compiler_params=pltpu.CompilerParams(
            vmem_limit_bytes=62 * 2**20, dimension_semantics=("arbitrary",)
        ),
        name="finish",
    )(sums, sums, sums, sums, sums, sums, grad_inputs, shared)


def local(
    inputs,
    targets,
    mel,
    speakers,
    speaker_sample_counts,
    segment_offsets,
    dilations,
    dilated_kernel,
    conditioning_projection,
    dilated_gate_bias,
    residual_projection,
    skip_projection,
    upsample_weight,
    speaker_table,
    first_output_projection,
    class_projection,
):
    sections = lax.axis_size("section")
    groups = lax.axis_size("dp")
    micro = segment_offsets.shape[0]
    res, tokens = inputs.shape
    length = tokens // micro
    mel_rows = mel.shape[0]
    hop = upsample_weight.shape[0]
    half = residual_projection.shape[2]
    classes = class_projection.shape[0]
    pieces = 2 * micro
    assert length == 2 * PIECE and hop == length and mel_rows + 16 == EXT and 2 * half == WIDE

    slots, keep = (pieces, micro) if pieces <= 8 else (2, 1)
    dims = (sections, groups, micro, res, half, classes, slots, keep, mel_rows)
    sums, shared, grad_inputs = run_step(
        dims,
        (dilations, segment_offsets.T, speakers.T, speaker_sample_counts),
        (
            targets.reshape(micro, 1, length),
            mel.T,
            speaker_table,
            dilated_gate_bias,
        ),
        (
            inputs,
            upsample_weight.transpose(1, 2, 0).reshape(mel_rows * mel_rows, hop),
            conditioning_projection[0].T,
            dilated_kernel[0],
            residual_projection[0],
            skip_projection[0],
            first_output_projection,
            class_projection,
        ),
    )
    shared = shared.reshape(groups * micro, 2, EXT, PIECE)
    grad_inputs, dil, cond, bias, grad_res, grad_skip, post, out, up, table, loss = finish(
        sums, shared, grad_inputs, half, classes, mel_rows, speaker_table.shape[1]
    )
    return (
        loss.reshape(()),
        grad_inputs,
        dil,
        cond.T[None],
        bias,
        grad_res.reshape(1, half, half),
        grad_skip.reshape(1, half, half),
        up.transpose(2, 0, 1),
        table,
        post.reshape(half, half),
        out.reshape(classes, half),
    )


def solution(mesh):
    return jax.shard_map(
        local,
        mesh=mesh,
        in_specs=(
            P(None, "dp"),
            P("dp"),
            P(None, "dp"),
            P("dp", None),
            P(),
            P("dp", None),
            P("section"),
            P("section", None, None),
            P("section", None, None),
            P("section", None),
            P("section", None, None),
            P("section", None, None),
            P(),
            P(),
            P(),
            P(),
        ),
        out_specs=(
            P(),
            P("section", "dp"),
            P("section", None, None),
            P("section", None, None),
            P("section", None),
            P("section", None, None),
            P("section", None, None),
            P(),
            P(),
            P(),
            P(),
        ),
        check_vma=False,
    )
```

```python
import functools
import math

import jax
import jax.numpy as jnp
from jax import lax
from jax.experimental import pallas as pl
from jax.experimental.pallas import tpu as pltpu
from jax.sharding import PartitionSpec as P

HALF_ROOT = 0.7071067811865476
WEIGHT_SCALE = 64.0
MESH = pl.DeviceIdType.MESH
BF16 = jnp.bfloat16
F32 = jnp.float32

PIECE = 128
EXT = 96
WIDE = 1024
BLOCK = 32
LAG = 4


def dot(left, right):
    return jnp.dot(left, right, preferred_element_type=F32)


def dot_nt(left, right):
    return lax.dot_general(left, right, (((1,), (1,)), ((), ())), preferred_element_type=F32)


def dot_tn(left, right):
    return lax.dot_general(left, right, (((0,), (0,)), ((), ())), preferred_element_type=F32)


def sigmoid(values):
    return 0.5 * jnp.tanh(0.5 * values) + 0.5


def step_kernel(
    dims,
    dil_ref,
    offs_ref,
    spk_ref,
    cnt_ref,
    tgt_ref,
    mel_ref,
    tab_ref,
    bias_in,
    inp_hbm,
    up_hbm,
    wc_hbm,
    wd_hbm,
    wr_hbm,
    ws_hbm,
    wp_hbm,
    wk_hbm,
    o_acc,
    o_g,
    o_gin,
    x_buf,
    sg_buf,
    gx_buf,
    gc_buf,
    hid_buf,
    d1_buf,
    d2_buf,
    x_out,
    k_out,
    gx_out,
    gc_out,
    gate_buf,
    gh_buf,
    gg_buf,
    inp_buf,
    shift_buf,
    shift_back,
    cond_ref,
    cond_t,
    wc_ref,
    wd_ref,
    wr_ref,
    ws_ref,
    wp_ref,
    wk_ref,
    wd_t,
    wr_t,
    ws_t,
    wp_t,
    wk_t,
    gl_buf,
    a2_buf,
    gp_buf,
    a1_buf,
    acc,
    part_out,
    part_in,
    gin_buf,
    up_buf,
    extra_buf,
    inp_sem,
    load_sem,
    loc_sem,
    x_ss,
    x_rs,
    k_ss,
    k_rs,
    gs_ss,
    gs_rs,
    gx_ss,
    gx_rs,
    gc_ss,
    gc_rs,
    zi_ss,
    zo_ss,
    zp_rs,
    zt_rs,
    hd_ss,
    hd_rs,
    g_rs,
    gown_ss,
    gpeer_ss,
    ghub_ss,
    gnext_ss,
    gin_ss,
    gin_rs,
):
    sections, groups, micro, res, half, classes, slots, keep, mel_rows = dims
    pieces = 2 * micro
    s = lax.axis_index("section")
    z = lax.axis_index("dp")
    is_first = s == 0
    is_last = s == sections - 1
    hub = sections - 2
    is_hub = s == hub
    head_scale = 1.0 / math.sqrt(sections)
    main_rows = 2 * half + EXT + half
    head_rows = half // 2 + classes // 2
    main_blocks = main_rows // BLOCK
    head_blocks = head_rows // BLOCK
    share = res // sections
    feeder = sections - 3 if sections > 4 else sections - 1

    barrier = pltpu.get_barrier_semaphore()

    def greet(cond, dev_s, dev_z):
        @pl.when(cond)
        def _():
            pl.semaphore_signal(barrier, 1, device_id=(dev_s, dev_z), device_id_type=MESH)

    greet(s > 0, s - 1, z)
    greet(s < sections - 1, s + 1, z)
    greet(z > 0, s, z - 1)
    greet(z < groups - 1, s, z + 1)
    greet(s >= 2, 0, z)
    told = (lax.rem(s, 2) == 0) & (s > 0) & (s < hub)
    greet(told, hub, z)

    @pl.when(is_first)
    def _():
        @pl.loop(2, sections)
        def _(other):
            pl.semaphore_signal(barrier, 1, device_id=(other, z), device_id_type=MESH)

    @pl.when(is_hub)
    def _():
        @pl.loop(1, sections // 2 - 1)
        def _(chip):
            pl.semaphore_signal(barrier, 1, device_id=(2 * chip, z), device_id_type=MESH)

        for other in range(groups):
            greet((other > z + 1) | (other < z - 1), s, other)

    far = (lax.rem(s, 2) == 1) & (s > 1) & (s < sections - 1)
    greet(far, sections - 1, z)

    @pl.when(is_last)
    def _():
        @pl.loop(1, sections // 2 - 1)
        def _(chip):
            pl.semaphore_signal(barrier, 1, device_id=(2 * chip + 1, z), device_id_type=MESH)

    greet(s == 1, feeder, z)
    greet(s == feeder, 1, z)

    def flag(cond):
        return jnp.where(cond, 1, 0)

    z_near = flag(z > 0) + flag(z < groups - 1)
    expected = (
        flag(s > 0)
        + flag(s < sections - 1)
        + z_near
        + jnp.where(is_first, sections - 2, flag(s >= 2))
        + flag(told)
        + flag(far)
        + flag(s == 1)
        + flag(s == feeder)
        + jnp.where(is_last, sections // 2 - 2, 0)
        + jnp.where(is_hub, groups - 1 - z_near + sections // 2 - 2, 0)
    )

    def input_copy(c):
        slot = lax.rem(c, slots)
        return pltpu.make_async_copy(
            inp_hbm.at[:, pl.ds(pl.multiple_of(c * PIECE, PIECE), PIECE)],
            inp_buf.at[slot],
            inp_sem.at[slot],
        )

    quarter = mel_rows // 4
    weight_refs = (
        (wd_hbm, wd_ref),
        (wr_hbm, wr_ref),
        (ws_hbm, ws_ref),
        (wc_hbm, wc_ref.at[0:mel_rows]),
        (wp_hbm, wp_ref),
        (wk_hbm, wk_ref),
    )
    loads = [
        pltpu.make_async_copy(source, target, load_sem.at[4 + position])
        for position, (source, target) in enumerate(weight_refs)
    ]
    frame_loads = [
        pltpu.make_async_copy(
            up_hbm.at[pl.ds(q * quarter * mel_rows, quarter * mel_rows), :],
            part_out.at[pl.ds(0, quarter * mel_rows), pl.ds(q * 2 * PIECE, 2 * PIECE)],
            load_sem.at[q],
        )
        for q in range(4)
    ]
    for load in loads[:4] + frame_loads:
        load.start()

    @pl.when(is_first)
    def _():
        @pl.loop(0, slots)
        def _(c):
            input_copy(c).start()

    for load in loads[4:]:
        load.start()
    spare = lax.broadcasted_iota(jnp.int32, (EXT - mel_rows, 2 * half), 0)
    bias = jnp.broadcast_to(bias_in[...].astype(F32), (EXT - mel_rows, 2 * half))
    wc_ref[mel_rows:EXT] = jnp.where(spare == 0, bias, 0.0).astype(BF16)
    loads[0].wait()
    wd_t[...] = jnp.transpose(wd_ref[...])
    for load in loads[1:]:
        load.wait()
    wr_t[...] = jnp.transpose(wr_ref[...])
    ws_t[...] = jnp.transpose(ws_ref[...])

    for load in frame_loads:
        load.wait()

    @pl.loop(0, quarter // 4)
    def _(group):
        for q in range(4):
            for part in range(4):
                row = group * 4 + part
                lanes = slice(q * 2 * PIECE, (q + 1) * 2 * PIECE)
                matrix = part_out[pl.ds(pl.multiple_of(row * mel_rows, 16), mel_rows), lanes]
                frames = dot(mel_ref[...], matrix)
                rows = pl.ds(q * quarter + row, micro, stride=mel_rows)
                for h in range(2):
                    up_buf[h, rows, :] = frames[:, h * PIECE : (h + 1) * PIECE]

    speaker_lane = lax.broadcasted_iota(jnp.int32, tab_ref.shape, 1)
    spare = lax.broadcasted_iota(jnp.int32, (EXT - mel_rows, PIECE), 0)
    table = tab_ref[...].astype(F32)

    @pl.loop(0, micro)
    def _(m):
        def column(which):
            return jnp.sum(jnp.where(speaker_lane == spk_ref[which, m], table, 0.0), axis=1, keepdims=True)

        first, second = column(0), column(1)
        for h in range(2):
            time = lax.broadcasted_iota(jnp.int32, (mel_rows, PIECE), 1) + h * PIECE
            speaker = jnp.where(time >= offs_ref[0, m], second, first)
            rows = pl.ds(pl.multiple_of(m * mel_rows, 16), mel_rows)
            cond_ref[2 * m + h, 0:mel_rows, :] = (up_buf[h, rows, :] + speaker).astype(BF16)
            cond_ref[2 * m + h, mel_rows:EXT, :] = jnp.where(spare == 0, 1.0, 0.0).astype(BF16)
            cond_t[2 * m + h] = jnp.transpose(cond_ref[2 * m + h])

    @pl.when(s > 0)
    def _():
        acc[...] = jnp.zeros_like(acc)

    @pl.when(is_last)
    def _():
        wp_t[...] = jnp.transpose(wp_ref[...])
        wk_t[...] = jnp.transpose(wk_ref[...])
        gx_buf[...] = jnp.zeros_like(gx_buf)

    pl.semaphore_wait(barrier, expected)

    def remote(src, dst, send_sem, recv_sem, dev_s, dev_z):
        return pltpu.make_async_remote_copy(
            src_ref=src,
            dst_ref=dst,
            send_sem=send_sem,
            recv_sem=recv_sem,
            device_id=(dev_s, dev_z),
            device_id_type=MESH,
        )

    ring = pieces > slots

    def send_of(semaphores, slot):
        return semaphores.at[slot if ring else 0]

    def x_copy(c):
        slot = lax.rem(c, slots)
        return remote(x_out.at[slot], x_buf.at[c], send_of(x_ss, slot), x_rs.at[c], s + 1, z)

    def k_copy(c):
        slot = lax.rem(c, slots)
        return remote(k_out.at[slot], sg_buf.at[c], send_of(k_ss, slot), k_rs.at[c], s + 1, z)

    def gx_copy(c):
        slot = lax.rem(c, slots)
        return remote(gx_out.at[slot], gx_buf.at[c], send_of(gx_ss, slot), gx_rs.at[c], s - 1, z)

    def gc_copy(c):
        slot = lax.rem(c, slots)
        return remote(gc_out.at[slot], gc_buf.at[c], send_of(gc_ss, slot), gc_rs.at[c], s - 1, z)

    def reuse(copy, c):
        if ring:

            @pl.when(c >= slots)
            def _():
                copy(c).wait_send()

    def drain(copy, whole):
        if ring:

            @pl.loop(0, slots)
            def _(c):
                copy(c).wait_send()

        else:
            whole().wait_send()

    chips = sections // 2
    far_chips = range(chips - 2, 0, -1)

    def gs_copy(c):
        return remote(sg_buf.at[c], sg_buf.at[c], gs_ss.at[0], gs_rs.at[c], s - 1, z)

    def gs_first(c):
        return remote(sg_buf.at[c], sg_buf.at[c], gs_ss.at[1], gs_rs.at[c], 1, z)

    def gs_chip(c, chip):
        return remote(sg_buf.at[c], sg_buf.at[c], gs_ss.at[1 + chip], gs_rs.at[c], 2 * chip + 1, z)

    def gs_whole(position):
        return remote(sg_buf, sg_buf, gs_ss.at[position], gs_rs.at[0], s - 1, z)

    def build_shift(m):
        dilation = dil_ref[0]
        middle = offs_ref[0, m]
        shape = (2 * PIECE, 2 * PIECE)

        def matrix(source, target):
            start = jnp.where(target >= middle, middle, 0)
            hit = (source == target - dilation) & (source >= start)
            return jnp.where(hit, 1.0, 0.0).astype(BF16)

        rows = lax.broadcasted_iota(jnp.int32, shape, 0)
        lanes = lax.broadcasted_iota(jnp.int32, shape, 1)
        shift_buf[...] = matrix(lanes, rows)
        shift_back[...] = matrix(rows, lanes)

    def pair(ref, first):
        return jnp.concatenate([ref[first], ref[first + 1]], axis=1)

    def put_pair(ref, first, value):
        for h in range(2):
            ref[first + h] = value[:, h * PIECE : (h + 1) * PIECE]

    def both(ref, first, parts):
        return jnp.concatenate([ref[first + h] for h in parts], axis=0)

    def put(ref, first, parts, value):
        for position, h in enumerate(parts):
            ref[first + h] = value[position * PIECE : (position + 1) * PIECE]

    def head(m, total):
        width = 2 * PIECE
        total = jnp.transpose(total.astype(BF16)).astype(F32) * head_scale
        sig_1 = sigmoid(total)
        act_1 = (total * sig_1).astype(BF16)
        slope_1 = sig_1 * (1.0 + total * (1.0 - sig_1)) * head_scale
        post = dot(wp_ref[...], act_1)
        sig_2 = sigmoid(post)
        act_2 = (post * sig_2).astype(BF16)
        slope_2 = sig_2 * (1.0 + post * (1.0 - sig_2))
        logits = dot(wk_ref[...], act_2)
        top = jnp.max(logits, axis=0, keepdims=True)
        expo = jnp.exp(logits - top)
        denominator = jnp.sum(expo, axis=0, keepdims=True)
        hit = tgt_ref[m] == lax.broadcasted_iota(jnp.int32, (classes, width), 0)
        picked = jnp.sum(jnp.where(hit, logits, 0.0), axis=0, keepdims=True)
        time = lax.broadcasted_iota(jnp.int32, (1, width), 1)

        def speaker_weight(which):
            count = cnt_ref[spk_ref[which, m]].astype(F32)
            return WEIGHT_SCALE * lax.rsqrt(jnp.full((1, width), count, F32))

        weight = jnp.where(time >= offs_ref[0, m], speaker_weight(1), speaker_weight(0))
        weight = jnp.where(time < offs_ref[1, m], weight, 0.0)
        grad_logits = (weight * (expo / denominator - jnp.where(hit, 1.0, 0.0))).astype(BF16)
        grad_post = (dot(wk_t[...], grad_logits) * slope_2).astype(BF16)
        grad_total = (dot(wp_t[...], grad_post) * slope_1).astype(BF16)
        put(sg_buf, 2 * m, (0, 1), jnp.transpose(grad_total))
        for h in (1, 0):
            c = 2 * m + h
            for chip in far_chips:
                gs_chip(c, chip).start()
            gs_copy(c).start()
            if feeder == sections - 1:
                gs_first(c).start()
        kept = 2 * lax.rem(m, keep)
        put_pair(gl_buf, kept, grad_logits)
        put_pair(a2_buf, kept, act_2)
        put_pair(gp_buf, kept, grad_post)
        put_pair(a1_buf, kept, act_1)
        loss_row = weight * (top + jnp.log(denominator) - picked)
        high = loss_row.astype(BF16)
        rest = loss_row - high.astype(F32)
        middle = rest.astype(BF16)
        low = (rest - middle.astype(F32)).astype(BF16)
        row = lax.broadcasted_iota(jnp.int32, (EXT, width), 0)
        message = jnp.where(row == mel_rows + 2, high.astype(F32), 0.0)
        message = jnp.where(row == mel_rows + 3, middle.astype(F32), message)
        message = jnp.where(row == mel_rows + 4, low.astype(F32), message)
        put_pair(gc_buf, 2 * m, message.astype(BF16))

    def forward(m, parts):
        high = len(parts) * PIECE
        for h in parts:
            c = 2 * m + h

            @pl.when(is_first)
            def _():
                input_copy(c).wait()
                x_buf[c] = jnp.transpose(inp_buf[lax.rem(c, slots)])
                if ring:

                    @pl.when(c + slots < pieces)
                    def _():
                        input_copy(c + slots).start()

            @pl.when(s > 0)
            def _():
                x_copy(c).wait_recv()

        x = both(x_buf, 2 * m, parts)
        if parts == (0,):
            prev = dot(shift_buf[0:PIECE, 0:PIECE], x)
        elif parts == (1,):
            prev = dot(shift_buf[PIECE : 2 * PIECE, :], both(x_buf, 2 * m, (0, 1)))
        else:
            prev = dot(shift_buf[...], x)
        gate = (
            dot(x, wd_t[res : 2 * res])
            + dot(both(cond_t, 2 * m, parts), wc_ref[...])
            + dot(prev.astype(BF16), wd_t[0:res])
        )
        th = jnp.tanh(gate[:, 0:half])
        sg = sigmoid(gate[:, half : 2 * half])
        gate_buf[0:high, 0:half] = th
        gate_buf[0:high, half : 2 * half] = sg
        put(hid_buf, 2 * m, parts, (th * sg).astype(BF16))

    def forward_rest(m, parts):
        high = len(parts) * PIECE
        th = gate_buf[0:high, 0:half]
        sg = gate_buf[0:high, half : 2 * half]
        put(d1_buf, 2 * m, parts, (sg * (1.0 - th * th)).astype(BF16))
        put(d2_buf, 2 * m, parts, (th * sg * (1.0 - sg)).astype(BF16))

    def forward_piece(m, h):
        c = 2 * m + h
        forward(m, (h,))
        reuse(x_copy, c)
        out = (x_buf[c].astype(F32) + dot(hid_buf[c], wr_t[...])) * HALF_ROOT
        x_out[lax.rem(c, slots)] = out.astype(BF16)
        x_copy(c).start()
        gh_buf[...] = dot(hid_buf[c], ws_t[...])
        forward_rest(m, (h,))

        @pl.when(s > 0)
        def _():
            k_copy(c).wait_recv()
            gh_buf[...] += sg_buf[c].astype(F32)

        reuse(k_copy, c)
        k_out[lax.rem(c, slots)] = gh_buf[...].astype(BF16)
        k_copy(c).start()

    def forward_head(m):
        forward(m, (0, 1))
        total = dot(both(hid_buf, 2 * m, (0, 1)), ws_t[...])
        for h in (0, 1):
            k_copy(2 * m + h).wait_recv()
        head(m, total + both(sg_buf, 2 * m, (0, 1)).astype(F32))
        forward_rest(m, (0, 1))

    def grad_field(m, parts, grad_hidden):
        kept = 2 * lax.rem(m, keep)
        grad_gate = jnp.concatenate(
            [
                grad_hidden * both(d1_buf, 2 * m, parts).astype(F32),
                grad_hidden * both(d2_buf, 2 * m, parts).astype(F32),
            ],
            axis=1,
        ).astype(BF16)
        put(gg_buf, kept, parts, grad_gate)
        if parts == (1,):
            back = dot(shift_back[PIECE:, PIECE:], grad_gate)
        elif parts == (0,):
            back = dot(shift_back[0:PIECE, :], jnp.concatenate([grad_gate, gg_buf[kept + 1]], axis=0))
        else:
            back = dot(shift_back[...], grad_gate)
        return dot(grad_gate, wd_ref[:, res : 2 * res]) + dot(back.astype(BF16), wd_ref[:, 0:res])

    def cond_message(m, h):
        kept = 2 * lax.rem(m, keep)
        row = lax.broadcasted_iota(jnp.int32, (EXT, PIECE), 0)
        own = jnp.where(row < mel_rows, dot_nt(wc_ref[...], gg_buf[kept + h]), 0.0)
        return own + gc_buf[2 * m + h].astype(F32)

    def backward_piece(m, h):
        c = 2 * m + h
        gs_copy(c).wait_recv()

        @pl.when(lax.rem(s, 2) == 1)
        def _():
            gs_copy(c).start()

        if feeder < sections - 1:

            @pl.when(s == feeder)
            def _():
                gs_first(c).start()

        gh_buf[...] = dot(sg_buf[c], ws_ref[...])
        gx_copy(c).wait_recv()
        grad_hidden = gh_buf[...] + HALF_ROOT * dot(gx_buf[c], wr_ref[...])
        grad_x = (HALF_ROOT * gx_buf[c].astype(F32) + grad_field(m, (h,), grad_hidden)).astype(BF16)

        @pl.when(s > 0)
        def _():
            reuse(gx_copy, c)
            gx_out[lax.rem(c, slots)] = grad_x
            gx_copy(c).start()

        @pl.when(is_first)
        def _():
            inp_buf[lax.rem(c, slots)] = jnp.transpose(grad_x)

        gc_copy(c).wait_recv()
        message = cond_message(m, h)

        @pl.when(s > 0)
        def _():
            reuse(gc_copy, c)
            gc_out[lax.rem(c, slots)] = message.astype(BF16)
            gc_copy(c).start()

        @pl.when(is_first)
        def _():
            gc_buf[c, 0:mel_rows, :] = message[0:mel_rows].astype(BF16)
            tail = message[mel_rows:EXT]
            if h == 0:
                frame = lax.broadcasted_iota(jnp.int32, mel_ref.shape, 0) == m
                extra_buf[0:1, 0:mel_rows] = jnp.sum(
                    jnp.where(frame, mel_ref[...].astype(F32), 0.0), axis=0, keepdims=True
                )
                lane = lax.broadcasted_iota(jnp.int32, (1, PIECE), 1)
                ids = jnp.where(lane == 0, spk_ref[0, m], 0)
                ids = jnp.where(lane == 1, spk_ref[1, m], ids)
                ids = jnp.where(lane == 2, offs_ref[0, m], ids)
                extra_buf[1:2, :] = ids.astype(F32)
                tail = tail + extra_buf[...]
            gc_buf[c, mel_rows:EXT, :] = tail.astype(BF16)

    def backward_pair(m):
        grad_hidden = dot(both(sg_buf, 2 * m, (0, 1)), ws_ref[...])
        grad_x = grad_field(m, (0, 1), grad_hidden).astype(BF16)
        for h in (1, 0):
            c = 2 * m + h
            reuse(gx_copy, c)
            gx_out[lax.rem(c, slots)] = grad_x[h * PIECE : (h + 1) * PIECE]
            gx_copy(c).start()
        for h in (1, 0):
            c = 2 * m + h
            reuse(gc_copy, c)
            gc_out[lax.rem(c, slots)] = cond_message(m, h).astype(BF16)
            gc_copy(c).start()

    def add_halves(first_row, value):
        rows = value.shape[0] // 2
        acc[first_row : first_row + rows, 0:half] += value[0:rows]
        acc[first_row : first_row + rows, half : 2 * half] += value[rows : 2 * rows]

    def weight_gradients(m):
        parts = (0, 1)
        kept = 2 * lax.rem(m, keep)
        grad_gate = both(gg_buf, kept, parts)
        x = both(x_buf, 2 * m, parts)
        prev = dot(shift_buf[...], x).astype(BF16)
        acc[0 : 2 * half, :] += dot_tn(grad_gate, jnp.concatenate([prev, x], axis=1))
        acc[2 * half : 2 * half + EXT, :] += dot(pair(cond_ref, 2 * m), grad_gate)
        hidden = both(hid_buf, 2 * m, parts)
        row = 2 * half + EXT

        @pl.when(s < sections - 1)
        def _():
            add_halves(row, HALF_ROOT * dot_tn(both(gx_buf, 2 * m, parts), hidden))

        add_halves(row + half // 2, dot_tn(both(sg_buf, 2 * m, parts), hidden))

        @pl.when(is_last)
        def _():
            add_halves(main_rows, dot_nt(pair(gp_buf, kept), pair(a1_buf, kept)))
            add_halves(main_rows + half // 2, dot_nt(pair(gl_buf, kept), pair(a2_buf, kept)))

    def gin_rows(other, group):
        return remote(
            inp_buf.at[:, pl.ds(pl.multiple_of(other * share, share), share), :],
            gin_buf.at[pl.ds(pl.multiple_of(group * slots, slots), slots)],
            gin_ss.at[0],
            gin_rs.at[0],
            other,
            z,
        )

    def gin_sent():
        return remote(
            inp_buf.at[:, share:res, :], inp_buf.at[:, share:res, :], gin_ss.at[0], gin_rs.at[0], 1, z
        )

    def gin_arrived():
        return remote(gin_buf, gin_buf, gin_ss.at[0], gin_rs.at[0], 1, z)

    def hand_out(group):
        @pl.loop(1, sections)
        def _(other):
            gin_rows(other, group).start()

        gin_buf[pl.ds(pl.multiple_of(group * slots, slots), slots)] = inp_buf[:, 0:share, :]

    def own_local():
        return pltpu.make_async_copy(gc_buf, o_g.at[z], loc_sem.at[0])

    def own_hub():
        return remote(gc_buf, o_g.at[z], gown_ss.at[0], g_rs.at[z], hub, z)

    def own_peer(other):
        return remote(o_g.at[z], o_g.at[z], gpeer_ss.at[other], g_rs.at[z], hub, other)

    def part_chip(j, chip):
        return remote(o_g.at[j], o_g.at[j], ghub_ss.at[j, chip], g_rs.at[j], 2 * chip, z)

    def part_next(j):
        return remote(o_g.at[j], o_g.at[j], gnext_ss.at[j], g_rs.at[j], s + 1, z)

    def spread(j):
        part_next(j).start()

        @pl.loop(0, sections // 2 - 1)
        def _(chip):
            @pl.when((chip > 0) | (z != j))
            def _():
                part_chip(j, chip).start()

    @pl.when(is_last)
    def _():
        @pl.loop(0, micro)
        def _(m):
            build_shift(m)
            forward_head(m)
            backward_pair(m)
            if keep < micro:
                weight_gradients(m)

    roomy = keep == micro
    swings = (s == sections - 2) if roomy else False
    late = (s >= sections // 2) if roomy else is_last

    @pl.loop(0, 3 * micro)
    def _(step):
        after = step - micro
        odd = lax.rem(step, 2) == 1
        forth = step < micro
        back = jnp.where(late, (after >= 0) & (after < micro), (after >= 0) & (lax.rem(after, 2) == 0))
        m = jnp.where(forth, step, jnp.where(late, lax.rem(step, micro), after // 2))
        if roomy:
            turning = swings & (step < 2 * micro)
            end = step == 2 * micro - 1
            swing_forth = (step == 0) | (odd & jnp.logical_not(end))
            forth = jnp.where(turning, swing_forth, forth)
            back = jnp.where(turning, jnp.logical_not(swing_forth), back)
            swing_m = jnp.where(swing_forth, (step + 1) // 2, jnp.where(end, micro - 1, step // 2 - 1))
            m = jnp.where(turning, swing_m, m)
        build_shift(m)

        @pl.when(forth & jnp.logical_not(is_last))
        def _():
            forward_piece(m, 0)
            forward_piece(m, 1)

        @pl.when(is_first & (step == micro))
        def _():
            acc[...] = jnp.zeros_like(acc)
            extra_buf[...] = jnp.zeros_like(extra_buf)

        @pl.when(back & jnp.logical_not(is_last))
        def _():
            if ring:

                @pl.when(is_first & (m > 0))
                def _():
                    gin_sent().wait_send()

            backward_piece(m, 1)
            backward_piece(m, 0)

            @pl.when(is_first & (lax.rem(2 * m + 2, slots) == 0))
            def _():
                hand_out((2 * m + 2) // slots - 1)

            @pl.when(is_first & (m == micro - 1))
            def _():
                own_hub().start()
                own_local().start()

        @pl.when(jnp.logical_not(forth | back) & (roomy | jnp.logical_not(is_last)))
        def _():
            weight_gradients(m)

    @pl.when(is_first)
    def _():
        own_local().wait()

    left = z < groups // 2
    inward = jnp.where(left, z + 1, z - 1)
    outward = jnp.where(left, z - 1, z + 1)
    is_edge = (z == 0) | (z == groups - 1)
    is_mid = (z == groups // 2 - 1) | (z == groups // 2)
    distance = jnp.where(left, groups // 2 - 1 - z, z - groups // 2)
    lag = LAG * (2 * distance + 1) + 4 * distance
    count = jnp.where(is_last, main_blocks + head_blocks, main_blocks)

    def block_of(i):
        return jnp.where(is_last, jnp.where(i < head_blocks, i + main_blocks, i - head_blocks), i)

    def rows_of(b):
        return pl.ds(pl.multiple_of(b * BLOCK, BLOCK), BLOCK)

    cycle = zp_rs.shape[0]

    def swap_copy(i):
        rows = rows_of(block_of(i))
        return remote(part_out.at[rows], o_acc.at[rows], zi_ss.at[0], zt_rs.at[lax.rem(i, cycle)], s, inward)

    def part_copy(i):
        rows = rows_of(block_of(i))
        return remote(part_out.at[rows], part_in.at[rows], zi_ss.at[0], zp_rs.at[lax.rem(i, cycle)], s, inward)

    def total_copy(i):
        rows = rows_of(block_of(i))
        return remote(o_acc.at[rows], o_acc.at[rows], zo_ss.at[0], zt_rs.at[lax.rem(i, cycle)], s, outward)

    def head_copy(j):
        rows = rows_of(main_blocks + j)
        return remote(o_acc.at[rows], o_acc.at[rows], hd_ss.at[0], hd_rs.at[j], s - 1, z)

    def send_part(i):
        rows = rows_of(block_of(i))

        @pl.when(is_edge)
        def _():
            part_out[rows, :] = acc[rows, :].astype(BF16)

        @pl.when(jnp.logical_not(is_edge))
        def _():
            part_copy(i).wait_recv()
            part_out[rows, :] = (acc[rows, :] + part_in[rows, :].astype(F32)).astype(BF16)

        @pl.when(is_mid)
        def _():
            swap_copy(i).start()

        @pl.when(jnp.logical_not(is_mid))
        def _():
            part_copy(i).start()

    def finish_part(i):
        rows = rows_of(block_of(i))
        swap_copy(i).wait_recv()

        @pl.when(is_mid)
        def _():
            o_acc[rows, :] = (part_out[rows, :].astype(F32) + o_acc[rows, :].astype(F32)).astype(BF16)

        @pl.when(jnp.logical_not(is_edge))
        def _():
            total_copy(i).start()

    last_step = main_blocks + lag - 1
    head_at = lag + 2
    own_at = jnp.minimum(23 + 9 * distance, last_step)
    rest_at = jnp.where(is_hub, 36, jnp.where(is_first, 34, jnp.where(s < sections // 2, 37, 45)))
    rest_at = jnp.minimum(rest_at + 9 * distance, last_step)

    @pl.loop(0, count + lag)
    def _(i):
        @pl.when(i < count)
        def _():
            send_part(i)

        @pl.when(i >= lag)
        def _():
            finish_part(i - lag)
            b = block_of(i - lag)

            @pl.when(b >= main_blocks)
            def _():
                head_copy(b - main_blocks).start()

        @pl.when(jnp.logical_not(is_last) & (i >= head_at) & (i < head_at + head_blocks))
        def _():
            j = i - head_at
            head_copy(j).wait_recv()

            @pl.when(s > 0)
            def _():
                head_copy(j).start()

        @pl.when(is_hub & (i == own_at))
        def _():
            own_hub().wait_recv()
            for other in range(groups):

                @pl.when(z != other)
                def _():
                    own_peer(other).start()

            spread(z)

        @pl.when((lax.rem(s, 2) == 0) & (i == rest_at))
        def _():
            for j in range(groups):

                @pl.when((z != j) | ((s > 0) & (s < hub)))
                def _():
                    part_next(j).wait_recv()

                @pl.when(is_hub & (z != j))
                def _():
                    spread(j)

                @pl.when(jnp.logical_not(is_hub))
                def _():
                    part_next(j).start()

    @pl.when(s > 0)
    def _():
        gin_arrived().wait_recv()

    for c in range(pieces):
        o_gin[:, c * PIECE : (c + 1) * PIECE] = gin_buf[c]

    @pl.when(is_first)
    def _():
        own_hub().wait_send()
        gin_sent().wait_send()

    @pl.when(is_hub)
    def _():
        for j in range(groups):

            @pl.when(z != j)
            def _():
                own_peer(j).wait_send()

            @pl.loop(0, sections // 2 - 1)
            def _(chip):
                @pl.when((chip > 0) | (z != j))
                def _():
                    part_chip(j, chip).wait_send()

    for j in range(groups):

        @pl.when(lax.rem(s, 2) == 0)
        def _():
            part_next(j).wait_send()

        @pl.when(lax.rem(s, 2) == 1)
        def _():
            part_next(j).wait_recv()

    def sum_sent(rows):
        remote(part_out.at[rows], part_out.at[rows], zi_ss.at[0], zp_rs.at[0], s, inward).wait_send()

        @pl.when(jnp.logical_not(is_edge))
        def _():
            remote(o_acc.at[rows], o_acc.at[rows], zo_ss.at[0], zt_rs.at[0], s, outward).wait_send()

    @pl.when(is_last)
    def _():
        sum_sent(pl.ds(0, main_rows + head_rows))

    @pl.when(jnp.logical_not(is_last))
    def _():
        sum_sent(pl.ds(0, main_rows))
        drain(x_copy, lambda: remote(x_out, x_out, x_ss.at[0], x_rs.at[0], s + 1, z))
        drain(k_copy, lambda: remote(k_out, k_out, k_ss.at[0], k_rs.at[0], s + 1, z))

    @pl.when(s > 0)
    def _():
        rows = pl.ds(main_rows, head_rows)
        remote(o_acc.at[rows], o_acc.at[rows], hd_ss.at[0], hd_rs.at[0], s - 1, z).wait_send()
        drain(gx_copy, lambda: remote(gx_out, gx_out, gx_ss.at[0], gx_rs.at[0], s - 1, z))
        drain(gc_copy, lambda: remote(gc_out, gc_out, gc_ss.at[0], gc_rs.at[0], s - 1, z))

    @pl.when(lax.rem(s, 2) == 1)
    def _():
        gs_whole(0).wait_send()

    @pl.when(is_last)
    def _():
        for chip in far_chips:
            gs_whole(1 + chip).wait_send()

    @pl.when(s == feeder)
    def _():
        gs_whole(1).wait_send()


def run_step(dims, tables, arrays, weights):
    sections, groups, micro, res, half, classes, slots, keep, mel_rows = dims
    pieces = 2 * micro
    rows = 2 * half + EXT + half + half // 2 + classes // 2
    head_blocks = (half // 2 + classes // 2) // BLOCK
    share = res // sections
    smem = pl.BlockSpec(memory_space=pltpu.SMEM)
    vmem = pl.BlockSpec(memory_space=pltpu.VMEM)
    anywhere = pl.BlockSpec(memory_space=pl.ANY)
    dma = pltpu.SemaphoreType.DMA

    def tile(*shape, dtype=BF16):
        return pltpu.VMEM(shape, dtype)

    distance = groups // 2 - 1
    cycle = max(LAG * (2 * distance + 1) + 4 * distance + 4, 2 * LAG + 4)
    sends = slots if pieces > slots else 1

    scratch = [
        tile(pieces, PIECE, res),
        tile(pieces, PIECE, half),
        tile(pieces, PIECE, res),
        tile(pieces, EXT, PIECE),
        tile(pieces, PIECE, half),
        tile(pieces, PIECE, half),
        tile(pieces, PIECE, half),
        tile(slots, PIECE, res),
        tile(slots, PIECE, half),
        tile(slots, PIECE, res),
        tile(slots, EXT, PIECE),
        tile(2 * PIECE, 2 * half, dtype=F32),
        tile(PIECE, half, dtype=F32),
        tile(2 * keep, PIECE, 2 * half),
        tile(slots, res, PIECE),
        tile(2 * PIECE, 2 * PIECE),
        tile(2 * PIECE, 2 * PIECE),
        tile(pieces, EXT, PIECE),
        tile(pieces, PIECE, EXT),
        tile(EXT, 2 * half),
        tile(2 * half, 2 * res),
        tile(res, half),
        tile(half, half),
        tile(half, half),
        tile(classes, half),
        tile(2 * res, 2 * half),
        tile(half, res),
        tile(half, half),
        tile(half, half),
        tile(half, classes),
        tile(2 * keep, classes, PIECE),
        tile(2 * keep, half, PIECE),
        tile(2 * keep, half, PIECE),
        tile(2 * keep, half, PIECE),
        tile(rows, WIDE, dtype=F32),
        tile(rows, WIDE),
        tile(rows, WIDE),
        tile(pieces, share, PIECE),
        tile(2, micro * mel_rows, PIECE, dtype=F32),
        tile(EXT - mel_rows, PIECE, dtype=F32),
        dma((slots,)),
        dma((10,)),
        dma((1,)),
        dma((sends,)),
        dma((pieces,)),
        dma((sends,)),
        dma((pieces,)),
        dma((max(2, sections // 2),)),
        dma((pieces,)),
        dma((sends,)),
        dma((pieces,)),
        dma((sends,)),
        dma((pieces,)),
        dma((1,)),
        dma((1,)),
        dma((cycle,)),
        dma((cycle,)),
        dma((1,)),
        dma((head_blocks,)),
        dma((groups,)),
        dma((1,)),
        dma((groups,)),
        dma((groups, sections // 2)),
        dma((groups,)),
        dma((1,)),
        dma((1,)),
    ]
    return pl.pallas_call(
        functools.partial(step_kernel, dims),
        out_shape=(
            jax.ShapeDtypeStruct((rows, WIDE), BF16),
            jax.ShapeDtypeStruct((groups, pieces, EXT, PIECE), BF16),
            jax.ShapeDtypeStruct((share, pieces * PIECE), BF16),
        ),
        in_specs=[smem] * 4 + [vmem] * 4 + [anywhere] * 8,
        out_specs=(vmem, anywhere, vmem),
        scratch_shapes=scratch,
        compiler_params=pltpu.CompilerParams(
            collective_id=0, has_side_effects=True, vmem_limit_bytes=63 * 2**20
        ),
        cost_estimate=pl.CostEstimate(flops=10**10, bytes_accessed=3 * 10**7, transcendentals=10**6),
        name="train_step",
    )(*tables, *arrays, *weights)


def finish_kernel(
    dims,
    sums,
    gin,
    shared_hbm,
    o_gin,
    o_dil,
    o_cond,
    o_res,
    o_skip,
    o_post,
    o_out,
    o_up,
    o_bias,
    o_table,
    o_loss,
    sums_buf,
    shared,
    dil_buf,
    cond_buf,
    res_buf,
    skip_buf,
    post_buf,
    out_buf,
    up_buf,
    field,
    mel_rows_buf,
    mel_columns,
    table,
    load_sem,
    store_sem,
):
    mel_rows, half = dims
    frames = shared.shape[0]
    first = 2 * half
    total_rows = sums_buf.shape[0]
    strips = ((0, half), (half, half), (first, total_rows - first))
    loads = [
        pltpu.make_async_copy(sums.at[pl.ds(row, rows), :], sums_buf.at[pl.ds(row, rows), :], load_sem.at[k])
        for k, (row, rows) in enumerate(strips)
    ]
    loads.append(pltpu.make_async_copy(shared_hbm, shared, load_sem.at[3]))
    for load in loads:
        load.start()
    stores = []

    def store(source, target):
        copy = pltpu.make_async_copy(source, target, store_sem.at[len(stores)])
        copy.start()
        stores.append(copy)

    store(gin, o_gin)

    for k in range(2):
        loads[k].wait()
        rows = pl.ds(k * half, half)
        dil_buf[rows, :] = sums_buf[rows, :].astype(F32)
        store(dil_buf.at[rows, :], o_dil.at[0, rows, :])
    loads[2].wait()
    cond_buf[...] = sums_buf[first : first + mel_rows, :].astype(F32)
    o_bias[...] = sums_buf[first + mel_rows : first + EXT, :].astype(F32)[0:1]
    store(cond_buf, o_cond)
    row = first + EXT
    for buffer, target in ((res_buf, o_res), (skip_buf, o_skip), (post_buf, o_post), (out_buf, o_out)):
        rows = buffer.shape[1]
        buffer[0] = sums_buf[row : row + rows, 0:half].astype(F32)
        buffer[1] = sums_buf[row : row + rows, half : 2 * half].astype(F32)
        store(buffer, target)
        row += rows

    loads[3].wait()

    def by_channel(f, loss):
        extra = shared[f, 0, mel_rows:EXT, :].astype(F32)
        mel_rows_buf[pl.ds(f, 1), :] = extra[0:1]
        for h in range(2):
            rows = pl.ds(pl.multiple_of(f * mel_rows, 16), mel_rows)
            field[h, rows, :] = shared[f, h, 0:mel_rows, :].astype(F32)
        return loss + extra + shared[f, 1, mel_rows:EXT, :].astype(F32)

    loss = lax.fori_loop(0, frames, by_channel, jnp.zeros((EXT - mel_rows, PIECE), F32))
    row = lax.broadcasted_iota(jnp.int32, loss.shape, 0)
    loss = jnp.where((row >= 2) & (row < 5), loss, 0.0)
    o_loss[...] = jnp.sum(jnp.sum(loss, axis=1, keepdims=True), axis=0, keepdims=True)
    mel_columns[...] = jnp.transpose(mel_rows_buf[...])[0:mel_rows].astype(BF16)

    parts = 4
    channels = mel_rows // parts
    for part in range(parts):

        @pl.loop(0, channels // 10)
        def _(group):
            for j in range(10):
                c = part * channels + group * 10 + j
                rows = pl.ds(c, frames, stride=mel_rows)
                matrix = jnp.concatenate([field[0, rows, :], field[1, rows, :]], axis=1)
                up_buf[c] = dot(mel_columns[...], matrix.astype(BF16))

        rows = pl.ds(part * channels, channels)
        store(up_buf.at[rows], o_up.at[rows])

    table[...] = jnp.zeros_like(table)

    @pl.loop(0, frames)
    def _(f):
        ids = shared[f, 0, mel_rows:EXT, :].astype(F32)[1:2]
        time = lax.broadcasted_iota(jnp.int32, (PIECE, PIECE), 0).astype(F32)
        number = lax.broadcasted_iota(jnp.int32, (PIECE, PIECE), 1).astype(F32)
        for h in range(2):
            speaker = jnp.where(time + float(h * PIECE) >= ids[:, 2:3], ids[:, 1:2], ids[:, 0:1])
            hot = jnp.where(number == speaker, 1.0, 0.0).astype(BF16)
            table[...] += dot(shared[f, h, 0:mel_rows, :], hot)

    o_table[...] = table[:, 0 : o_table.shape[1]]
    for copy in stores:
        copy.wait()


def finish(sums, shared, grad_inputs, half, classes, mel_rows, speakers):
    frames = shared.shape[0]
    first = 2 * half
    vmem = pl.BlockSpec(memory_space=pltpu.VMEM)
    anywhere = pl.BlockSpec(memory_space=pl.ANY)
    large = (
        (first, WIDE),
        (mel_rows, WIDE),
        (2, half // 2, half),
        (2, half // 2, half),
        (2, half // 2, half),
        (2, classes // 2, half),
        (mel_rows, mel_rows, 2 * PIECE),
    )

    def f32(*shape):
        return jax.ShapeDtypeStruct(shape, F32)

    return pl.pallas_call(
        functools.partial(finish_kernel, (mel_rows, half)),
        out_shape=(
            jax.ShapeDtypeStruct(grad_inputs.shape, grad_inputs.dtype),
            f32(1, *large[0]),
            *[f32(*shape) for shape in large[1:]],
            f32(1, WIDE),
            f32(mel_rows, speakers),
            f32(1, 1),
        ),
        in_specs=[anywhere] * 3,
        out_specs=(anywhere,) * 8 + (vmem,) * 3,
        scratch_shapes=[
            pltpu.VMEM(sums.shape, BF16),
            pltpu.VMEM(shared.shape, BF16),
            *[pltpu.VMEM(shape, F32) for shape in large],
            pltpu.VMEM((2, frames * mel_rows, PIECE), F32),
            pltpu.VMEM((frames, PIECE), F32),
            pltpu.VMEM((mel_rows, frames), BF16),
            pltpu.VMEM((mel_rows, PIECE), F32),
            pltpu.SemaphoreType.DMA((4,)),
            pltpu.SemaphoreType.DMA((12,)),
        ],
        compiler_params=pltpu.CompilerParams(vmem_limit_bytes=62 * 2**20),
        name="finish",
    )(sums, grad_inputs, shared)


def local(
    inputs,
    targets,
    mel,
    speakers,
    speaker_sample_counts,
    segment_offsets,
    dilations,
    dilated_kernel,
    conditioning_projection,
    dilated_gate_bias,
    residual_projection,
    skip_projection,
    upsample_weight,
    speaker_table,
    first_output_projection,
    class_projection,
):
    sections = lax.axis_size("section")
    groups = lax.axis_size("dp")
    micro = segment_offsets.shape[0]
    res, tokens = inputs.shape
    length = tokens // micro
    mel_rows = mel.shape[0]
    hop = upsample_weight.shape[0]
    half = residual_projection.shape[2]
    classes = class_projection.shape[0]
    pieces = 2 * micro
    assert length == 2 * PIECE and hop == length and mel_rows + 16 == EXT and 2 * half == WIDE

    slots, keep = (pieces, micro) if pieces <= 8 else (2, 1)
    dims = (sections, groups, micro, res, half, classes, slots, keep, mel_rows)
    sums, shared, grad_inputs = run_step(
        dims,
        (dilations, segment_offsets.T, speakers.T, speaker_sample_counts),
        (
            targets.reshape(micro, 1, length),
            mel.T,
            speaker_table,
            dilated_gate_bias,
        ),
        (
            inputs,
            upsample_weight.transpose(1, 2, 0).reshape(mel_rows * mel_rows, hop),
            conditioning_projection[0].T,
            dilated_kernel[0],
            residual_projection[0],
            skip_projection[0],
            first_output_projection,
            class_projection,
        ),
    )
    shared = shared.reshape(groups * micro, 2, EXT, PIECE)
    grad_inputs, dil, cond, grad_res, grad_skip, post, out, up, bias, table, loss = finish(
        sums, shared, grad_inputs, half, classes, mel_rows, speaker_table.shape[1]
    )
    return (
        loss.reshape(()),
        grad_inputs,
        dil,
        cond.T[None],
        bias,
        grad_res.reshape(1, half, half),
        grad_skip.reshape(1, half, half),
        up.transpose(2, 0, 1),
        table,
        post.reshape(half, half),
        out.reshape(classes, half),
    )


def solution(mesh):
    return jax.shard_map(
        local,
        mesh=mesh,
        in_specs=(
            P(None, "dp"),
            P("dp"),
            P(None, "dp"),
            P("dp", None),
            P(),
            P("dp", None),
            P("section"),
            P("section", None, None),
            P("section", None, None),
            P("section", None),
            P("section", None, None),
            P("section", None, None),
            P(),
            P(),
            P(),
            P(),
        ),
        out_specs=(
            P(),
            P("section", "dp"),
            P("section", None, None),
            P("section", None, None),
            P("section", None),
            P("section", None, None),
            P("section", None, None),
            P(),
            P(),
            P(),
            P(),
        ),
        check_vma=False,
    )
```

```python
import functools
import math

import jax
import jax.numpy as jnp
from jax import lax
from jax.experimental import pallas as pl
from jax.experimental.pallas import tpu as pltpu
from jax.sharding import PartitionSpec as P

HALF_ROOT = 0.7071067811865476
WEIGHT_SCALE = 64.0
MESH = pl.DeviceIdType.MESH
BF16 = jnp.bfloat16
F32 = jnp.float32

PIECE = 128
EXT = 96
WIDE = 1024
BLOCK = 32
EXPORT = 4
LAG = 4


def dot(left, right):
    return jnp.dot(left, right, preferred_element_type=F32)


def dot_nt(left, right):
    return lax.dot_general(left, right, (((1,), (1,)), ((), ())), preferred_element_type=F32)


def dot_tn(left, right):
    return lax.dot_general(left, right, (((0,), (0,)), ((), ())), preferred_element_type=F32)


def sigmoid(values):
    return 0.5 * jnp.tanh(0.5 * values) + 0.5


def exported_blocks(dims):
    sections, groups, micro, keep = dims[0], dims[1], dims[2], dims[7]
    feeder = sections - 3 if sections > 4 else sections - 1
    return EXPORT if keep == micro and feeder == sections // 2 + 1 else 0


def step_kernel(
    dims,
    dil_ref,
    offs_ref,
    spk_ref,
    cnt_ref,
    tgt_ref,
    mel_ref,
    tab_ref,
    bias_in,
    inp_hbm,
    up_hbm,
    wc_hbm,
    wd_hbm,
    wr_hbm,
    ws_hbm,
    wp_hbm,
    wk_hbm,
    o_sum,
    o_g,
    o_gin,
    x_buf,
    sg_buf,
    gx_buf,
    gc_buf,
    hid_buf,
    d1_buf,
    d2_buf,
    x_out,
    k_out,
    gx_out,
    gc_out,
    gate_buf,
    gh_buf,
    gg_buf,
    inp_buf,
    shift_buf,
    shift_back,
    cond_ref,
    cond_t,
    wc_ref,
    wd_ref,
    wr_ref,
    ws_ref,
    wp_ref,
    wk_ref,
    wd_t,
    wr_t,
    ws_t,
    wp_t,
    wk_t,
    gl_buf,
    a2_buf,
    gp_buf,
    a1_buf,
    acc,
    part_out,
    part_in,
    o_acc,
    taken_buf,
    gin_buf,
    up_buf,
    extra_buf,
    inp_sem,
    load_sem,
    out_sem,
    loc_sem,
    x_ss,
    x_rs,
    k_ss,
    k_rs,
    gs_ss,
    gs_rs,
    gx_ss,
    gx_rs,
    gc_ss,
    gc_rs,
    zi_ss,
    zo_ss,
    zp_rs,
    zt_rs,
    hd_ss,
    hd_rs,
    g_rs,
    gown_ss,
    gpeer_ss,
    ghub_ss,
    gnext_ss,
    gin_ss,
    gin_rs,
    give_ss,
    give_rs,
):
    sections, groups, micro, res, half, classes, slots, keep, mel_rows = dims
    pieces = 2 * micro
    s = lax.axis_index("section")
    z = lax.axis_index("dp")
    is_first = s == 0
    is_last = s == sections - 1
    hub = sections - 2
    is_hub = s == hub
    head_scale = 1.0 / math.sqrt(sections)
    main_rows = 2 * half + EXT + half
    head_rows = half // 2 + classes // 2
    main_blocks = main_rows // BLOCK
    head_blocks = head_rows // BLOCK
    share = res // sections
    feeder = sections - 3 if sections > 4 else sections - 1
    exports = exported_blocks(dims)
    helper = sections // 2

    barrier = pltpu.get_barrier_semaphore()

    def greet(cond, dev_s, dev_z):
        @pl.when(cond)
        def _():
            pl.semaphore_signal(barrier, 1, device_id=(dev_s, dev_z), device_id_type=MESH)

    greet(s > 0, s - 1, z)
    greet(s < sections - 1, s + 1, z)
    greet(z > 0, s, z - 1)
    greet(z < groups - 1, s, z + 1)
    greet(s >= 2, 0, z)
    told = (lax.rem(s, 2) == 0) & (s > 0) & (s < hub)
    greet(told, hub, z)

    @pl.when(is_first)
    def _():
        @pl.loop(2, sections)
        def _(other):
            pl.semaphore_signal(barrier, 1, device_id=(other, z), device_id_type=MESH)

    @pl.when(is_hub)
    def _():
        @pl.loop(1, sections // 2 - 1)
        def _(chip):
            pl.semaphore_signal(barrier, 1, device_id=(2 * chip, z), device_id_type=MESH)

        for other in range(groups):
            greet((other > z + 1) | (other < z - 1), s, other)

    far = (lax.rem(s, 2) == 1) & (s > 1) & (s < sections - 1)
    greet(far, sections - 1, z)

    @pl.when(is_last)
    def _():
        @pl.loop(1, sections // 2 - 1)
        def _(chip):
            pl.semaphore_signal(barrier, 1, device_id=(2 * chip + 1, z), device_id_type=MESH)

    greet(s == 1, feeder, z)
    greet(s == feeder, 1, z)

    def flag(cond):
        return jnp.where(cond, 1, 0)

    z_near = flag(z > 0) + flag(z < groups - 1)
    expected = (
        flag(s > 0)
        + flag(s < sections - 1)
        + z_near
        + jnp.where(is_first, sections - 2, flag(s >= 2))
        + flag(told)
        + flag(far)
        + flag(s == 1)
        + flag(s == feeder)
        + jnp.where(is_last, sections // 2 - 2, 0)
        + jnp.where(is_hub, groups - 1 - z_near + sections // 2 - 2, 0)
    )

    def input_copy(c):
        slot = lax.rem(c, slots)
        return pltpu.make_async_copy(
            inp_hbm.at[:, pl.ds(pl.multiple_of(c * PIECE, PIECE), PIECE)],
            inp_buf.at[slot],
            inp_sem.at[slot],
        )

    quarter = mel_rows // 4
    weight_refs = (
        (wd_hbm, wd_ref),
        (wr_hbm, wr_ref),
        (ws_hbm, ws_ref),
        (wc_hbm, wc_ref.at[0:mel_rows]),
        (wp_hbm, wp_ref),
        (wk_hbm, wk_ref),
    )
    loads = [
        pltpu.make_async_copy(source, target, load_sem.at[4 + position])
        for position, (source, target) in enumerate(weight_refs)
    ]
    frame_loads = [
        pltpu.make_async_copy(
            up_hbm.at[pl.ds(q * quarter * mel_rows, quarter * mel_rows), :],
            part_out.at[pl.ds(0, quarter * mel_rows), pl.ds(q * 2 * PIECE, 2 * PIECE)],
            load_sem.at[q],
        )
        for q in range(4)
    ]
    for load in loads[:4] + frame_loads:
        load.start()

    @pl.when(is_first)
    def _():
        @pl.loop(0, slots)
        def _(c):
            input_copy(c).start()

    @pl.when(is_last)
    def _():
        for load in loads[4:]:
            load.start()

    spare = lax.broadcasted_iota(jnp.int32, (EXT - mel_rows, 2 * half), 0)
    bias = jnp.broadcast_to(bias_in[...].astype(F32), (EXT - mel_rows, 2 * half))
    wc_ref[mel_rows:EXT] = jnp.where(spare == 0, bias, 0.0).astype(BF16)
    loads[0].wait()
    wd_t[...] = jnp.transpose(wd_ref[...])
    for load in loads[1:4]:
        load.wait()
    wr_t[...] = jnp.transpose(wr_ref[...])
    ws_t[...] = jnp.transpose(ws_ref[...])

    for load in frame_loads:
        load.wait()

    @pl.loop(0, quarter // 4)
    def _(group):
        for q in range(4):
            for part in range(4):
                row = group * 4 + part
                lanes = slice(q * 2 * PIECE, (q + 1) * 2 * PIECE)
                matrix = part_out[pl.ds(pl.multiple_of(row * mel_rows, 16), mel_rows), lanes]
                frames = dot(mel_ref[...], matrix)
                rows = pl.ds(q * quarter + row, micro, stride=mel_rows)
                for h in range(2):
                    up_buf[h, rows, :] = frames[:, h * PIECE : (h + 1) * PIECE]

    def condition(m):
        shape = (tab_ref.shape[1], 2 * PIECE)
        time = lax.broadcasted_iota(jnp.int32, shape, 1)
        speaker = jnp.where(time >= offs_ref[0, m], spk_ref[1, m], spk_ref[0, m])
        hot = jnp.where(lax.broadcasted_iota(jnp.int32, shape, 0) == speaker, 1.0, 0.0).astype(BF16)
        columns = dot(tab_ref[...], hot)
        ones = jnp.where(lax.broadcasted_iota(jnp.int32, (EXT - mel_rows, PIECE), 0) == 0, 1.0, 0.0)
        rows = pl.ds(pl.multiple_of(m * mel_rows, 16), mel_rows)
        for h in range(2):
            c = 2 * m + h
            value = up_buf[h, rows, :] + columns[:, h * PIECE : (h + 1) * PIECE]
            cond_ref[c] = jnp.concatenate([value, ones], axis=0).astype(BF16)
            cond_t[c] = jnp.transpose(cond_ref[c])

    @pl.when(is_first)
    def _():
        condition(0)

    @pl.when(s > 0)
    def _():
        @pl.loop(0, micro)
        def _(m):
            condition(m)

    @pl.when(s > 0)
    def _():
        acc[...] = jnp.zeros_like(acc)

    @pl.when(is_last)
    def _():
        for load in loads[4:]:
            load.wait()
        wp_t[...] = jnp.transpose(wp_ref[...])
        wk_t[...] = jnp.transpose(wk_ref[...])
        gx_buf[...] = jnp.zeros_like(gx_buf)

    pl.semaphore_wait(barrier, expected)

    def remote(src, dst, send_sem, recv_sem, dev_s, dev_z):
        return pltpu.make_async_remote_copy(
            src_ref=src,
            dst_ref=dst,
            send_sem=send_sem,
            recv_sem=recv_sem,
            device_id=(dev_s, dev_z),
            device_id_type=MESH,
        )

    ring = pieces > slots

    def send_of(semaphores, slot):
        return semaphores.at[slot if ring else 0]

    def x_copy(c):
        slot = lax.rem(c, slots)
        return remote(x_out.at[slot], x_buf.at[c], send_of(x_ss, slot), x_rs.at[c], s + 1, z)

    def k_copy(c):
        slot = lax.rem(c, slots)
        return remote(k_out.at[slot], sg_buf.at[c], send_of(k_ss, slot), k_rs.at[c], s + 1, z)

    def gx_copy(c):
        slot = lax.rem(c, slots)
        return remote(gx_out.at[slot], gx_buf.at[c], send_of(gx_ss, slot), gx_rs.at[c], s - 1, z)

    def gc_copy(c):
        slot = lax.rem(c, slots)
        return remote(gc_out.at[slot], gc_buf.at[c], send_of(gc_ss, slot), gc_rs.at[c], s - 1, z)

    def reuse(copy, c):
        if ring:

            @pl.when(c >= slots)
            def _():
                copy(c).wait_send()

    def drain(copy, whole):
        if ring:

            @pl.loop(0, slots)
            def _(c):
                copy(c).wait_send()

        else:
            whole().wait_send()

    chips = sections // 2
    far_chips = range(chips - 2, 0, -1)

    def gs_copy(c):
        return remote(sg_buf.at[c], sg_buf.at[c], gs_ss.at[0], gs_rs.at[c], s - 1, z)

    def gs_first(c):
        return remote(sg_buf.at[c], sg_buf.at[c], gs_ss.at[1], gs_rs.at[c], 1, z)

    def gs_chip(c, chip):
        return remote(sg_buf.at[c], sg_buf.at[c], gs_ss.at[1 + chip], gs_rs.at[c], 2 * chip + 1, z)

    def gs_whole(position):
        return remote(sg_buf, sg_buf, gs_ss.at[position], gs_rs.at[0], s - 1, z)

    def build_shift(m):
        dilation = dil_ref[0]
        middle = offs_ref[0, m]
        shape = (2 * PIECE, 2 * PIECE)

        def matrix(source, target):
            start = jnp.where(target >= middle, middle, 0)
            hit = (source == target - dilation) & (source >= start)
            return jnp.where(hit, 1.0, 0.0).astype(BF16)

        rows = lax.broadcasted_iota(jnp.int32, shape, 0)
        lanes = lax.broadcasted_iota(jnp.int32, shape, 1)
        shift_buf[...] = matrix(lanes, rows)
        shift_back[...] = matrix(rows, lanes)

    def pair(ref, first):
        return jnp.concatenate([ref[first], ref[first + 1]], axis=1)

    def put_pair(ref, first, value):
        for h in range(2):
            ref[first + h] = value[:, h * PIECE : (h + 1) * PIECE]

    def both(ref, first, parts):
        return jnp.concatenate([ref[first + h] for h in parts], axis=0)

    def put(ref, first, parts, value):
        for position, h in enumerate(parts):
            ref[first + h] = value[position * PIECE : (position + 1) * PIECE]

    def head(m, total):
        width = 2 * PIECE
        total = jnp.transpose(total.astype(BF16)).astype(F32) * head_scale
        sig_1 = sigmoid(total)
        act_1 = (total * sig_1).astype(BF16)
        slope_1 = sig_1 * (1.0 + total * (1.0 - sig_1)) * head_scale
        post = dot(wp_ref[...], act_1)
        sig_2 = sigmoid(post)
        act_2 = (post * sig_2).astype(BF16)
        slope_2 = sig_2 * (1.0 + post * (1.0 - sig_2))
        logits = dot(wk_ref[...], act_2)
        top = jnp.max(logits, axis=0, keepdims=True)
        expo = jnp.exp(logits - top)
        denominator = jnp.sum(expo, axis=0, keepdims=True)
        hit = tgt_ref[m] == lax.broadcasted_iota(jnp.int32, (classes, width), 0)
        picked = jnp.sum(jnp.where(hit, logits, 0.0), axis=0, keepdims=True)
        time = lax.broadcasted_iota(jnp.int32, (1, width), 1)

        def speaker_weight(which):
            count = cnt_ref[spk_ref[which, m]].astype(F32)
            return WEIGHT_SCALE * lax.rsqrt(jnp.full((1, width), count, F32))

        weight = jnp.where(time >= offs_ref[0, m], speaker_weight(1), speaker_weight(0))
        weight = jnp.where(time < offs_ref[1, m], weight, 0.0)
        grad_logits = (weight * (expo / denominator - jnp.where(hit, 1.0, 0.0))).astype(BF16)
        grad_post = (dot(wk_t[...], grad_logits) * slope_2).astype(BF16)
        grad_total = (dot(wp_t[...], grad_post) * slope_1).astype(BF16)
        put(sg_buf, 2 * m, (0, 1), jnp.transpose(grad_total))
        for h in (1, 0):
            c = 2 * m + h
            for chip in far_chips:
                gs_chip(c, chip).start()
            gs_copy(c).start()
            if feeder == sections - 1:
                gs_first(c).start()
        kept = 2 * lax.rem(m, keep)
        put_pair(gl_buf, kept, grad_logits)
        put_pair(a2_buf, kept, act_2)
        put_pair(gp_buf, kept, grad_post)
        put_pair(a1_buf, kept, act_1)
        loss_row = weight * (top + jnp.log(denominator) - picked)
        high = loss_row.astype(BF16)
        rest = loss_row - high.astype(F32)
        middle = rest.astype(BF16)
        low = (rest - middle.astype(F32)).astype(BF16)
        row = lax.broadcasted_iota(jnp.int32, (EXT, width), 0)
        message = jnp.where(row == mel_rows + 2, high.astype(F32), 0.0)
        message = jnp.where(row == mel_rows + 3, middle.astype(F32), message)
        message = jnp.where(row == mel_rows + 4, low.astype(F32), message)
        put_pair(gc_buf, 2 * m, message.astype(BF16))

    def forward(m, parts):
        high = len(parts) * PIECE
        for h in parts:
            c = 2 * m + h

            @pl.when(is_first)
            def _():
                input_copy(c).wait()
                x_buf[c] = jnp.transpose(inp_buf[lax.rem(c, slots)])
                if ring:

                    @pl.when(c + slots < pieces)
                    def _():
                        input_copy(c + slots).start()

            @pl.when(s > 0)
            def _():
                x_copy(c).wait_recv()

        x = both(x_buf, 2 * m, parts)
        if parts == (0,):
            prev = dot(shift_buf[0:PIECE, 0:PIECE], x)
        elif parts == (1,):
            prev = dot(shift_buf[PIECE : 2 * PIECE, :], both(x_buf, 2 * m, (0, 1)))
        else:
            prev = dot(shift_buf[...], x)
        gate = (
            dot(x, wd_t[res : 2 * res])
            + dot(both(cond_t, 2 * m, parts), wc_ref[...])
            + dot(prev.astype(BF16), wd_t[0:res])
        )
        th = jnp.tanh(gate[:, 0:half])
        sg = sigmoid(gate[:, half : 2 * half])
        gate_buf[0:high, 0:half] = th
        gate_buf[0:high, half : 2 * half] = sg
        put(hid_buf, 2 * m, parts, (th * sg).astype(BF16))

    def forward_rest(m, parts):
        high = len(parts) * PIECE
        th = gate_buf[0:high, 0:half]
        sg = gate_buf[0:high, half : 2 * half]
        put(d1_buf, 2 * m, parts, (sg * (1.0 - th * th)).astype(BF16))
        put(d2_buf, 2 * m, parts, (th * sg * (1.0 - sg)).astype(BF16))

    def forward_piece(m, h):
        c = 2 * m + h
        forward(m, (h,))
        reuse(x_copy, c)
        out = (x_buf[c].astype(F32) + dot(hid_buf[c], wr_t[...])) * HALF_ROOT
        x_out[lax.rem(c, slots)] = out.astype(BF16)
        x_copy(c).start()
        gh_buf[...] = dot(hid_buf[c], ws_t[...])
        forward_rest(m, (h,))

        @pl.when(s > 0)
        def _():
            k_copy(c).wait_recv()
            gh_buf[...] += sg_buf[c].astype(F32)

        reuse(k_copy, c)
        k_out[lax.rem(c, slots)] = gh_buf[...].astype(BF16)
        k_copy(c).start()

    def forward_head(m):
        forward(m, (0, 1))
        total = dot(both(hid_buf, 2 * m, (0, 1)), ws_t[...])
        for h in (0, 1):
            k_copy(2 * m + h).wait_recv()
        head(m, total + both(sg_buf, 2 * m, (0, 1)).astype(F32))
        forward_rest(m, (0, 1))

    def grad_field(m, parts, grad_hidden):
        kept = 2 * lax.rem(m, keep)
        grad_gate = jnp.concatenate(
            [
                grad_hidden * both(d1_buf, 2 * m, parts).astype(F32),
                grad_hidden * both(d2_buf, 2 * m, parts).astype(F32),
            ],
            axis=1,
        ).astype(BF16)
        put(gg_buf, kept, parts, grad_gate)
        if parts == (1,):
            back = dot(shift_back[PIECE:, PIECE:], grad_gate)
        elif parts == (0,):
            back = dot(shift_back[0:PIECE, :], jnp.concatenate([grad_gate, gg_buf[kept + 1]], axis=0))
        else:
            back = dot(shift_back[...], grad_gate)
        return dot(grad_gate, wd_ref[:, res : 2 * res]) + dot(back.astype(BF16), wd_ref[:, 0:res])

    def cond_message(m, h):
        kept = 2 * lax.rem(m, keep)
        row = lax.broadcasted_iota(jnp.int32, (EXT, PIECE), 0)
        own = jnp.where(row < mel_rows, dot_nt(wc_ref[...], gg_buf[kept + h]), 0.0)
        return own + gc_buf[2 * m + h].astype(F32)

    def backward_piece(m, h):
        c = 2 * m + h
        gs_copy(c).wait_recv()

        @pl.when(lax.rem(s, 2) == 1)
        def _():
            gs_copy(c).start()

        if feeder < sections - 1:

            @pl.when(s == feeder)
            def _():
                gs_first(c).start()

        gh_buf[...] = dot(sg_buf[c], ws_ref[...])
        gx_copy(c).wait_recv()
        grad_hidden = gh_buf[...] + HALF_ROOT * dot(gx_buf[c], wr_ref[...])
        grad_x = (HALF_ROOT * gx_buf[c].astype(F32) + grad_field(m, (h,), grad_hidden)).astype(BF16)

        @pl.when(s > 0)
        def _():
            reuse(gx_copy, c)
            gx_out[lax.rem(c, slots)] = grad_x
            gx_copy(c).start()

        @pl.when(is_first)
        def _():
            inp_buf[lax.rem(c, slots)] = jnp.transpose(grad_x)

        gc_copy(c).wait_recv()
        message = cond_message(m, h)

        @pl.when(s > 0)
        def _():
            reuse(gc_copy, c)
            gc_out[lax.rem(c, slots)] = message.astype(BF16)
            gc_copy(c).start()

        @pl.when(is_first)
        def _():
            gc_buf[c, 0:mel_rows, :] = message[0:mel_rows].astype(BF16)
            tail = message[mel_rows:EXT]
            if h == 0:
                frame = lax.broadcasted_iota(jnp.int32, mel_ref.shape, 0) == m
                extra_buf[0:1, 0:mel_rows] = jnp.sum(
                    jnp.where(frame, mel_ref[...].astype(F32), 0.0), axis=0, keepdims=True
                )
                lane = lax.broadcasted_iota(jnp.int32, (1, PIECE), 1)
                ids = jnp.where(lane == 0, spk_ref[0, m], 0)
                ids = jnp.where(lane == 1, spk_ref[1, m], ids)
                ids = jnp.where(lane == 2, offs_ref[0, m], ids)
                extra_buf[1:2, :] = ids.astype(F32)
                tail = tail + extra_buf[...]
            gc_buf[c, mel_rows:EXT, :] = tail.astype(BF16)

    def backward_pair(m):
        grad_hidden = dot(both(sg_buf, 2 * m, (0, 1)), ws_ref[...])
        grad_x = grad_field(m, (0, 1), grad_hidden).astype(BF16)
        for h in (1, 0):
            c = 2 * m + h
            reuse(gx_copy, c)
            gx_out[lax.rem(c, slots)] = grad_x[h * PIECE : (h + 1) * PIECE]
            gx_copy(c).start()
        for h in (1, 0):
            c = 2 * m + h
            reuse(gc_copy, c)
            gc_out[lax.rem(c, slots)] = cond_message(m, h).astype(BF16)
            gc_copy(c).start()

    def add_halves(first_row, value):
        rows = value.shape[0] // 2
        acc[first_row : first_row + rows, 0:half] += value[0:rows]
        acc[first_row : first_row + rows, half : 2 * half] += value[rows : 2 * rows]

    def weight_gradients(m):
        parts = (0, 1)
        kept = 2 * lax.rem(m, keep)
        grad_gate = both(gg_buf, kept, parts)
        x = both(x_buf, 2 * m, parts)
        prev = dot(shift_buf[...], x).astype(BF16)
        acc[0 : 2 * half, :] += dot_tn(grad_gate, jnp.concatenate([prev, x], axis=1))
        acc[2 * half : 2 * half + EXT, :] += dot(pair(cond_ref, 2 * m), grad_gate)
        hidden = both(hid_buf, 2 * m, parts)
        row = 2 * half + EXT

        @pl.when(s < sections - 1)
        def _():
            add_halves(row, HALF_ROOT * dot_tn(both(gx_buf, 2 * m, parts), hidden))

        add_halves(row + half // 2, dot_tn(both(sg_buf, 2 * m, parts), hidden))

        @pl.when(is_last)
        def _():
            add_halves(main_rows, dot_nt(pair(gp_buf, kept), pair(a1_buf, kept)))
            add_halves(main_rows + half // 2, dot_nt(pair(gl_buf, kept), pair(a2_buf, kept)))

    def gin_rows(other, group):
        return remote(
            inp_buf.at[:, pl.ds(pl.multiple_of(other * share, share), share), :],
            gin_buf.at[pl.ds(pl.multiple_of(group * slots, slots), slots)],
            gin_ss.at[0],
            gin_rs.at[0],
            other,
            z,
        )

    def gin_sent():
        return remote(
            inp_buf.at[:, share:res, :], inp_buf.at[:, share:res, :], gin_ss.at[0], gin_rs.at[0], 1, z
        )

    def gin_arrived():
        return remote(gin_buf, gin_buf, gin_ss.at[0], gin_rs.at[0], 1, z)

    def hand_out(group):
        @pl.loop(1, sections)
        def _(other):
            gin_rows(other, group).start()

        gin_buf[pl.ds(pl.multiple_of(group * slots, slots), slots)] = inp_buf[:, 0:share, :]

    def own_local():
        return pltpu.make_async_copy(gc_buf, o_g.at[z], loc_sem.at[0])

    def own_hub():
        return remote(gc_buf, o_g.at[z], gown_ss.at[0], g_rs.at[z], hub, z)

    def own_peer(other):
        return remote(o_g.at[z], o_g.at[z], gpeer_ss.at[other], g_rs.at[z], hub, other)

    def part_chip(j, chip):
        return remote(o_g.at[j], o_g.at[j], ghub_ss.at[j, chip], g_rs.at[j], 2 * chip, z)

    def part_next(j):
        return remote(o_g.at[j], o_g.at[j], gnext_ss.at[j], g_rs.at[j], s + 1, z)

    def spread(j):
        part_next(j).start()

        @pl.loop(0, sections // 2 - 1)
        def _(chip):
            @pl.when((chip > 0) | (z != j))
            def _():
                part_chip(j, chip).start()

    @pl.when(is_last)
    def _():
        @pl.loop(0, micro)
        def _(m):
            build_shift(m)
            forward_head(m)
            backward_pair(m)
            if keep < micro:
                weight_gradients(m)

    roomy = keep == micro
    swings = (s == sections - 2) if roomy else False
    late = (s >= sections // 2) if roomy else is_last

    @pl.loop(0, 3 * micro)
    def _(step):
        after = step - micro
        odd = lax.rem(step, 2) == 1
        forth = step < micro
        back = jnp.where(late, (after >= 0) & (after < micro), (after >= 0) & (lax.rem(after, 2) == 0))
        m = jnp.where(forth, step, jnp.where(late, lax.rem(step, micro), after // 2))
        if roomy:
            turning = swings & (step < 2 * micro)
            end = step == 2 * micro - 1
            swing_forth = (step == 0) | (odd & jnp.logical_not(end))
            forth = jnp.where(turning, swing_forth, forth)
            back = jnp.where(turning, jnp.logical_not(swing_forth), back)
            swing_m = jnp.where(swing_forth, (step + 1) // 2, jnp.where(end, micro - 1, step // 2 - 1))
            m = jnp.where(turning, swing_m, m)
        build_shift(m)

        @pl.when(forth & is_first & (m > 0))
        def _():
            condition(m)

        @pl.when(forth & jnp.logical_not(is_last))
        def _():
            forward_piece(m, 0)
            forward_piece(m, 1)

        @pl.when(is_first & (step == micro))
        def _():
            acc[...] = jnp.zeros_like(acc)
            extra_buf[...] = jnp.zeros_like(extra_buf)

        @pl.when(back & jnp.logical_not(is_last))
        def _():
            if ring:

                @pl.when(is_first & (m > 0))
                def _():
                    gin_sent().wait_send()

            backward_piece(m, 1)
            backward_piece(m, 0)

            @pl.when(is_first & (lax.rem(2 * m + 2, slots) == 0))
            def _():
                hand_out((2 * m + 2) // slots - 1)

            @pl.when(is_first & (m == micro - 1))
            def _():
                own_hub().start()
                own_local().start()

        @pl.when(jnp.logical_not(forth | back) & (roomy | jnp.logical_not(is_last)))
        def _():
            weight_gradients(m)

    @pl.when(is_first)
    def _():
        own_local().wait()

    left = z < groups // 2
    inward = jnp.where(left, z + 1, z - 1)
    outward = jnp.where(left, z - 1, z + 1)
    is_edge = (z == 0) | (z == groups - 1)
    is_mid = (z == groups // 2 - 1) | (z == groups // 2)
    distance = jnp.where(left, groups // 2 - 1 - z, z - groups // 2)
    lag = LAG * (2 * distance + 1) + 4 * distance
    base = jnp.where(is_last, main_blocks + head_blocks, main_blocks)
    gives = (s < 2) if exports else False
    takes = ((s == helper) | (s == helper + 1)) if exports else False
    count = base - jnp.where(gives, exports, 0) + jnp.where(takes, exports, 0)

    all_blocks = main_blocks + head_blocks
    taken_at = base - 2 * exports

    def block_of(i):
        j = jnp.where(takes & (i >= taken_at + exports), i - exports, i)
        own = jnp.where(is_last, jnp.where(j < head_blocks, j + main_blocks, j - head_blocks), j)
        return jnp.where(takes & (j == i) & (i >= taken_at), i - taken_at + all_blocks, own)

    def rows_of(b):
        return pl.ds(pl.multiple_of(b * BLOCK, BLOCK), BLOCK)

    cycle = zp_rs.shape[0]

    def swap_copy(i):
        rows = rows_of(block_of(i))
        return remote(part_out.at[rows], o_acc.at[rows], zi_ss.at[0], zt_rs.at[lax.rem(i, cycle)], s, inward)

    def part_copy(i):
        rows = rows_of(block_of(i))
        return remote(part_out.at[rows], part_in.at[rows], zi_ss.at[0], zp_rs.at[lax.rem(i, cycle)], s, inward)

    def total_copy(i):
        rows = rows_of(block_of(i))
        return remote(o_acc.at[rows], o_acc.at[rows], zo_ss.at[0], zt_rs.at[lax.rem(i, cycle)], s, outward)

    def head_copy(j):
        rows = rows_of(main_blocks + j)
        return remote(o_acc.at[rows], o_acc.at[rows], hd_ss.at[0], hd_rs.at[j], s - 1, z)

    def send_part(i):
        rows = rows_of(block_of(i))

        @pl.when(is_edge)
        def _():
            part_out[rows, :] = acc[rows, :].astype(BF16)

        @pl.when(jnp.logical_not(is_edge))
        def _():
            part_copy(i).wait_recv()
            part_out[rows, :] = (acc[rows, :] + part_in[rows, :].astype(F32)).astype(BF16)

        @pl.when(is_mid)
        def _():
            swap_copy(i).start()

        @pl.when(jnp.logical_not(is_mid))
        def _():
            part_copy(i).start()

    def keep_rows(rows):
        return pltpu.make_async_copy(o_acc.at[rows], o_sum.at[rows], out_sem.at[0])

    def finish_part(i):
        rows = rows_of(block_of(i))
        swap_copy(i).wait_recv()

        @pl.when(is_mid)
        def _():
            o_acc[rows, :] = (part_out[rows, :].astype(F32) + o_acc[rows, :].astype(F32)).astype(BF16)

        @pl.when(jnp.logical_not(is_edge))
        def _():
            total_copy(i).start()

        @pl.when(block_of(i) < all_blocks)
        def _():
            keep_rows(rows).start()

    given_rows = pl.ds(main_rows - exports * BLOCK, exports * BLOCK)
    taken_rows = pl.ds(main_rows + head_rows, exports * BLOCK)

    def give_copy():
        return remote(part_out.at[given_rows], taken_buf, give_ss.at[0], give_rs.at[0], s + helper, z)

    def return_copy():
        return remote(o_acc.at[taken_rows], o_acc.at[given_rows], give_ss.at[1], give_rs.at[1], s - helper, z)

    if exports:

        @pl.when(gives)
        def _():
            part_out[given_rows, :] = acc[given_rows, :].astype(BF16)
            give_copy().start()

    last_step = main_blocks - exports + lag - 1
    head_at = lag + 2
    own_at = jnp.minimum(17 + 9 * distance, last_step)
    rest_at = jnp.where(is_hub, 33, jnp.where(s < sections // 2, 40, 45))
    rest_at = jnp.minimum(rest_at + 9 * distance, last_step)

    @pl.loop(0, count + lag)
    def _(i):
        if exports:

            @pl.when(takes & (i == taken_at))
            def _():
                give_copy().wait_recv()
                acc[taken_rows, :] = taken_buf[...].astype(F32)

        @pl.when(i < count)
        def _():
            send_part(i)

        @pl.when(i >= lag)
        def _():
            finish_part(i - lag)
            b = block_of(i - lag)

            @pl.when((b >= main_blocks) & (b < all_blocks))
            def _():
                head_copy(b - main_blocks).start()

            if exports:

                @pl.when(b == all_blocks + exports - 1)
                def _():
                    return_copy().start()

        @pl.when(jnp.logical_not(is_last) & (i >= head_at) & (i < head_at + head_blocks))
        def _():
            j = i - head_at
            head_copy(j).wait_recv()
            keep_rows(rows_of(main_blocks + j)).start()

            @pl.when(s > 0)
            def _():
                head_copy(j).start()

        @pl.when(is_hub & (i == own_at))
        def _():
            own_hub().wait_recv()
            for other in range(groups):

                @pl.when(z != other)
                def _():
                    own_peer(other).start()

            spread(z)

        @pl.when((lax.rem(s, 2) == 0) & (i == rest_at))
        def _():
            for j in range(groups):

                @pl.when((z != j) | ((s > 0) & (s < hub)))
                def _():
                    part_next(j).wait_recv()

                @pl.when(is_hub & (z != j))
                def _():
                    spread(j)

                @pl.when(jnp.logical_not(is_hub))
                def _():
                    part_next(j).start()

    @pl.when(s > 0)
    def _():
        gin_arrived().wait_recv()

    for c in range(pieces):
        o_gin[:, c * PIECE : (c + 1) * PIECE] = gin_buf[c]

    @pl.when(is_first)
    def _():
        own_hub().wait_send()
        gin_sent().wait_send()

    @pl.when(is_hub)
    def _():
        for j in range(groups):

            @pl.when(z != j)
            def _():
                own_peer(j).wait_send()

            @pl.loop(0, sections // 2 - 1)
            def _(chip):
                @pl.when((chip > 0) | (z != j))
                def _():
                    part_chip(j, chip).wait_send()

    for j in range(groups):

        @pl.when(lax.rem(s, 2) == 0)
        def _():
            part_next(j).wait_send()

        @pl.when(lax.rem(s, 2) == 1)
        def _():
            part_next(j).wait_recv()

    if exports:

        @pl.when(gives)
        def _():
            return_copy().wait_recv()
            keep_rows(given_rows).start()
            give_copy().wait_send()

        @pl.when(takes)
        def _():
            return_copy().wait_send()

    keep_rows(pl.ds(0, main_rows + head_rows)).wait()

    def sum_sent(rows):
        remote(part_out.at[rows], part_out.at[rows], zi_ss.at[0], zp_rs.at[0], s, inward).wait_send()

        @pl.when(jnp.logical_not(is_edge))
        def _():
            remote(o_acc.at[rows], o_acc.at[rows], zo_ss.at[0], zt_rs.at[0], s, outward).wait_send()

    @pl.when(is_last)
    def _():
        sum_sent(pl.ds(0, main_rows + head_rows + (exports * BLOCK if helper + 1 == sections - 1 else 0)))

    if exports:

        @pl.when(takes & jnp.logical_not(is_last))
        def _():
            sum_sent(pl.ds(0, main_rows + exports * BLOCK))

        @pl.when(gives)
        def _():
            sum_sent(pl.ds(0, main_rows - exports * BLOCK))

    @pl.when(jnp.logical_not(is_last | gives | takes))
    def _():
        sum_sent(pl.ds(0, main_rows))

    @pl.when(jnp.logical_not(is_last))
    def _():
        drain(x_copy, lambda: remote(x_out, x_out, x_ss.at[0], x_rs.at[0], s + 1, z))
        drain(k_copy, lambda: remote(k_out, k_out, k_ss.at[0], k_rs.at[0], s + 1, z))

    @pl.when(s > 0)
    def _():
        rows = pl.ds(main_rows, head_rows)
        remote(o_acc.at[rows], o_acc.at[rows], hd_ss.at[0], hd_rs.at[0], s - 1, z).wait_send()
        drain(gx_copy, lambda: remote(gx_out, gx_out, gx_ss.at[0], gx_rs.at[0], s - 1, z))
        drain(gc_copy, lambda: remote(gc_out, gc_out, gc_ss.at[0], gc_rs.at[0], s - 1, z))

    @pl.when(lax.rem(s, 2) == 1)
    def _():
        gs_whole(0).wait_send()

    @pl.when(is_last)
    def _():
        for chip in far_chips:
            gs_whole(1 + chip).wait_send()

    @pl.when(s == feeder)
    def _():
        gs_whole(1).wait_send()


def run_step(dims, tables, arrays, weights):
    sections, groups, micro, res, half, classes, slots, keep, mel_rows = dims
    pieces = 2 * micro
    rows = 2 * half + EXT + half + half // 2 + classes // 2
    head_blocks = (half // 2 + classes // 2) // BLOCK
    share = res // sections
    smem = pl.BlockSpec(memory_space=pltpu.SMEM)
    vmem = pl.BlockSpec(memory_space=pltpu.VMEM)
    anywhere = pl.BlockSpec(memory_space=pl.ANY)
    dma = pltpu.SemaphoreType.DMA

    def tile(*shape, dtype=BF16):
        return pltpu.VMEM(shape, dtype)

    distance = groups // 2 - 1
    cycle = max(LAG * (2 * distance + 1) + 4 * distance + 4, 2 * LAG + 4)
    sends = slots if pieces > slots else 1
    taken = exported_blocks(dims) * BLOCK

    scratch = [
        tile(pieces, PIECE, res),
        tile(pieces, PIECE, half),
        tile(pieces, PIECE, res),
        tile(pieces, EXT, PIECE),
        tile(pieces, PIECE, half),
        tile(pieces, PIECE, half),
        tile(pieces, PIECE, half),
        tile(slots, PIECE, res),
        tile(slots, PIECE, half),
        tile(slots, PIECE, res),
        tile(slots, EXT, PIECE),
        tile(2 * PIECE, 2 * half, dtype=F32),
        tile(PIECE, half, dtype=F32),
        tile(2 * keep, PIECE, 2 * half),
        tile(slots, res, PIECE),
        tile(2 * PIECE, 2 * PIECE),
        tile(2 * PIECE, 2 * PIECE),
        tile(pieces, EXT, PIECE),
        tile(pieces, PIECE, EXT),
        tile(EXT, 2 * half),
        tile(2 * half, 2 * res),
        tile(res, half),
        tile(half, half),
        tile(half, half),
        tile(classes, half),
        tile(2 * res, 2 * half),
        tile(half, res),
        tile(half, half),
        tile(half, half),
        tile(half, classes),
        tile(2 * keep, classes, PIECE),
        tile(2 * keep, half, PIECE),
        tile(2 * keep, half, PIECE),
        tile(2 * keep, half, PIECE),
        tile(rows + taken, WIDE, dtype=F32),
        tile(rows + taken, WIDE),
        tile(rows + taken, WIDE),
        tile(rows + taken, WIDE),
        tile(max(taken, 16), WIDE),
        tile(pieces, share, PIECE),
        tile(2, micro * mel_rows, PIECE, dtype=F32),
        tile(EXT - mel_rows, PIECE, dtype=F32),
        dma((slots,)),
        dma((10,)),
        dma((1,)),
        dma((1,)),
        dma((sends,)),
        dma((pieces,)),
        dma((sends,)),
        dma((pieces,)),
        dma((max(2, sections // 2),)),
        dma((pieces,)),
        dma((sends,)),
        dma((pieces,)),
        dma((sends,)),
        dma((pieces,)),
        dma((1,)),
        dma((1,)),
        dma((cycle,)),
        dma((cycle,)),
        dma((1,)),
        dma((head_blocks,)),
        dma((groups,)),
        dma((1,)),
        dma((groups,)),
        dma((groups, sections // 2)),
        dma((groups,)),
        dma((1,)),
        dma((1,)),
        dma((2,)),
        dma((2,)),
    ]
    return pl.pallas_call(
        functools.partial(step_kernel, dims),
        out_shape=(
            jax.ShapeDtypeStruct((rows, WIDE), BF16),
            jax.ShapeDtypeStruct((groups, pieces, EXT, PIECE), BF16),
            jax.ShapeDtypeStruct((share, pieces * PIECE), BF16),
        ),
        in_specs=[smem] * 4 + [vmem] * 4 + [anywhere] * 8,
        out_specs=(anywhere, anywhere, vmem),
        scratch_shapes=scratch,
        compiler_params=pltpu.CompilerParams(
            collective_id=0, has_side_effects=True, vmem_limit_bytes=63 * 2**20
        ),
        cost_estimate=pl.CostEstimate(flops=10**10, bytes_accessed=3 * 10**7, transcendentals=10**6),
        name="train_step",
    )(*tables, *arrays, *weights)


def finish_kernel(
    dims,
    sums,
    gin,
    shared_hbm,
    o_gin,
    o_dil,
    o_cond,
    o_res,
    o_skip,
    o_post,
    o_out,
    o_up,
    o_bias,
    o_table,
    o_loss,
    sums_buf,
    shared,
    dil_buf,
    cond_buf,
    res_buf,
    skip_buf,
    post_buf,
    out_buf,
    up_buf,
    field,
    mel_rows_buf,
    mel_columns,
    table,
    load_sem,
    store_sem,
):
    mel_rows, half = dims
    frames = shared.shape[0]
    first = 2 * half
    total_rows = sums_buf.shape[0]
    strips = ((0, half), (half, half), (first, total_rows - first))
    loads = [
        pltpu.make_async_copy(sums.at[pl.ds(row, rows), :], sums_buf.at[pl.ds(row, rows), :], load_sem.at[k])
        for k, (row, rows) in enumerate(strips)
    ]
    loads.append(pltpu.make_async_copy(shared_hbm, shared, load_sem.at[3]))
    for load in loads:
        load.start()
    stores = []

    def store(source, target):
        copy = pltpu.make_async_copy(source, target, store_sem.at[len(stores)])
        copy.start()
        stores.append(copy)

    store(gin, o_gin)

    for k in range(2):
        loads[k].wait()
        rows = pl.ds(k * half, half)
        dil_buf[rows, :] = sums_buf[rows, :].astype(F32)
        store(dil_buf.at[rows, :], o_dil.at[0, rows, :])
    loads[2].wait()
    cond_buf[...] = sums_buf[first : first + mel_rows, :].astype(F32)
    o_bias[...] = sums_buf[first + mel_rows : first + EXT, :].astype(F32)[0:1]
    store(cond_buf, o_cond)
    row = first + EXT
    for buffer, target in ((res_buf, o_res), (skip_buf, o_skip), (post_buf, o_post), (out_buf, o_out)):
        rows = buffer.shape[1]
        buffer[0] = sums_buf[row : row + rows, 0:half].astype(F32)
        buffer[1] = sums_buf[row : row + rows, half : 2 * half].astype(F32)
        store(buffer, target)
        row += rows

    loads[3].wait()

    def by_channel(f, loss):
        extra = shared[f, 0, mel_rows:EXT, :].astype(F32)
        mel_rows_buf[pl.ds(f, 1), :] = extra[0:1]
        for h in range(2):
            rows = pl.ds(pl.multiple_of(f * mel_rows, 16), mel_rows)
            field[h, rows, :] = shared[f, h, 0:mel_rows, :].astype(F32)
        return loss + extra + shared[f, 1, mel_rows:EXT, :].astype(F32)

    loss = lax.fori_loop(0, frames, by_channel, jnp.zeros((EXT - mel_rows, PIECE), F32))
    row = lax.broadcasted_iota(jnp.int32, loss.shape, 0)
    loss = jnp.where((row >= 2) & (row < 5), loss, 0.0)
    o_loss[...] = jnp.sum(jnp.sum(loss, axis=1, keepdims=True), axis=0, keepdims=True)
    mel_columns[...] = jnp.transpose(mel_rows_buf[...])[0:mel_rows].astype(BF16)

    parts = 4
    channels = mel_rows // parts

    def upsampling(part):
        @pl.loop(0, channels // 10)
        def _(group):
            for j in range(10):
                c = part * channels + group * 10 + j
                rows = pl.ds(c, frames, stride=mel_rows)
                matrix = jnp.concatenate([field[0, rows, :], field[1, rows, :]], axis=1)
                up_buf[c] = dot(mel_columns[...], matrix.astype(BF16))

        rows = pl.ds(part * channels, channels)
        store(up_buf.at[rows], o_up.at[rows])

    for part in range(parts - 2):
        upsampling(part)

    table[...] = jnp.zeros_like(table)
    time = lax.broadcasted_iota(jnp.int32, (2 * PIECE, PIECE), 0).astype(F32)
    number = lax.broadcasted_iota(jnp.int32, (2 * PIECE, PIECE), 1).astype(F32)

    @pl.loop(0, frames // 4)
    def _(group):
        grads, hots = [], []
        for k in range(4):
            f = group * 4 + k
            ids = shared[f, 0, mel_rows:EXT, :].astype(F32)[1:2]
            speaker = jnp.where(time >= ids[:, 2:3], ids[:, 1:2], ids[:, 0:1])
            hots.append(jnp.where(number == speaker, 1.0, 0.0).astype(BF16))
            grads += [shared[f, 0, 0:mel_rows, :], shared[f, 1, 0:mel_rows, :]]
        table[...] += dot(jnp.concatenate(grads, axis=1), jnp.concatenate(hots, axis=0))

    o_table[...] = table[:, 0 : o_table.shape[1]]
    for part in range(parts - 2, parts):
        upsampling(part)

    for copy in stores:
        copy.wait()


def finish(sums, shared, grad_inputs, half, classes, mel_rows, speakers):
    frames = shared.shape[0]
    first = 2 * half
    vmem = pl.BlockSpec(memory_space=pltpu.VMEM)
    anywhere = pl.BlockSpec(memory_space=pl.ANY)
    large = (
        (first, WIDE),
        (mel_rows, WIDE),
        (2, half // 2, half),
        (2, half // 2, half),
        (2, half // 2, half),
        (2, classes // 2, half),
        (mel_rows, mel_rows, 2 * PIECE),
    )

    def f32(*shape):
        return jax.ShapeDtypeStruct(shape, F32)

    return pl.pallas_call(
        functools.partial(finish_kernel, (mel_rows, half)),
        out_shape=(
            jax.ShapeDtypeStruct(grad_inputs.shape, grad_inputs.dtype),
            f32(1, *large[0]),
            *[f32(*shape) for shape in large[1:]],
            f32(1, WIDE),
            f32(mel_rows, speakers),
            f32(1, 1),
        ),
        in_specs=[anywhere] * 3,
        out_specs=(anywhere,) * 8 + (vmem,) * 3,
        scratch_shapes=[
            pltpu.VMEM(sums.shape, BF16),
            pltpu.VMEM(shared.shape, BF16),
            *[pltpu.VMEM(shape, F32) for shape in large],
            pltpu.VMEM((2, frames * mel_rows, PIECE), F32),
            pltpu.VMEM((frames, PIECE), F32),
            pltpu.VMEM((mel_rows, frames), BF16),
            pltpu.VMEM((mel_rows, PIECE), F32),
            pltpu.SemaphoreType.DMA((4,)),
            pltpu.SemaphoreType.DMA((12,)),
        ],
        compiler_params=pltpu.CompilerParams(vmem_limit_bytes=62 * 2**20),
        name="finish",
    )(sums, grad_inputs, shared)


def local(
    inputs,
    targets,
    mel,
    speakers,
    speaker_sample_counts,
    segment_offsets,
    dilations,
    dilated_kernel,
    conditioning_projection,
    dilated_gate_bias,
    residual_projection,
    skip_projection,
    upsample_weight,
    speaker_table,
    first_output_projection,
    class_projection,
):
    sections = lax.axis_size("section")
    groups = lax.axis_size("dp")
    micro = segment_offsets.shape[0]
    res, tokens = inputs.shape
    length = tokens // micro
    mel_rows = mel.shape[0]
    hop = upsample_weight.shape[0]
    half = residual_projection.shape[2]
    classes = class_projection.shape[0]
    pieces = 2 * micro
    assert length == 2 * PIECE and hop == length and mel_rows + 16 == EXT and 2 * half == WIDE

    slots, keep = (pieces, micro) if pieces <= 8 else (2, 1)
    dims = (sections, groups, micro, res, half, classes, slots, keep, mel_rows)
    sums, shared, grad_inputs = run_step(
        dims,
        (dilations, segment_offsets.T, speakers.T, speaker_sample_counts),
        (
            targets.reshape(micro, 1, length),
            mel.T,
            speaker_table,
            dilated_gate_bias,
        ),
        (
            inputs,
            upsample_weight.transpose(1, 2, 0).reshape(mel_rows * mel_rows, hop),
            conditioning_projection[0].T,
            dilated_kernel[0],
            residual_projection[0],
            skip_projection[0],
            first_output_projection,
            class_projection,
        ),
    )
    shared = shared.reshape(groups * micro, 2, EXT, PIECE)
    grad_inputs, dil, cond, grad_res, grad_skip, post, out, up, bias, table, loss = finish(
        sums, shared, grad_inputs, half, classes, mel_rows, speaker_table.shape[1]
    )
    return (
        loss.reshape(()),
        grad_inputs,
        dil,
        cond.T[None],
        bias,
        grad_res.reshape(1, half, half),
        grad_skip.reshape(1, half, half),
        up.transpose(2, 0, 1),
        table,
        post.reshape(half, half),
        out.reshape(classes, half),
    )


def solution(mesh):
    return jax.shard_map(
        local,
        mesh=mesh,
        in_specs=(
            P(None, "dp"),
            P("dp"),
            P(None, "dp"),
            P("dp", None),
            P(),
            P("dp", None),
            P("section"),
            P("section", None, None),
            P("section", None, None),
            P("section", None),
            P("section", None, None),
            P("section", None, None),
            P(),
            P(),
            P(),
            P(),
        ),
        out_specs=(
            P(),
            P("section", "dp"),
            P("section", None, None),
            P("section", None, None),
            P("section", None),
            P("section", None, None),
            P("section", None, None),
            P(),
            P(),
            P(),
            P(),
        ),
        check_vma=False,
    )
```

```python
import functools
import math

import jax
import jax.numpy as jnp
from jax import lax
from jax.experimental import pallas as pl
from jax.experimental.pallas import tpu as pltpu
from jax.sharding import PartitionSpec as P

HALF_ROOT = 0.7071067811865476
WEIGHT_SCALE = 64.0
MESH = pl.DeviceIdType.MESH
BF16 = jnp.bfloat16
F32 = jnp.float32

PIECE = 128
EXT = 96
WIDE = 1024
BLOCK = 32
EXPORTS = (6,)
LARGE_AT = 3
LAG = 4


def dot(left, right):
    return jnp.dot(left, right, preferred_element_type=F32)


def dot_nt(left, right):
    return lax.dot_general(left, right, (((1,), (1,)), ((), ())), preferred_element_type=F32)


def dot_tn(left, right):
    return lax.dot_general(left, right, (((0,), (0,)), ((), ())), preferred_element_type=F32)


def sigmoid(values):
    return 0.5 * jnp.tanh(0.5 * values) + 0.5


def exported_blocks(dims):
    sections, groups, micro, keep = dims[0], dims[1], dims[2], dims[7]
    helped = sections // 4
    return EXPORTS[:helped] if keep == micro and sections <= 8 else ()


def step_kernel(
    dims,
    dil_ref,
    offs_ref,
    spk_ref,
    cnt_ref,
    tgt_ref,
    mel_ref,
    tab_ref,
    bias_in,
    inp_hbm,
    up_hbm,
    wc_hbm,
    wd_hbm,
    wr_hbm,
    ws_hbm,
    wp_hbm,
    wk_hbm,
    o_sum,
    o_g,
    o_gin,
    x_buf,
    sg_buf,
    gx_buf,
    gc_buf,
    hid_buf,
    d1_buf,
    d2_buf,
    x_out,
    k_out,
    gx_out,
    gc_out,
    gate_buf,
    gh_buf,
    gg_buf,
    inp_buf,
    shift_buf,
    shift_back,
    cond_ref,
    cond_t,
    wc_ref,
    wd_ref,
    wr_ref,
    ws_ref,
    wp_ref,
    wk_ref,
    wd_t,
    wr_t,
    ws_t,
    wp_t,
    wk_t,
    gl_buf,
    a2_buf,
    gp_buf,
    a1_buf,
    acc,
    part_out,
    part_in,
    o_acc,
    taken_buf,
    gin_buf,
    up_buf,
    extra_buf,
    inp_sem,
    load_sem,
    out_sem,
    loc_sem,
    x_ss,
    x_rs,
    k_ss,
    k_rs,
    gs_ss,
    gs_rs,
    gx_ss,
    gx_rs,
    gc_ss,
    gc_rs,
    zi_ss,
    zo_ss,
    zp_rs,
    zt_rs,
    hd_ss,
    hd_rs,
    g_rs,
    gown_ss,
    gpeer_ss,
    ghub_ss,
    gnext_ss,
    gin_ss,
    gin_rs,
    give_ss,
    give_rs,
):
    sections, groups, micro, res, half, classes, slots, keep, mel_rows = dims
    pieces = 2 * micro
    s = lax.axis_index("section")
    z = lax.axis_index("dp")
    is_first = s == 0
    is_last = s == sections - 1
    hub = sections - 2
    is_hub = s == hub
    head_scale = 1.0 / math.sqrt(sections)
    main_rows = 2 * half + EXT + half
    head_rows = half // 2 + classes // 2
    main_blocks = main_rows // BLOCK
    head_blocks = head_rows // BLOCK
    share = res // sections
    feeder = sections - 3 if sections > 4 else sections - 1
    exports = exported_blocks(dims)
    helper = sections // 2

    barrier = pltpu.get_barrier_semaphore()

    def greet(cond, dev_s, dev_z):
        @pl.when(cond)
        def _():
            pl.semaphore_signal(barrier, 1, device_id=(dev_s, dev_z), device_id_type=MESH)

    greet(s > 0, s - 1, z)
    greet(s < sections - 1, s + 1, z)
    greet(z > 0, s, z - 1)
    greet(z < groups - 1, s, z + 1)
    greet(s >= 2, 0, z)
    told = (lax.rem(s, 2) == 0) & (s > 0) & (s < hub)
    greet(told, hub, z)

    @pl.when(is_first)
    def _():
        @pl.loop(2, sections)
        def _(other):
            pl.semaphore_signal(barrier, 1, device_id=(other, z), device_id_type=MESH)

    @pl.when(is_hub)
    def _():
        @pl.loop(1, sections // 2 - 1)
        def _(chip):
            pl.semaphore_signal(barrier, 1, device_id=(2 * chip, z), device_id_type=MESH)

    far = (lax.rem(s, 2) == 1) & (s > 1) & (s < sections - 1)
    greet(far, sections - 1, z)

    @pl.when(is_last)
    def _():
        @pl.loop(1, sections // 2 - 1)
        def _(chip):
            pl.semaphore_signal(barrier, 1, device_id=(2 * chip + 1, z), device_id_type=MESH)

    greet(s == 1, feeder, z)
    greet(s == feeder, 1, z)

    def flag(cond):
        return jnp.where(cond, 1, 0)

    z_near = flag(z > 0) + flag(z < groups - 1)
    expected = (
        flag(s > 0)
        + flag(s < sections - 1)
        + z_near
        + jnp.where(is_first, sections - 2, flag(s >= 2))
        + flag(told)
        + flag(far)
        + flag(s == 1)
        + flag(s == feeder)
        + jnp.where(is_last, sections // 2 - 2, 0)
        + jnp.where(is_hub, sections // 2 - 2, 0)
    )

    def input_copy(c):
        slot = lax.rem(c, slots)
        return pltpu.make_async_copy(
            inp_hbm.at[:, pl.ds(pl.multiple_of(c * PIECE, PIECE), PIECE)],
            inp_buf.at[slot],
            inp_sem.at[slot],
        )

    quarter = mel_rows // 4
    weight_refs = (
        (wd_hbm, wd_ref),
        (wr_hbm, wr_ref),
        (ws_hbm, ws_ref),
        (wc_hbm, wc_ref.at[0:mel_rows]),
        (wp_hbm, wp_ref),
        (wk_hbm, wk_ref),
    )
    loads = [
        pltpu.make_async_copy(source, target, load_sem.at[4 + position])
        for position, (source, target) in enumerate(weight_refs)
    ]
    frame_loads = [
        pltpu.make_async_copy(
            up_hbm.at[pl.ds(q * quarter * mel_rows, quarter * mel_rows), :],
            part_out.at[pl.ds(0, quarter * mel_rows), pl.ds(q * 2 * PIECE, 2 * PIECE)],
            load_sem.at[q],
        )
        for q in range(4)
    ]
    for load in loads[:4] + frame_loads:
        load.start()

    @pl.when(is_first)
    def _():
        @pl.loop(0, slots)
        def _(c):
            input_copy(c).start()

    @pl.when(is_last)
    def _():
        for load in loads[4:]:
            load.start()

    spare = lax.broadcasted_iota(jnp.int32, (EXT - mel_rows, 2 * half), 0)
    bias = jnp.broadcast_to(bias_in[...].astype(F32), (EXT - mel_rows, 2 * half))
    wc_ref[mel_rows:EXT] = jnp.where(spare == 0, bias, 0.0).astype(BF16)
    loads[0].wait()
    wd_t[...] = jnp.transpose(wd_ref[...])
    for load in loads[1:4]:
        load.wait()
    wr_t[...] = jnp.transpose(wr_ref[...])
    ws_t[...] = jnp.transpose(ws_ref[...])

    for load in frame_loads:
        load.wait()

    @pl.loop(0, quarter // 4)
    def _(group):
        for q in range(4):
            for part in range(4):
                row = group * 4 + part
                lanes = slice(q * 2 * PIECE, (q + 1) * 2 * PIECE)
                matrix = part_out[pl.ds(pl.multiple_of(row * mel_rows, 16), mel_rows), lanes]
                frames = dot(mel_ref[...], matrix)
                rows = pl.ds(q * quarter + row, micro, stride=mel_rows)
                for h in range(2):
                    up_buf[h, rows, :] = frames[:, h * PIECE : (h + 1) * PIECE]

    def condition(m):
        shape = (tab_ref.shape[1], 2 * PIECE)
        time = lax.broadcasted_iota(jnp.int32, shape, 1)
        speaker = jnp.where(time >= offs_ref[0, m], spk_ref[1, m], spk_ref[0, m])
        hot = jnp.where(lax.broadcasted_iota(jnp.int32, shape, 0) == speaker, 1.0, 0.0).astype(BF16)
        columns = dot(tab_ref[...], hot)
        ones = jnp.where(lax.broadcasted_iota(jnp.int32, (EXT - mel_rows, PIECE), 0) == 0, 1.0, 0.0)
        rows = pl.ds(pl.multiple_of(m * mel_rows, 16), mel_rows)
        for h in range(2):
            c = 2 * m + h
            value = up_buf[h, rows, :] + columns[:, h * PIECE : (h + 1) * PIECE]
            cond_ref[c] = jnp.concatenate([value, ones], axis=0).astype(BF16)
            cond_t[c] = jnp.transpose(cond_ref[c])

    @pl.when(is_first)
    def _():
        condition(0)

    @pl.when(s > 0)
    def _():
        @pl.loop(0, micro)
        def _(m):
            condition(m)

    @pl.when(s > 0)
    def _():
        acc[...] = jnp.zeros_like(acc)

    @pl.when(is_last)
    def _():
        for load in loads[4:]:
            load.wait()
        wp_t[...] = jnp.transpose(wp_ref[...])
        wk_t[...] = jnp.transpose(wk_ref[...])
        gx_buf[...] = jnp.zeros_like(gx_buf)

    pl.semaphore_wait(barrier, expected)

    def remote(src, dst, send_sem, recv_sem, dev_s, dev_z):
        return pltpu.make_async_remote_copy(
            src_ref=src,
            dst_ref=dst,
            send_sem=send_sem,
            recv_sem=recv_sem,
            device_id=(dev_s, dev_z),
            device_id_type=MESH,
        )

    ring = pieces > slots

    def send_of(semaphores, slot):
        return semaphores.at[slot if ring else 0]

    def x_copy(c):
        slot = lax.rem(c, slots)
        return remote(x_out.at[slot], x_buf.at[c], send_of(x_ss, slot), x_rs.at[c], s + 1, z)

    def k_copy(c):
        slot = lax.rem(c, slots)
        return remote(k_out.at[slot], sg_buf.at[c], send_of(k_ss, slot), k_rs.at[c], s + 1, z)

    def gx_copy(c):
        slot = lax.rem(c, slots)
        return remote(gx_out.at[slot], gx_buf.at[c], send_of(gx_ss, slot), gx_rs.at[c], s - 1, z)

    def gc_copy(c):
        slot = lax.rem(c, slots)
        return remote(gc_out.at[slot], gc_buf.at[c], send_of(gc_ss, slot), gc_rs.at[c], s - 1, z)

    def reuse(copy, c):
        if ring:

            @pl.when(c >= slots)
            def _():
                copy(c).wait_send()

    def drain(copy, whole):
        if ring:

            @pl.loop(0, slots)
            def _(c):
                copy(c).wait_send()

        else:
            whole().wait_send()

    chips = sections // 2
    far_chips = range(chips - 2, 0, -1)

    def gs_copy(c):
        return remote(sg_buf.at[c], sg_buf.at[c], gs_ss.at[0], gs_rs.at[c], s - 1, z)

    def gs_first(c):
        return remote(sg_buf.at[c], sg_buf.at[c], gs_ss.at[1], gs_rs.at[c], 1, z)

    def gs_chip(c, chip):
        return remote(sg_buf.at[c], sg_buf.at[c], gs_ss.at[1 + chip], gs_rs.at[c], 2 * chip + 1, z)

    def gs_whole(position):
        return remote(sg_buf, sg_buf, gs_ss.at[position], gs_rs.at[0], s - 1, z)

    def build_shift(m):
        dilation = dil_ref[0]
        middle = offs_ref[0, m]
        shape = (2 * PIECE, 2 * PIECE)

        def matrix(source, target):
            start = jnp.where(target >= middle, middle, 0)
            hit = (source == target - dilation) & (source >= start)
            return jnp.where(hit, 1.0, 0.0).astype(BF16)

        rows = lax.broadcasted_iota(jnp.int32, shape, 0)
        lanes = lax.broadcasted_iota(jnp.int32, shape, 1)
        shift_buf[...] = matrix(lanes, rows)
        shift_back[...] = matrix(rows, lanes)

    def pair(ref, first):
        return jnp.concatenate([ref[first], ref[first + 1]], axis=1)

    def put_pair(ref, first, value):
        for h in range(2):
            ref[first + h] = value[:, h * PIECE : (h + 1) * PIECE]

    def both(ref, first, parts):
        return jnp.concatenate([ref[first + h] for h in parts], axis=0)

    def put(ref, first, parts, value):
        for position, h in enumerate(parts):
            ref[first + h] = value[position * PIECE : (position + 1) * PIECE]

    def head(m, total):
        width = 2 * PIECE
        total = jnp.transpose(total.astype(BF16)).astype(F32) * head_scale
        sig_1 = sigmoid(total)
        act_1 = (total * sig_1).astype(BF16)
        slope_1 = sig_1 * (1.0 + total * (1.0 - sig_1)) * head_scale
        post = dot(wp_ref[...], act_1)
        sig_2 = sigmoid(post)
        act_2 = (post * sig_2).astype(BF16)
        slope_2 = sig_2 * (1.0 + post * (1.0 - sig_2))
        logits = dot(wk_ref[...], act_2)
        top = jnp.max(logits, axis=0, keepdims=True)
        expo = jnp.exp(logits - top)
        denominator = jnp.sum(expo, axis=0, keepdims=True)
        hit = tgt_ref[m] == lax.broadcasted_iota(jnp.int32, (classes, width), 0)
        picked = jnp.sum(jnp.where(hit, logits, 0.0), axis=0, keepdims=True)
        time = lax.broadcasted_iota(jnp.int32, (1, width), 1)

        def speaker_weight(which):
            count = cnt_ref[spk_ref[which, m]].astype(F32)
            return WEIGHT_SCALE * lax.rsqrt(jnp.full((1, width), count, F32))

        weight = jnp.where(time >= offs_ref[0, m], speaker_weight(1), speaker_weight(0))
        weight = jnp.where(time < offs_ref[1, m], weight, 0.0)
        grad_logits = (weight * (expo / denominator - jnp.where(hit, 1.0, 0.0))).astype(BF16)
        grad_post = (dot(wk_t[...], grad_logits) * slope_2).astype(BF16)
        grad_total = (dot(wp_t[...], grad_post) * slope_1).astype(BF16)
        put(sg_buf, 2 * m, (0, 1), jnp.transpose(grad_total))
        for h in (1, 0):
            c = 2 * m + h
            for chip in far_chips:
                gs_chip(c, chip).start()
            gs_copy(c).start()
            if feeder == sections - 1:
                gs_first(c).start()
        kept = 2 * lax.rem(m, keep)
        put_pair(gl_buf, kept, grad_logits)
        put_pair(a2_buf, kept, act_2)
        put_pair(gp_buf, kept, grad_post)
        put_pair(a1_buf, kept, act_1)
        loss_row = weight * (top + jnp.log(denominator) - picked)
        high = loss_row.astype(BF16)
        rest = loss_row - high.astype(F32)
        middle = rest.astype(BF16)
        low = (rest - middle.astype(F32)).astype(BF16)
        row = lax.broadcasted_iota(jnp.int32, (EXT, width), 0)
        message = jnp.where(row == mel_rows + 2, high.astype(F32), 0.0)
        message = jnp.where(row == mel_rows + 3, middle.astype(F32), message)
        message = jnp.where(row == mel_rows + 4, low.astype(F32), message)
        put_pair(gc_buf, 2 * m, message.astype(BF16))

    def forward(m, parts):
        high = len(parts) * PIECE
        for h in parts:
            c = 2 * m + h

            @pl.when(is_first)
            def _():
                input_copy(c).wait()
                x_buf[c] = jnp.transpose(inp_buf[lax.rem(c, slots)])
                if ring:

                    @pl.when(c + slots < pieces)
                    def _():
                        input_copy(c + slots).start()

            @pl.when(s > 0)
            def _():
                x_copy(c).wait_recv()

        x = both(x_buf, 2 * m, parts)
        if parts == (0,):
            prev = dot(shift_buf[0:PIECE, 0:PIECE], x)
        elif parts == (1,):
            prev = dot(shift_buf[PIECE : 2 * PIECE, :], both(x_buf, 2 * m, (0, 1)))
        else:
            prev = dot(shift_buf[...], x)
        gate = (
            dot(x, wd_t[res : 2 * res])
            + dot(both(cond_t, 2 * m, parts), wc_ref[...])
            + dot(prev.astype(BF16), wd_t[0:res])
        )
        th = jnp.tanh(gate[:, 0:half])
        sg = sigmoid(gate[:, half : 2 * half])
        gate_buf[0:high, 0:half] = th
        gate_buf[0:high, half : 2 * half] = sg
        put(hid_buf, 2 * m, parts, (th * sg).astype(BF16))

    def forward_rest(m, parts):
        high = len(parts) * PIECE
        th = gate_buf[0:high, 0:half]
        sg = gate_buf[0:high, half : 2 * half]
        put(d1_buf, 2 * m, parts, (sg * (1.0 - th * th)).astype(BF16))
        put(d2_buf, 2 * m, parts, (th * sg * (1.0 - sg)).astype(BF16))

    def forward_piece(m, h):
        c = 2 * m + h
        forward(m, (h,))
        reuse(x_copy, c)
        out = (x_buf[c].astype(F32) + dot(hid_buf[c], wr_t[...])) * HALF_ROOT
        x_out[lax.rem(c, slots)] = out.astype(BF16)
        x_copy(c).start()
        gh_buf[...] = dot(hid_buf[c], ws_t[...])
        forward_rest(m, (h,))

        @pl.when(s > 0)
        def _():
            k_copy(c).wait_recv()
            gh_buf[...] += sg_buf[c].astype(F32)

        reuse(k_copy, c)
        k_out[lax.rem(c, slots)] = gh_buf[...].astype(BF16)
        k_copy(c).start()

    def forward_head(m):
        forward(m, (0, 1))
        total = dot(both(hid_buf, 2 * m, (0, 1)), ws_t[...])
        for h in (0, 1):
            k_copy(2 * m + h).wait_recv()
        head(m, total + both(sg_buf, 2 * m, (0, 1)).astype(F32))
        forward_rest(m, (0, 1))

    def grad_field(m, parts, grad_hidden):
        kept = 2 * lax.rem(m, keep)
        grad_gate = jnp.concatenate(
            [
                grad_hidden * both(d1_buf, 2 * m, parts).astype(F32),
                grad_hidden * both(d2_buf, 2 * m, parts).astype(F32),
            ],
            axis=1,
        ).astype(BF16)
        put(gg_buf, kept, parts, grad_gate)
        if parts == (1,):
            back = dot(shift_back[PIECE:, PIECE:], grad_gate)
        elif parts == (0,):
            back = dot(shift_back[0:PIECE, :], jnp.concatenate([grad_gate, gg_buf[kept + 1]], axis=0))
        else:
            back = dot(shift_back[...], grad_gate)
        return dot(grad_gate, wd_ref[:, res : 2 * res]) + dot(back.astype(BF16), wd_ref[:, 0:res])

    def cond_message(m, h):
        kept = 2 * lax.rem(m, keep)
        row = lax.broadcasted_iota(jnp.int32, (EXT, PIECE), 0)
        own = jnp.where(row < mel_rows, dot_nt(wc_ref[...], gg_buf[kept + h]), 0.0)
        return own + gc_buf[2 * m + h].astype(F32)

    def backward_piece(m, h):
        c = 2 * m + h
        gs_copy(c).wait_recv()

        @pl.when(lax.rem(s, 2) == 1)
        def _():
            gs_copy(c).start()

        if feeder < sections - 1:

            @pl.when(s == feeder)
            def _():
                gs_first(c).start()

        gh_buf[...] = dot(sg_buf[c], ws_ref[...])
        gx_copy(c).wait_recv()
        grad_hidden = gh_buf[...] + HALF_ROOT * dot(gx_buf[c], wr_ref[...])
        grad_x = (HALF_ROOT * gx_buf[c].astype(F32) + grad_field(m, (h,), grad_hidden)).astype(BF16)

        @pl.when(s > 0)
        def _():
            reuse(gx_copy, c)
            gx_out[lax.rem(c, slots)] = grad_x
            gx_copy(c).start()

        @pl.when(is_first)
        def _():
            inp_buf[lax.rem(c, slots)] = jnp.transpose(grad_x)

        gc_copy(c).wait_recv()
        message = cond_message(m, h)

        @pl.when(s > 0)
        def _():
            reuse(gc_copy, c)
            gc_out[lax.rem(c, slots)] = message.astype(BF16)
            gc_copy(c).start()

        @pl.when(is_first)
        def _():
            gc_buf[c, 0:mel_rows, :] = message[0:mel_rows].astype(BF16)
            tail = message[mel_rows:EXT]
            if h == 0:
                frame = lax.broadcasted_iota(jnp.int32, mel_ref.shape, 0) == m
                extra_buf[0:1, 0:mel_rows] = jnp.sum(
                    jnp.where(frame, mel_ref[...].astype(F32), 0.0), axis=0, keepdims=True
                )
                lane = lax.broadcasted_iota(jnp.int32, (1, PIECE), 1)
                ids = jnp.where(lane == 0, spk_ref[0, m], 0)
                ids = jnp.where(lane == 1, spk_ref[1, m], ids)
                ids = jnp.where(lane == 2, offs_ref[0, m], ids)
                extra_buf[1:2, :] = ids.astype(F32)
                tail = tail + extra_buf[...]
            gc_buf[c, mel_rows:EXT, :] = tail.astype(BF16)

    def backward_pair(m):
        grad_hidden = dot(both(sg_buf, 2 * m, (0, 1)), ws_ref[...])
        grad_x = grad_field(m, (0, 1), grad_hidden).astype(BF16)
        for h in (1, 0):
            c = 2 * m + h
            reuse(gx_copy, c)
            gx_out[lax.rem(c, slots)] = grad_x[h * PIECE : (h + 1) * PIECE]
            gx_copy(c).start()
        for h in (1, 0):
            c = 2 * m + h
            reuse(gc_copy, c)
            gc_out[lax.rem(c, slots)] = cond_message(m, h).astype(BF16)
            gc_copy(c).start()

    def add_halves(first_row, value):
        rows = value.shape[0] // 2
        acc[first_row : first_row + rows, 0:half] += value[0:rows]
        acc[first_row : first_row + rows, half : 2 * half] += value[rows : 2 * rows]

    small_row = 2 * half + EXT

    def small_gradients(m):
        parts = (0, 1)
        hidden = both(hid_buf, 2 * m, parts)

        @pl.when(s < sections - 1)
        def _():
            add_halves(small_row, HALF_ROOT * dot_tn(both(gx_buf, 2 * m, parts), hidden))

        add_halves(small_row + half // 2, dot_tn(both(sg_buf, 2 * m, parts), hidden))

        @pl.when(is_last)
        def _():
            kept = 2 * lax.rem(m, keep)
            add_halves(main_rows, dot_nt(pair(gp_buf, kept), pair(a1_buf, kept)))
            add_halves(main_rows + half // 2, dot_nt(pair(gl_buf, kept), pair(a2_buf, kept)))

    def large_gradients(m):
        parts = (0, 1)
        grad_gate = both(gg_buf, 2 * lax.rem(m, keep), parts)
        x = both(x_buf, 2 * m, parts)
        prev = dot(shift_buf[...], x).astype(BF16)
        acc[0 : 2 * half, :] += dot_tn(grad_gate, jnp.concatenate([prev, x], axis=1))
        acc[2 * half : small_row, :] += dot(pair(cond_ref, 2 * m), grad_gate)

    def samples(ref):
        return ref[...].reshape(pieces * PIECE, ref.shape[2])

    def by_channel(ref):
        return jnp.concatenate([ref[c] for c in range(pieces)], axis=1)

    def set_halves(first_row, value):
        rows = value.shape[0] // 2
        acc[first_row : first_row + rows, 0:half] = value[0:rows]
        acc[first_row : first_row + rows, half : 2 * half] = value[rows : 2 * rows]

    def all_small_gradients():
        @pl.when(is_last)
        def _():
            set_halves(main_rows, dot_nt(by_channel(gp_buf), by_channel(a1_buf)))
            set_halves(main_rows + half // 2, dot_nt(by_channel(gl_buf), by_channel(a2_buf)))

        hidden = samples(hid_buf)
        set_halves(small_row + half // 2, dot_tn(samples(sg_buf), hidden))

        @pl.when(s < sections - 1)
        def _():
            set_halves(small_row, HALF_ROOT * dot_tn(samples(gx_buf), hidden))

    def all_large_gradients():
        @pl.loop(0, micro)
        def _(m):
            build_shift(m)
            put(d1_buf, 2 * m, (0, 1), dot(shift_buf[...], both(x_buf, 2 * m, (0, 1))).astype(BF16))

        grad_gate = samples(gg_buf)
        acc[0 : 2 * half, 0:res] = dot_tn(grad_gate, samples(d1_buf))
        acc[0 : 2 * half, res : 2 * res] = dot_tn(grad_gate, samples(x_buf))
        acc[2 * half : small_row, :] = dot(by_channel(cond_ref), grad_gate)

    def gin_rows(other, group):
        return remote(
            inp_buf.at[:, pl.ds(pl.multiple_of(other * share, share), share), :],
            gin_buf.at[pl.ds(pl.multiple_of(group * slots, slots), slots)],
            gin_ss.at[0],
            gin_rs.at[0],
            other,
            z,
        )

    def gin_sent():
        return remote(
            inp_buf.at[:, share:res, :], inp_buf.at[:, share:res, :], gin_ss.at[0], gin_rs.at[0], 1, z
        )

    def gin_arrived():
        return remote(gin_buf, gin_buf, gin_ss.at[0], gin_rs.at[0], 1, z)

    def hand_out(group):
        @pl.loop(1, sections)
        def _(other):
            gin_rows(other, group).start()

        gin_buf[pl.ds(pl.multiple_of(group * slots, slots), slots)] = inp_buf[:, 0:share, :]

    def own_local():
        return pltpu.make_async_copy(gc_buf, o_g.at[z], loc_sem.at[0])

    def own_hub():
        return remote(gc_buf, o_g.at[z], gown_ss.at[0], g_rs.at[z], hub, z)

    def part_along(j, step):
        sem = gpeer_ss.at[j if step > 0 else groups + j]
        return remote(o_g.at[j], o_g.at[j], sem, g_rs.at[j], s, z + step)

    def part_chip(j, chip):
        return remote(o_g.at[j], o_g.at[j], ghub_ss.at[j, chip], g_rs.at[j], 2 * chip, z)

    def part_next(j):
        return remote(o_g.at[j], o_g.at[j], gnext_ss.at[j], g_rs.at[j], s + 1, z)

    def spread(j):
        part_next(j).start()

        @pl.loop(0, sections // 2 - 1)
        def _(chip):
            @pl.when((chip > 0) | (z != j))
            def _():
                part_chip(j, chip).start()

    @pl.when(is_last)
    def _():
        @pl.loop(0, micro)
        def _(m):
            build_shift(m)
            forward_head(m)
            backward_pair(m)
            if keep < micro:
                small_gradients(m)
                large_gradients(m)

    roomy = keep == micro
    swings = (s == sections - 2) if roomy else False
    late = (s >= sections - 2) if roomy else is_last

    @pl.loop(0, 3 * micro)
    def _(step):
        after = step - micro
        odd = lax.rem(step, 2) == 1
        forth = step < micro
        back = jnp.where(late, (after >= 0) & (after < micro), (after >= 0) & (lax.rem(after, 2) == 0))
        m = jnp.where(forth, step, jnp.where(late, lax.rem(step, micro), after // 2))
        if roomy:
            turning = swings & (step < 2 * micro)
            end = step == 2 * micro - 1
            swing_forth = (step == 0) | (odd & jnp.logical_not(end))
            forth = jnp.where(turning, swing_forth, forth)
            back = jnp.where(turning, jnp.logical_not(swing_forth), back)
            swing_m = jnp.where(swing_forth, (step + 1) // 2, jnp.where(end, micro - 1, step // 2 - 1))
            m = jnp.where(turning, swing_m, m)
        build_shift(m)

        @pl.when(forth & is_first & (m > 0))
        def _():
            condition(m)

        @pl.when(forth & jnp.logical_not(is_last))
        def _():
            forward_piece(m, 0)
            forward_piece(m, 1)

        @pl.when(is_first & (step == micro))
        def _():
            acc[...] = jnp.zeros_like(acc)
            extra_buf[...] = jnp.zeros_like(extra_buf)

        @pl.when(back & jnp.logical_not(is_last))
        def _():
            if ring:

                @pl.when(is_first & (m > 0))
                def _():
                    gin_sent().wait_send()

            backward_piece(m, 1)
            backward_piece(m, 0)

            @pl.when(is_first & (lax.rem(2 * m + 2, slots) == 0))
            def _():
                hand_out((2 * m + 2) // slots - 1)

            @pl.when(is_first & (m == micro - 1))
            def _():
                own_hub().start()
                own_local().start()

        @pl.when(jnp.logical_not(forth | back | late))
        def _():
            small_gradients(m)

            @pl.when(m < micro - 1)
            def _():
                large_gradients(m)

    if roomy:

        @pl.when(late)
        def _():
            all_small_gradients()

    @pl.when(is_first)
    def _():
        own_local().wait()

    left = z < groups // 2
    inward = jnp.where(left, z + 1, z - 1)
    outward = jnp.where(left, z - 1, z + 1)
    is_edge = (z == 0) | (z == groups - 1)
    is_mid = (z == groups // 2 - 1) | (z == groups // 2)
    distance = jnp.where(left, groups // 2 - 1 - z, z - groups // 2)
    lag = LAG * (2 * distance + 1) + 4 * distance
    base = jnp.where(is_last, main_blocks + head_blocks, main_blocks)
    helped = 2 * len(exports)
    gives = (s < helped) if exports else False
    takes = ((s >= helper) & (s < helper + helped)) if exports else False
    moved = 0
    for chip, amount in enumerate(exports):
        moved = jnp.where(lax.rem(s, helper) // 2 == chip, amount, moved)
    count = base - jnp.where(gives, moved, 0) + jnp.where(takes, moved, 0)

    all_blocks = main_blocks + head_blocks
    taken_at = base - 12

    def block_of(i):
        j = jnp.where(takes & (i >= taken_at + moved), i - moved, i)
        heads = jnp.where(is_last, head_blocks, 0)
        own = jnp.where(j < heads, j + main_blocks, lax.rem(j - heads + small_row // BLOCK, main_blocks))
        return jnp.where(takes & (j == i) & (i >= taken_at), i - taken_at + all_blocks, own)

    def rows_of(b):
        return pl.ds(pl.multiple_of(b * BLOCK, BLOCK), BLOCK)

    cycle = zp_rs.shape[0]

    def swap_copy(i):
        rows = rows_of(block_of(i))
        return remote(part_out.at[rows], o_acc.at[rows], zi_ss.at[0], zt_rs.at[lax.rem(i, cycle)], s, inward)

    def part_copy(i):
        rows = rows_of(block_of(i))
        return remote(part_out.at[rows], part_in.at[rows], zi_ss.at[0], zp_rs.at[lax.rem(i, cycle)], s, inward)

    def total_copy(i):
        rows = rows_of(block_of(i))
        return remote(o_acc.at[rows], o_acc.at[rows], zo_ss.at[0], zt_rs.at[lax.rem(i, cycle)], s, outward)

    def head_copy(j):
        rows = rows_of(main_blocks + j)
        return remote(o_acc.at[rows], o_acc.at[rows], hd_ss.at[0], hd_rs.at[j], s - 1, z)

    def send_part(i):
        rows = rows_of(block_of(i))

        @pl.when(is_edge)
        def _():
            part_out[rows, :] = acc[rows, :].astype(BF16)

        @pl.when(jnp.logical_not(is_edge))
        def _():
            part_copy(i).wait_recv()
            part_out[rows, :] = (acc[rows, :] + part_in[rows, :].astype(F32)).astype(BF16)

        @pl.when(is_mid)
        def _():
            swap_copy(i).start()

        @pl.when(jnp.logical_not(is_mid))
        def _():
            part_copy(i).start()

    def keep_rows(rows):
        return pltpu.make_async_copy(o_acc.at[rows], o_sum.at[rows], out_sem.at[0])

    def finish_part(i):
        rows = rows_of(block_of(i))
        swap_copy(i).wait_recv()

        @pl.when(is_mid)
        def _():
            o_acc[rows, :] = (part_out[rows, :].astype(F32) + o_acc[rows, :].astype(F32)).astype(BF16)

        @pl.when(jnp.logical_not(is_edge))
        def _():
            total_copy(i).start()

        @pl.when(block_of(i) < all_blocks)
        def _():
            keep_rows(rows).start()

    def given_rows(amount):
        return pl.ds(small_row - amount * BLOCK, amount * BLOCK)

    def taken_rows(amount):
        return pl.ds(main_rows + head_rows, amount * BLOCK)

    def give_copy(amount):
        target = taken_buf.at[0 : amount * BLOCK]
        return remote(part_out.at[given_rows(amount)], target, give_ss.at[0], give_rs.at[0], s + helper, z)

    def return_copy(amount):
        source, target = o_acc.at[taken_rows(amount)], o_acc.at[given_rows(amount)]
        return remote(source, target, give_ss.at[1], give_rs.at[1], s - helper, z)

    def each_export(cond, act):
        for chip, amount in enumerate(exports):

            @pl.when(cond & (lax.rem(s, helper) // 2 == chip))
            def _():
                act(amount)

    def give(amount):
        part_out[given_rows(amount), :] = acc[given_rows(amount), :].astype(BF16)
        give_copy(amount).start()

    def take(amount):
        give_copy(amount).wait_recv()
        acc[taken_rows(amount), :] = taken_buf[0 : amount * BLOCK].astype(F32)

    def rest_of_gradients():
        @pl.when(jnp.logical_not(late))
        def _():
            build_shift(micro - 1)
            large_gradients(micro - 1)

        if roomy:

            @pl.when(late)
            def _():
                all_large_gradients()

        each_export(gives, give)

    last_step = main_blocks - max(exports, default=0) + lag - 1
    head_at = lag + 2
    own_at = jnp.minimum(22 + 9 * distance, last_step)
    rest_at = 50
    rest_at = jnp.minimum(rest_at + 9 * distance, last_step)

    @pl.loop(0, count + lag)
    def _(i):
        @pl.when(i == LARGE_AT)
        def _():
            rest_of_gradients()

        if exports:

            each_export(takes & (i == taken_at), take)

        @pl.when(i < count)
        def _():
            send_part(i)

        @pl.when(i >= lag)
        def _():
            finish_part(i - lag)
            b = block_of(i - lag)

            @pl.when((b >= main_blocks) & (b < all_blocks))
            def _():
                head_copy(b - main_blocks).start()

            if exports:

                each_export(b == all_blocks + moved - 1, lambda amount: return_copy(amount).start())

        @pl.when(jnp.logical_not(is_last) & (i >= head_at) & (i < head_at + head_blocks))
        def _():
            j = i - head_at
            head_copy(j).wait_recv()
            keep_rows(rows_of(main_blocks + j)).start()

            @pl.when(s > 0)
            def _():
                head_copy(j).start()

        for hop in range(groups):

            @pl.when(is_hub & (i == jnp.minimum(own_at + 8 * hop, last_step)))
            def _():
                def pass_on(j, step, known, far):
                    @pl.when(known)
                    def _():
                        if hop:
                            part_along(j, 1).wait_recv()
                            spread(j)

                        @pl.when(far)
                        def _():
                            part_along(j, step).start()

                if hop == 0:
                    own_hub().wait_recv()
                    spread(z)
                pass_on(z - hop, 1, z >= hop, z < groups - 1)
                pass_on(z + hop, -1, z + hop < groups, z > 0)

        @pl.when((lax.rem(s, 2) == 0) & jnp.logical_not(is_hub) & (i == rest_at))
        def _():
            for j in range(groups):

                @pl.when((z != j) | (s > 0))
                def _():
                    part_next(j).wait_recv()

                part_next(j).start()

    @pl.when(s > 0)
    def _():
        gin_arrived().wait_recv()

    for c in range(pieces):
        o_gin[:, c * PIECE : (c + 1) * PIECE] = gin_buf[c]

    @pl.when(is_first)
    def _():
        own_hub().wait_send()
        gin_sent().wait_send()

    @pl.when(is_hub)
    def _():
        for j in range(groups):

            @pl.when((j <= z) & (z < groups - 1))
            def _():
                part_along(j, 1).wait_send()

            @pl.when((j >= z) & (z > 0))
            def _():
                part_along(j, -1).wait_send()

            @pl.loop(0, sections // 2 - 1)
            def _(chip):
                @pl.when((chip > 0) | (z != j))
                def _():
                    part_chip(j, chip).wait_send()

    for j in range(groups):

        @pl.when(lax.rem(s, 2) == 0)
        def _():
            part_next(j).wait_send()

        @pl.when(lax.rem(s, 2) == 1)
        def _():
            part_next(j).wait_recv()

    if exports:

        def returned(amount):
            return_copy(amount).wait_recv()
            keep_rows(given_rows(amount)).start()
            give_copy(amount).wait_send()

        each_export(gives, returned)
        each_export(takes, lambda amount: return_copy(amount).wait_send())

    keep_rows(pl.ds(0, main_rows + head_rows)).wait()

    def sum_sent(rows):
        remote(part_out.at[rows], part_out.at[rows], zi_ss.at[0], zp_rs.at[0], s, inward).wait_send()

        @pl.when(jnp.logical_not(is_edge))
        def _():
            remote(o_acc.at[rows], o_acc.at[rows], zo_ss.at[0], zt_rs.at[0], s, outward).wait_send()

    if exports:
        each_export(gives, lambda amount: sum_sent(pl.ds(0, main_rows - amount * BLOCK)))
        each_export(takes & jnp.logical_not(is_last), lambda amount: sum_sent(pl.ds(0, main_rows + amount * BLOCK)))

    @pl.when(is_last)
    def _():
        last_takes = exports[-1] if helper + helped == sections and exports else 0
        sum_sent(pl.ds(0, main_rows + head_rows + last_takes * BLOCK))

    @pl.when(jnp.logical_not(is_last | gives | takes))
    def _():
        sum_sent(pl.ds(0, main_rows))

    @pl.when(jnp.logical_not(is_last))
    def _():
        drain(x_copy, lambda: remote(x_out, x_out, x_ss.at[0], x_rs.at[0], s + 1, z))
        drain(k_copy, lambda: remote(k_out, k_out, k_ss.at[0], k_rs.at[0], s + 1, z))

    @pl.when(s > 0)
    def _():
        rows = pl.ds(main_rows, head_rows)
        remote(o_acc.at[rows], o_acc.at[rows], hd_ss.at[0], hd_rs.at[0], s - 1, z).wait_send()
        drain(gx_copy, lambda: remote(gx_out, gx_out, gx_ss.at[0], gx_rs.at[0], s - 1, z))
        drain(gc_copy, lambda: remote(gc_out, gc_out, gc_ss.at[0], gc_rs.at[0], s - 1, z))

    @pl.when(lax.rem(s, 2) == 1)
    def _():
        gs_whole(0).wait_send()

    @pl.when(is_last)
    def _():
        for chip in far_chips:
            gs_whole(1 + chip).wait_send()

    @pl.when(s == feeder)
    def _():
        gs_whole(1).wait_send()


def run_step(dims, tables, arrays, weights):
    sections, groups, micro, res, half, classes, slots, keep, mel_rows = dims
    pieces = 2 * micro
    rows = 2 * half + EXT + half + half // 2 + classes // 2
    head_blocks = (half // 2 + classes // 2) // BLOCK
    share = res // sections
    smem = pl.BlockSpec(memory_space=pltpu.SMEM)
    vmem = pl.BlockSpec(memory_space=pltpu.VMEM)
    anywhere = pl.BlockSpec(memory_space=pl.ANY)
    dma = pltpu.SemaphoreType.DMA

    def tile(*shape, dtype=BF16):
        return pltpu.VMEM(shape, dtype)

    distance = groups // 2 - 1
    cycle = max(LAG * (2 * distance + 1) + 4 * distance + 4, 2 * LAG + 4)
    sends = slots if pieces > slots else 1
    taken = max(exported_blocks(dims), default=0) * BLOCK

    scratch = [
        tile(pieces, PIECE, res),
        tile(pieces, PIECE, half),
        tile(pieces, PIECE, res),
        tile(pieces, EXT, PIECE),
        tile(pieces, PIECE, half),
        tile(pieces, PIECE, half),
        tile(pieces, PIECE, half),
        tile(slots, PIECE, res),
        tile(slots, PIECE, half),
        tile(slots, PIECE, res),
        tile(slots, EXT, PIECE),
        tile(2 * PIECE, 2 * half, dtype=F32),
        tile(PIECE, half, dtype=F32),
        tile(2 * keep, PIECE, 2 * half),
        tile(slots, res, PIECE),
        tile(2 * PIECE, 2 * PIECE),
        tile(2 * PIECE, 2 * PIECE),
        tile(pieces, EXT, PIECE),
        tile(pieces, PIECE, EXT),
        tile(EXT, 2 * half),
        tile(2 * half, 2 * res),
        tile(res, half),
        tile(half, half),
        tile(half, half),
        tile(classes, half),
        tile(2 * res, 2 * half),
        tile(half, res),
        tile(half, half),
        tile(half, half),
        tile(half, classes),
        tile(2 * keep, classes, PIECE),
        tile(2 * keep, half, PIECE),
        tile(2 * keep, half, PIECE),
        tile(2 * keep, half, PIECE),
        tile(rows + taken, WIDE, dtype=F32),
        tile(rows + taken, WIDE),
        tile(rows + taken, WIDE),
        tile(rows + taken, WIDE),
        tile(max(taken, 16), WIDE),
        tile(pieces, share, PIECE),
        tile(2, micro * mel_rows, PIECE, dtype=F32),
        tile(EXT - mel_rows, PIECE, dtype=F32),
        dma((slots,)),
        dma((10,)),
        dma((1,)),
        dma((1,)),
        dma((sends,)),
        dma((pieces,)),
        dma((sends,)),
        dma((pieces,)),
        dma((max(2, sections // 2),)),
        dma((pieces,)),
        dma((sends,)),
        dma((pieces,)),
        dma((sends,)),
        dma((pieces,)),
        dma((1,)),
        dma((1,)),
        dma((cycle,)),
        dma((cycle,)),
        dma((1,)),
        dma((head_blocks,)),
        dma((groups,)),
        dma((1,)),
        dma((2 * groups,)),
        dma((groups, sections // 2)),
        dma((groups,)),
        dma((1,)),
        dma((1,)),
        dma((2,)),
        dma((2,)),
    ]
    return pl.pallas_call(
        functools.partial(step_kernel, dims),
        out_shape=(
            jax.ShapeDtypeStruct((rows, WIDE), BF16),
            jax.ShapeDtypeStruct((groups, pieces, EXT, PIECE), BF16),
            jax.ShapeDtypeStruct((share, pieces * PIECE), BF16),
        ),
        in_specs=[smem] * 4 + [vmem] * 4 + [anywhere] * 8,
        out_specs=(anywhere, anywhere, vmem),
        scratch_shapes=scratch,
        compiler_params=pltpu.CompilerParams(
            collective_id=0, has_side_effects=True, vmem_limit_bytes=63 * 2**20
        ),
        cost_estimate=pl.CostEstimate(flops=10**10, bytes_accessed=3 * 10**7, transcendentals=10**6),
        name="train_step",
    )(*tables, *arrays, *weights)


def finish_kernel(
    dims,
    sums,
    gin,
    shared_hbm,
    o_gin,
    o_dil,
    o_cond,
    o_res,
    o_skip,
    o_post,
    o_out,
    o_up,
    o_bias,
    o_table,
    o_loss,
    sums_buf,
    shared,
    dil_buf,
    cond_buf,
    res_buf,
    skip_buf,
    post_buf,
    out_buf,
    up_buf,
    field,
    mel_rows_buf,
    mel_columns,
    table,
    load_sem,
    store_sem,
):
    mel_rows, half = dims
    frames = shared.shape[0]
    first = 2 * half
    total_rows = sums_buf.shape[0]
    strips = ((0, half), (half, half), (first, total_rows - first))
    loads = [
        pltpu.make_async_copy(sums.at[pl.ds(row, rows), :], sums_buf.at[pl.ds(row, rows), :], load_sem.at[k])
        for k, (row, rows) in enumerate(strips)
    ]
    loads.append(pltpu.make_async_copy(shared_hbm, shared, load_sem.at[3]))
    for load in loads:
        load.start()
    stores = []

    def store(source, target):
        copy = pltpu.make_async_copy(source, target, store_sem.at[len(stores)])
        copy.start()
        stores.append(copy)

    store(gin, o_gin)

    for k in range(2):
        loads[k].wait()
        rows = pl.ds(k * half, half)
        dil_buf[rows, :] = sums_buf[rows, :].astype(F32)
        store(dil_buf.at[rows, :], o_dil.at[0, rows, :])
    loads[2].wait()
    cond_buf[...] = sums_buf[first : first + mel_rows, :].astype(F32)
    o_bias[...] = sums_buf[first + mel_rows : first + EXT, :].astype(F32)[0:1]
    store(cond_buf, o_cond)
    row = first + EXT
    for buffer, target in ((res_buf, o_res), (skip_buf, o_skip), (post_buf, o_post), (out_buf, o_out)):
        rows = buffer.shape[1]
        buffer[0] = sums_buf[row : row + rows, 0:half].astype(F32)
        buffer[1] = sums_buf[row : row + rows, half : 2 * half].astype(F32)
        store(buffer, target)
        row += rows

    loads[3].wait()

    def by_channel(f, loss):
        extra = shared[f, 0, mel_rows:EXT, :].astype(F32)
        mel_rows_buf[pl.ds(f, 1), :] = extra[0:1]
        for h in range(2):
            rows = pl.ds(pl.multiple_of(f * mel_rows, 16), mel_rows)
            field[h, rows, :] = shared[f, h, 0:mel_rows, :].astype(F32)
        return loss + extra + shared[f, 1, mel_rows:EXT, :].astype(F32)

    loss = lax.fori_loop(0, frames, by_channel, jnp.zeros((EXT - mel_rows, PIECE), F32))
    row = lax.broadcasted_iota(jnp.int32, loss.shape, 0)
    loss = jnp.where((row >= 2) & (row < 5), loss, 0.0)
    o_loss[...] = jnp.sum(jnp.sum(loss, axis=1, keepdims=True), axis=0, keepdims=True)
    mel_columns[...] = jnp.transpose(mel_rows_buf[...])[0:mel_rows].astype(BF16)

    parts = 4
    channels = mel_rows // parts

    def upsampling(part):
        @pl.loop(0, channels // 10)
        def _(group):
            for j in range(10):
                c = part * channels + group * 10 + j
                rows = pl.ds(c, frames, stride=mel_rows)
                matrix = jnp.concatenate([field[0, rows, :], field[1, rows, :]], axis=1)
                up_buf[c] = dot(mel_columns[...], matrix.astype(BF16))

        rows = pl.ds(part * channels, channels)
        store(up_buf.at[rows], o_up.at[rows])

    for part in range(parts - 2):
        upsampling(part)

    table[...] = jnp.zeros_like(table)
    time = lax.broadcasted_iota(jnp.int32, (2 * PIECE, PIECE), 0).astype(F32)
    number = lax.broadcasted_iota(jnp.int32, (2 * PIECE, PIECE), 1).astype(F32)

    @pl.loop(0, frames // 4)
    def _(group):
        grads, hots = [], []
        for k in range(4):
            f = group * 4 + k
            ids = shared[f, 0, mel_rows:EXT, :].astype(F32)[1:2]
            speaker = jnp.where(time >= ids[:, 2:3], ids[:, 1:2], ids[:, 0:1])
            hots.append(jnp.where(number == speaker, 1.0, 0.0).astype(BF16))
            grads += [shared[f, 0, 0:mel_rows, :], shared[f, 1, 0:mel_rows, :]]
        table[...] += dot(jnp.concatenate(grads, axis=1), jnp.concatenate(hots, axis=0))

    o_table[...] = table[:, 0 : o_table.shape[1]]
    for part in range(parts - 2, parts):
        upsampling(part)

    for copy in stores:
        copy.wait()


def finish(sums, shared, grad_inputs, half, classes, mel_rows, speakers):
    frames = shared.shape[0]
    first = 2 * half
    vmem = pl.BlockSpec(memory_space=pltpu.VMEM)
    anywhere = pl.BlockSpec(memory_space=pl.ANY)
    large = (
        (first, WIDE),
        (mel_rows, WIDE),
        (2, half // 2, half),
        (2, half // 2, half),
        (2, half // 2, half),
        (2, classes // 2, half),
        (mel_rows, mel_rows, 2 * PIECE),
    )

    def f32(*shape):
        return jax.ShapeDtypeStruct(shape, F32)

    return pl.pallas_call(
        functools.partial(finish_kernel, (mel_rows, half)),
        out_shape=(
            jax.ShapeDtypeStruct(grad_inputs.shape, grad_inputs.dtype),
            f32(1, *large[0]),
            *[f32(*shape) for shape in large[1:]],
            f32(1, WIDE),
            f32(mel_rows, speakers),
            f32(1, 1),
        ),
        in_specs=[anywhere] * 3,
        out_specs=(anywhere,) * 8 + (vmem,) * 3,
        scratch_shapes=[
            pltpu.VMEM(sums.shape, BF16),
            pltpu.VMEM(shared.shape, BF16),
            *[pltpu.VMEM(shape, F32) for shape in large],
            pltpu.VMEM((2, frames * mel_rows, PIECE), F32),
            pltpu.VMEM((frames, PIECE), F32),
            pltpu.VMEM((mel_rows, frames), BF16),
            pltpu.VMEM((mel_rows, PIECE), F32),
            pltpu.SemaphoreType.DMA((4,)),
            pltpu.SemaphoreType.DMA((12,)),
        ],
        compiler_params=pltpu.CompilerParams(vmem_limit_bytes=62 * 2**20),
        name="finish",
    )(sums, grad_inputs, shared)


def local(
    inputs,
    targets,
    mel,
    speakers,
    speaker_sample_counts,
    segment_offsets,
    dilations,
    dilated_kernel,
    conditioning_projection,
    dilated_gate_bias,
    residual_projection,
    skip_projection,
    upsample_weight,
    speaker_table,
    first_output_projection,
    class_projection,
):
    sections = lax.axis_size("section")
    groups = lax.axis_size("dp")
    micro = segment_offsets.shape[0]
    res, tokens = inputs.shape
    length = tokens // micro
    mel_rows = mel.shape[0]
    hop = upsample_weight.shape[0]
    half = residual_projection.shape[2]
    classes = class_projection.shape[0]
    pieces = 2 * micro
    assert length == 2 * PIECE and hop == length and mel_rows + 16 == EXT and 2 * half == WIDE

    slots, keep = (pieces, micro) if pieces <= 8 else (2, 1)
    dims = (sections, groups, micro, res, half, classes, slots, keep, mel_rows)
    sums, shared, grad_inputs = run_step(
        dims,
        (dilations, segment_offsets.T, speakers.T, speaker_sample_counts),
        (
            targets.reshape(micro, 1, length),
            mel.T,
            speaker_table,
            dilated_gate_bias,
        ),
        (
            inputs,
            upsample_weight.transpose(1, 2, 0).reshape(mel_rows * mel_rows, hop),
            conditioning_projection[0].T,
            dilated_kernel[0],
            residual_projection[0],
            skip_projection[0],
            first_output_projection,
            class_projection,
        ),
    )
    shared = shared.reshape(groups * micro, 2, EXT, PIECE)
    grad_inputs, dil, cond, grad_res, grad_skip, post, out, up, bias, table, loss = finish(
        sums, shared, grad_inputs, half, classes, mel_rows, speaker_table.shape[1]
    )
    return (
        loss.reshape(()),
        grad_inputs,
        dil,
        cond.T[None],
        bias,
        grad_res.reshape(1, half, half),
        grad_skip.reshape(1, half, half),
        up.transpose(2, 0, 1),
        table,
        post.reshape(half, half),
        out.reshape(classes, half),
    )


def solution(mesh):
    return jax.shard_map(
        local,
        mesh=mesh,
        in_specs=(
            P(None, "dp"),
            P("dp"),
            P(None, "dp"),
            P("dp", None),
            P(),
            P("dp", None),
            P("section"),
            P("section", None, None),
            P("section", None, None),
            P("section", None),
            P("section", None, None),
            P("section", None, None),
            P(),
            P(),
            P(),
            P(),
        ),
        out_specs=(
            P(),
            P("section", "dp"),
            P("section", None, None),
            P("section", None, None),
            P("section", None),
            P("section", None, None),
            P("section", None, None),
            P(),
            P(),
            P(),
            P(),
        ),
        check_vma=False,
    )
```

```python
import functools
import math

import jax
import jax.numpy as jnp
from jax import lax
from jax.experimental import pallas as pl
from jax.experimental.pallas import tpu as pltpu
from jax.sharding import PartitionSpec as P

HALF_ROOT = 0.7071067811865476
WEIGHT_SCALE = 64.0
MESH = pl.DeviceIdType.MESH
BF16 = jnp.bfloat16
F32 = jnp.float32

PIECE = 128
EXT = 96
WIDE = 1024
BLOCK = 16
EXPORTS = (12,)
HEAD_GROUP = 4
LARGE_AT = 6
LAG = 8


def dot(left, right):
    return jnp.dot(left, right, preferred_element_type=F32)


def dot_nt(left, right):
    return lax.dot_general(left, right, (((1,), (1,)), ((), ())), preferred_element_type=F32)


def dot_tn(left, right):
    return lax.dot_general(left, right, (((0,), (0,)), ((), ())), preferred_element_type=F32)


def sigmoid(values):
    return 0.5 * jnp.tanh(0.5 * values) + 0.5


def exported_blocks(dims):
    sections, groups, micro, keep = dims[0], dims[1], dims[2], dims[7]
    helped = sections // 4
    return EXPORTS[:helped] if keep == micro and sections <= 8 else ()


def step_kernel(
    dims,
    dil_ref,
    offs_ref,
    spk_ref,
    cnt_ref,
    tgt_ref,
    mel_ref,
    tab_ref,
    bias_in,
    inp_hbm,
    up_hbm,
    wc_hbm,
    wd_hbm,
    wr_hbm,
    ws_hbm,
    wp_hbm,
    wk_hbm,
    o_sum,
    o_g,
    o_gin,
    x_buf,
    sg_buf,
    gx_buf,
    gc_buf,
    hid_buf,
    d1_buf,
    d2_buf,
    x_out,
    k_out,
    gx_out,
    gc_out,
    gate_buf,
    gh_buf,
    gg_buf,
    inp_buf,
    shift_buf,
    shift_back,
    cond_ref,
    cond_t,
    wc_ref,
    wd_ref,
    wr_ref,
    ws_ref,
    wp_ref,
    wk_ref,
    wd_t,
    wr_t,
    ws_t,
    wp_t,
    wk_t,
    gl_buf,
    a2_buf,
    gp_buf,
    a1_buf,
    acc,
    part_out,
    part_in,
    o_acc,
    taken_buf,
    gin_buf,
    up_buf,
    extra_buf,
    inp_sem,
    load_sem,
    out_sem,
    loc_sem,
    x_ss,
    x_rs,
    k_ss,
    k_rs,
    gs_ss,
    gs_rs,
    gx_ss,
    gx_rs,
    gc_ss,
    gc_rs,
    zi_ss,
    zo_ss,
    zp_rs,
    zt_rs,
    hd_ss,
    hd_rs,
    g_rs,
    gown_ss,
    gpeer_ss,
    ghub_ss,
    gnext_ss,
    gin_ss,
    gin_rs,
    give_ss,
    give_rs,
):
    sections, groups, micro, res, half, classes, slots, keep, mel_rows = dims
    pieces = 2 * micro
    s = lax.axis_index("section")
    z = lax.axis_index("dp")
    is_first = s == 0
    is_last = s == sections - 1
    hub = sections - 2
    is_hub = s == hub
    head_scale = 1.0 / math.sqrt(sections)
    main_rows = 2 * half + EXT + half
    head_rows = half // 2 + classes // 2
    main_blocks = main_rows // BLOCK
    head_blocks = head_rows // BLOCK
    share = res // sections
    feeder = sections - 3 if sections > 4 else sections - 1
    exports = exported_blocks(dims)
    helper = sections // 2

    barrier = pltpu.get_barrier_semaphore()

    def greet(cond, dev_s, dev_z):
        @pl.when(cond)
        def _():
            pl.semaphore_signal(barrier, 1, device_id=(dev_s, dev_z), device_id_type=MESH)

    greet(s > 0, s - 1, z)
    greet(s < sections - 1, s + 1, z)
    greet(z > 0, s, z - 1)
    greet(z < groups - 1, s, z + 1)
    greet(s >= 2, 0, z)
    told = (lax.rem(s, 2) == 0) & (s > 0) & (s < hub)
    greet(told, hub, z)

    @pl.when(is_first)
    def _():
        @pl.loop(2, sections)
        def _(other):
            pl.semaphore_signal(barrier, 1, device_id=(other, z), device_id_type=MESH)

    @pl.when(is_hub)
    def _():
        @pl.loop(1, sections // 2 - 1)
        def _(chip):
            pl.semaphore_signal(barrier, 1, device_id=(2 * chip, z), device_id_type=MESH)

    far = (lax.rem(s, 2) == 1) & (s > 1) & (s < sections - 1)
    greet(far, sections - 1, z)

    @pl.when(is_last)
    def _():
        @pl.loop(1, sections // 2 - 1)
        def _(chip):
            pl.semaphore_signal(barrier, 1, device_id=(2 * chip + 1, z), device_id_type=MESH)

    greet(s == 1, feeder, z)
    greet(s == feeder, 1, z)

    def flag(cond):
        return jnp.where(cond, 1, 0)

    z_near = flag(z > 0) + flag(z < groups - 1)
    expected = (
        flag(s > 0)
        + flag(s < sections - 1)
        + z_near
        + jnp.where(is_first, sections - 2, flag(s >= 2))
        + flag(told)
        + flag(far)
        + flag(s == 1)
        + flag(s == feeder)
        + jnp.where(is_last, sections // 2 - 2, 0)
        + jnp.where(is_hub, sections // 2 - 2, 0)
    )

    def input_copy(c):
        slot = lax.rem(c, slots)
        return pltpu.make_async_copy(
            inp_hbm.at[:, pl.ds(pl.multiple_of(c * PIECE, PIECE), PIECE)],
            inp_buf.at[slot],
            inp_sem.at[slot],
        )

    quarter = mel_rows // 4
    weight_refs = (
        (wd_hbm, wd_ref),
        (wr_hbm, wr_ref),
        (ws_hbm, ws_ref),
        (wc_hbm, wc_ref.at[0:mel_rows]),
        (wp_hbm, wp_ref),
        (wk_hbm, wk_ref),
    )
    loads = [
        pltpu.make_async_copy(source, target, load_sem.at[4 + position])
        for position, (source, target) in enumerate(weight_refs)
    ]
    frame_loads = [
        pltpu.make_async_copy(
            up_hbm.at[pl.ds(q * quarter * mel_rows, quarter * mel_rows), :],
            part_out.at[pl.ds(0, quarter * mel_rows), pl.ds(q * 2 * PIECE, 2 * PIECE)],
            load_sem.at[q],
        )
        for q in range(4)
    ]
    for load in loads[:4] + frame_loads:
        load.start()

    @pl.when(is_first)
    def _():
        @pl.loop(0, slots)
        def _(c):
            input_copy(c).start()

    @pl.when(is_last)
    def _():
        for load in loads[4:]:
            load.start()

    spare = lax.broadcasted_iota(jnp.int32, (EXT - mel_rows, 2 * half), 0)
    bias = jnp.broadcast_to(bias_in[...].astype(F32), (EXT - mel_rows, 2 * half))
    wc_ref[mel_rows:EXT] = jnp.where(spare == 0, bias, 0.0).astype(BF16)
    loads[0].wait()
    wd_t[...] = jnp.transpose(wd_ref[...])
    for load in loads[1:4]:
        load.wait()
    wr_t[...] = jnp.transpose(wr_ref[...])
    ws_t[...] = jnp.transpose(ws_ref[...])

    for load in frame_loads:
        load.wait()

    @pl.loop(0, quarter // 4)
    def _(group):
        for q in range(4):
            for part in range(4):
                row = group * 4 + part
                lanes = slice(q * 2 * PIECE, (q + 1) * 2 * PIECE)
                matrix = part_out[pl.ds(pl.multiple_of(row * mel_rows, 16), mel_rows), lanes]
                frames = dot(mel_ref[...], matrix)
                rows = pl.ds(q * quarter + row, micro, stride=mel_rows)
                for h in range(2):
                    up_buf[h, rows, :] = frames[:, h * PIECE : (h + 1) * PIECE]

    def condition(m):
        shape = (tab_ref.shape[1], 2 * PIECE)
        time = lax.broadcasted_iota(jnp.int32, shape, 1)
        speaker = jnp.where(time >= offs_ref[0, m], spk_ref[1, m], spk_ref[0, m])
        hot = jnp.where(lax.broadcasted_iota(jnp.int32, shape, 0) == speaker, 1.0, 0.0).astype(BF16)
        columns = dot(tab_ref[...], hot)
        ones = jnp.where(lax.broadcasted_iota(jnp.int32, (EXT - mel_rows, PIECE), 0) == 0, 1.0, 0.0)
        rows = pl.ds(pl.multiple_of(m * mel_rows, 16), mel_rows)
        for h in range(2):
            c = 2 * m + h
            value = up_buf[h, rows, :] + columns[:, h * PIECE : (h + 1) * PIECE]
            cond_ref[c] = jnp.concatenate([value, ones], axis=0).astype(BF16)
            cond_t[c] = jnp.transpose(cond_ref[c])

    @pl.when(is_first)
    def _():
        condition(0)

    @pl.when(s > 0)
    def _():
        @pl.loop(0, micro)
        def _(m):
            condition(m)

    @pl.when(s > 0)
    def _():
        acc[...] = jnp.zeros_like(acc)

    @pl.when(is_last)
    def _():
        for load in loads[4:]:
            load.wait()
        wp_t[...] = jnp.transpose(wp_ref[...])
        wk_t[...] = jnp.transpose(wk_ref[...])
        gx_buf[...] = jnp.zeros_like(gx_buf)

    pl.semaphore_wait(barrier, expected)

    def remote(src, dst, send_sem, recv_sem, dev_s, dev_z):
        return pltpu.make_async_remote_copy(
            src_ref=src,
            dst_ref=dst,
            send_sem=send_sem,
            recv_sem=recv_sem,
            device_id=(dev_s, dev_z),
            device_id_type=MESH,
        )

    ring = pieces > slots

    def send_of(semaphores, slot):
        return semaphores.at[slot if ring else 0]

    def x_copy(c):
        slot = lax.rem(c, slots)
        return remote(x_out.at[slot], x_buf.at[c], send_of(x_ss, slot), x_rs.at[c], s + 1, z)

    def k_copy(c):
        slot = lax.rem(c, slots)
        return remote(k_out.at[slot], sg_buf.at[c], send_of(k_ss, slot), k_rs.at[c], s + 1, z)

    def gx_copy(c):
        slot = lax.rem(c, slots)
        return remote(gx_out.at[slot], gx_buf.at[c], send_of(gx_ss, slot), gx_rs.at[c], s - 1, z)

    def gc_copy(c):
        slot = lax.rem(c, slots)
        return remote(gc_out.at[slot], gc_buf.at[c], send_of(gc_ss, slot), gc_rs.at[c], s - 1, z)

    def reuse(copy, c):
        if ring:

            @pl.when(c >= slots)
            def _():
                copy(c).wait_send()

    def drain(copy, whole):
        if ring:

            @pl.loop(0, slots)
            def _(c):
                copy(c).wait_send()

        else:
            whole().wait_send()

    chips = sections // 2
    far_chips = range(chips - 2, 0, -1)

    def gs_copy(c):
        return remote(sg_buf.at[c], sg_buf.at[c], gs_ss.at[0], gs_rs.at[c], s - 1, z)

    def gs_first(c):
        return remote(sg_buf.at[c], sg_buf.at[c], gs_ss.at[1], gs_rs.at[c], 1, z)

    def gs_chip(c, chip):
        return remote(sg_buf.at[c], sg_buf.at[c], gs_ss.at[1 + chip], gs_rs.at[c], 2 * chip + 1, z)

    def gs_whole(position):
        return remote(sg_buf, sg_buf, gs_ss.at[position], gs_rs.at[0], s - 1, z)

    def build_shift(m):
        dilation = dil_ref[0]
        middle = offs_ref[0, m]
        shape = (2 * PIECE, 2 * PIECE)

        def matrix(source, target):
            start = jnp.where(target >= middle, middle, 0)
            hit = (source == target - dilation) & (source >= start)
            return jnp.where(hit, 1.0, 0.0).astype(BF16)

        rows = lax.broadcasted_iota(jnp.int32, shape, 0)
        lanes = lax.broadcasted_iota(jnp.int32, shape, 1)
        shift_buf[...] = matrix(lanes, rows)
        shift_back[...] = matrix(rows, lanes)

    def pair(ref, first):
        return jnp.concatenate([ref[first], ref[first + 1]], axis=1)

    def put_pair(ref, first, value):
        for h in range(2):
            ref[first + h] = value[:, h * PIECE : (h + 1) * PIECE]

    def both(ref, first, parts):
        return jnp.concatenate([ref[first + h] for h in parts], axis=0)

    def put(ref, first, parts, value):
        for position, h in enumerate(parts):
            ref[first + h] = value[position * PIECE : (position + 1) * PIECE]

    def head(m, total):
        width = 2 * PIECE
        total = jnp.transpose(total.astype(BF16)).astype(F32) * head_scale
        sig_1 = sigmoid(total)
        act_1 = (total * sig_1).astype(BF16)
        slope_1 = sig_1 * (1.0 + total * (1.0 - sig_1)) * head_scale
        post = dot(wp_ref[...], act_1)
        sig_2 = sigmoid(post)
        act_2 = (post * sig_2).astype(BF16)
        slope_2 = sig_2 * (1.0 + post * (1.0 - sig_2))
        logits = dot(wk_ref[...], act_2)
        top = jnp.max(logits, axis=0, keepdims=True)
        expo = jnp.exp(logits - top)
        denominator = jnp.sum(expo, axis=0, keepdims=True)
        hit = tgt_ref[m] == lax.broadcasted_iota(jnp.int32, (classes, width), 0)
        picked = jnp.sum(jnp.where(hit, logits, 0.0), axis=0, keepdims=True)
        time = lax.broadcasted_iota(jnp.int32, (1, width), 1)

        def speaker_weight(which):
            count = cnt_ref[spk_ref[which, m]].astype(F32)
            return WEIGHT_SCALE * lax.rsqrt(jnp.full((1, width), count, F32))

        weight = jnp.where(time >= offs_ref[0, m], speaker_weight(1), speaker_weight(0))
        weight = jnp.where(time < offs_ref[1, m], weight, 0.0)
        grad_logits = (weight * (expo / denominator - jnp.where(hit, 1.0, 0.0))).astype(BF16)
        grad_post = (dot(wk_t[...], grad_logits) * slope_2).astype(BF16)
        grad_total = (dot(wp_t[...], grad_post) * slope_1).astype(BF16)
        put(sg_buf, 2 * m, (0, 1), jnp.transpose(grad_total))
        for h in (1, 0):
            c = 2 * m + h
            for chip in far_chips:
                gs_chip(c, chip).start()
            gs_copy(c).start()
            if feeder == sections - 1:
                gs_first(c).start()
        kept = 2 * lax.rem(m, keep)
        put_pair(gl_buf, kept, grad_logits)
        put_pair(a2_buf, kept, act_2)
        put_pair(gp_buf, kept, grad_post)
        put_pair(a1_buf, kept, act_1)
        loss_row = weight * (top + jnp.log(denominator) - picked)
        high = loss_row.astype(BF16)
        rest = loss_row - high.astype(F32)
        middle = rest.astype(BF16)
        low = (rest - middle.astype(F32)).astype(BF16)
        row = lax.broadcasted_iota(jnp.int32, (EXT, width), 0)
        message = jnp.where(row == mel_rows + 2, high.astype(F32), 0.0)
        message = jnp.where(row == mel_rows + 3, middle.astype(F32), message)
        message = jnp.where(row == mel_rows + 4, low.astype(F32), message)
        put_pair(gc_buf, 2 * m, message.astype(BF16))

    def forward(m, parts):
        high = len(parts) * PIECE
        for h in parts:
            c = 2 * m + h

            @pl.when(is_first)
            def _():
                input_copy(c).wait()
                x_buf[c] = jnp.transpose(inp_buf[lax.rem(c, slots)])
                if ring:

                    @pl.when(c + slots < pieces)
                    def _():
                        input_copy(c + slots).start()

            @pl.when(s > 0)
            def _():
                x_copy(c).wait_recv()

        x = both(x_buf, 2 * m, parts)
        if parts == (0,):
            prev = dot(shift_buf[0:PIECE, 0:PIECE], x)
        elif parts == (1,):
            prev = dot(shift_buf[PIECE : 2 * PIECE, :], both(x_buf, 2 * m, (0, 1)))
        else:
            prev = dot(shift_buf[...], x)
        gate = (
            dot(x, wd_t[res : 2 * res])
            + dot(both(cond_t, 2 * m, parts), wc_ref[...])
            + dot(prev.astype(BF16), wd_t[0:res])
        )
        th = jnp.tanh(gate[:, 0:half])
        sg = sigmoid(gate[:, half : 2 * half])
        gate_buf[0:high, 0:half] = th
        gate_buf[0:high, half : 2 * half] = sg
        put(hid_buf, 2 * m, parts, (th * sg).astype(BF16))

    def forward_rest(m, parts):
        high = len(parts) * PIECE
        th = gate_buf[0:high, 0:half]
        sg = gate_buf[0:high, half : 2 * half]
        put(d1_buf, 2 * m, parts, (sg * (1.0 - th * th)).astype(BF16))
        put(d2_buf, 2 * m, parts, (th * sg * (1.0 - sg)).astype(BF16))

    def forward_piece(m, h):
        c = 2 * m + h
        forward(m, (h,))
        reuse(x_copy, c)
        out = (x_buf[c].astype(F32) + dot(hid_buf[c], wr_t[...])) * HALF_ROOT
        x_out[lax.rem(c, slots)] = out.astype(BF16)
        x_copy(c).start()
        gh_buf[...] = dot(hid_buf[c], ws_t[...])
        forward_rest(m, (h,))

        @pl.when(s > 0)
        def _():
            k_copy(c).wait_recv()
            gh_buf[...] += sg_buf[c].astype(F32)

        reuse(k_copy, c)
        k_out[lax.rem(c, slots)] = gh_buf[...].astype(BF16)
        k_copy(c).start()

    def forward_head(m):
        forward(m, (0, 1))
        total = dot(both(hid_buf, 2 * m, (0, 1)), ws_t[...])
        for h in (0, 1):
            k_copy(2 * m + h).wait_recv()
        head(m, total + both(sg_buf, 2 * m, (0, 1)).astype(F32))
        forward_rest(m, (0, 1))

    def grad_field(m, parts, grad_hidden):
        kept = 2 * lax.rem(m, keep)
        grad_gate = jnp.concatenate(
            [
                grad_hidden * both(d1_buf, 2 * m, parts).astype(F32),
                grad_hidden * both(d2_buf, 2 * m, parts).astype(F32),
            ],
            axis=1,
        ).astype(BF16)
        put(gg_buf, kept, parts, grad_gate)
        if parts == (1,):
            back = dot(shift_back[PIECE:, PIECE:], grad_gate)
        elif parts == (0,):
            back = dot(shift_back[0:PIECE, :], jnp.concatenate([grad_gate, gg_buf[kept + 1]], axis=0))
        else:
            back = dot(shift_back[...], grad_gate)
        return dot(grad_gate, wd_ref[:, res : 2 * res]) + dot(back.astype(BF16), wd_ref[:, 0:res])

    def cond_message(m, h):
        kept = 2 * lax.rem(m, keep)
        row = lax.broadcasted_iota(jnp.int32, (EXT, PIECE), 0)
        own = jnp.where(row < mel_rows, dot_nt(wc_ref[...], gg_buf[kept + h]), 0.0)
        return own + gc_buf[2 * m + h].astype(F32)

    def backward_piece(m, h):
        c = 2 * m + h
        gs_copy(c).wait_recv()

        @pl.when(lax.rem(s, 2) == 1)
        def _():
            gs_copy(c).start()

        if feeder < sections - 1:

            @pl.when(s == feeder)
            def _():
                gs_first(c).start()

        gh_buf[...] = dot(sg_buf[c], ws_ref[...])
        gx_copy(c).wait_recv()
        grad_hidden = gh_buf[...] + HALF_ROOT * dot(gx_buf[c], wr_ref[...])
        grad_x = (HALF_ROOT * gx_buf[c].astype(F32) + grad_field(m, (h,), grad_hidden)).astype(BF16)

        @pl.when(s > 0)
        def _():
            reuse(gx_copy, c)
            gx_out[lax.rem(c, slots)] = grad_x
            gx_copy(c).start()

        @pl.when(is_first)
        def _():
            inp_buf[lax.rem(c, slots)] = jnp.transpose(grad_x)

        gc_copy(c).wait_recv()
        message = cond_message(m, h)

        @pl.when(s > 0)
        def _():
            reuse(gc_copy, c)
            gc_out[lax.rem(c, slots)] = message.astype(BF16)
            gc_copy(c).start()

        @pl.when(is_first)
        def _():
            gc_buf[c, 0:mel_rows, :] = message[0:mel_rows].astype(BF16)
            tail = message[mel_rows:EXT]
            if h == 0:
                frame = lax.broadcasted_iota(jnp.int32, mel_ref.shape, 0) == m
                extra_buf[0:1, 0:mel_rows] = jnp.sum(
                    jnp.where(frame, mel_ref[...].astype(F32), 0.0), axis=0, keepdims=True
                )
                lane = lax.broadcasted_iota(jnp.int32, (1, PIECE), 1)
                ids = jnp.where(lane == 0, spk_ref[0, m], 0)
                ids = jnp.where(lane == 1, spk_ref[1, m], ids)
                ids = jnp.where(lane == 2, offs_ref[0, m], ids)
                extra_buf[1:2, :] = ids.astype(F32)
                tail = tail + extra_buf[...]
            gc_buf[c, mel_rows:EXT, :] = tail.astype(BF16)

    def backward_pair(m):
        grad_hidden = dot(both(sg_buf, 2 * m, (0, 1)), ws_ref[...])
        grad_x = grad_field(m, (0, 1), grad_hidden).astype(BF16)
        for h in (1, 0):
            c = 2 * m + h
            reuse(gx_copy, c)
            gx_out[lax.rem(c, slots)] = grad_x[h * PIECE : (h + 1) * PIECE]
            gx_copy(c).start()
        for h in (1, 0):
            c = 2 * m + h
            reuse(gc_copy, c)
            gc_out[lax.rem(c, slots)] = cond_message(m, h).astype(BF16)
            gc_copy(c).start()

    def add_halves(first_row, value):
        rows = value.shape[0] // 2
        acc[first_row : first_row + rows, 0:half] += value[0:rows]
        acc[first_row : first_row + rows, half : 2 * half] += value[rows : 2 * rows]

    small_row = 2 * half + EXT

    def small_gradients(m):
        parts = (0, 1)
        hidden = both(hid_buf, 2 * m, parts)

        @pl.when(s < sections - 1)
        def _():
            add_halves(small_row, HALF_ROOT * dot_tn(both(gx_buf, 2 * m, parts), hidden))

        add_halves(small_row + half // 2, dot_tn(both(sg_buf, 2 * m, parts), hidden))

        @pl.when(is_last)
        def _():
            kept = 2 * lax.rem(m, keep)
            add_halves(main_rows, dot_nt(pair(gp_buf, kept), pair(a1_buf, kept)))
            add_halves(main_rows + half // 2, dot_nt(pair(gl_buf, kept), pair(a2_buf, kept)))

    def large_gradients(m):
        parts = (0, 1)
        grad_gate = both(gg_buf, 2 * lax.rem(m, keep), parts)
        x = both(x_buf, 2 * m, parts)
        prev = dot(shift_buf[...], x).astype(BF16)
        acc[0 : 2 * half, :] += dot_tn(grad_gate, jnp.concatenate([prev, x], axis=1))
        acc[2 * half : small_row, :] += dot(pair(cond_ref, 2 * m), grad_gate)

    def samples(ref):
        return ref[...].reshape(pieces * PIECE, ref.shape[2])

    def by_channel(ref):
        return jnp.concatenate([ref[c] for c in range(pieces)], axis=1)

    def set_halves(first_row, value):
        rows = value.shape[0] // 2
        acc[first_row : first_row + rows, 0:half] = value[0:rows]
        acc[first_row : first_row + rows, half : 2 * half] = value[rows : 2 * rows]

    def all_small_gradients():
        @pl.when(is_last)
        def _():
            set_halves(main_rows, dot_nt(by_channel(gp_buf), by_channel(a1_buf)))
            set_halves(main_rows + half // 2, dot_nt(by_channel(gl_buf), by_channel(a2_buf)))

        hidden = samples(hid_buf)
        set_halves(small_row + half // 2, dot_tn(samples(sg_buf), hidden))

        @pl.when(s < sections - 1)
        def _():
            set_halves(small_row, HALF_ROOT * dot_tn(samples(gx_buf), hidden))

    def all_large_gradients():
        @pl.loop(0, micro)
        def _(m):
            build_shift(m)
            put(d1_buf, 2 * m, (0, 1), dot(shift_buf[...], both(x_buf, 2 * m, (0, 1))).astype(BF16))

        grad_gate = samples(gg_buf)
        acc[0 : 2 * half, 0:res] = dot_tn(grad_gate, samples(d1_buf))
        acc[0 : 2 * half, res : 2 * res] = dot_tn(grad_gate, samples(x_buf))
        acc[2 * half : small_row, :] = dot(by_channel(cond_ref), grad_gate)

    def gin_rows(other, group):
        return remote(
            inp_buf.at[:, pl.ds(pl.multiple_of(other * share, share), share), :],
            gin_buf.at[pl.ds(pl.multiple_of(group * slots, slots), slots)],
            gin_ss.at[0],
            gin_rs.at[0],
            other,
            z,
        )

    def gin_sent():
        return remote(
            inp_buf.at[:, share:res, :], inp_buf.at[:, share:res, :], gin_ss.at[0], gin_rs.at[0], 1, z
        )

    def gin_arrived():
        return remote(gin_buf, gin_buf, gin_ss.at[0], gin_rs.at[0], 1, z)

    def hand_out(group):
        @pl.loop(1, sections)
        def _(other):
            gin_rows(other, group).start()

        gin_buf[pl.ds(pl.multiple_of(group * slots, slots), slots)] = inp_buf[:, 0:share, :]

    def own_local():
        return pltpu.make_async_copy(gc_buf, o_g.at[z], loc_sem.at[0])

    def own_hub():
        return remote(gc_buf, o_g.at[z], gown_ss.at[0], g_rs.at[z], hub, z)

    def part_along(j, step):
        sem = gpeer_ss.at[j if step > 0 else groups + j]
        return remote(o_g.at[j], o_g.at[j], sem, g_rs.at[j], s, z + step)

    def part_chip(j, chip):
        return remote(o_g.at[j], o_g.at[j], ghub_ss.at[j, chip], g_rs.at[j], 2 * chip, z)

    def part_next(j):
        return remote(o_g.at[j], o_g.at[j], gnext_ss.at[j], g_rs.at[j], s + 1, z)

    def spread(j):
        part_next(j).start()

        @pl.loop(0, sections // 2 - 1)
        def _(chip):
            @pl.when((chip > 0) | (z != j))
            def _():
                part_chip(j, chip).start()

    @pl.when(is_last)
    def _():
        @pl.loop(0, micro)
        def _(m):
            build_shift(m)
            forward_head(m)
            backward_pair(m)
            if keep < micro:
                small_gradients(m)
                large_gradients(m)

    roomy = keep == micro
    swings = (s == sections - 2) if roomy else False
    late = (s >= sections - 2) if roomy else is_last

    @pl.loop(0, 3 * micro)
    def _(step):
        after = step - micro
        odd = lax.rem(step, 2) == 1
        forth = step < micro
        back = jnp.where(late, (after >= 0) & (after < micro), (after >= 0) & (lax.rem(after, 2) == 0))
        m = jnp.where(forth, step, jnp.where(late, lax.rem(step, micro), after // 2))
        if roomy:
            turning = swings & (step < 2 * micro)
            end = step == 2 * micro - 1
            swing_forth = (step == 0) | (odd & jnp.logical_not(end))
            forth = jnp.where(turning, swing_forth, forth)
            back = jnp.where(turning, jnp.logical_not(swing_forth), back)
            swing_m = jnp.where(swing_forth, (step + 1) // 2, jnp.where(end, micro - 1, step // 2 - 1))
            m = jnp.where(turning, swing_m, m)
        build_shift(m)

        @pl.when(forth & is_first & (m > 0))
        def _():
            condition(m)

        @pl.when(forth & jnp.logical_not(is_last))
        def _():
            forward_piece(m, 0)
            forward_piece(m, 1)

        @pl.when(is_first & (step == micro))
        def _():
            acc[...] = jnp.zeros_like(acc)
            extra_buf[...] = jnp.zeros_like(extra_buf)

        @pl.when(back & jnp.logical_not(is_last))
        def _():
            if ring:

                @pl.when(is_first & (m > 0))
                def _():
                    gin_sent().wait_send()

            backward_piece(m, 1)
            backward_piece(m, 0)

            @pl.when(is_first & (lax.rem(2 * m + 2, slots) == 0))
            def _():
                hand_out((2 * m + 2) // slots - 1)

            @pl.when(is_first & (m == micro - 1))
            def _():
                own_hub().start()
                own_local().start()

        @pl.when(jnp.logical_not(forth | back | late))
        def _():
            small_gradients(m)

            @pl.when(m < micro - 1)
            def _():
                large_gradients(m)

    if roomy:

        @pl.when(late)
        def _():
            all_small_gradients()

    @pl.when(is_first)
    def _():
        own_local().wait()

    left = z < groups // 2
    inward = jnp.where(left, z + 1, z - 1)
    outward = jnp.where(left, z - 1, z + 1)
    is_edge = (z == 0) | (z == groups - 1)
    is_mid = (z == groups // 2 - 1) | (z == groups // 2)
    distance = jnp.where(left, groups // 2 - 1 - z, z - groups // 2)
    lag = LAG * (2 * distance + 1) + 8 * distance
    base = jnp.where(is_last, main_blocks + head_blocks, main_blocks)
    helped = 2 * len(exports)
    gives = (s < helped) if exports else False
    takes = ((s >= helper) & (s < helper + helped)) if exports else False
    moved = 0
    for chip, amount in enumerate(exports):
        moved = jnp.where(lax.rem(s, helper) // 2 == chip, amount, moved)
    count = base - jnp.where(gives, moved, 0) + jnp.where(takes, moved, 0)

    all_blocks = main_blocks + head_blocks
    taken_at = base - 50

    def block_of(i):
        j = jnp.where(takes & (i >= taken_at + moved), i - moved, i)
        heads = jnp.where(is_last, head_blocks, 0)
        own = jnp.where(j < heads, j + main_blocks, lax.rem(j - heads + small_row // BLOCK, main_blocks))
        return jnp.where(takes & (j == i) & (i >= taken_at), i - taken_at + all_blocks, own)

    def rows_of(b):
        return pl.ds(pl.multiple_of(b * BLOCK, BLOCK), BLOCK)

    cycle = zp_rs.shape[0]

    def swap_copy(i):
        rows = rows_of(block_of(i))
        return remote(part_out.at[rows], o_acc.at[rows], zi_ss.at[0], zt_rs.at[lax.rem(i, cycle)], s, inward)

    def part_copy(i):
        rows = rows_of(block_of(i))
        return remote(part_out.at[rows], part_in.at[rows], zi_ss.at[0], zp_rs.at[lax.rem(i, cycle)], s, inward)

    def total_copy(i):
        rows = rows_of(block_of(i))
        return remote(o_acc.at[rows], o_acc.at[rows], zo_ss.at[0], zt_rs.at[lax.rem(i, cycle)], s, outward)

    def head_rows_of(j):
        start = main_rows + j * HEAD_GROUP * BLOCK
        return pl.ds(pl.multiple_of(start, BLOCK), HEAD_GROUP * BLOCK)

    def head_copy(j):
        rows = head_rows_of(j)
        return remote(o_acc.at[rows], o_acc.at[rows], hd_ss.at[0], hd_rs.at[j], s - 1, z)

    def send_part(i):
        rows = rows_of(block_of(i))

        @pl.when(is_edge)
        def _():
            part_out[rows, :] = acc[rows, :].astype(BF16)

        @pl.when(jnp.logical_not(is_edge))
        def _():
            part_copy(i).wait_recv()
            part_out[rows, :] = (acc[rows, :] + part_in[rows, :].astype(F32)).astype(BF16)

        @pl.when(is_mid)
        def _():
            swap_copy(i).start()

        @pl.when(jnp.logical_not(is_mid))
        def _():
            part_copy(i).start()

    def keep_rows(rows):
        return pltpu.make_async_copy(o_acc.at[rows], o_sum.at[rows], out_sem.at[0])

    def finish_part(i):
        rows = rows_of(block_of(i))
        swap_copy(i).wait_recv()

        @pl.when(is_mid)
        def _():
            o_acc[rows, :] = (part_out[rows, :].astype(F32) + o_acc[rows, :].astype(F32)).astype(BF16)

        @pl.when(jnp.logical_not(is_edge))
        def _():
            total_copy(i).start()

        @pl.when(block_of(i) < all_blocks)
        def _():
            keep_rows(rows).start()

    def given_rows(amount):
        return pl.ds(small_row - amount * BLOCK, amount * BLOCK)

    def taken_rows(amount):
        return pl.ds(main_rows + head_rows, amount * BLOCK)

    def give_copy(amount):
        target = taken_buf.at[0 : amount * BLOCK]
        return remote(part_out.at[given_rows(amount)], target, give_ss.at[0], give_rs.at[0], s + helper, z)

    def return_copy(amount):
        source, target = o_acc.at[taken_rows(amount)], o_acc.at[given_rows(amount)]
        return remote(source, target, give_ss.at[1], give_rs.at[1], s - helper, z)

    def each_export(cond, act):
        for chip, amount in enumerate(exports):

            @pl.when(cond & (lax.rem(s, helper) // 2 == chip))
            def _():
                act(amount)

    def give(amount):
        part_out[given_rows(amount), :] = acc[given_rows(amount), :].astype(BF16)
        give_copy(amount).start()

    def take(amount):
        give_copy(amount).wait_recv()
        acc[taken_rows(amount), :] = taken_buf[0 : amount * BLOCK].astype(F32)

    def rest_of_gradients():
        @pl.when(jnp.logical_not(late))
        def _():
            build_shift(micro - 1)
            large_gradients(micro - 1)

        if roomy:

            @pl.when(late)
            def _():
                all_large_gradients()

        each_export(gives, give)

    last_step = count + lag - 1
    head_at = lag + 4 + HEAD_GROUP
    own_at = jnp.minimum(40 + 18 * distance, last_step)
    rest_at = jnp.minimum(88 + 9 * (s // 2) + 18 * distance, last_step)

    @pl.loop(0, count + lag)
    def _(i):
        @pl.when(i == LARGE_AT)
        def _():
            rest_of_gradients()

        if exports:

            each_export(takes & (i == taken_at), take)

        @pl.when(i < count)
        def _():
            send_part(i)

        @pl.when(i >= lag)
        def _():
            finish_part(i - lag)
            b = block_of(i - lag)

            in_group = b - main_blocks

            @pl.when((b >= main_blocks) & (b < all_blocks) & (lax.rem(in_group, HEAD_GROUP) == HEAD_GROUP - 1))
            def _():
                head_copy(in_group // HEAD_GROUP).start()

            if exports:

                each_export(b == all_blocks + moved - 1, lambda amount: return_copy(amount).start())

        since = i - head_at

        @pl.when(
            jnp.logical_not(is_last) & (since >= 0) & (since < head_blocks) & (lax.rem(since, HEAD_GROUP) == 0)
        )
        def _():
            j = since // HEAD_GROUP
            head_copy(j).wait_recv()
            keep_rows(head_rows_of(j)).start()

            @pl.when(s > 0)
            def _():
                head_copy(j).start()

        for hop in range(groups):

            @pl.when(is_hub & (i == jnp.minimum(own_at + 14 * hop, last_step)))
            def _():
                def pass_on(j, step, known, far):
                    @pl.when(known)
                    def _():
                        if hop:
                            part_along(j, 1).wait_recv()
                            spread(j)

                        @pl.when(far)
                        def _():
                            part_along(j, step).start()

                if hop == 0:
                    own_hub().wait_recv()
                    spread(z)
                pass_on(z - hop, 1, z >= hop, z < groups - 1)
                pass_on(z + hop, -1, z + hop < groups, z > 0)

        @pl.when((lax.rem(s, 2) == 0) & jnp.logical_not(is_hub) & (i == rest_at))
        def _():
            for j in range(groups):

                @pl.when((z != j) | (s > 0))
                def _():
                    part_next(j).wait_recv()

                part_next(j).start()

    @pl.when(s > 0)
    def _():
        gin_arrived().wait_recv()

    for c in range(pieces):
        o_gin[:, c * PIECE : (c + 1) * PIECE] = gin_buf[c]

    @pl.when(is_first)
    def _():
        own_hub().wait_send()
        gin_sent().wait_send()

    @pl.when(is_hub)
    def _():
        for j in range(groups):

            @pl.when((j <= z) & (z < groups - 1))
            def _():
                part_along(j, 1).wait_send()

            @pl.when((j >= z) & (z > 0))
            def _():
                part_along(j, -1).wait_send()

            @pl.loop(0, sections // 2 - 1)
            def _(chip):
                @pl.when((chip > 0) | (z != j))
                def _():
                    part_chip(j, chip).wait_send()

    for j in range(groups):

        @pl.when(lax.rem(s, 2) == 0)
        def _():
            part_next(j).wait_send()

        @pl.when(lax.rem(s, 2) == 1)
        def _():
            part_next(j).wait_recv()

    if exports:

        def returned(amount):
            return_copy(amount).wait_recv()
            keep_rows(given_rows(amount)).start()
            give_copy(amount).wait_send()

        each_export(gives, returned)
        each_export(takes, lambda amount: return_copy(amount).wait_send())

    keep_rows(pl.ds(0, main_rows + head_rows)).wait()

    def sum_sent(rows):
        remote(part_out.at[rows], part_out.at[rows], zi_ss.at[0], zp_rs.at[0], s, inward).wait_send()

        @pl.when(jnp.logical_not(is_edge))
        def _():
            remote(o_acc.at[rows], o_acc.at[rows], zo_ss.at[0], zt_rs.at[0], s, outward).wait_send()

    if exports:
        each_export(gives, lambda amount: sum_sent(pl.ds(0, main_rows - amount * BLOCK)))
        each_export(takes & jnp.logical_not(is_last), lambda amount: sum_sent(pl.ds(0, main_rows + amount * BLOCK)))

    @pl.when(is_last)
    def _():
        last_takes = exports[-1] if helper + helped == sections and exports else 0
        sum_sent(pl.ds(0, main_rows + head_rows + last_takes * BLOCK))

    @pl.when(jnp.logical_not(is_last | gives | takes))
    def _():
        sum_sent(pl.ds(0, main_rows))

    @pl.when(jnp.logical_not(is_last))
    def _():
        drain(x_copy, lambda: remote(x_out, x_out, x_ss.at[0], x_rs.at[0], s + 1, z))
        drain(k_copy, lambda: remote(k_out, k_out, k_ss.at[0], k_rs.at[0], s + 1, z))

    @pl.when(s > 0)
    def _():
        rows = pl.ds(main_rows, head_rows)
        remote(o_acc.at[rows], o_acc.at[rows], hd_ss.at[0], hd_rs.at[0], s - 1, z).wait_send()
        drain(gx_copy, lambda: remote(gx_out, gx_out, gx_ss.at[0], gx_rs.at[0], s - 1, z))
        drain(gc_copy, lambda: remote(gc_out, gc_out, gc_ss.at[0], gc_rs.at[0], s - 1, z))

    @pl.when(lax.rem(s, 2) == 1)
    def _():
        gs_whole(0).wait_send()

    @pl.when(is_last)
    def _():
        for chip in far_chips:
            gs_whole(1 + chip).wait_send()

    @pl.when(s == feeder)
    def _():
        gs_whole(1).wait_send()


def run_step(dims, tables, arrays, weights):
    sections, groups, micro, res, half, classes, slots, keep, mel_rows = dims
    pieces = 2 * micro
    rows = 2 * half + EXT + half + half // 2 + classes // 2
    head_blocks = (half // 2 + classes // 2) // BLOCK
    share = res // sections
    smem = pl.BlockSpec(memory_space=pltpu.SMEM)
    vmem = pl.BlockSpec(memory_space=pltpu.VMEM)
    anywhere = pl.BlockSpec(memory_space=pl.ANY)
    dma = pltpu.SemaphoreType.DMA

    def tile(*shape, dtype=BF16):
        return pltpu.VMEM(shape, dtype)

    distance = groups // 2 - 1
    cycle = max(LAG * (2 * distance + 1) + 8 * distance + 4, 2 * LAG + 4)
    sends = slots if pieces > slots else 1
    taken = max(exported_blocks(dims), default=0) * BLOCK

    scratch = [
        tile(pieces, PIECE, res),
        tile(pieces, PIECE, half),
        tile(pieces, PIECE, res),
        tile(pieces, EXT, PIECE),
        tile(pieces, PIECE, half),
        tile(pieces, PIECE, half),
        tile(pieces, PIECE, half),
        tile(slots, PIECE, res),
        tile(slots, PIECE, half),
        tile(slots, PIECE, res),
        tile(slots, EXT, PIECE),
        tile(2 * PIECE, 2 * half, dtype=F32),
        tile(PIECE, half, dtype=F32),
        tile(2 * keep, PIECE, 2 * half),
        tile(slots, res, PIECE),
        tile(2 * PIECE, 2 * PIECE),
        tile(2 * PIECE, 2 * PIECE),
        tile(pieces, EXT, PIECE),
        tile(pieces, PIECE, EXT),
        tile(EXT, 2 * half),
        tile(2 * half, 2 * res),
        tile(res, half),
        tile(half, half),
        tile(half, half),
        tile(classes, half),
        tile(2 * res, 2 * half),
        tile(half, res),
        tile(half, half),
        tile(half, half),
        tile(half, classes),
        tile(2 * keep, classes, PIECE),
        tile(2 * keep, half, PIECE),
        tile(2 * keep, half, PIECE),
        tile(2 * keep, half, PIECE),
        tile(rows + taken, WIDE, dtype=F32),
        tile(rows + taken, WIDE),
        tile(rows + taken, WIDE),
        tile(rows + taken, WIDE),
        tile(max(taken, 16), WIDE),
        tile(pieces, share, PIECE),
        tile(2, micro * mel_rows, PIECE, dtype=F32),
        tile(EXT - mel_rows, PIECE, dtype=F32),
        dma((slots,)),
        dma((10,)),
        dma((1,)),
        dma((1,)),
        dma((sends,)),
        dma((pieces,)),
        dma((sends,)),
        dma((pieces,)),
        dma((max(2, sections // 2),)),
        dma((pieces,)),
        dma((sends,)),
        dma((pieces,)),
        dma((sends,)),
        dma((pieces,)),
        dma((1,)),
        dma((1,)),
        dma((cycle,)),
        dma((cycle,)),
        dma((1,)),
        dma((head_blocks // HEAD_GROUP,)),
        dma((groups,)),
        dma((1,)),
        dma((2 * groups,)),
        dma((groups, sections // 2)),
        dma((groups,)),
        dma((1,)),
        dma((1,)),
        dma((2,)),
        dma((2,)),
    ]
    return pl.pallas_call(
        functools.partial(step_kernel, dims),
        out_shape=(
            jax.ShapeDtypeStruct((rows, WIDE), BF16),
            jax.ShapeDtypeStruct((groups, pieces, EXT, PIECE), BF16),
            jax.ShapeDtypeStruct((share, pieces * PIECE), BF16),
        ),
        in_specs=[smem] * 4 + [vmem] * 4 + [anywhere] * 8,
        out_specs=(anywhere, anywhere, vmem),
        scratch_shapes=scratch,
        compiler_params=pltpu.CompilerParams(
            collective_id=0, has_side_effects=True, vmem_limit_bytes=63 * 2**20
        ),
        cost_estimate=pl.CostEstimate(flops=10**10, bytes_accessed=3 * 10**7, transcendentals=10**6),
        name="train_step",
    )(*tables, *arrays, *weights)


def finish_kernel(
    dims,
    sums,
    gin,
    shared_hbm,
    o_gin,
    o_dil,
    o_cond,
    o_res,
    o_skip,
    o_post,
    o_out,
    o_up,
    o_bias,
    o_table,
    o_loss,
    sums_buf,
    shared,
    dil_buf,
    cond_buf,
    res_buf,
    skip_buf,
    post_buf,
    out_buf,
    up_buf,
    field,
    mel_rows_buf,
    mel_columns,
    table,
    load_sem,
    store_sem,
):
    mel_rows, half = dims
    frames = shared.shape[0]
    first = 2 * half
    total_rows = sums_buf.shape[0]
    strips = ((0, half), (half, half), (first, total_rows - first))
    loads = [
        pltpu.make_async_copy(sums.at[pl.ds(row, rows), :], sums_buf.at[pl.ds(row, rows), :], load_sem.at[k])
        for k, (row, rows) in enumerate(strips)
    ]
    loads.append(pltpu.make_async_copy(shared_hbm, shared, load_sem.at[3]))
    for k in (0, 3, 1, 2):
        loads[k].start()
    stores = []

    def store(source, target):
        copy = pltpu.make_async_copy(source, target, store_sem.at[len(stores)])
        copy.start()
        stores.append(copy)

    store(gin, o_gin)

    def dilated(k):
        loads[k].wait()
        rows = pl.ds(k * half, half)
        dil_buf[rows, :] = sums_buf[rows, :].astype(F32)
        store(dil_buf.at[rows, :], o_dil.at[0, rows, :])

    dilated(0)

    loads[3].wait()

    def by_channel(f, loss):
        extra = shared[f, 0, mel_rows:EXT, :].astype(F32)
        mel_rows_buf[pl.ds(f, 1), :] = extra[0:1]
        for h in range(2):
            rows = pl.ds(pl.multiple_of(f * mel_rows, 16), mel_rows)
            field[h, rows, :] = shared[f, h, 0:mel_rows, :].astype(F32)
        return loss + extra + shared[f, 1, mel_rows:EXT, :].astype(F32)

    loss = lax.fori_loop(0, frames, by_channel, jnp.zeros((EXT - mel_rows, PIECE), F32))
    row = lax.broadcasted_iota(jnp.int32, loss.shape, 0)
    loss = jnp.where((row >= 2) & (row < 5), loss, 0.0)
    o_loss[...] = jnp.sum(jnp.sum(loss, axis=1, keepdims=True), axis=0, keepdims=True)
    mel_columns[...] = jnp.transpose(mel_rows_buf[...])[0:mel_rows].astype(BF16)

    parts = 4
    channels = mel_rows // parts

    def upsampling(part):
        @pl.loop(0, channels // 10)
        def _(group):
            for j in range(10):
                c = part * channels + group * 10 + j
                rows = pl.ds(c, frames, stride=mel_rows)
                matrix = jnp.concatenate([field[0, rows, :], field[1, rows, :]], axis=1)
                up_buf[c] = dot(mel_columns[...], matrix.astype(BF16))

        rows = pl.ds(part * channels, channels)
        store(up_buf.at[rows], o_up.at[rows])

    upsampling(0)
    upsampling(1)
    dilated(1)
    upsampling(2)
    upsampling(3)

    loads[2].wait()
    cond_buf[...] = sums_buf[first : first + mel_rows, :].astype(F32)
    o_bias[...] = sums_buf[first + mel_rows : first + EXT, :].astype(F32)[0:1]
    store(cond_buf, o_cond)
    row = first + EXT
    for buffer, target in ((res_buf, o_res), (skip_buf, o_skip), (post_buf, o_post), (out_buf, o_out)):
        rows = buffer.shape[1]
        buffer[0] = sums_buf[row : row + rows, 0:half].astype(F32)
        buffer[1] = sums_buf[row : row + rows, half : 2 * half].astype(F32)
        store(buffer, target)
        row += rows

    table[...] = jnp.zeros_like(table)
    time = lax.broadcasted_iota(jnp.int32, (2 * PIECE, PIECE), 0).astype(F32)
    number = lax.broadcasted_iota(jnp.int32, (2 * PIECE, PIECE), 1).astype(F32)

    @pl.loop(0, frames // 4)
    def _(group):
        grads, hots = [], []
        for k in range(4):
            f = group * 4 + k
            ids = shared[f, 0, mel_rows:EXT, :].astype(F32)[1:2]
            speaker = jnp.where(time >= ids[:, 2:3], ids[:, 1:2], ids[:, 0:1])
            hots.append(jnp.where(number == speaker, 1.0, 0.0).astype(BF16))
            grads += [shared[f, 0, 0:mel_rows, :], shared[f, 1, 0:mel_rows, :]]
        table[...] += dot(jnp.concatenate(grads, axis=1), jnp.concatenate(hots, axis=0))

    o_table[...] = table[:, 0 : o_table.shape[1]]
    for copy in stores:
        copy.wait()


def finish(sums, shared, grad_inputs, half, classes, mel_rows, speakers):
    frames = shared.shape[0]
    first = 2 * half
    vmem = pl.BlockSpec(memory_space=pltpu.VMEM)
    anywhere = pl.BlockSpec(memory_space=pl.ANY)
    large = (
        (first, WIDE),
        (mel_rows, WIDE),
        (2, half // 2, half),
        (2, half // 2, half),
        (2, half // 2, half),
        (2, classes // 2, half),
        (mel_rows, mel_rows, 2 * PIECE),
    )

    def f32(*shape):
        return jax.ShapeDtypeStruct(shape, F32)

    return pl.pallas_call(
        functools.partial(finish_kernel, (mel_rows, half)),
        out_shape=(
            jax.ShapeDtypeStruct(grad_inputs.shape, grad_inputs.dtype),
            f32(1, *large[0]),
            *[f32(*shape) for shape in large[1:]],
            f32(1, WIDE),
            f32(mel_rows, speakers),
            f32(1, 1),
        ),
        in_specs=[anywhere] * 3,
        out_specs=(anywhere,) * 8 + (vmem,) * 3,
        scratch_shapes=[
            pltpu.VMEM(sums.shape, BF16),
            pltpu.VMEM(shared.shape, BF16),
            *[pltpu.VMEM(shape, F32) for shape in large],
            pltpu.VMEM((2, frames * mel_rows, PIECE), F32),
            pltpu.VMEM((frames, PIECE), F32),
            pltpu.VMEM((mel_rows, frames), BF16),
            pltpu.VMEM((mel_rows, PIECE), F32),
            pltpu.SemaphoreType.DMA((4,)),
            pltpu.SemaphoreType.DMA((12,)),
        ],
        compiler_params=pltpu.CompilerParams(vmem_limit_bytes=62 * 2**20),
        name="finish",
    )(sums, grad_inputs, shared)


def local(
    inputs,
    targets,
    mel,
    speakers,
    speaker_sample_counts,
    segment_offsets,
    dilations,
    dilated_kernel,
    conditioning_projection,
    dilated_gate_bias,
    residual_projection,
    skip_projection,
    upsample_weight,
    speaker_table,
    first_output_projection,
    class_projection,
):
    sections = lax.axis_size("section")
    groups = lax.axis_size("dp")
    micro = segment_offsets.shape[0]
    res, tokens = inputs.shape
    length = tokens // micro
    mel_rows = mel.shape[0]
    hop = upsample_weight.shape[0]
    half = residual_projection.shape[2]
    classes = class_projection.shape[0]
    pieces = 2 * micro
    assert length == 2 * PIECE and hop == length and mel_rows + 16 == EXT and 2 * half == WIDE

    slots, keep = (pieces, micro) if pieces <= 8 else (2, 1)
    dims = (sections, groups, micro, res, half, classes, slots, keep, mel_rows)
    sums, shared, grad_inputs = run_step(
        dims,
        (dilations, segment_offsets.T, speakers.T, speaker_sample_counts),
        (
            targets.reshape(micro, 1, length),
            mel.T,
            speaker_table,
            dilated_gate_bias,
        ),
        (
            inputs,
            upsample_weight.transpose(1, 2, 0).reshape(mel_rows * mel_rows, hop),
            conditioning_projection[0].T,
            dilated_kernel[0],
            residual_projection[0],
            skip_projection[0],
            first_output_projection,
            class_projection,
        ),
    )
    shared = shared.reshape(groups * micro, 2, EXT, PIECE)
    grad_inputs, dil, cond, grad_res, grad_skip, post, out, up, bias, table, loss = finish(
        sums, shared, grad_inputs, half, classes, mel_rows, speaker_table.shape[1]
    )
    return (
        loss.reshape(()),
        grad_inputs,
        dil,
        cond.T[None],
        bias,
        grad_res.reshape(1, half, half),
        grad_skip.reshape(1, half, half),
        up.transpose(2, 0, 1),
        table,
        post.reshape(half, half),
        out.reshape(classes, half),
    )


def solution(mesh):
    return jax.shard_map(
        local,
        mesh=mesh,
        in_specs=(
            P(None, "dp"),
            P("dp"),
            P(None, "dp"),
            P("dp", None),
            P(),
            P("dp", None),
            P("section"),
            P("section", None, None),
            P("section", None, None),
            P("section", None),
            P("section", None, None),
            P("section", None, None),
            P(),
            P(),
            P(),
            P(),
        ),
        out_specs=(
            P(),
            P("section", "dp"),
            P("section", None, None),
            P("section", None, None),
            P("section", None),
            P("section", None, None),
            P("section", None, None),
            P(),
            P(),
            P(),
            P(),
        ),
        check_vma=False,
    )
```

```python
import functools
import math

import jax
import jax.numpy as jnp
from jax import lax
from jax.experimental import pallas as pl
from jax.experimental.pallas import tpu as pltpu
from jax.sharding import PartitionSpec as P

HALF_ROOT = 0.7071067811865476
WEIGHT_SCALE = 64.0
MESH = pl.DeviceIdType.MESH
BF16 = jnp.bfloat16
F32 = jnp.float32

PIECE = 128
EXT = 96
WIDE = 1024
BLOCK = 16
EXPORTS = (12,)
HEAD_GROUP = 4
LARGE_AT = 6
LAG = 7


def dot(left, right):
    return jnp.dot(left, right, preferred_element_type=F32)


def dot_nt(left, right):
    return lax.dot_general(left, right, (((1,), (1,)), ((), ())), preferred_element_type=F32)


def dot_tn(left, right):
    return lax.dot_general(left, right, (((0,), (0,)), ((), ())), preferred_element_type=F32)


def sigmoid(values):
    return 0.5 * jnp.tanh(0.5 * values) + 0.5


def exported_blocks(dims):
    sections, groups, micro, keep = dims[0], dims[1], dims[2], dims[7]
    helped = sections // 4
    return EXPORTS[:helped] if keep == micro and sections <= 8 else ()


def step_kernel(
    dims,
    dil_ref,
    offs_ref,
    spk_ref,
    cnt_ref,
    tgt_ref,
    mel_ref,
    tab_ref,
    bias_in,
    inp_hbm,
    up_hbm,
    wc_hbm,
    wd_hbm,
    wr_hbm,
    ws_hbm,
    wp_hbm,
    wk_hbm,
    o_sum,
    o_g,
    o_gin,
    x_buf,
    sg_buf,
    gx_buf,
    gc_buf,
    hid_buf,
    d1_buf,
    d2_buf,
    x_out,
    k_out,
    gx_out,
    gc_out,
    gate_buf,
    gh_buf,
    gg_buf,
    inp_buf,
    shift_buf,
    shift_back,
    cond_ref,
    cond_t,
    wc_ref,
    wd_ref,
    wr_ref,
    ws_ref,
    wp_ref,
    wk_ref,
    wd_t,
    wr_t,
    ws_t,
    wp_t,
    wk_t,
    gl_buf,
    a2_buf,
    gp_buf,
    a1_buf,
    acc,
    part_out,
    part_in,
    o_acc,
    taken_buf,
    gin_buf,
    up_buf,
    extra_buf,
    inp_sem,
    load_sem,
    out_sem,
    loc_sem,
    x_ss,
    x_rs,
    k_ss,
    k_rs,
    gs_ss,
    gs_rs,
    gx_ss,
    gx_rs,
    gc_ss,
    gc_rs,
    zi_ss,
    zo_ss,
    zp_rs,
    zt_rs,
    hd_ss,
    hd_rs,
    g_rs,
    gown_ss,
    gpeer_ss,
    ghub_ss,
    gnext_ss,
    gin_ss,
    gin_rs,
    give_ss,
    give_rs,
):
    sections, groups, micro, res, half, classes, slots, keep, mel_rows = dims
    pieces = 2 * micro
    s = lax.axis_index("section")
    z = lax.axis_index("dp")
    is_first = s == 0
    is_last = s == sections - 1
    hub = sections - 2
    is_hub = s == hub
    head_scale = 1.0 / math.sqrt(sections)
    main_rows = 2 * half + EXT + half
    head_rows = half // 2 + classes // 2
    main_blocks = main_rows // BLOCK
    head_blocks = head_rows // BLOCK
    share = res // sections
    feeder = sections - 3 if sections > 4 else sections - 1
    exports = exported_blocks(dims)
    helper = sections // 2

    barrier = pltpu.get_barrier_semaphore()

    def greet(cond, dev_s, dev_z):
        @pl.when(cond)
        def _():
            pl.semaphore_signal(barrier, 1, device_id=(dev_s, dev_z), device_id_type=MESH)

    greet(s > 0, s - 1, z)
    greet(s < sections - 1, s + 1, z)
    greet(z > 0, s, z - 1)
    greet(z < groups - 1, s, z + 1)
    greet(s >= 2, 0, z)
    told = (lax.rem(s, 2) == 0) & (s > 0) & (s < hub)
    greet(told, hub, z)

    @pl.when(is_first)
    def _():
        @pl.loop(2, sections)
        def _(other):
            pl.semaphore_signal(barrier, 1, device_id=(other, z), device_id_type=MESH)

    @pl.when(is_hub)
    def _():
        @pl.loop(1, sections // 2 - 1)
        def _(chip):
            pl.semaphore_signal(barrier, 1, device_id=(2 * chip, z), device_id_type=MESH)

    far = (lax.rem(s, 2) == 1) & (s > 1) & (s < sections - 1)
    greet(far, sections - 1, z)

    @pl.when(is_last)
    def _():
        @pl.loop(1, sections // 2 - 1)
        def _(chip):
            pl.semaphore_signal(barrier, 1, device_id=(2 * chip + 1, z), device_id_type=MESH)

    greet(s == 1, feeder, z)
    greet(s == feeder, 1, z)

    def flag(cond):
        return jnp.where(cond, 1, 0)

    z_near = flag(z > 0) + flag(z < groups - 1)
    expected = (
        flag(s > 0)
        + flag(s < sections - 1)
        + z_near
        + jnp.where(is_first, sections - 2, flag(s >= 2))
        + flag(told)
        + flag(far)
        + flag(s == 1)
        + flag(s == feeder)
        + jnp.where(is_last, sections // 2 - 2, 0)
        + jnp.where(is_hub, sections // 2 - 2, 0)
    )

    def input_copy(c):
        slot = lax.rem(c, slots)
        return pltpu.make_async_copy(
            inp_hbm.at[:, pl.ds(pl.multiple_of(c * PIECE, PIECE), PIECE)],
            inp_buf.at[slot],
            inp_sem.at[slot],
        )

    quarter = mel_rows // 4
    weight_refs = (
        (wd_hbm, wd_ref),
        (wr_hbm, wr_ref),
        (ws_hbm, ws_ref),
        (wc_hbm, wc_ref.at[0:mel_rows]),
        (wp_hbm, wp_ref),
        (wk_hbm, wk_ref),
    )
    loads = [
        pltpu.make_async_copy(source, target, load_sem.at[4 + position])
        for position, (source, target) in enumerate(weight_refs)
    ]
    frame_loads = [
        pltpu.make_async_copy(
            up_hbm.at[pl.ds(q * quarter * mel_rows, quarter * mel_rows), :],
            part_out.at[pl.ds(0, quarter * mel_rows), pl.ds(q * 2 * PIECE, 2 * PIECE)],
            load_sem.at[q],
        )
        for q in range(4)
    ]
    for load in loads[:4] + frame_loads:
        load.start()

    @pl.when(is_first)
    def _():
        @pl.loop(0, slots)
        def _(c):
            input_copy(c).start()

    @pl.when(is_last)
    def _():
        for load in loads[4:]:
            load.start()

    spare = lax.broadcasted_iota(jnp.int32, (EXT - mel_rows, 2 * half), 0)
    bias = jnp.broadcast_to(bias_in[...].astype(F32), (EXT - mel_rows, 2 * half))
    wc_ref[mel_rows:EXT] = jnp.where(spare == 0, bias, 0.0).astype(BF16)
    loads[0].wait()
    wd_t[...] = jnp.transpose(wd_ref[...])
    for load in loads[1:4]:
        load.wait()
    wr_t[...] = jnp.transpose(wr_ref[...])
    ws_t[...] = jnp.transpose(ws_ref[...])

    for load in frame_loads:
        load.wait()

    @pl.loop(0, quarter // 4)
    def _(group):
        for q in range(4):
            for part in range(4):
                row = group * 4 + part
                lanes = slice(q * 2 * PIECE, (q + 1) * 2 * PIECE)
                matrix = part_out[pl.ds(pl.multiple_of(row * mel_rows, 16), mel_rows), lanes]
                frames = dot(mel_ref[...], matrix)
                rows = pl.ds(q * quarter + row, micro, stride=mel_rows)
                for h in range(2):
                    up_buf[h, rows, :] = frames[:, h * PIECE : (h + 1) * PIECE]

    def condition(m):
        shape = (tab_ref.shape[1], 2 * PIECE)
        time = lax.broadcasted_iota(jnp.int32, shape, 1)
        speaker = jnp.where(time >= offs_ref[0, m], spk_ref[1, m], spk_ref[0, m])
        hot = jnp.where(lax.broadcasted_iota(jnp.int32, shape, 0) == speaker, 1.0, 0.0).astype(BF16)
        columns = dot(tab_ref[...], hot)
        ones = jnp.where(lax.broadcasted_iota(jnp.int32, (EXT - mel_rows, PIECE), 0) == 0, 1.0, 0.0)
        rows = pl.ds(pl.multiple_of(m * mel_rows, 16), mel_rows)
        for h in range(2):
            c = 2 * m + h
            value = up_buf[h, rows, :] + columns[:, h * PIECE : (h + 1) * PIECE]
            cond_ref[c] = jnp.concatenate([value, ones], axis=0).astype(BF16)
            cond_t[c] = jnp.transpose(cond_ref[c])

    @pl.when(is_first)
    def _():
        condition(0)

    @pl.when(s > 0)
    def _():
        @pl.loop(0, micro)
        def _(m):
            condition(m)

    @pl.when(s > 0)
    def _():
        acc[...] = jnp.zeros_like(acc)

    @pl.when(is_last)
    def _():
        for load in loads[4:]:
            load.wait()
        wp_t[...] = jnp.transpose(wp_ref[...])
        wk_t[...] = jnp.transpose(wk_ref[...])
        gx_buf[...] = jnp.zeros_like(gx_buf)

    pl.semaphore_wait(barrier, expected)

    def remote(src, dst, send_sem, recv_sem, dev_s, dev_z):
        return pltpu.make_async_remote_copy(
            src_ref=src,
            dst_ref=dst,
            send_sem=send_sem,
            recv_sem=recv_sem,
            device_id=(dev_s, dev_z),
            device_id_type=MESH,
        )

    ring = pieces > slots

    def send_of(semaphores, slot):
        return semaphores.at[slot if ring else 0]

    def x_copy(c):
        slot = lax.rem(c, slots)
        return remote(x_out.at[slot], x_buf.at[c], send_of(x_ss, slot), x_rs.at[c], s + 1, z)

    def k_copy(c):
        slot = lax.rem(c, slots)
        return remote(k_out.at[slot], sg_buf.at[c], send_of(k_ss, slot), k_rs.at[c], s + 1, z)

    def gx_copy(c):
        slot = lax.rem(c, slots)
        return remote(gx_out.at[slot], gx_buf.at[c], send_of(gx_ss, slot), gx_rs.at[c], s - 1, z)

    def gc_copy(c):
        slot = lax.rem(c, slots)
        return remote(gc_out.at[slot], gc_buf.at[c], send_of(gc_ss, slot), gc_rs.at[c], s - 1, z)

    def reuse(copy, c):
        if ring:

            @pl.when(c >= slots)
            def _():
                copy(c).wait_send()

    def drain(copy, whole):
        if ring:

            @pl.loop(0, slots)
            def _(c):
                copy(c).wait_send()

        else:
            whole().wait_send()

    chips = sections // 2
    far_chips = range(chips - 2, 0, -1)

    def gs_copy(c):
        return remote(sg_buf.at[c], sg_buf.at[c], gs_ss.at[0], gs_rs.at[c], s - 1, z)

    def gs_first(c):
        return remote(sg_buf.at[c], sg_buf.at[c], gs_ss.at[1], gs_rs.at[c], 1, z)

    def gs_chip(c, chip):
        return remote(sg_buf.at[c], sg_buf.at[c], gs_ss.at[1 + chip], gs_rs.at[c], 2 * chip + 1, z)

    def gs_whole(position):
        return remote(sg_buf, sg_buf, gs_ss.at[position], gs_rs.at[0], s - 1, z)

    def build_shift(m):
        dilation = dil_ref[0]
        middle = offs_ref[0, m]
        shape = (2 * PIECE, 2 * PIECE)

        def matrix(source, target):
            start = jnp.where(target >= middle, middle, 0)
            hit = (source == target - dilation) & (source >= start)
            return jnp.where(hit, 1.0, 0.0).astype(BF16)

        rows = lax.broadcasted_iota(jnp.int32, shape, 0)
        lanes = lax.broadcasted_iota(jnp.int32, shape, 1)
        shift_buf[...] = matrix(lanes, rows)
        shift_back[...] = matrix(rows, lanes)

    def pair(ref, first):
        return jnp.concatenate([ref[first], ref[first + 1]], axis=1)

    def put_pair(ref, first, value):
        for h in range(2):
            ref[first + h] = value[:, h * PIECE : (h + 1) * PIECE]

    def both(ref, first, parts):
        return jnp.concatenate([ref[first + h] for h in parts], axis=0)

    def put(ref, first, parts, value):
        for position, h in enumerate(parts):
            ref[first + h] = value[position * PIECE : (position + 1) * PIECE]

    def head(m, total):
        width = 2 * PIECE
        total = jnp.transpose(total.astype(BF16)).astype(F32) * head_scale
        sig_1 = sigmoid(total)
        act_1 = (total * sig_1).astype(BF16)
        slope_1 = sig_1 * (1.0 + total * (1.0 - sig_1)) * head_scale
        post = dot(wp_ref[...], act_1)
        sig_2 = sigmoid(post)
        act_2 = (post * sig_2).astype(BF16)
        slope_2 = sig_2 * (1.0 + post * (1.0 - sig_2))
        logits = dot(wk_ref[...], act_2)
        top = jnp.max(logits, axis=0, keepdims=True)
        expo = jnp.exp(logits - top)
        denominator = jnp.sum(expo, axis=0, keepdims=True)
        hit = tgt_ref[m] == lax.broadcasted_iota(jnp.int32, (classes, width), 0)
        picked = jnp.sum(jnp.where(hit, logits, 0.0), axis=0, keepdims=True)
        time = lax.broadcasted_iota(jnp.int32, (1, width), 1)

        def speaker_weight(which):
            count = cnt_ref[spk_ref[which, m]].astype(F32)
            return WEIGHT_SCALE * lax.rsqrt(jnp.full((1, width), count, F32))

        weight = jnp.where(time >= offs_ref[0, m], speaker_weight(1), speaker_weight(0))
        weight = jnp.where(time < offs_ref[1, m], weight, 0.0)
        grad_logits = (weight * (expo / denominator - jnp.where(hit, 1.0, 0.0))).astype(BF16)
        grad_post = (dot(wk_t[...], grad_logits) * slope_2).astype(BF16)
        grad_total = (dot(wp_t[...], grad_post) * slope_1).astype(BF16)
        put(sg_buf, 2 * m, (0, 1), jnp.transpose(grad_total))
        for h in (1, 0):
            c = 2 * m + h
            for chip in far_chips:
                gs_chip(c, chip).start()
            gs_copy(c).start()
            if feeder == sections - 1:
                gs_first(c).start()
        kept = 2 * lax.rem(m, keep)
        put_pair(gl_buf, kept, grad_logits)
        put_pair(a2_buf, kept, act_2)
        put_pair(gp_buf, kept, grad_post)
        put_pair(a1_buf, kept, act_1)
        loss_row = weight * (top + jnp.log(denominator) - picked)
        high = loss_row.astype(BF16)
        rest = loss_row - high.astype(F32)
        middle = rest.astype(BF16)
        low = (rest - middle.astype(F32)).astype(BF16)
        row = lax.broadcasted_iota(jnp.int32, (EXT, width), 0)
        message = jnp.where(row == mel_rows + 2, high.astype(F32), 0.0)
        message = jnp.where(row == mel_rows + 3, middle.astype(F32), message)
        message = jnp.where(row == mel_rows + 4, low.astype(F32), message)
        put_pair(gc_buf, 2 * m, message.astype(BF16))

    def forward(m, parts):
        high = len(parts) * PIECE
        for h in parts:
            c = 2 * m + h

            @pl.when(is_first)
            def _():
                input_copy(c).wait()
                x_buf[c] = jnp.transpose(inp_buf[lax.rem(c, slots)])
                if ring:

                    @pl.when(c + slots < pieces)
                    def _():
                        input_copy(c + slots).start()

            @pl.when(s > 0)
            def _():
                x_copy(c).wait_recv()

        x = both(x_buf, 2 * m, parts)
        if parts == (0,):
            prev = dot(shift_buf[0:PIECE, 0:PIECE], x)
        elif parts == (1,):
            prev = dot(shift_buf[PIECE : 2 * PIECE, :], both(x_buf, 2 * m, (0, 1)))
        else:
            prev = dot(shift_buf[...], x)
        gate = (
            dot(x, wd_t[res : 2 * res])
            + dot(both(cond_t, 2 * m, parts), wc_ref[...])
            + dot(prev.astype(BF16), wd_t[0:res])
        )
        th = jnp.tanh(gate[:, 0:half])
        sg = sigmoid(gate[:, half : 2 * half])
        gate_buf[0:high, 0:half] = th
        gate_buf[0:high, half : 2 * half] = sg
        put(hid_buf, 2 * m, parts, (th * sg).astype(BF16))

    def forward_rest(m, parts):
        high = len(parts) * PIECE
        th = gate_buf[0:high, 0:half]
        sg = gate_buf[0:high, half : 2 * half]
        put(d1_buf, 2 * m, parts, (sg * (1.0 - th * th)).astype(BF16))
        put(d2_buf, 2 * m, parts, (th * sg * (1.0 - sg)).astype(BF16))

    def forward_piece(m, h):
        c = 2 * m + h
        forward(m, (h,))
        reuse(x_copy, c)
        out = (x_buf[c].astype(F32) + dot(hid_buf[c], wr_t[...])) * HALF_ROOT
        x_out[lax.rem(c, slots)] = out.astype(BF16)
        x_copy(c).start()
        gh_buf[...] = dot(hid_buf[c], ws_t[...])
        forward_rest(m, (h,))

        @pl.when(s > 0)
        def _():
            k_copy(c).wait_recv()
            gh_buf[...] += sg_buf[c].astype(F32)

        reuse(k_copy, c)
        k_out[lax.rem(c, slots)] = gh_buf[...].astype(BF16)
        k_copy(c).start()

    def forward_head(m):
        forward(m, (0, 1))
        total = dot(both(hid_buf, 2 * m, (0, 1)), ws_t[...])
        for h in (0, 1):
            k_copy(2 * m + h).wait_recv()
        head(m, total + both(sg_buf, 2 * m, (0, 1)).astype(F32))
        forward_rest(m, (0, 1))

    def grad_field(m, parts, grad_hidden):
        kept = 2 * lax.rem(m, keep)
        grad_gate = jnp.concatenate(
            [
                grad_hidden * both(d1_buf, 2 * m, parts).astype(F32),
                grad_hidden * both(d2_buf, 2 * m, parts).astype(F32),
            ],
            axis=1,
        ).astype(BF16)
        put(gg_buf, kept, parts, grad_gate)
        if parts == (1,):
            back = dot(shift_back[PIECE:, PIECE:], grad_gate)
        elif parts == (0,):
            back = dot(shift_back[0:PIECE, :], jnp.concatenate([grad_gate, gg_buf[kept + 1]], axis=0))
        else:
            back = dot(shift_back[...], grad_gate)
        return dot(grad_gate, wd_ref[:, res : 2 * res]) + dot(back.astype(BF16), wd_ref[:, 0:res])

    def cond_message(m, h):
        kept = 2 * lax.rem(m, keep)
        row = lax.broadcasted_iota(jnp.int32, (EXT, PIECE), 0)
        own = jnp.where(row < mel_rows, dot_nt(wc_ref[...], gg_buf[kept + h]), 0.0)
        return own + gc_buf[2 * m + h].astype(F32)

    def backward_piece(m, h):
        c = 2 * m + h
        gs_copy(c).wait_recv()

        @pl.when(lax.rem(s, 2) == 1)
        def _():
            gs_copy(c).start()

        if feeder < sections - 1:

            @pl.when(s == feeder)
            def _():
                gs_first(c).start()

        gh_buf[...] = dot(sg_buf[c], ws_ref[...])
        gx_copy(c).wait_recv()
        grad_hidden = gh_buf[...] + HALF_ROOT * dot(gx_buf[c], wr_ref[...])
        grad_x = (HALF_ROOT * gx_buf[c].astype(F32) + grad_field(m, (h,), grad_hidden)).astype(BF16)

        @pl.when(s > 0)
        def _():
            reuse(gx_copy, c)
            gx_out[lax.rem(c, slots)] = grad_x
            gx_copy(c).start()

        @pl.when(is_first)
        def _():
            inp_buf[lax.rem(c, slots)] = jnp.transpose(grad_x)

    def backward_message(m, h):
        c = 2 * m + h
        gc_copy(c).wait_recv()
        message = cond_message(m, h)

        @pl.when(s > 0)
        def _():
            reuse(gc_copy, c)
            gc_out[lax.rem(c, slots)] = message.astype(BF16)
            gc_copy(c).start()

        @pl.when(is_first)
        def _():
            gc_buf[c, 0:mel_rows, :] = message[0:mel_rows].astype(BF16)
            tail = message[mel_rows:EXT]
            if h == 0:
                frame = lax.broadcasted_iota(jnp.int32, mel_ref.shape, 0) == m
                extra_buf[0:1, 0:mel_rows] = jnp.sum(
                    jnp.where(frame, mel_ref[...].astype(F32), 0.0), axis=0, keepdims=True
                )
                lane = lax.broadcasted_iota(jnp.int32, (1, PIECE), 1)
                ids = jnp.where(lane == 0, spk_ref[0, m], 0)
                ids = jnp.where(lane == 1, spk_ref[1, m], ids)
                ids = jnp.where(lane == 2, offs_ref[0, m], ids)
                extra_buf[1:2, :] = ids.astype(F32)
                tail = tail + extra_buf[...]
            gc_buf[c, mel_rows:EXT, :] = tail.astype(BF16)

    def backward_pair(m):
        for h in (1, 0):
            c = 2 * m + h
            reuse(gx_copy, c)
            grad_hidden = dot(sg_buf[c], ws_ref[...])
            gx_out[lax.rem(c, slots)] = grad_field(m, (h,), grad_hidden).astype(BF16)
            gx_copy(c).start()
        for h in (1, 0):
            c = 2 * m + h
            reuse(gc_copy, c)
            gc_out[lax.rem(c, slots)] = cond_message(m, h).astype(BF16)
            gc_copy(c).start()

    def add_halves(first_row, value):
        rows = value.shape[0] // 2
        acc[first_row : first_row + rows, 0:half] += value[0:rows]
        acc[first_row : first_row + rows, half : 2 * half] += value[rows : 2 * rows]

    small_row = 2 * half + EXT

    def small_gradients(m):
        parts = (0, 1)
        hidden = both(hid_buf, 2 * m, parts)

        @pl.when(s < sections - 1)
        def _():
            add_halves(small_row, HALF_ROOT * dot_tn(both(gx_buf, 2 * m, parts), hidden))

        add_halves(small_row + half // 2, dot_tn(both(sg_buf, 2 * m, parts), hidden))

        @pl.when(is_last)
        def _():
            kept = 2 * lax.rem(m, keep)
            add_halves(main_rows, dot_nt(pair(gp_buf, kept), pair(a1_buf, kept)))
            add_halves(main_rows + half // 2, dot_nt(pair(gl_buf, kept), pair(a2_buf, kept)))

    def large_gradients(m):
        parts = (0, 1)
        grad_gate = both(gg_buf, 2 * lax.rem(m, keep), parts)
        x = both(x_buf, 2 * m, parts)
        prev = dot(shift_buf[...], x).astype(BF16)
        acc[0 : 2 * half, :] += dot_tn(grad_gate, jnp.concatenate([prev, x], axis=1))
        acc[2 * half : small_row, :] += dot(pair(cond_ref, 2 * m), grad_gate)

    def samples(ref):
        return ref[...].reshape(pieces * PIECE, ref.shape[2])

    def by_channel(ref):
        return jnp.concatenate([ref[c] for c in range(pieces)], axis=1)

    def set_halves(first_row, value):
        rows = value.shape[0] // 2
        acc[first_row : first_row + rows, 0:half] = value[0:rows]
        acc[first_row : first_row + rows, half : 2 * half] = value[rows : 2 * rows]

    def all_small_gradients():
        @pl.when(is_last)
        def _():
            set_halves(main_rows, dot_nt(by_channel(gp_buf), by_channel(a1_buf)))
            set_halves(main_rows + half // 2, dot_nt(by_channel(gl_buf), by_channel(a2_buf)))

        hidden = samples(hid_buf)
        set_halves(small_row + half // 2, dot_tn(samples(sg_buf), hidden))

        @pl.when(s < sections - 1)
        def _():
            set_halves(small_row, HALF_ROOT * dot_tn(samples(gx_buf), hidden))

    def all_large_gradients():
        @pl.loop(0, micro)
        def _(m):
            build_shift(m)
            put(d1_buf, 2 * m, (0, 1), dot(shift_buf[...], both(x_buf, 2 * m, (0, 1))).astype(BF16))

        grad_gate = samples(gg_buf)
        acc[0 : 2 * half, 0:res] = dot_tn(grad_gate, samples(d1_buf))
        acc[0 : 2 * half, res : 2 * res] = dot_tn(grad_gate, samples(x_buf))
        acc[2 * half : small_row, :] = dot(by_channel(cond_ref), grad_gate)

    def gin_rows(other, group):
        return remote(
            inp_buf.at[:, pl.ds(pl.multiple_of(other * share, share), share), :],
            gin_buf.at[pl.ds(pl.multiple_of(group * slots, slots), slots)],
            gin_ss.at[0],
            gin_rs.at[0],
            other,
            z,
        )

    def gin_sent():
        return remote(
            inp_buf.at[:, share:res, :], inp_buf.at[:, share:res, :], gin_ss.at[0], gin_rs.at[0], 1, z
        )

    def gin_arrived():
        return remote(gin_buf, gin_buf, gin_ss.at[0], gin_rs.at[0], 1, z)

    def hand_out(group):
        @pl.loop(1, sections)
        def _(other):
            gin_rows(other, group).start()

        gin_buf[pl.ds(pl.multiple_of(group * slots, slots), slots)] = inp_buf[:, 0:share, :]

    def own_local():
        return pltpu.make_async_copy(gc_buf, o_g.at[z], loc_sem.at[0])

    def own_hub():
        return remote(gc_buf, o_g.at[z], gown_ss.at[0], g_rs.at[z], hub, z)

    def part_along(j, step):
        sem = gpeer_ss.at[j if step > 0 else groups + j]
        return remote(o_g.at[j], o_g.at[j], sem, g_rs.at[j], s, z + step)

    def part_chip(j, chip):
        return remote(o_g.at[j], o_g.at[j], ghub_ss.at[j, chip], g_rs.at[j], 2 * chip, z)

    def part_next(j):
        return remote(o_g.at[j], o_g.at[j], gnext_ss.at[j], g_rs.at[j], s + 1, z)

    def spread(j):
        part_next(j).start()

        @pl.loop(0, sections // 2 - 1)
        def _(chip):
            @pl.when((chip > 0) | (z != j))
            def _():
                part_chip(j, chip).start()

    @pl.when(is_last)
    def _():
        @pl.loop(0, micro)
        def _(m):
            build_shift(m)
            forward_head(m)
            backward_pair(m)
            if keep < micro:
                small_gradients(m)
                large_gradients(m)

    roomy = keep == micro
    swings = (s == sections - 2) if roomy else False
    late = (s >= sections - 2) if roomy else is_last

    @pl.loop(0, 3 * micro)
    def _(step):
        after = step - micro
        odd = lax.rem(step, 2) == 1
        forth = step < micro
        back = jnp.where(late, (after >= 0) & (after < micro), (after >= 0) & (lax.rem(after, 2) == 0))
        m = jnp.where(forth, step, jnp.where(late, lax.rem(step, micro), after // 2))
        if roomy:
            turning = swings & (step < 2 * micro)
            end = step == 2 * micro - 1
            swing_forth = (step == 0) | (odd & jnp.logical_not(end))
            forth = jnp.where(turning, swing_forth, forth)
            back = jnp.where(turning, jnp.logical_not(swing_forth), back)
            swing_m = jnp.where(swing_forth, (step + 1) // 2, jnp.where(end, micro - 1, step // 2 - 1))
            m = jnp.where(turning, swing_m, m)
        build_shift(m)

        @pl.when(forth & is_first & (m > 0))
        def _():
            condition(m)

        @pl.when(forth & jnp.logical_not(is_last))
        def _():
            forward_piece(m, 0)
            forward_piece(m, 1)

        @pl.when(is_first & (step == micro))
        def _():
            acc[...] = jnp.zeros_like(acc)
            extra_buf[...] = jnp.zeros_like(extra_buf)

        @pl.when(back & jnp.logical_not(is_last))
        def _():
            if ring:

                @pl.when(is_first & (m > 0))
                def _():
                    gin_sent().wait_send()

            backward_piece(m, 1)
            backward_piece(m, 0)
            backward_message(m, 1)
            backward_message(m, 0)

            @pl.when(is_first & (lax.rem(2 * m + 2, slots) == 0))
            def _():
                hand_out((2 * m + 2) // slots - 1)

            @pl.when(is_first & (m == micro - 1))
            def _():
                own_hub().start()
                own_local().start()

        @pl.when(jnp.logical_not(forth | back | late))
        def _():
            small_gradients(m)

            @pl.when(m < micro - 1)
            def _():
                large_gradients(m)

    if roomy:

        @pl.when(late)
        def _():
            all_small_gradients()

    @pl.when(is_first)
    def _():
        own_local().wait()

    left = z < groups // 2
    inward = jnp.where(left, z + 1, z - 1)
    outward = jnp.where(left, z - 1, z + 1)
    is_edge = (z == 0) | (z == groups - 1)
    is_mid = (z == groups // 2 - 1) | (z == groups // 2)
    distance = jnp.where(left, groups // 2 - 1 - z, z - groups // 2)
    lag = LAG * (2 * distance + 1) + 8 * distance
    base = jnp.where(is_last, main_blocks + head_blocks, main_blocks)
    helped = 2 * len(exports)
    gives = (s < helped) if exports else False
    takes = ((s >= helper) & (s < helper + helped)) if exports else False
    moved = 0
    for chip, amount in enumerate(exports):
        moved = jnp.where(lax.rem(s, helper) // 2 == chip, amount, moved)
    count = base - jnp.where(gives, moved, 0) + jnp.where(takes, moved, 0)

    all_blocks = main_blocks + head_blocks
    taken_at = base - 50

    def block_of(i):
        j = jnp.where(takes & (i >= taken_at + moved), i - moved, i)
        heads = jnp.where(is_last, head_blocks, 0)
        own = jnp.where(j < heads, j + main_blocks, lax.rem(j - heads + small_row // BLOCK, main_blocks))
        return jnp.where(takes & (j == i) & (i >= taken_at), i - taken_at + all_blocks, own)

    def rows_of(b):
        return pl.ds(pl.multiple_of(b * BLOCK, BLOCK), BLOCK)

    cycle = zp_rs.shape[0]

    def swap_copy(i):
        rows = rows_of(block_of(i))
        return remote(part_out.at[rows], o_acc.at[rows], zi_ss.at[0], zt_rs.at[lax.rem(i, cycle)], s, inward)

    def part_copy(i):
        rows = rows_of(block_of(i))
        return remote(part_out.at[rows], part_in.at[rows], zi_ss.at[0], zp_rs.at[lax.rem(i, cycle)], s, inward)

    def total_copy(i):
        rows = rows_of(block_of(i))
        return remote(o_acc.at[rows], o_acc.at[rows], zo_ss.at[0], zt_rs.at[lax.rem(i, cycle)], s, outward)

    def head_rows_of(j):
        start = main_rows + j * HEAD_GROUP * BLOCK
        return pl.ds(pl.multiple_of(start, BLOCK), HEAD_GROUP * BLOCK)

    def head_copy(j):
        rows = head_rows_of(j)
        return remote(o_acc.at[rows], o_acc.at[rows], hd_ss.at[0], hd_rs.at[j], s - 1, z)

    def send_part(i):
        rows = rows_of(block_of(i))

        @pl.when(is_edge)
        def _():
            part_out[rows, :] = acc[rows, :].astype(BF16)

        @pl.when(jnp.logical_not(is_edge))
        def _():
            part_copy(i).wait_recv()
            part_out[rows, :] = (acc[rows, :] + part_in[rows, :].astype(F32)).astype(BF16)

        @pl.when(is_mid)
        def _():
            swap_copy(i).start()

        @pl.when(jnp.logical_not(is_mid))
        def _():
            part_copy(i).start()

    def keep_rows(rows):
        return pltpu.make_async_copy(o_acc.at[rows], o_sum.at[rows], out_sem.at[0])

    def finish_part(i):
        rows = rows_of(block_of(i))
        swap_copy(i).wait_recv()

        @pl.when(is_mid)
        def _():
            o_acc[rows, :] = (part_out[rows, :].astype(F32) + o_acc[rows, :].astype(F32)).astype(BF16)

        @pl.when(jnp.logical_not(is_edge))
        def _():
            total_copy(i).start()

        @pl.when(block_of(i) < all_blocks)
        def _():
            keep_rows(rows).start()

    def given_rows(amount):
        return pl.ds(small_row - amount * BLOCK, amount * BLOCK)

    def taken_rows(amount):
        return pl.ds(main_rows + head_rows, amount * BLOCK)

    def give_copy(amount):
        target = taken_buf.at[0 : amount * BLOCK]
        return remote(part_out.at[given_rows(amount)], target, give_ss.at[0], give_rs.at[0], s + helper, z)

    def return_copy(amount):
        source, target = o_acc.at[taken_rows(amount)], o_acc.at[given_rows(amount)]
        return remote(source, target, give_ss.at[1], give_rs.at[1], s - helper, z)

    def each_export(cond, act):
        for chip, amount in enumerate(exports):

            @pl.when(cond & (lax.rem(s, helper) // 2 == chip))
            def _():
                act(amount)

    def give(amount):
        part_out[given_rows(amount), :] = acc[given_rows(amount), :].astype(BF16)
        give_copy(amount).start()

    def take(amount):
        give_copy(amount).wait_recv()
        acc[taken_rows(amount), :] = taken_buf[0 : amount * BLOCK].astype(F32)

    def rest_of_gradients():
        @pl.when(jnp.logical_not(late))
        def _():
            build_shift(micro - 1)
            large_gradients(micro - 1)

        if roomy:

            @pl.when(late)
            def _():
                all_large_gradients()

        each_export(gives, give)

    last_step = count + lag - 1
    head_at = lag + 4 + HEAD_GROUP
    own_at = jnp.minimum(48 + 18 * distance, last_step)
    rest_at = jnp.minimum(88 + 9 * (s // 2) + 18 * distance, last_step)

    @pl.loop(0, count + lag)
    def _(i):
        @pl.when(i == LARGE_AT)
        def _():
            rest_of_gradients()

        if exports:

            each_export(takes & (i == taken_at), take)

        @pl.when(i < count)
        def _():
            send_part(i)

        @pl.when(i >= lag)
        def _():
            finish_part(i - lag)
            b = block_of(i - lag)

            in_group = b - main_blocks

            @pl.when((b >= main_blocks) & (b < all_blocks) & (lax.rem(in_group, HEAD_GROUP) == HEAD_GROUP - 1))
            def _():
                head_copy(in_group // HEAD_GROUP).start()

            if exports:

                each_export(b == all_blocks + moved - 1, lambda amount: return_copy(amount).start())

        since = i - head_at

        @pl.when(
            jnp.logical_not(is_last) & (since >= 0) & (since < head_blocks) & (lax.rem(since, HEAD_GROUP) == 0)
        )
        def _():
            j = since // HEAD_GROUP
            head_copy(j).wait_recv()
            keep_rows(head_rows_of(j)).start()

            @pl.when(s > 0)
            def _():
                head_copy(j).start()

        for hop in range(groups):

            @pl.when(is_hub & (i == jnp.minimum(own_at + 14 * hop, last_step)))
            def _():
                def pass_on(j, step, known, far):
                    @pl.when(known)
                    def _():
                        if hop:
                            part_along(j, 1).wait_recv()
                            spread(j)

                        @pl.when(far)
                        def _():
                            part_along(j, step).start()

                if hop == 0:
                    own_hub().wait_recv()
                    spread(z)
                pass_on(z - hop, 1, z >= hop, z < groups - 1)
                pass_on(z + hop, -1, z + hop < groups, z > 0)

        @pl.when((lax.rem(s, 2) == 0) & jnp.logical_not(is_hub) & (i == rest_at))
        def _():
            for j in range(groups):

                @pl.when((z != j) | (s > 0))
                def _():
                    part_next(j).wait_recv()

                part_next(j).start()

    @pl.when(s > 0)
    def _():
        gin_arrived().wait_recv()

    for c in range(pieces):
        o_gin[:, c * PIECE : (c + 1) * PIECE] = gin_buf[c]

    @pl.when(is_first)
    def _():
        own_hub().wait_send()
        gin_sent().wait_send()

    @pl.when(is_hub)
    def _():
        for j in range(groups):

            @pl.when((j <= z) & (z < groups - 1))
            def _():
                part_along(j, 1).wait_send()

            @pl.when((j >= z) & (z > 0))
            def _():
                part_along(j, -1).wait_send()

            @pl.loop(0, sections // 2 - 1)
            def _(chip):
                @pl.when((chip > 0) | (z != j))
                def _():
                    part_chip(j, chip).wait_send()

    for j in range(groups):

        @pl.when(lax.rem(s, 2) == 0)
        def _():
            part_next(j).wait_send()

        @pl.when(lax.rem(s, 2) == 1)
        def _():
            part_next(j).wait_recv()

    if exports:

        def returned(amount):
            return_copy(amount).wait_recv()
            keep_rows(given_rows(amount)).start()
            give_copy(amount).wait_send()

        each_export(gives, returned)
        each_export(takes, lambda amount: return_copy(amount).wait_send())

    keep_rows(pl.ds(0, main_rows + head_rows)).wait()

    def sum_sent(rows):
        remote(part_out.at[rows], part_out.at[rows], zi_ss.at[0], zp_rs.at[0], s, inward).wait_send()

        @pl.when(jnp.logical_not(is_edge))
        def _():
            remote(o_acc.at[rows], o_acc.at[rows], zo_ss.at[0], zt_rs.at[0], s, outward).wait_send()

    if exports:
        each_export(gives, lambda amount: sum_sent(pl.ds(0, main_rows - amount * BLOCK)))
        each_export(takes & jnp.logical_not(is_last), lambda amount: sum_sent(pl.ds(0, main_rows + amount * BLOCK)))

    @pl.when(is_last)
    def _():
        last_takes = exports[-1] if helper + helped == sections and exports else 0
        sum_sent(pl.ds(0, main_rows + head_rows + last_takes * BLOCK))

    @pl.when(jnp.logical_not(is_last | gives | takes))
    def _():
        sum_sent(pl.ds(0, main_rows))

    @pl.when(jnp.logical_not(is_last))
    def _():
        drain(x_copy, lambda: remote(x_out, x_out, x_ss.at[0], x_rs.at[0], s + 1, z))
        drain(k_copy, lambda: remote(k_out, k_out, k_ss.at[0], k_rs.at[0], s + 1, z))

    @pl.when(s > 0)
    def _():
        rows = pl.ds(main_rows, head_rows)
        remote(o_acc.at[rows], o_acc.at[rows], hd_ss.at[0], hd_rs.at[0], s - 1, z).wait_send()
        drain(gx_copy, lambda: remote(gx_out, gx_out, gx_ss.at[0], gx_rs.at[0], s - 1, z))
        drain(gc_copy, lambda: remote(gc_out, gc_out, gc_ss.at[0], gc_rs.at[0], s - 1, z))

    @pl.when(lax.rem(s, 2) == 1)
    def _():
        gs_whole(0).wait_send()

    @pl.when(is_last)
    def _():
        for chip in far_chips:
            gs_whole(1 + chip).wait_send()

    @pl.when(s == feeder)
    def _():
        gs_whole(1).wait_send()


def run_step(dims, tables, arrays, weights):
    sections, groups, micro, res, half, classes, slots, keep, mel_rows = dims
    pieces = 2 * micro
    rows = 2 * half + EXT + half + half // 2 + classes // 2
    head_blocks = (half // 2 + classes // 2) // BLOCK
    share = res // sections
    smem = pl.BlockSpec(memory_space=pltpu.SMEM)
    vmem = pl.BlockSpec(memory_space=pltpu.VMEM)
    anywhere = pl.BlockSpec(memory_space=pl.ANY)
    dma = pltpu.SemaphoreType.DMA

    def tile(*shape, dtype=BF16):
        return pltpu.VMEM(shape, dtype)

    distance = groups // 2 - 1
    cycle = max(LAG * (2 * distance + 1) + 8 * distance + 4, 2 * LAG + 4)
    sends = slots if pieces > slots else 1
    taken = max(exported_blocks(dims), default=0) * BLOCK

    scratch = [
        tile(pieces, PIECE, res),
        tile(pieces, PIECE, half),
        tile(pieces, PIECE, res),
        tile(pieces, EXT, PIECE),
        tile(pieces, PIECE, half),
        tile(pieces, PIECE, half),
        tile(pieces, PIECE, half),
        tile(slots, PIECE, res),
        tile(slots, PIECE, half),
        tile(slots, PIECE, res),
        tile(slots, EXT, PIECE),
        tile(2 * PIECE, 2 * half, dtype=F32),
        tile(PIECE, half, dtype=F32),
        tile(2 * keep, PIECE, 2 * half),
        tile(slots, res, PIECE),
        tile(2 * PIECE, 2 * PIECE),
        tile(2 * PIECE, 2 * PIECE),
        tile(pieces, EXT, PIECE),
        tile(pieces, PIECE, EXT),
        tile(EXT, 2 * half),
        tile(2 * half, 2 * res),
        tile(res, half),
        tile(half, half),
        tile(half, half),
        tile(classes, half),
        tile(2 * res, 2 * half),
        tile(half, res),
        tile(half, half),
        tile(half, half),
        tile(half, classes),
        tile(2 * keep, classes, PIECE),
        tile(2 * keep, half, PIECE),
        tile(2 * keep, half, PIECE),
        tile(2 * keep, half, PIECE),
        tile(rows + taken, WIDE, dtype=F32),
        tile(rows + taken, WIDE),
        tile(rows + taken, WIDE),
        tile(rows + taken, WIDE),
        tile(max(taken, 16), WIDE),
        tile(pieces, share, PIECE),
        tile(2, micro * mel_rows, PIECE, dtype=F32),
        tile(EXT - mel_rows, PIECE, dtype=F32),
        dma((slots,)),
        dma((10,)),
        dma((1,)),
        dma((1,)),
        dma((sends,)),
        dma((pieces,)),
        dma((sends,)),
        dma((pieces,)),
        dma((max(2, sections // 2),)),
        dma((pieces,)),
        dma((sends,)),
        dma((pieces,)),
        dma((sends,)),
        dma((pieces,)),
        dma((1,)),
        dma((1,)),
        dma((cycle,)),
        dma((cycle,)),
        dma((1,)),
        dma((head_blocks // HEAD_GROUP,)),
        dma((groups,)),
        dma((1,)),
        dma((2 * groups,)),
        dma((groups, sections // 2)),
        dma((groups,)),
        dma((1,)),
        dma((1,)),
        dma((2,)),
        dma((2,)),
    ]
    return pl.pallas_call(
        functools.partial(step_kernel, dims),
        out_shape=(
            jax.ShapeDtypeStruct((rows, WIDE), BF16),
            jax.ShapeDtypeStruct((groups, pieces, EXT, PIECE), BF16),
            jax.ShapeDtypeStruct((share, pieces * PIECE), BF16),
        ),
        in_specs=[smem] * 4 + [vmem] * 4 + [anywhere] * 8,
        out_specs=(anywhere, anywhere, vmem),
        scratch_shapes=scratch,
        compiler_params=pltpu.CompilerParams(
            collective_id=0, has_side_effects=True, vmem_limit_bytes=63 * 2**20
        ),
        cost_estimate=pl.CostEstimate(flops=10**10, bytes_accessed=3 * 10**7, transcendentals=10**6),
        name="train_step",
    )(*tables, *arrays, *weights)


def finish_kernel(
    dims,
    sums,
    gin,
    shared_hbm,
    o_gin,
    o_dil,
    o_cond,
    o_res,
    o_skip,
    o_post,
    o_out,
    o_up,
    o_bias,
    o_table,
    o_loss,
    sums_buf,
    shared,
    dil_buf,
    cond_buf,
    res_buf,
    skip_buf,
    post_buf,
    out_buf,
    up_buf,
    field,
    mel_rows_buf,
    mel_columns,
    table,
    load_sem,
    store_sem,
):
    mel_rows, half = dims
    frames = shared.shape[0]
    first = 2 * half
    total_rows = sums_buf.shape[0]
    strips = ((0, half), (half, half), (first, total_rows - first))
    loads = [
        pltpu.make_async_copy(sums.at[pl.ds(row, rows), :], sums_buf.at[pl.ds(row, rows), :], load_sem.at[k])
        for k, (row, rows) in enumerate(strips)
    ]
    loads.append(pltpu.make_async_copy(shared_hbm, shared, load_sem.at[3]))
    for k in (0, 3, 1, 2):
        loads[k].start()
    stores = []

    def store(source, target):
        copy = pltpu.make_async_copy(source, target, store_sem.at[len(stores)])
        copy.start()
        stores.append(copy)

    store(gin, o_gin)

    def dilated(k):
        loads[k].wait()
        rows = pl.ds(k * half, half)
        dil_buf[rows, :] = sums_buf[rows, :].astype(F32)
        store(dil_buf.at[rows, :], o_dil.at[0, rows, :])

    dilated(0)

    loads[3].wait()

    def by_channel(f, loss):
        extra = shared[f, 0, mel_rows:EXT, :].astype(F32)
        mel_rows_buf[pl.ds(f, 1), :] = extra[0:1]
        for h in range(2):
            rows = pl.ds(pl.multiple_of(f * mel_rows, 16), mel_rows)
            field[h, rows, :] = shared[f, h, 0:mel_rows, :].astype(F32)
        return loss + extra + shared[f, 1, mel_rows:EXT, :].astype(F32)

    loss = lax.fori_loop(0, frames, by_channel, jnp.zeros((EXT - mel_rows, PIECE), F32))
    row = lax.broadcasted_iota(jnp.int32, loss.shape, 0)
    loss = jnp.where((row >= 2) & (row < 5), loss, 0.0)
    o_loss[...] = jnp.sum(jnp.sum(loss, axis=1, keepdims=True), axis=0, keepdims=True)
    mel_columns[...] = jnp.transpose(mel_rows_buf[...])[0:mel_rows].astype(BF16)

    parts = 4
    channels = mel_rows // parts

    def upsampling(part):
        @pl.loop(0, channels // 10)
        def _(group):
            for j in range(10):
                c = part * channels + group * 10 + j
                rows = pl.ds(c, frames, stride=mel_rows)
                matrix = jnp.concatenate([field[0, rows, :], field[1, rows, :]], axis=1)
                up_buf[c] = dot(mel_columns[...], matrix.astype(BF16))

        rows = pl.ds(part * channels, channels)
        store(up_buf.at[rows], o_up.at[rows])

    upsampling(0)
    upsampling(1)
    dilated(1)
    upsampling(2)
    upsampling(3)

    loads[2].wait()
    cond_buf[...] = sums_buf[first : first + mel_rows, :].astype(F32)
    o_bias[...] = sums_buf[first + mel_rows : first + EXT, :].astype(F32)[0:1]
    store(cond_buf, o_cond)
    row = first + EXT
    for buffer, target in ((res_buf, o_res), (skip_buf, o_skip), (post_buf, o_post), (out_buf, o_out)):
        rows = buffer.shape[1]
        buffer[0] = sums_buf[row : row + rows, 0:half].astype(F32)
        buffer[1] = sums_buf[row : row + rows, half : 2 * half].astype(F32)
        store(buffer, target)
        row += rows

    table[...] = jnp.zeros_like(table)
    time = lax.broadcasted_iota(jnp.int32, (2 * PIECE, PIECE), 0).astype(F32)
    number = lax.broadcasted_iota(jnp.int32, (2 * PIECE, PIECE), 1).astype(F32)

    @pl.loop(0, frames // 4)
    def _(group):
        grads, hots = [], []
        for k in range(4):
            f = group * 4 + k
            ids = shared[f, 0, mel_rows:EXT, :].astype(F32)[1:2]
            speaker = jnp.where(time >= ids[:, 2:3], ids[:, 1:2], ids[:, 0:1])
            hots.append(jnp.where(number == speaker, 1.0, 0.0).astype(BF16))
            grads += [shared[f, 0, 0:mel_rows, :], shared[f, 1, 0:mel_rows, :]]
        table[...] += dot(jnp.concatenate(grads, axis=1), jnp.concatenate(hots, axis=0))

    o_table[...] = table[:, 0 : o_table.shape[1]]
    for copy in stores:
        copy.wait()


def finish(sums, shared, grad_inputs, half, classes, mel_rows, speakers):
    frames = shared.shape[0]
    first = 2 * half
    vmem = pl.BlockSpec(memory_space=pltpu.VMEM)
    anywhere = pl.BlockSpec(memory_space=pl.ANY)
    large = (
        (first, WIDE),
        (mel_rows, WIDE),
        (2, half // 2, half),
        (2, half // 2, half),
        (2, half // 2, half),
        (2, classes // 2, half),
        (mel_rows, mel_rows, 2 * PIECE),
    )

    def f32(*shape):
        return jax.ShapeDtypeStruct(shape, F32)

    return pl.pallas_call(
        functools.partial(finish_kernel, (mel_rows, half)),
        out_shape=(
            jax.ShapeDtypeStruct(grad_inputs.shape, grad_inputs.dtype),
            f32(1, *large[0]),
            *[f32(*shape) for shape in large[1:]],
            f32(1, WIDE),
            f32(mel_rows, speakers),
            f32(1, 1),
        ),
        in_specs=[anywhere] * 3,
        out_specs=(anywhere,) * 8 + (vmem,) * 3,
        scratch_shapes=[
            pltpu.VMEM(sums.shape, BF16),
            pltpu.VMEM(shared.shape, BF16),
            *[pltpu.VMEM(shape, F32) for shape in large],
            pltpu.VMEM((2, frames * mel_rows, PIECE), F32),
            pltpu.VMEM((frames, PIECE), F32),
            pltpu.VMEM((mel_rows, frames), BF16),
            pltpu.VMEM((mel_rows, PIECE), F32),
            pltpu.SemaphoreType.DMA((4,)),
            pltpu.SemaphoreType.DMA((12,)),
        ],
        compiler_params=pltpu.CompilerParams(vmem_limit_bytes=62 * 2**20),
        name="finish",
    )(sums, grad_inputs, shared)


def local(
    inputs,
    targets,
    mel,
    speakers,
    speaker_sample_counts,
    segment_offsets,
    dilations,
    dilated_kernel,
    conditioning_projection,
    dilated_gate_bias,
    residual_projection,
    skip_projection,
    upsample_weight,
    speaker_table,
    first_output_projection,
    class_projection,
):
    sections = lax.axis_size("section")
    groups = lax.axis_size("dp")
    micro = segment_offsets.shape[0]
    res, tokens = inputs.shape
    length = tokens // micro
    mel_rows = mel.shape[0]
    hop = upsample_weight.shape[0]
    half = residual_projection.shape[2]
    classes = class_projection.shape[0]
    pieces = 2 * micro
    assert length == 2 * PIECE and hop == length and mel_rows + 16 == EXT and 2 * half == WIDE

    slots, keep = (pieces, micro) if pieces <= 8 else (2, 1)
    dims = (sections, groups, micro, res, half, classes, slots, keep, mel_rows)
    sums, shared, grad_inputs = run_step(
        dims,
        (dilations, segment_offsets.T, speakers.T, speaker_sample_counts),
        (
            targets.reshape(micro, 1, length),
            mel.T,
            speaker_table,
            dilated_gate_bias,
        ),
        (
            inputs,
            upsample_weight.transpose(1, 2, 0).reshape(mel_rows * mel_rows, hop),
            conditioning_projection[0].T,
            dilated_kernel[0],
            residual_projection[0],
            skip_projection[0],
            first_output_projection,
            class_projection,
        ),
    )
    shared = shared.reshape(groups * micro, 2, EXT, PIECE)
    grad_inputs, dil, cond, grad_res, grad_skip, post, out, up, bias, table, loss = finish(
        sums, shared, grad_inputs, half, classes, mel_rows, speaker_table.shape[1]
    )
    return (
        loss.reshape(()),
        grad_inputs,
        dil,
        cond.T[None],
        bias,
        grad_res.reshape(1, half, half),
        grad_skip.reshape(1, half, half),
        up.transpose(2, 0, 1),
        table,
        post.reshape(half, half),
        out.reshape(classes, half),
    )


def solution(mesh):
    return jax.shard_map(
        local,
        mesh=mesh,
        in_specs=(
            P(None, "dp"),
            P("dp"),
            P(None, "dp"),
            P("dp", None),
            P(),
            P("dp", None),
            P("section"),
            P("section", None, None),
            P("section", None, None),
            P("section", None),
            P("section", None, None),
            P("section", None, None),
            P(),
            P(),
            P(),
            P(),
        ),
        out_specs=(
            P(),
            P("section", "dp"),
            P("section", None, None),
            P("section", None, None),
            P("section", None),
            P("section", None, None),
            P("section", None, None),
            P(),
            P(),
            P(),
            P(),
        ),
        check_vma=False,
    )
```

```python
import functools
import math

import jax
import jax.numpy as jnp
from jax import lax
from jax.experimental import pallas as pl
from jax.experimental.pallas import tpu as pltpu
from jax.sharding import PartitionSpec as P

HALF_ROOT = 0.7071067811865476
WEIGHT_SCALE = 64.0
MESH = pl.DeviceIdType.MESH
BF16 = jnp.bfloat16
F32 = jnp.float32

PIECE = 128
EXT = 96
WIDE = 1024
BLOCK = 16
EXPORTS = (12,)
HEAD_GROUP = 4
LARGE_AT = 6
LAG = 7


def dot(left, right):
    return jnp.dot(left, right, preferred_element_type=F32)


def dot_nt(left, right):
    return lax.dot_general(left, right, (((1,), (1,)), ((), ())), preferred_element_type=F32)


def dot_tn(left, right):
    return lax.dot_general(left, right, (((0,), (0,)), ((), ())), preferred_element_type=F32)


def sigmoid(values):
    return 0.5 * jnp.tanh(0.5 * values) + 0.5


def exported_blocks(dims):
    sections, groups, micro, keep = dims[0], dims[1], dims[2], dims[7]
    helped = sections // 4
    return EXPORTS[:helped] if keep == micro and sections <= 8 else ()


def step_kernel(
    dims,
    dil_ref,
    offs_ref,
    spk_ref,
    cnt_ref,
    tgt_ref,
    mel_ref,
    tab_ref,
    bias_in,
    inp_hbm,
    up_hbm,
    wc_hbm,
    wd_hbm,
    wr_hbm,
    ws_hbm,
    wp_hbm,
    wk_hbm,
    o_sum,
    o_g,
    o_gin,
    x_buf,
    sg_buf,
    gx_buf,
    gc_buf,
    hid_buf,
    d1_buf,
    d2_buf,
    x_out,
    k_out,
    gx_out,
    gc_out,
    gate_buf,
    gh_buf,
    gg_buf,
    inp_buf,
    shift_buf,
    shift_back,
    cond_ref,
    cond_t,
    wc_ref,
    wd_ref,
    wr_ref,
    ws_ref,
    wp_ref,
    wk_ref,
    wd_t,
    wr_t,
    ws_t,
    wp_t,
    wk_t,
    gl_buf,
    a2_buf,
    gp_buf,
    a1_buf,
    acc,
    part_out,
    part_in,
    o_acc,
    taken_buf,
    gin_buf,
    up_buf,
    extra_buf,
    inp_sem,
    load_sem,
    out_sem,
    loc_sem,
    x_ss,
    x_rs,
    k_ss,
    k_rs,
    gs_ss,
    gs_rs,
    gx_ss,
    gx_rs,
    gc_ss,
    gc_rs,
    zi_ss,
    zo_ss,
    zp_rs,
    zt_rs,
    hd_ss,
    hd_rs,
    g_rs,
    gown_ss,
    gpeer_ss,
    ghub_ss,
    gnext_ss,
    gin_ss,
    gin_rs,
    give_ss,
    give_rs,
):
    sections, groups, micro, res, half, classes, slots, keep, mel_rows = dims
    pieces = 2 * micro
    s = lax.axis_index("section")
    z = lax.axis_index("dp")
    is_first = s == 0
    is_last = s == sections - 1
    hub = sections - 2
    is_hub = s == hub
    head_scale = 1.0 / math.sqrt(sections)
    main_rows = 2 * half + EXT + half
    head_rows = half // 2 + classes // 2
    main_blocks = main_rows // BLOCK
    head_blocks = head_rows // BLOCK
    share = res // sections
    feeder = sections - 3 if sections > 4 else sections - 1
    exports = exported_blocks(dims)
    helper = sections // 2

    barrier = pltpu.get_barrier_semaphore()

    def greet(cond, dev_s, dev_z):
        @pl.when(cond)
        def _():
            pl.semaphore_signal(barrier, 1, device_id=(dev_s, dev_z), device_id_type=MESH)

    greet(s > 0, s - 1, z)
    greet(s < sections - 1, s + 1, z)
    greet(z > 0, s, z - 1)
    greet(z < groups - 1, s, z + 1)
    greet(s >= 2, 0, z)
    told = (lax.rem(s, 2) == 0) & (s > 0) & (s < hub)
    greet(told, hub, z)

    @pl.when(is_first)
    def _():
        @pl.loop(2, sections)
        def _(other):
            pl.semaphore_signal(barrier, 1, device_id=(other, z), device_id_type=MESH)

    @pl.when(is_hub)
    def _():
        @pl.loop(1, sections // 2 - 1)
        def _(chip):
            pl.semaphore_signal(barrier, 1, device_id=(2 * chip, z), device_id_type=MESH)

    far = (lax.rem(s, 2) == 1) & (s > 1) & (s < sections - 1)
    greet(far, sections - 1, z)

    @pl.when(is_last)
    def _():
        @pl.loop(1, sections // 2 - 1)
        def _(chip):
            pl.semaphore_signal(barrier, 1, device_id=(2 * chip + 1, z), device_id_type=MESH)

    greet(s == 1, feeder, z)
    greet(s == feeder, 1, z)

    def flag(cond):
        return jnp.where(cond, 1, 0)

    z_near = flag(z > 0) + flag(z < groups - 1)
    expected = (
        flag(s > 0)
        + flag(s < sections - 1)
        + z_near
        + jnp.where(is_first, sections - 2, flag(s >= 2))
        + flag(told)
        + flag(far)
        + flag(s == 1)
        + flag(s == feeder)
        + jnp.where(is_last, sections // 2 - 2, 0)
        + jnp.where(is_hub, sections // 2 - 2, 0)
    )

    def input_copy(c):
        slot = lax.rem(c, slots)
        return pltpu.make_async_copy(
            inp_hbm.at[:, pl.ds(pl.multiple_of(c * PIECE, PIECE), PIECE)],
            inp_buf.at[slot],
            inp_sem.at[slot],
        )

    quarter = mel_rows // 4
    weight_refs = (
        (wd_hbm, wd_ref),
        (wr_hbm, wr_ref),
        (ws_hbm, ws_ref),
        (wc_hbm, wc_ref.at[0:mel_rows]),
        (wp_hbm, wp_ref),
        (wk_hbm, wk_ref),
    )
    loads = [
        pltpu.make_async_copy(source, target, load_sem.at[4 + position])
        for position, (source, target) in enumerate(weight_refs)
    ]
    frame_loads = [
        pltpu.make_async_copy(
            up_hbm.at[pl.ds(q * quarter * mel_rows, quarter * mel_rows), :],
            part_out.at[pl.ds(0, quarter * mel_rows), pl.ds(q * 2 * PIECE, 2 * PIECE)],
            load_sem.at[q],
        )
        for q in range(4)
    ]
    for load in loads[:4] + frame_loads:
        load.start()

    @pl.when(is_first)
    def _():
        @pl.loop(0, slots)
        def _(c):
            input_copy(c).start()

    @pl.when(is_last)
    def _():
        for load in loads[4:]:
            load.start()

    spare = lax.broadcasted_iota(jnp.int32, (EXT - mel_rows, 2 * half), 0)
    bias = jnp.broadcast_to(bias_in[...].astype(F32), (EXT - mel_rows, 2 * half))
    wc_ref[mel_rows:EXT] = jnp.where(spare == 0, bias, 0.0).astype(BF16)
    loads[0].wait()
    wd_t[...] = jnp.transpose(wd_ref[...])
    for load in loads[1:4]:
        load.wait()
    wr_t[...] = jnp.transpose(wr_ref[...])
    ws_t[...] = jnp.transpose(ws_ref[...])

    for load in frame_loads:
        load.wait()

    @pl.loop(0, quarter // 4)
    def _(group):
        for q in range(4):
            for part in range(4):
                row = group * 4 + part
                lanes = slice(q * 2 * PIECE, (q + 1) * 2 * PIECE)
                matrix = part_out[pl.ds(pl.multiple_of(row * mel_rows, 16), mel_rows), lanes]
                frames = dot(mel_ref[...], matrix)
                rows = pl.ds(q * quarter + row, micro, stride=mel_rows)
                for h in range(2):
                    up_buf[h, rows, :] = frames[:, h * PIECE : (h + 1) * PIECE]

    def condition(m):
        shape = (tab_ref.shape[1], 2 * PIECE)
        time = lax.broadcasted_iota(jnp.int32, shape, 1)
        speaker = jnp.where(time >= offs_ref[0, m], spk_ref[1, m], spk_ref[0, m])
        hot = jnp.where(lax.broadcasted_iota(jnp.int32, shape, 0) == speaker, 1.0, 0.0).astype(BF16)
        columns = dot(tab_ref[...], hot)
        ones = jnp.where(lax.broadcasted_iota(jnp.int32, (EXT - mel_rows, PIECE), 0) == 0, 1.0, 0.0)
        rows = pl.ds(pl.multiple_of(m * mel_rows, 16), mel_rows)
        for h in range(2):
            c = 2 * m + h
            value = up_buf[h, rows, :] + columns[:, h * PIECE : (h + 1) * PIECE]
            cond_ref[c] = jnp.concatenate([value, ones], axis=0).astype(BF16)
            cond_t[c] = jnp.transpose(cond_ref[c])

    @pl.when(is_first)
    def _():
        condition(0)

    @pl.when(s > 0)
    def _():
        @pl.loop(0, micro)
        def _(m):
            condition(m)

    @pl.when(s > 0)
    def _():
        acc[...] = jnp.zeros_like(acc)

    @pl.when(is_last)
    def _():
        for load in loads[4:]:
            load.wait()
        wp_t[...] = jnp.transpose(wp_ref[...])
        wk_t[...] = jnp.transpose(wk_ref[...])
        gx_buf[...] = jnp.zeros_like(gx_buf)

    pl.semaphore_wait(barrier, expected)

    def remote(src, dst, send_sem, recv_sem, dev_s, dev_z):
        return pltpu.make_async_remote_copy(
            src_ref=src,
            dst_ref=dst,
            send_sem=send_sem,
            recv_sem=recv_sem,
            device_id=(dev_s, dev_z),
            device_id_type=MESH,
        )

    ring = pieces > slots

    def send_of(semaphores, slot):
        return semaphores.at[slot if ring else 0]

    def x_copy(c):
        slot = lax.rem(c, slots)
        return remote(x_out.at[slot], x_buf.at[c], send_of(x_ss, slot), x_rs.at[c], s + 1, z)

    def k_copy(c):
        slot = lax.rem(c, slots)
        return remote(k_out.at[slot], sg_buf.at[c], send_of(k_ss, slot), k_rs.at[c], s + 1, z)

    def gx_copy(c):
        slot = lax.rem(c, slots)
        return remote(gx_out.at[slot], gx_buf.at[c], send_of(gx_ss, slot), gx_rs.at[c], s - 1, z)

    def gc_copy(c):
        slot = lax.rem(c, slots)
        return remote(gc_out.at[slot], gc_buf.at[c], send_of(gc_ss, slot), gc_rs.at[c], s - 1, z)

    def reuse(copy, c):
        if ring:

            @pl.when(c >= slots)
            def _():
                copy(c).wait_send()

    def drain(copy, whole):
        if ring:

            @pl.loop(0, slots)
            def _(c):
                copy(c).wait_send()

        else:
            whole().wait_send()

    chips = sections // 2
    far_chips = range(chips - 2, 0, -1)

    def gs_copy(c):
        return remote(sg_buf.at[c], sg_buf.at[c], gs_ss.at[0], gs_rs.at[c], s - 1, z)

    def gs_first(c):
        return remote(sg_buf.at[c], sg_buf.at[c], gs_ss.at[1], gs_rs.at[c], 1, z)

    def gs_chip(c, chip):
        return remote(sg_buf.at[c], sg_buf.at[c], gs_ss.at[1 + chip], gs_rs.at[c], 2 * chip + 1, z)

    def gs_whole(position):
        return remote(sg_buf, sg_buf, gs_ss.at[position], gs_rs.at[0], s - 1, z)

    def build_shift(m):
        dilation = dil_ref[0]
        middle = offs_ref[0, m]
        shape = (2 * PIECE, 2 * PIECE)

        def matrix(source, target):
            start = jnp.where(target >= middle, middle, 0)
            hit = (source == target - dilation) & (source >= start)
            return jnp.where(hit, 1.0, 0.0).astype(BF16)

        rows = lax.broadcasted_iota(jnp.int32, shape, 0)
        lanes = lax.broadcasted_iota(jnp.int32, shape, 1)
        shift_buf[...] = matrix(lanes, rows)
        shift_back[...] = matrix(rows, lanes)

    def pair(ref, first):
        return jnp.concatenate([ref[first], ref[first + 1]], axis=1)

    def put_pair(ref, first, value):
        for h in range(2):
            ref[first + h] = value[:, h * PIECE : (h + 1) * PIECE]

    def both(ref, first, parts):
        return jnp.concatenate([ref[first + h] for h in parts], axis=0)

    def put(ref, first, parts, value):
        for position, h in enumerate(parts):
            ref[first + h] = value[position * PIECE : (position + 1) * PIECE]

    def head(m, total):
        width = 2 * PIECE
        total = jnp.transpose(total.astype(BF16)).astype(F32) * head_scale
        sig_1 = sigmoid(total)
        act_1 = (total * sig_1).astype(BF16)
        slope_1 = sig_1 * (1.0 + total * (1.0 - sig_1)) * head_scale
        post = dot(wp_ref[...], act_1)
        sig_2 = sigmoid(post)
        act_2 = (post * sig_2).astype(BF16)
        slope_2 = sig_2 * (1.0 + post * (1.0 - sig_2))
        logits = dot(wk_ref[...], act_2)
        top = jnp.max(logits, axis=0, keepdims=True)
        expo = jnp.exp(logits - top)
        denominator = jnp.sum(expo, axis=0, keepdims=True)
        hit = tgt_ref[m] == lax.broadcasted_iota(jnp.int32, (classes, width), 0)
        picked = jnp.sum(jnp.where(hit, logits, 0.0), axis=0, keepdims=True)
        time = lax.broadcasted_iota(jnp.int32, (1, width), 1)

        def speaker_weight(which):
            count = cnt_ref[spk_ref[which, m]].astype(F32)
            return WEIGHT_SCALE * lax.rsqrt(jnp.full((1, width), count, F32))

        weight = jnp.where(time >= offs_ref[0, m], speaker_weight(1), speaker_weight(0))
        weight = jnp.where(time < offs_ref[1, m], weight, 0.0)
        grad_logits = (weight * (expo / denominator - jnp.where(hit, 1.0, 0.0))).astype(BF16)
        grad_post = (dot(wk_t[...], grad_logits) * slope_2).astype(BF16)
        grad_total = (dot(wp_t[...], grad_post) * slope_1).astype(BF16)
        put(sg_buf, 2 * m, (0, 1), jnp.transpose(grad_total))
        for h in (1, 0):
            c = 2 * m + h
            for chip in far_chips:
                gs_chip(c, chip).start()
            gs_copy(c).start()
            if feeder == sections - 1:
                gs_first(c).start()
        kept = 2 * lax.rem(m, keep)
        put_pair(gl_buf, kept, grad_logits)
        put_pair(a2_buf, kept, act_2)
        put_pair(gp_buf, kept, grad_post)
        put_pair(a1_buf, kept, act_1)
        loss_row = weight * (top + jnp.log(denominator) - picked)
        high = loss_row.astype(BF16)
        rest = loss_row - high.astype(F32)
        middle = rest.astype(BF16)
        low = (rest - middle.astype(F32)).astype(BF16)
        row = lax.broadcasted_iota(jnp.int32, (EXT, width), 0)
        message = jnp.where(row == mel_rows + 2, high.astype(F32), 0.0)
        message = jnp.where(row == mel_rows + 3, middle.astype(F32), message)
        message = jnp.where(row == mel_rows + 4, low.astype(F32), message)
        put_pair(gc_buf, 2 * m, message.astype(BF16))

    def forward(m, parts):
        high = len(parts) * PIECE
        for h in parts:
            c = 2 * m + h

            @pl.when(is_first)
            def _():
                input_copy(c).wait()
                x_buf[c] = jnp.transpose(inp_buf[lax.rem(c, slots)])
                if ring:

                    @pl.when(c + slots < pieces)
                    def _():
                        input_copy(c + slots).start()

            @pl.when(s > 0)
            def _():
                x_copy(c).wait_recv()

        x = both(x_buf, 2 * m, parts)
        if parts == (0,):
            prev = dot(shift_buf[0:PIECE, 0:PIECE], x)
        elif parts == (1,):
            prev = dot(shift_buf[PIECE : 2 * PIECE, :], both(x_buf, 2 * m, (0, 1)))
        else:
            prev = dot(shift_buf[...], x)
        gate = (
            dot(x, wd_t[res : 2 * res])
            + dot(both(cond_t, 2 * m, parts), wc_ref[...])
            + dot(prev.astype(BF16), wd_t[0:res])
        )
        th = jnp.tanh(gate[:, 0:half])
        sg = sigmoid(gate[:, half : 2 * half])
        gate_buf[0:high, 0:half] = th
        gate_buf[0:high, half : 2 * half] = sg
        put(hid_buf, 2 * m, parts, (th * sg).astype(BF16))

    def forward_rest(m, parts):
        high = len(parts) * PIECE
        th = gate_buf[0:high, 0:half]
        sg = gate_buf[0:high, half : 2 * half]
        put(d1_buf, 2 * m, parts, (sg * (1.0 - th * th)).astype(BF16))
        put(d2_buf, 2 * m, parts, (th * sg * (1.0 - sg)).astype(BF16))

    def forward_piece(m, h):
        c = 2 * m + h
        forward(m, (h,))
        reuse(x_copy, c)
        out = (x_buf[c].astype(F32) + dot(hid_buf[c], wr_t[...])) * HALF_ROOT
        x_out[lax.rem(c, slots)] = out.astype(BF16)
        x_copy(c).start()
        gh_buf[...] = dot(hid_buf[c], ws_t[...])
        forward_rest(m, (h,))

        @pl.when(s > 0)
        def _():
            k_copy(c).wait_recv()
            gh_buf[...] += sg_buf[c].astype(F32)

        reuse(k_copy, c)
        k_out[lax.rem(c, slots)] = gh_buf[...].astype(BF16)
        k_copy(c).start()

    def forward_head(m):
        forward(m, (0, 1))
        total = dot(both(hid_buf, 2 * m, (0, 1)), ws_t[...])
        for h in (0, 1):
            k_copy(2 * m + h).wait_recv()
        head(m, total + both(sg_buf, 2 * m, (0, 1)).astype(F32))
        forward_rest(m, (0, 1))

    def grad_field(m, parts, grad_hidden):
        kept = 2 * lax.rem(m, keep)
        grad_gate = jnp.concatenate(
            [
                grad_hidden * both(d1_buf, 2 * m, parts).astype(F32),
                grad_hidden * both(d2_buf, 2 * m, parts).astype(F32),
            ],
            axis=1,
        ).astype(BF16)
        put(gg_buf, kept, parts, grad_gate)
        if parts == (1,):
            back = dot(shift_back[PIECE:, PIECE:], grad_gate)
        elif parts == (0,):
            back = dot(shift_back[0:PIECE, :], jnp.concatenate([grad_gate, gg_buf[kept + 1]], axis=0))
        else:
            back = dot(shift_back[...], grad_gate)
        return dot(grad_gate, wd_ref[:, res : 2 * res]) + dot(back.astype(BF16), wd_ref[:, 0:res])

    def cond_message(m, h):
        kept = 2 * lax.rem(m, keep)
        row = lax.broadcasted_iota(jnp.int32, (EXT, PIECE), 0)
        own = jnp.where(row < mel_rows, dot_nt(wc_ref[...], gg_buf[kept + h]), 0.0)
        return own + gc_buf[2 * m + h].astype(F32)

    def backward_piece(m, h):
        c = 2 * m + h
        gs_copy(c).wait_recv()

        @pl.when(lax.rem(s, 2) == 1)
        def _():
            gs_copy(c).start()

        if feeder < sections - 1:

            @pl.when(s == feeder)
            def _():
                gs_first(c).start()

        gh_buf[...] = dot(sg_buf[c], ws_ref[...])
        gx_copy(c).wait_recv()
        grad_hidden = gh_buf[...] + HALF_ROOT * dot(gx_buf[c], wr_ref[...])
        grad_x = (HALF_ROOT * gx_buf[c].astype(F32) + grad_field(m, (h,), grad_hidden)).astype(BF16)

        @pl.when(s > 0)
        def _():
            reuse(gx_copy, c)
            gx_out[lax.rem(c, slots)] = grad_x
            gx_copy(c).start()

        @pl.when(is_first)
        def _():
            inp_buf[lax.rem(c, slots)] = jnp.transpose(grad_x)

    def backward_message(m, h):
        c = 2 * m + h
        gc_copy(c).wait_recv()
        message = cond_message(m, h)

        @pl.when(s > 0)
        def _():
            reuse(gc_copy, c)
            gc_out[lax.rem(c, slots)] = message.astype(BF16)
            gc_copy(c).start()

        @pl.when(is_first)
        def _():
            gc_buf[c, 0:mel_rows, :] = message[0:mel_rows].astype(BF16)
            tail = message[mel_rows:EXT]
            if h == 0:
                frame = lax.broadcasted_iota(jnp.int32, mel_ref.shape, 0) == m
                extra_buf[0:1, 0:mel_rows] = jnp.sum(
                    jnp.where(frame, mel_ref[...].astype(F32), 0.0), axis=0, keepdims=True
                )
                lane = lax.broadcasted_iota(jnp.int32, (1, PIECE), 1)
                ids = jnp.where(lane == 0, spk_ref[0, m], 0)
                ids = jnp.where(lane == 1, spk_ref[1, m], ids)
                ids = jnp.where(lane == 2, offs_ref[0, m], ids)
                extra_buf[1:2, :] = ids.astype(F32)
                tail = tail + extra_buf[...]
            gc_buf[c, mel_rows:EXT, :] = tail.astype(BF16)

    def backward_pair(m):
        for h in (1, 0):
            c = 2 * m + h
            reuse(gx_copy, c)
            grad_hidden = dot(sg_buf[c], ws_ref[...])
            gx_out[lax.rem(c, slots)] = grad_field(m, (h,), grad_hidden).astype(BF16)
            gx_copy(c).start()
        for h in (1, 0):
            c = 2 * m + h
            reuse(gc_copy, c)
            gc_out[lax.rem(c, slots)] = cond_message(m, h).astype(BF16)
            gc_copy(c).start()

    def add_halves(first_row, value):
        rows = value.shape[0] // 2
        acc[first_row : first_row + rows, 0:half] += value[0:rows]
        acc[first_row : first_row + rows, half : 2 * half] += value[rows : 2 * rows]

    small_row = 2 * half + EXT

    def small_gradients(m):
        parts = (0, 1)
        hidden = both(hid_buf, 2 * m, parts)

        @pl.when(s < sections - 1)
        def _():
            add_halves(small_row, HALF_ROOT * dot_tn(both(gx_buf, 2 * m, parts), hidden))

        add_halves(small_row + half // 2, dot_tn(both(sg_buf, 2 * m, parts), hidden))

        @pl.when(is_last)
        def _():
            kept = 2 * lax.rem(m, keep)
            add_halves(main_rows, dot_nt(pair(gp_buf, kept), pair(a1_buf, kept)))
            add_halves(main_rows + half // 2, dot_nt(pair(gl_buf, kept), pair(a2_buf, kept)))

    def large_gradients(m):
        parts = (0, 1)
        grad_gate = both(gg_buf, 2 * lax.rem(m, keep), parts)
        x = both(x_buf, 2 * m, parts)
        prev = dot(shift_buf[...], x).astype(BF16)
        acc[0 : 2 * half, :] += dot_tn(grad_gate, jnp.concatenate([prev, x], axis=1))
        acc[2 * half : small_row, :] += dot(pair(cond_ref, 2 * m), grad_gate)

    def samples(ref):
        return ref[...].reshape(pieces * PIECE, ref.shape[2])

    def by_channel(ref):
        return jnp.concatenate([ref[c] for c in range(pieces)], axis=1)

    def set_halves(first_row, value):
        rows = value.shape[0] // 2
        acc[first_row : first_row + rows, 0:half] = value[0:rows]
        acc[first_row : first_row + rows, half : 2 * half] = value[rows : 2 * rows]

    def all_small_gradients():
        @pl.when(is_last)
        def _():
            set_halves(main_rows, dot_nt(by_channel(gp_buf), by_channel(a1_buf)))
            set_halves(main_rows + half // 2, dot_nt(by_channel(gl_buf), by_channel(a2_buf)))

        hidden = samples(hid_buf)
        set_halves(small_row + half // 2, dot_tn(samples(sg_buf), hidden))

        @pl.when(s < sections - 1)
        def _():
            set_halves(small_row, HALF_ROOT * dot_tn(samples(gx_buf), hidden))

    def all_large_gradients():
        @pl.loop(0, micro)
        def _(m):
            build_shift(m)
            put(d1_buf, 2 * m, (0, 1), dot(shift_buf[...], both(x_buf, 2 * m, (0, 1))).astype(BF16))

        grad_gate = samples(gg_buf)
        acc[0 : 2 * half, 0:res] = dot_tn(grad_gate, samples(d1_buf))
        acc[0 : 2 * half, res : 2 * res] = dot_tn(grad_gate, samples(x_buf))
        acc[2 * half : small_row, :] = dot(by_channel(cond_ref), grad_gate)

    def gin_rows(other, group):
        return remote(
            inp_buf.at[:, pl.ds(pl.multiple_of(other * share, share), share), :],
            gin_buf.at[pl.ds(pl.multiple_of(group * slots, slots), slots)],
            gin_ss.at[0],
            gin_rs.at[0],
            other,
            z,
        )

    def gin_sent():
        return remote(
            inp_buf.at[:, share:res, :], inp_buf.at[:, share:res, :], gin_ss.at[0], gin_rs.at[0], 1, z
        )

    def gin_arrived():
        return remote(gin_buf, gin_buf, gin_ss.at[0], gin_rs.at[0], 1, z)

    def hand_out(group):
        @pl.loop(1, sections)
        def _(other):
            gin_rows(other, group).start()

        gin_buf[pl.ds(pl.multiple_of(group * slots, slots), slots)] = inp_buf[:, 0:share, :]

    def own_local():
        return pltpu.make_async_copy(gc_buf, o_g.at[z], loc_sem.at[0])

    def own_hub():
        return remote(gc_buf, o_g.at[z], gown_ss.at[0], g_rs.at[z], hub, z)

    def part_along(j, step):
        sem = gpeer_ss.at[j if step > 0 else groups + j]
        return remote(o_g.at[j], o_g.at[j], sem, g_rs.at[j], s, z + step)

    def part_chip(j, chip):
        return remote(o_g.at[j], o_g.at[j], ghub_ss.at[j, chip], g_rs.at[j], 2 * chip, z)

    def part_next(j):
        return remote(o_g.at[j], o_g.at[j], gnext_ss.at[j], g_rs.at[j], s + 1, z)

    def spread(j):
        part_next(j).start()

        @pl.loop(0, sections // 2 - 1)
        def _(chip):
            @pl.when((chip > 0) | (z != j))
            def _():
                part_chip(j, chip).start()

    @pl.when(is_last)
    def _():
        @pl.loop(0, micro)
        def _(m):
            build_shift(m)
            forward_head(m)
            backward_pair(m)
            if keep < micro:
                small_gradients(m)
                large_gradients(m)

    roomy = keep == micro
    swings = (s == sections - 2) if roomy else False
    late = (s >= sections - 2) if roomy else is_last

    @pl.loop(0, 3 * micro)
    def _(step):
        after = step - micro
        odd = lax.rem(step, 2) == 1
        forth = step < micro
        back = jnp.where(late, (after >= 0) & (after < micro), (after >= 0) & (lax.rem(after, 2) == 0))
        m = jnp.where(forth, step, jnp.where(late, lax.rem(step, micro), after // 2))
        if roomy:
            turning = swings & (step < 2 * micro)
            end = step == 2 * micro - 1
            swing_forth = (step == 0) | (odd & jnp.logical_not(end))
            forth = jnp.where(turning, swing_forth, forth)
            back = jnp.where(turning, jnp.logical_not(swing_forth), back)
            swing_m = jnp.where(swing_forth, (step + 1) // 2, jnp.where(end, micro - 1, step // 2 - 1))
            m = jnp.where(turning, swing_m, m)
        build_shift(m)

        @pl.when(forth & is_first & (m > 0))
        def _():
            condition(m)

        @pl.when(forth & jnp.logical_not(is_last))
        def _():
            forward_piece(m, 0)
            forward_piece(m, 1)

        @pl.when(is_first & (step == micro))
        def _():
            acc[...] = jnp.zeros_like(acc)
            extra_buf[...] = jnp.zeros_like(extra_buf)

        @pl.when(back & jnp.logical_not(is_last))
        def _():
            if ring:

                @pl.when(is_first & (m > 0))
                def _():
                    gin_sent().wait_send()

            backward_piece(m, 1)
            backward_piece(m, 0)
            backward_message(m, 1)
            backward_message(m, 0)

            @pl.when(is_first & (lax.rem(2 * m + 2, slots) == 0))
            def _():
                hand_out((2 * m + 2) // slots - 1)

            @pl.when(is_first & (m == micro - 1))
            def _():
                own_hub().start()
                own_local().start()

        @pl.when(jnp.logical_not(forth | back | late))
        def _():
            small_gradients(m)

            @pl.when(m < micro - 1)
            def _():
                large_gradients(m)

    if roomy:

        @pl.when(late)
        def _():
            all_small_gradients()

    @pl.when(is_first)
    def _():
        own_local().wait()

    left = z < groups // 2
    inward = jnp.where(left, z + 1, z - 1)
    outward = jnp.where(left, z - 1, z + 1)
    is_edge = (z == 0) | (z == groups - 1)
    is_mid = (z == groups // 2 - 1) | (z == groups // 2)
    distance = jnp.where(left, groups // 2 - 1 - z, z - groups // 2)
    lag = LAG * (2 * distance + 1) + 8 * distance
    base = jnp.where(is_last, main_blocks + head_blocks, main_blocks)
    helped = 2 * len(exports)
    gives = (s < helped) if exports else False
    takes = ((s >= helper) & (s < helper + helped)) if exports else False
    moved = 0
    for chip, amount in enumerate(exports):
        moved = jnp.where(lax.rem(s, helper) // 2 == chip, amount, moved)
    count = base - jnp.where(gives, moved, 0) + jnp.where(takes, moved, 0)

    all_blocks = main_blocks + head_blocks
    taken_at = base - 50

    def block_of(i):
        j = jnp.where(takes & (i >= taken_at + moved), i - moved, i)
        heads = jnp.where(is_last, head_blocks, 0)
        own = jnp.where(j < heads, j + main_blocks, lax.rem(j - heads + small_row // BLOCK, main_blocks))
        return jnp.where(takes & (j == i) & (i >= taken_at), i - taken_at + all_blocks, own)

    def rows_of(b):
        return pl.ds(pl.multiple_of(b * BLOCK, BLOCK), BLOCK)

    cycle = zp_rs.shape[0]

    def swap_copy(i):
        rows = rows_of(block_of(i))
        return remote(part_out.at[rows], o_acc.at[rows], zi_ss.at[0], zt_rs.at[lax.rem(i, cycle)], s, inward)

    def part_copy(i):
        rows = rows_of(block_of(i))
        return remote(part_out.at[rows], part_in.at[rows], zi_ss.at[0], zp_rs.at[lax.rem(i, cycle)], s, inward)

    def total_copy(i):
        rows = rows_of(block_of(i))
        return remote(o_acc.at[rows], o_acc.at[rows], zo_ss.at[0], zt_rs.at[lax.rem(i, cycle)], s, outward)

    def head_rows_of(j):
        start = main_rows + j * HEAD_GROUP * BLOCK
        return pl.ds(pl.multiple_of(start, BLOCK), HEAD_GROUP * BLOCK)

    def head_copy(j):
        rows = head_rows_of(j)
        return remote(o_acc.at[rows], o_acc.at[rows], hd_ss.at[0], hd_rs.at[j], s - 1, z)

    def send_part(i):
        rows = rows_of(block_of(i))

        @pl.when(is_edge)
        def _():
            part_out[rows, :] = acc[rows, :].astype(BF16)

        @pl.when(jnp.logical_not(is_edge))
        def _():
            part_copy(i).wait_recv()
            part_out[rows, :] = (acc[rows, :] + part_in[rows, :].astype(F32)).astype(BF16)

        @pl.when(is_mid)
        def _():
            swap_copy(i).start()

        @pl.when(jnp.logical_not(is_mid))
        def _():
            part_copy(i).start()

    def keep_rows(rows):
        return pltpu.make_async_copy(o_acc.at[rows], o_sum.at[rows], out_sem.at[0])

    def finish_part(i):
        rows = rows_of(block_of(i))
        swap_copy(i).wait_recv()

        @pl.when(is_mid)
        def _():
            o_acc[rows, :] = (part_out[rows, :].astype(F32) + o_acc[rows, :].astype(F32)).astype(BF16)

        @pl.when(jnp.logical_not(is_edge))
        def _():
            total_copy(i).start()

        @pl.when(block_of(i) < all_blocks)
        def _():
            keep_rows(rows).start()

    def given_rows(amount):
        return pl.ds(small_row - amount * BLOCK, amount * BLOCK)

    def taken_rows(amount):
        return pl.ds(main_rows + head_rows, amount * BLOCK)

    def give_copy(amount):
        target = taken_buf.at[0 : amount * BLOCK]
        return remote(part_out.at[given_rows(amount)], target, give_ss.at[0], give_rs.at[0], s + helper, z)

    def return_copy(amount):
        source, target = o_acc.at[taken_rows(amount)], o_acc.at[given_rows(amount)]
        return remote(source, target, give_ss.at[1], give_rs.at[1], s - helper, z)

    def each_export(cond, act):
        for chip, amount in enumerate(exports):

            @pl.when(cond & (lax.rem(s, helper) // 2 == chip))
            def _():
                act(amount)

    def give(amount):
        part_out[given_rows(amount), :] = acc[given_rows(amount), :].astype(BF16)
        give_copy(amount).start()

    def take(amount):
        give_copy(amount).wait_recv()
        acc[taken_rows(amount), :] = taken_buf[0 : amount * BLOCK].astype(F32)

    def rest_of_gradients():
        @pl.when(jnp.logical_not(late))
        def _():
            build_shift(micro - 1)
            large_gradients(micro - 1)

        if roomy:

            @pl.when(late)
            def _():
                all_large_gradients()

        each_export(gives, give)

    last_step = count + lag - 1
    head_at = lag + 4 + HEAD_GROUP
    own_at = jnp.minimum(48 + 18 * distance, last_step)
    rest_at = jnp.minimum(88 + 9 * (s // 2) + 18 * distance, last_step)

    @pl.loop(0, count + lag)
    def _(i):
        @pl.when(i == count - 1)
        def _():
            @pl.when(s > 0)
            def _():
                gin_arrived().wait_recv()

            for c in range(pieces):
                lanes = pl.ds(c * PIECE, PIECE)
                pltpu.make_async_copy(gin_buf.at[c], o_gin.at[:, lanes], out_sem.at[1]).start()

        @pl.when(i == LARGE_AT)
        def _():
            rest_of_gradients()

        if exports:

            each_export(takes & (i == taken_at), take)

        @pl.when(i < count)
        def _():
            send_part(i)

        @pl.when(i >= lag)
        def _():
            finish_part(i - lag)
            b = block_of(i - lag)

            in_group = b - main_blocks

            @pl.when((b >= main_blocks) & (b < all_blocks) & (lax.rem(in_group, HEAD_GROUP) == HEAD_GROUP - 1))
            def _():
                head_copy(in_group // HEAD_GROUP).start()

            if exports:

                each_export(b == all_blocks + moved - 1, lambda amount: return_copy(amount).start())

        since = i - head_at

        @pl.when(
            jnp.logical_not(is_last) & (since >= 0) & (since < head_blocks) & (lax.rem(since, HEAD_GROUP) == 0)
        )
        def _():
            j = since // HEAD_GROUP
            head_copy(j).wait_recv()
            keep_rows(head_rows_of(j)).start()

            @pl.when(s > 0)
            def _():
                head_copy(j).start()

        for hop in range(groups):

            @pl.when(is_hub & (i == jnp.minimum(own_at + 14 * hop, last_step)))
            def _():
                def pass_on(j, step, known, far):
                    @pl.when(known)
                    def _():
                        if hop:
                            part_along(j, 1).wait_recv()
                            spread(j)

                        @pl.when(far)
                        def _():
                            part_along(j, step).start()

                if hop == 0:
                    own_hub().wait_recv()
                    spread(z)
                pass_on(z - hop, 1, z >= hop, z < groups - 1)
                pass_on(z + hop, -1, z + hop < groups, z > 0)

        @pl.when((lax.rem(s, 2) == 0) & jnp.logical_not(is_hub) & (i == rest_at))
        def _():
            for j in range(groups):

                @pl.when((z != j) | (s > 0))
                def _():
                    part_next(j).wait_recv()

                part_next(j).start()

    pltpu.make_async_copy(gin_buf, gin_buf, out_sem.at[1]).wait()

    @pl.when(is_first)
    def _():
        own_hub().wait_send()
        gin_sent().wait_send()

    @pl.when(is_hub)
    def _():
        for j in range(groups):

            @pl.when((j <= z) & (z < groups - 1))
            def _():
                part_along(j, 1).wait_send()

            @pl.when((j >= z) & (z > 0))
            def _():
                part_along(j, -1).wait_send()

            @pl.loop(0, sections // 2 - 1)
            def _(chip):
                @pl.when((chip > 0) | (z != j))
                def _():
                    part_chip(j, chip).wait_send()

    for j in range(groups):

        @pl.when(lax.rem(s, 2) == 0)
        def _():
            part_next(j).wait_send()

        @pl.when(lax.rem(s, 2) == 1)
        def _():
            part_next(j).wait_recv()

    if exports:

        def returned(amount):
            return_copy(amount).wait_recv()
            keep_rows(given_rows(amount)).start()
            give_copy(amount).wait_send()

        each_export(gives, returned)
        each_export(takes, lambda amount: return_copy(amount).wait_send())

    keep_rows(pl.ds(0, main_rows + head_rows)).wait()

    def sum_sent(rows):
        remote(part_out.at[rows], part_out.at[rows], zi_ss.at[0], zp_rs.at[0], s, inward).wait_send()

        @pl.when(jnp.logical_not(is_edge))
        def _():
            remote(o_acc.at[rows], o_acc.at[rows], zo_ss.at[0], zt_rs.at[0], s, outward).wait_send()

    if exports:
        each_export(gives, lambda amount: sum_sent(pl.ds(0, main_rows - amount * BLOCK)))
        each_export(takes & jnp.logical_not(is_last), lambda amount: sum_sent(pl.ds(0, main_rows + amount * BLOCK)))

    @pl.when(is_last)
    def _():
        last_takes = exports[-1] if helper + helped == sections and exports else 0
        sum_sent(pl.ds(0, main_rows + head_rows + last_takes * BLOCK))

    @pl.when(jnp.logical_not(is_last | gives | takes))
    def _():
        sum_sent(pl.ds(0, main_rows))

    @pl.when(jnp.logical_not(is_last))
    def _():
        drain(x_copy, lambda: remote(x_out, x_out, x_ss.at[0], x_rs.at[0], s + 1, z))
        drain(k_copy, lambda: remote(k_out, k_out, k_ss.at[0], k_rs.at[0], s + 1, z))

    @pl.when(s > 0)
    def _():
        rows = pl.ds(main_rows, head_rows)
        remote(o_acc.at[rows], o_acc.at[rows], hd_ss.at[0], hd_rs.at[0], s - 1, z).wait_send()
        drain(gx_copy, lambda: remote(gx_out, gx_out, gx_ss.at[0], gx_rs.at[0], s - 1, z))
        drain(gc_copy, lambda: remote(gc_out, gc_out, gc_ss.at[0], gc_rs.at[0], s - 1, z))

    @pl.when(lax.rem(s, 2) == 1)
    def _():
        gs_whole(0).wait_send()

    @pl.when(is_last)
    def _():
        for chip in far_chips:
            gs_whole(1 + chip).wait_send()

    @pl.when(s == feeder)
    def _():
        gs_whole(1).wait_send()


def run_step(dims, tables, arrays, weights):
    sections, groups, micro, res, half, classes, slots, keep, mel_rows = dims
    pieces = 2 * micro
    rows = 2 * half + EXT + half + half // 2 + classes // 2
    head_blocks = (half // 2 + classes // 2) // BLOCK
    share = res // sections
    smem = pl.BlockSpec(memory_space=pltpu.SMEM)
    vmem = pl.BlockSpec(memory_space=pltpu.VMEM)
    anywhere = pl.BlockSpec(memory_space=pl.ANY)
    dma = pltpu.SemaphoreType.DMA

    def tile(*shape, dtype=BF16):
        return pltpu.VMEM(shape, dtype)

    distance = groups // 2 - 1
    cycle = max(LAG * (2 * distance + 1) + 8 * distance + 4, 2 * LAG + 4)
    sends = slots if pieces > slots else 1
    taken = max(exported_blocks(dims), default=0) * BLOCK

    scratch = [
        tile(pieces, PIECE, res),
        tile(pieces, PIECE, half),
        tile(pieces, PIECE, res),
        tile(pieces, EXT, PIECE),
        tile(pieces, PIECE, half),
        tile(pieces, PIECE, half),
        tile(pieces, PIECE, half),
        tile(slots, PIECE, res),
        tile(slots, PIECE, half),
        tile(slots, PIECE, res),
        tile(slots, EXT, PIECE),
        tile(2 * PIECE, 2 * half, dtype=F32),
        tile(PIECE, half, dtype=F32),
        tile(2 * keep, PIECE, 2 * half),
        tile(slots, res, PIECE),
        tile(2 * PIECE, 2 * PIECE),
        tile(2 * PIECE, 2 * PIECE),
        tile(pieces, EXT, PIECE),
        tile(pieces, PIECE, EXT),
        tile(EXT, 2 * half),
        tile(2 * half, 2 * res),
        tile(res, half),
        tile(half, half),
        tile(half, half),
        tile(classes, half),
        tile(2 * res, 2 * half),
        tile(half, res),
        tile(half, half),
        tile(half, half),
        tile(half, classes),
        tile(2 * keep, classes, PIECE),
        tile(2 * keep, half, PIECE),
        tile(2 * keep, half, PIECE),
        tile(2 * keep, half, PIECE),
        tile(rows + taken, WIDE, dtype=F32),
        tile(rows + taken, WIDE),
        tile(rows + taken, WIDE),
        tile(rows + taken, WIDE),
        tile(max(taken, 16), WIDE),
        tile(pieces, share, PIECE),
        tile(2, micro * mel_rows, PIECE, dtype=F32),
        tile(EXT - mel_rows, PIECE, dtype=F32),
        dma((slots,)),
        dma((10,)),
        dma((2,)),
        dma((1,)),
        dma((sends,)),
        dma((pieces,)),
        dma((sends,)),
        dma((pieces,)),
        dma((max(2, sections // 2),)),
        dma((pieces,)),
        dma((sends,)),
        dma((pieces,)),
        dma((sends,)),
        dma((pieces,)),
        dma((1,)),
        dma((1,)),
        dma((cycle,)),
        dma((cycle,)),
        dma((1,)),
        dma((head_blocks // HEAD_GROUP,)),
        dma((groups,)),
        dma((1,)),
        dma((2 * groups,)),
        dma((groups, sections // 2)),
        dma((groups,)),
        dma((1,)),
        dma((1,)),
        dma((2,)),
        dma((2,)),
    ]
    return pl.pallas_call(
        functools.partial(step_kernel, dims),
        out_shape=(
            jax.ShapeDtypeStruct((rows, WIDE), BF16),
            jax.ShapeDtypeStruct((groups, pieces, EXT, PIECE), BF16),
            jax.ShapeDtypeStruct((share, pieces * PIECE), BF16),
        ),
        in_specs=[smem] * 4 + [vmem] * 4 + [anywhere] * 8,
        out_specs=(anywhere, anywhere, anywhere),
        scratch_shapes=scratch,
        compiler_params=pltpu.CompilerParams(
            collective_id=0, has_side_effects=True, vmem_limit_bytes=63 * 2**20
        ),
        cost_estimate=pl.CostEstimate(flops=10**10, bytes_accessed=3 * 10**7, transcendentals=10**6),
        name="train_step",
    )(*tables, *arrays, *weights)


def finish_kernel(
    dims,
    sums,
    gin,
    shared_hbm,
    o_gin,
    o_dil,
    o_cond,
    o_res,
    o_skip,
    o_post,
    o_out,
    o_up,
    o_bias,
    o_table,
    o_loss,
    sums_buf,
    shared,
    dil_buf,
    cond_buf,
    res_buf,
    skip_buf,
    post_buf,
    out_buf,
    up_buf,
    field,
    mel_rows_buf,
    mel_columns,
    table,
    load_sem,
    store_sem,
):
    mel_rows, half = dims
    frames = shared.shape[0]
    first = 2 * half
    total_rows = sums_buf.shape[0]
    strips = ((0, half), (half, half), (first, total_rows - first))
    loads = [
        pltpu.make_async_copy(sums.at[pl.ds(row, rows), :], sums_buf.at[pl.ds(row, rows), :], load_sem.at[k])
        for k, (row, rows) in enumerate(strips)
    ]
    loads.append(pltpu.make_async_copy(shared_hbm, shared, load_sem.at[3]))
    for k in (0, 3, 1, 2):
        loads[k].start()
    stores = []

    def store(source, target):
        copy = pltpu.make_async_copy(source, target, store_sem.at[len(stores)])
        copy.start()
        stores.append(copy)

    store(gin, o_gin)

    def dilated(k):
        loads[k].wait()
        rows = pl.ds(k * half, half)
        dil_buf[rows, :] = sums_buf[rows, :].astype(F32)
        store(dil_buf.at[rows, :], o_dil.at[0, rows, :])

    dilated(0)

    loads[3].wait()

    def by_channel(f, loss):
        extra = shared[f, 0, mel_rows:EXT, :].astype(F32)
        mel_rows_buf[pl.ds(f, 1), :] = extra[0:1]
        for h in range(2):
            rows = pl.ds(pl.multiple_of(f * mel_rows, 16), mel_rows)
            field[h, rows, :] = shared[f, h, 0:mel_rows, :].astype(F32)
        return loss + extra + shared[f, 1, mel_rows:EXT, :].astype(F32)

    loss = lax.fori_loop(0, frames, by_channel, jnp.zeros((EXT - mel_rows, PIECE), F32))
    row = lax.broadcasted_iota(jnp.int32, loss.shape, 0)
    loss = jnp.where((row >= 2) & (row < 5), loss, 0.0)
    o_loss[...] = jnp.sum(jnp.sum(loss, axis=1, keepdims=True), axis=0, keepdims=True)
    mel_columns[...] = jnp.transpose(mel_rows_buf[...])[0:mel_rows].astype(BF16)

    parts = 4
    channels = mel_rows // parts

    def upsampling(part):
        @pl.loop(0, channels // 10)
        def _(group):
            for j in range(10):
                c = part * channels + group * 10 + j
                rows = pl.ds(c, frames, stride=mel_rows)
                matrix = jnp.concatenate([field[0, rows, :], field[1, rows, :]], axis=1)
                up_buf[c] = dot(mel_columns[...], matrix.astype(BF16))

        rows = pl.ds(part * channels, channels)
        store(up_buf.at[rows], o_up.at[rows])

    upsampling(0)
    upsampling(1)
    dilated(1)
    upsampling(2)
    upsampling(3)

    loads[2].wait()
    cond_buf[...] = sums_buf[first : first + mel_rows, :].astype(F32)
    o_bias[...] = sums_buf[first + mel_rows : first + EXT, :].astype(F32)[0:1]
    store(cond_buf, o_cond)
    row = first + EXT
    for buffer, target in ((res_buf, o_res), (skip_buf, o_skip), (post_buf, o_post), (out_buf, o_out)):
        rows = buffer.shape[1]
        buffer[0] = sums_buf[row : row + rows, 0:half].astype(F32)
        buffer[1] = sums_buf[row : row + rows, half : 2 * half].astype(F32)
        store(buffer, target)
        row += rows

    table[...] = jnp.zeros_like(table)
    time = lax.broadcasted_iota(jnp.int32, (2 * PIECE, PIECE), 0).astype(F32)
    number = lax.broadcasted_iota(jnp.int32, (2 * PIECE, PIECE), 1).astype(F32)

    @pl.loop(0, frames // 4)
    def _(group):
        grads, hots = [], []
        for k in range(4):
            f = group * 4 + k
            ids = shared[f, 0, mel_rows:EXT, :].astype(F32)[1:2]
            speaker = jnp.where(time >= ids[:, 2:3], ids[:, 1:2], ids[:, 0:1])
            hots.append(jnp.where(number == speaker, 1.0, 0.0).astype(BF16))
            grads += [shared[f, 0, 0:mel_rows, :], shared[f, 1, 0:mel_rows, :]]
        table[...] += dot(jnp.concatenate(grads, axis=1), jnp.concatenate(hots, axis=0))

    o_table[...] = table[:, 0 : o_table.shape[1]]
    for copy in stores:
        copy.wait()


def finish(sums, shared, grad_inputs, half, classes, mel_rows, speakers):
    frames = shared.shape[0]
    first = 2 * half
    vmem = pl.BlockSpec(memory_space=pltpu.VMEM)
    anywhere = pl.BlockSpec(memory_space=pl.ANY)
    large = (
        (first, WIDE),
        (mel_rows, WIDE),
        (2, half // 2, half),
        (2, half // 2, half),
        (2, half // 2, half),
        (2, classes // 2, half),
        (mel_rows, mel_rows, 2 * PIECE),
    )

    def f32(*shape):
        return jax.ShapeDtypeStruct(shape, F32)

    return pl.pallas_call(
        functools.partial(finish_kernel, (mel_rows, half)),
        out_shape=(
            jax.ShapeDtypeStruct(grad_inputs.shape, grad_inputs.dtype),
            f32(1, *large[0]),
            *[f32(*shape) for shape in large[1:]],
            f32(1, WIDE),
            f32(mel_rows, speakers),
            f32(1, 1),
        ),
        in_specs=[anywhere] * 3,
        out_specs=(anywhere,) * 8 + (vmem,) * 3,
        scratch_shapes=[
            pltpu.VMEM(sums.shape, BF16),
            pltpu.VMEM(shared.shape, BF16),
            *[pltpu.VMEM(shape, F32) for shape in large],
            pltpu.VMEM((2, frames * mel_rows, PIECE), F32),
            pltpu.VMEM((frames, PIECE), F32),
            pltpu.VMEM((mel_rows, frames), BF16),
            pltpu.VMEM((mel_rows, PIECE), F32),
            pltpu.SemaphoreType.DMA((4,)),
            pltpu.SemaphoreType.DMA((12,)),
        ],
        compiler_params=pltpu.CompilerParams(vmem_limit_bytes=62 * 2**20),
        name="finish",
    )(sums, grad_inputs, shared)


def local(
    inputs,
    targets,
    mel,
    speakers,
    speaker_sample_counts,
    segment_offsets,
    dilations,
    dilated_kernel,
    conditioning_projection,
    dilated_gate_bias,
    residual_projection,
    skip_projection,
    upsample_weight,
    speaker_table,
    first_output_projection,
    class_projection,
):
    sections = lax.axis_size("section")
    groups = lax.axis_size("dp")
    micro = segment_offsets.shape[0]
    res, tokens = inputs.shape
    length = tokens // micro
    mel_rows = mel.shape[0]
    hop = upsample_weight.shape[0]
    half = residual_projection.shape[2]
    classes = class_projection.shape[0]
    pieces = 2 * micro
    assert length == 2 * PIECE and hop == length and mel_rows + 16 == EXT and 2 * half == WIDE

    slots, keep = (pieces, micro) if pieces <= 8 else (2, 1)
    dims = (sections, groups, micro, res, half, classes, slots, keep, mel_rows)
    sums, shared, grad_inputs = run_step(
        dims,
        (dilations, segment_offsets.T, speakers.T, speaker_sample_counts),
        (
            targets.reshape(micro, 1, length),
            mel.T,
            speaker_table,
            dilated_gate_bias,
        ),
        (
            inputs,
            upsample_weight.transpose(1, 2, 0).reshape(mel_rows * mel_rows, hop),
            conditioning_projection[0].T,
            dilated_kernel[0],
            residual_projection[0],
            skip_projection[0],
            first_output_projection,
            class_projection,
        ),
    )
    shared = shared.reshape(groups * micro, 2, EXT, PIECE)
    grad_inputs, dil, cond, grad_res, grad_skip, post, out, up, bias, table, loss = finish(
        sums, shared, grad_inputs, half, classes, mel_rows, speaker_table.shape[1]
    )
    return (
        loss.reshape(()),
        grad_inputs,
        dil,
        cond.T[None],
        bias,
        grad_res.reshape(1, half, half),
        grad_skip.reshape(1, half, half),
        up.transpose(2, 0, 1),
        table,
        post.reshape(half, half),
        out.reshape(classes, half),
    )


def solution(mesh):
    return jax.shard_map(
        local,
        mesh=mesh,
        in_specs=(
            P(None, "dp"),
            P("dp"),
            P(None, "dp"),
            P("dp", None),
            P(),
            P("dp", None),
            P("section"),
            P("section", None, None),
            P("section", None, None),
            P("section", None),
            P("section", None, None),
            P("section", None, None),
            P(),
            P(),
            P(),
            P(),
        ),
        out_specs=(
            P(),
            P("section", "dp"),
            P("section", None, None),
            P("section", None, None),
            P("section", None),
            P("section", None, None),
            P("section", None, None),
            P(),
            P(),
            P(),
            P(),
        ),
        check_vma=False,
    )
```
